32 devices in a mesh: rep: 8 (over y, x, core), fsdp: 4 (over z).
Axes of the slice: x: 2, y: 2, z: 4, core: 2. Of those that a mesh axis runs over, the one named last changes fastest.
Arguments:
- tokens: bfloat16 [32768, 768], P(('rep', 'fsdp')), may hold values from -6 to 6
- prev_logits: bfloat16 [32768, 8], P(('rep', 'fsdp')), may hold values from -3 to 3
- out_grad: bfloat16 [32768, 768], P(('rep', 'fsdp')), may hold values from -6 to 6
- routes: int32 [32768, 2], P(('rep', 'fsdp')), may hold values from 0 to 7, all different within a row; in each aligned block of 1024 rows (0 to 1023, 1024 to 2047, ...) at most 384 rows name the same one
- doc_ids: int32 [32, 1024], P(('rep', 'fsdp')), may hold values from 0 to 5, never falling along the last dimension, each value on 1 to 512 neighbouring positions
- valid_mask: int32 [32, 1024], P(('rep', 'fsdp')), may hold values 0 or 1
- qkv_weight: bfloat16 [768, 2304], P('fsdp'), may hold values from -0.21875 to 0.21875
- proj_weight: bfloat16 [768, 768], P('fsdp'), may hold values from -0.875 to 0.875
- gain_attn: bfloat16 [768], P('fsdp'), may hold values from 0.5 to 1.5
- gain_ffn: bfloat16 [768], P('fsdp'), may hold values from 0.5 to 1.5
- router: bfloat16 [768, 8], P('fsdp'), may hold values from -0.15625 to 0.15625
- const_mix: bfloat16 [768, 4], P('fsdp'), may hold values from -0.21875 to 0.21875
- prev_mix: bfloat16 [8, 8], P('fsdp'), may hold values from -2 to 2
- const_vec: bfloat16 [768, 2], P('fsdp'), may hold values from -6 to 6
- expert_in: bfloat16 [768, 4, 4096], P('fsdp'), may hold values from -0.21875 to 0.21875
- expert_out: bfloat16 [2048, 4, 768], P('fsdp'), may hold values from -1 to 1
Outputs:
- layer_out: bfloat16 [32768, 768], P(('rep', 'fsdp'))
- input_grad: bfloat16 [32768, 768], P(('rep', 'fsdp'))
- qkv_grad: float32 [768, 2304], P('fsdp')
- proj_grad: float32 [768, 768], P('fsdp')
- gain_attn_grad: float32 [768], P('fsdp')
- gain_ffn_grad: float32 [768], P('fsdp')
- router_grad: float32 [768, 8], P('fsdp')
- const_mix_grad: float32 [768, 4], P('fsdp')
- prev_mix_grad: float32 [8, 8], P('fsdp')
- const_vec_grad: float32 [768, 2], P('fsdp')
- expert_in_grad: float32 [768, 4, 4096], P('fsdp')
- expert_out_grad: float32 [2048, 4, 768], P('fsdp')
The draws below stay inside these ranges and needn't reach their ends.
Inputs may be any that keep to these rules, and one draw needn't show every extreme that they name: `routes`: within the rows of one device no choice is named more than 384 times, a bound that some block reaches; the two choices of a row differ; choice 4 is the zero expert, 5 the copy expert, 6 and 7 the constant experts. `doc_ids`: within a sequence the ids never fall; a document has 1 to 512 positions, one exactly 512.
All inputs are finite; a program needn't handle non-finite values. No bound on the sum of `valid_mask` on one device may be relied on, other than what follows from the above.
Results may differ from the reference program's by a relative error of at most 0.015.
Values may be sent and summed in bfloat16 or wider, within the bound.
No kernel may reach another device: no remote copies, remote signals or barrier semaphores. Data moves between devices by JAX's collectives and lax.ppermute only.
A program may use at most 320 MiB of HBM per device.

```python
import math
import jax
import jax.numpy as jnp
import numpy as np
from jax import lax

D = 768
HEADS = 12
HDIM = 64
FF = 2048
EXPERTS = 4
NCH = 8
TOPK = 2
SEQ = 1024
DOCS = 6
SEQ_DEV = 1
TOK_DEV = 1024
CAP = 384
SEQS = 32
TOKENS = 32768


def place_ends(drawn, stream_key, smallest, high):
    dims = drawn.shape
    index_at = [jax.random.randint(jax.random.fold_in(stream_key, axis), (), 0, dims[axis]) for axis in range(len(dims))]
    drawn = drawn.at[tuple(index_at)].set(smallest)
    longest = dims.index(max(dims))
    index_at[longest] = (index_at[longest] + 1) % dims[longest]
    return drawn.at[tuple(index_at)].set(high)


def block_scale(rng, shape, split, low, high):
    def one(dim, shards_of):
        heights = jax.random.uniform(jax.random.fold_in(jax.random.fold_in(rng, 6), dim), (shards_of,), jnp.float32, low / len(split), high / len(split))
        return jnp.repeat(jnp.exp(heights), shape[dim] // shards_of).reshape((-1,) + (1,) * (len(shape) - dim - 1))

    level = one(*split[0])
    for cut in split[1:]:
        level = level * one(*cut)
    return level


def profile(amount, total, reach, skew):
    portions = [(1 << 20) // math.isqrt(grade ** skew) + 1 for grade in range(2, amount + 1)]
    rest, given = total - reach - (amount - 1), [1] * (amount - 1)
    while rest > 0:
        candidates = [i for i in range(amount - 1) if given[i] < reach]
        whole, remaining = sum([portions[i] for i in candidates]), rest
        for i in candidates:
            addition = min(reach - given[i], max(1, remaining * portions[i] // whole), rest)
            given[i] = given[i] + addition
            rest = rest - addition
    return np.array([reach] + given)


def uneven_parts(own_key, number_of, total, reach, skew):
    if number_of == 2:
        one = jax.random.randint(own_key, (), max(1, total - reach), min(reach, total - 1) + 1)
        return jnp.stack([one, total - one])
    lengths = jnp.asarray(profile(number_of, total, reach, skew), jnp.int32)
    couples = (number_of - 1) // 2
    donor, receiver = lengths[1:1 + 2 * couples:2], lengths[2:2 + 2 * couples:2]
    slack = jnp.minimum(donor - 1, reach - receiver)
    moved = jax.random.randint(jax.random.fold_in(own_key, 1), (couples,), 0, 1 << 20) % (slack + 1)
    lengths = lengths.at[1:1 + 2 * couples:2].set(donor - moved).at[2:2 + 2 * couples:2].set(receiver + moved)
    return lengths[jax.random.permutation(jax.random.fold_in(own_key, 2), number_of)]


def routed_block(key, own, number, rows, amount, top, limit, skew):
    ranking = jax.random.permutation(key, amount)
    crowded, common = shares(amount, rows * top, limit, skew, True), shares(amount, rows * top, limit, skew, False)
    places = jnp.arange(amount)

    def named(sizes, offset_by):
        used = int((sizes > 0).sum())
        fixed = max(1, used // 4)
        shifted = fixed + (places - fixed + offset_by * (used - fixed)) % max(1, amount - fixed)
        return jnp.zeros((amount,), jnp.int32).at[ranking[jnp.where(places < fixed, places, shifted)]].set(jnp.asarray(sizes, jnp.int32))

    sizes = jnp.where(number % 4 == 0, named(crowded, number // 4), named(common, number - number // 4 - 1))
    mixed = jax.random.permutation(jax.random.fold_in(own, 3), amount)
    donor, receiver = mixed[0:amount // 2 * 2:2], mixed[1:amount // 2 * 2:2]
    slack = jnp.minimum(sizes[donor] - 1, limit - sizes[receiver]) // 2
    slack = jnp.where((donor == ranking[0]) | (receiver == ranking[0]) | (sizes[receiver] == 0), 0, jnp.maximum(slack, 0))
    shifted = jax.random.randint(jax.random.fold_in(own, 4), (amount // 2,), 0, 1 << 20) % (slack + 1)
    sizes = sizes.at[donor].add(-shifted).at[receiver].add(shifted)
    items = jnp.searchsorted(jnp.cumsum(sizes), jnp.arange(rows * top), side="right").astype(jnp.int32)
    table = items.reshape(top, rows).T
    table = table[jax.random.permutation(jax.random.fold_in(own, 1), rows)]
    offset_by = jax.random.randint(jax.random.fold_in(own, 2), (rows, 1), 0, top)
    return jnp.take_along_axis(table, (jnp.arange(top)[None, :] + offset_by) % top, axis=1)


def shares(number_of, total, reach, slope, full):
    loads = [(1 << 20) // math.isqrt(grade ** slope) + 1 for grade in range(1, number_of + 1)]
    largest = reach if full else min(reach, max(-(-total // number_of), total * loads[0] // sum(loads)))
    least = 1 if total - largest >= number_of - 1 else 0
    given, spare = [largest] + [least] * (number_of - 1), total - largest - least * (number_of - 1)
    while spare > 0:
        movable = [i for i in range(1, number_of) if given[i] < largest] or [i for i in range(1, number_of) if given[i] < reach]
        mass, remaining = sum([loads[i] for i in movable]), spare
        for i in movable:
            addition = min(reach - given[i], max(1, remaining * loads[i] // mass), spare)
            given[i] = given[i] + addition
            spare = spare - addition
    return np.array(given)


def centred(key, dims, deviation, reach, split=(), held_as=jnp.bfloat16):
    result = jax.random.normal(key, dims, jnp.float32) * deviation
    if len(split) > 0:
        result = block_scale(key, dims, split, -0.22, 0.18) * result
    return jnp.clip(result, min=-reach, max=reach).astype(held_as)


def setup_inputs(seed: int = 0) -> dict:
    key_list = jax.random.split(jax.random.key(seed), 17)
    tokens = centred(key_list[0], (TOKENS, D), 1.0, 6.0, ((0, 32),))
    prev_logits = centred(key_list[1], (TOKENS, NCH), 0.5, 3.0, ((0, 32),))
    out_grad = centred(key_list[2], (TOKENS, D), 1.0, 6.0, ((0, 32),))
    routes_keys = jax.random.split(jax.random.fold_in(key_list[3], 1), TOKENS // TOK_DEV)
    routes_turns = jax.random.permutation(jax.random.fold_in(key_list[3], 3), TOKENS // TOK_DEV)
    routes = jax.vmap(lambda own, number: routed_block(jax.random.fold_in(key_list[3], 2), own, number, TOK_DEV, NCH, TOPK, CAP, 2))(routes_keys, routes_turns).reshape((TOKENS, TOPK))
    doc_ids = jax.vmap(lambda own: jnp.searchsorted(jnp.cumsum(uneven_parts(own, DOCS, SEQ, SEQ // 2, 2)), jnp.arange(SEQ), side="right"))(jax.random.split(key_list[4], SEQS)).reshape((SEQS, SEQ)).astype(jnp.int32)
    valid_mask = place_ends((jax.random.randint(key_list[5], (SEQS, SEQ), 0, 8) < 7).astype(jnp.int32), jax.random.fold_in(key_list[5], 1), 0, 1)
    qkv_weight = centred(key_list[6], (D, 3 * D), D ** -0.5, 0.21875, ((0, 4),))
    proj_weight = centred(key_list[7], (D, D), (D // 16) ** -0.5, 0.875, ((0, 4),))
    gain_attn = jnp.clip(1.0 + 0.1 * jax.random.normal(key_list[8], (D,), jnp.float32), 0.5, 1.5).astype(jnp.bfloat16)
    gain_ffn = jnp.clip(1.0 + 0.1 * jax.random.normal(key_list[9], (D,), jnp.float32), 0.5, 1.5).astype(jnp.bfloat16)
    router = centred(key_list[10], (D, NCH), (2 * D) ** -0.5, 0.15625, ((0, 4),))
    const_mix = centred(key_list[11], (D, 4), D ** -0.5, 0.21875, ((0, 4),))
    prev_mix = centred(key_list[12], (NCH, NCH), NCH ** -0.5, 2.0, ((0, 4),))
    const_vec = centred(key_list[13], (D, 2), 1.0, 6.0, ((0, 4),))
    expert_in = centred(key_list[14], (D, EXPERTS, 2 * FF), D ** -0.5, 0.21875, ((0, 4),))
    expert_out = centred(key_list[15], (FF, EXPERTS, D), (FF // 64) ** -0.5, 1.0, ((0, 4),))
    return {"tokens": tokens, "prev_logits": prev_logits, "out_grad": out_grad, "routes": routes, "doc_ids": doc_ids, "valid_mask": valid_mask, "qkv_weight": qkv_weight, "proj_weight": proj_weight, "gain_attn": gain_attn, "gain_ffn": gain_ffn, "router": router, "const_mix": const_mix, "prev_mix": prev_mix, "const_vec": const_vec, "expert_in": expert_in, "expert_out": expert_out}


@jax.custom_vjp
def low(v):
    return lax.optimization_barrier(v.astype(jnp.bfloat16)).astype(jnp.float32)

@jax.custom_vjp
def low_back(v):
    return v

def low_keep(v):
    return (low(v), None)

def low_pass(kept, grad):
    return (grad,)

def back_keep(v):
    return (v, None)

def back_low(kept, grad):
    return (low(grad),)
low.defvjp(low_keep, low_pass)
low_back.defvjp(back_keep, back_low)
highest = lax.Precision.HIGHEST
norm_eps = 1e-06

def rms_norm(values, gain_vec):
    inverse = lax.rsqrt(lax.optimization_barrier(jnp.mean(values * values, axis=-1, keepdims=True)) + norm_eps)
    return values * inverse * gain_vec[None, :]

def rope_tables(doc_ids):
    length = doc_ids.shape[1]
    places = jnp.arange(length, dtype=jnp.int32)
    changes = (doc_ids[:, 1:] != doc_ids[:, :-1]).astype(jnp.int32)
    starts = jnp.concatenate([jnp.ones_like(doc_ids[:, :1]), changes], axis=1)
    first_place = lax.cummax(jnp.where(starts > 0, places[None, :], 0), axis=1)
    offsets = (places[None, :] - first_place).reshape(-1).astype(jnp.float32)
    frequency = jnp.exp(jnp.arange(HDIM // 2, dtype=jnp.float32) * (-2.0 * math.log(10000.0) / HDIM))
    angles = offsets[:, None] * frequency[None, :]
    return (jnp.cos(angles), jnp.sin(angles))

def rotate(values, cosine_rows, sine_rows):
    row_count = values.shape[0]
    halves = values.reshape(row_count, HEADS, 2, HDIM // 2)
    first_half = halves[:, :, 0]
    second_half = halves[:, :, 1]
    cosine_b = cosine_rows[:, None, :]
    sine_b = sine_rows[:, None, :]
    turned = jnp.stack([first_half * cosine_b - second_half * sine_b, second_half * cosine_b + first_half * sine_b], axis=2)
    return turned.reshape(row_count, HEADS * HDIM)

def attention_mask(doc_ids, valid_mask):
    length = doc_ids.shape[1]
    places = jnp.arange(length, dtype=jnp.int32)
    same_doc = doc_ids[:, :, None] == doc_ids[:, None, :]
    causal = (places[:, None] >= places[None, :])[None]
    usable = (valid_mask[:, None, :] > 0) | (places[:, None] == places[None, :])[None]
    return same_doc & causal & usable

def expert_slots(routes):
    row_count = routes.shape[0]
    flat_routes = routes.reshape(-1).astype(jnp.int32)
    owners = jnp.arange(row_count * TOPK, dtype=jnp.int32) // TOPK
    one_hot = (flat_routes[:, None] == jnp.arange(NCH, dtype=jnp.int32)[None, :]).astype(jnp.int32)
    ranks = (lax.optimization_barrier(jnp.sum(jnp.cumsum(one_hot, axis=0) * one_hot, axis=1)) - 1).astype(jnp.int32)
    places = jnp.where(flat_routes < EXPERTS, flat_routes * CAP + ranks, EXPERTS * CAP).astype(jnp.int32)
    slot_token = jnp.full((EXPERTS * CAP + 1,), row_count, jnp.int32).at[places].set(owners)[:EXPERTS * CAP]
    return (slot_token, places)

def combine(small, prev_mix, const_vec, spread, residual, chosen, previous, routes):
    logits = small[:, :NCH] + jnp.dot(previous, prev_mix, precision=highest)
    probs = jax.nn.softmax(logits, axis=-1)
    gates = jnp.take_along_axis(probs, routes, axis=1)
    total = residual
    for column in range(TOPK):
        picked = routes[:, column:column + 1]
        branch = chosen[:, column] + jnp.where(picked == EXPERTS + 1, spread, 0.0)
        for const_index in range(2):
            mixing = jax.nn.softmax(small[:, NCH + 2 * const_index:NCH + 2 * const_index + 2], axis=-1)
            made = mixing[:, :1] * spread + mixing[:, 1:] * const_vec[:, const_index][None, :]
            branch = branch + jnp.where(picked == EXPERTS + 2 + const_index, made, 0.0)
        total = total + gates[:, column:column + 1] * branch
    return total

def layer_block(weights, block_items):
    qkv_weight, proj_weight, gain_attn, gain_ffn, router, const_mix, prev_mix, const_vec, expert_in, expert_out = weights
    token_rows, previous, routes, doc_ids, valid_mask = block_items
    row_count = token_rows.shape[0]
    seq_count = doc_ids.shape[0]
    cosine_rows, sine_rows = rope_tables(doc_ids)
    normed = low(rms_norm(token_rows, gain_attn))
    mixed = low_back(jnp.dot(normed, qkv_weight, precision=highest))
    queries = low(rotate(mixed[:, :D], cosine_rows, sine_rows))
    keys_rot = low(rotate(mixed[:, D:2 * D], cosine_rows, sine_rows))
    values = low(mixed[:, 2 * D:])
    shaped = (seq_count, SEQ, HEADS, HDIM)
    scores = jnp.einsum('bqhd,bkhd->bhqk', queries.reshape(shaped), keys_rot.reshape(shaped), precision=highest) * HDIM ** (-0.5)
    scores = low_back(scores)
    scores = jnp.where(attention_mask(doc_ids, valid_mask)[:, None], scores, -1e+30)
    weights_low = low(jax.nn.softmax(scores, axis=-1))
    context = jnp.einsum('bhqk,bkhd->bqhd', weights_low, values.reshape(shaped), precision=highest).reshape(row_count, D)
    context = low(low_back(context))
    residual = token_rows + low_back(jnp.dot(context, proj_weight, precision=highest))
    spread = rms_norm(residual, gain_ffn)
    spread_low = low(spread)
    small = low_back(jnp.dot(spread_low, jnp.concatenate([router, const_mix], axis=1), precision=highest))
    slot_token, places = expert_slots(routes)
    padded = jnp.concatenate([spread_low, jnp.zeros((1, D), jnp.float32)], axis=0)
    taken = padded[slot_token].reshape(EXPERTS, CAP, D)
    hidden_pair = low_back(jnp.einsum('ecd,def->ecf', taken, expert_in, precision=highest))
    activated = low(jax.nn.silu(hidden_pair[..., :FF]) * hidden_pair[..., FF:])
    returned = low_back(jnp.einsum('ecf,fed->ecd', activated, expert_out, precision=highest))
    flat_out = jnp.concatenate([returned.reshape(EXPERTS * CAP, D), jnp.zeros((1, D), jnp.float32)], axis=0)
    chosen = flat_out[places].reshape(row_count, TOPK, D)
    return combine(small, prev_mix, const_vec, spread, residual, chosen, previous, routes)

def reference(tokens, prev_logits, out_grad, routes, doc_ids, valid_mask, qkv_weight, proj_weight, gain_attn, gain_ffn, router, const_mix, prev_mix, const_vec, expert_in, expert_out):
    blocks = tokens.shape[0] // TOK_DEV
    params = (qkv_weight.astype(jnp.float32), proj_weight.astype(jnp.float32), gain_attn.astype(jnp.float32), gain_ffn.astype(jnp.float32), router.astype(jnp.float32), const_mix.astype(jnp.float32), prev_mix.astype(jnp.float32), const_vec.astype(jnp.float32), expert_in.astype(jnp.float32), expert_out.astype(jnp.float32))
    others = (prev_logits.astype(jnp.float32).reshape(blocks, TOK_DEV, NCH), routes.reshape(blocks, TOK_DEV, TOPK), doc_ids.reshape(blocks, SEQ_DEV, SEQ), valid_mask.reshape(blocks, SEQ_DEV, SEQ))
    checked = jax.checkpoint(layer_block)

    def forward(weights, token_blocks):

        def scan_step(carried, block_items):
            return (carried, checked(weights, block_items))
        unused, outputs = lax.scan(scan_step, jnp.zeros((), jnp.float32), (token_blocks,) + others)
        return outputs
    token_blocks = tokens.astype(jnp.float32).reshape(blocks, TOK_DEV, D)
    outputs, pullback = jax.vjp(forward, params, token_blocks)
    weight_grads, input_grads = pullback(out_grad.astype(jnp.float32).reshape(blocks, TOK_DEV, D))
    return (outputs.reshape(-1, D).astype(jnp.bfloat16), input_grads.reshape(-1, D).astype(jnp.bfloat16), weight_grads[0], weight_grads[1], weight_grads[2], weight_grads[3], weight_grads[4], weight_grads[5], weight_grads[6], weight_grads[7], weight_grads[8], weight_grads[9])
```

```python
from functools import partial
import math

import jax
import jax.numpy as jnp
from jax import lax
from jax.experimental import pallas as pl
from jax.experimental.pallas import tpu as pltpu
from jax.sharding import PartitionSpec as P

D = 768
HEADS = 12
HDIM = 64
EXPERTS = 4
NCH = 8
CAP = 384
LANES = 128
QB = 256
REACH = 512
VMEM_BYTES = 58 * 1024 * 1024
EPS = 1e-06
f32 = jnp.float32
bf16 = jnp.bfloat16

NT = (((1,), (1,)), ((), ()))
TN = (((0,), (0,)), ((), ()))


def mm(a, b):
    return jnp.dot(a, b, preferred_element_type=f32)


def mm_nt(a, b):
    return lax.dot_general(a, b, NT, preferred_element_type=f32)


def mm_tn(a, b):
    return lax.dot_general(a, b, TN, preferred_element_type=f32)


def params(steps=1):
    return pltpu.CompilerParams(
        dimension_semantics=("arbitrary",) * steps, vmem_limit_bytes=VMEM_BYTES
    )


def cost(flops, nbytes):
    return pl.CostEstimate(flops=int(flops), bytes_accessed=int(nbytes), transcendentals=0)


def whole(shape):
    return pl.BlockSpec(shape, lambda *_: (0,) * len(shape), pipeline_mode=pl.Buffered(1))


def rows_of(block, width):
    return pl.BlockSpec((block, width), lambda i: (i, 0))


def swap_halves(v):
    lane = lax.broadcasted_iota(jnp.int32, v.shape, 1)
    half = HDIM // 2
    ahead = pltpu.roll(v, LANES - half, 1)
    behind = pltpu.roll(v, half, 1)
    return jnp.where(lane % HDIM < half, ahead, behind)


def qkv_kernel(x_ref, gain_ref, w_ref, cos_ref, sin_ref, h_ref, q_ref, k_ref, v_ref):
    x = x_ref[...].astype(f32)
    inverse = lax.rsqrt(jnp.mean(x * x, axis=-1, keepdims=True) + EPS)
    h = (x * inverse * gain_ref[...]).astype(bf16)
    h_ref[...] = h
    cosine, sine = cos_ref[...], sin_ref[...]
    mixed = mm(h, w_ref[...])
    for out_ref, base, scale in ((q_ref, 0, HDIM**-0.5), (k_ref, D, 1.0)):
        for c in range(0, D, LANES):
            v = mixed[:, base + c : base + c + LANES]
            turned = v * cosine + swap_halves(v) * sine
            out_ref[:, c : c + LANES] = (turned.astype(bf16).astype(f32) * scale).astype(bf16)
    v_ref[...] = mixed[:, 2 * D :].astype(bf16)


def qkv_call(x, gain, w, cosine, sine):
    rows = x.shape[0]
    block = 256
    wide = jax.ShapeDtypeStruct((rows, D), bf16)
    return pl.pallas_call(
        qkv_kernel,
        grid=(rows // block,),
        in_specs=[
            rows_of(block, D),
            whole((1, D)),
            whole(w.shape),
            rows_of(block, LANES),
            rows_of(block, LANES),
        ],
        out_specs=[rows_of(block, D)] * 4,
        out_shape=[wide] * 4,
        compiler_params=params(),
        cost_estimate=cost(2 * rows * D * 3 * D, 2 * (5 * rows * D + 3 * D * D)),
        name="qkv_rope",
    )(x, gain, w, cosine, sine)


def fill_bias(bias_ref, dcol_ref, drow_ref, vcol_ref, length):
    for i in range(length // QB):
        start = i * QB
        low = max(0, start - REACH)
        size = start + QB - low
        key = low + lax.broadcasted_iota(jnp.int32, (size, QB), 0)
        query = start + lax.broadcasted_iota(jnp.int32, (size, QB), 1)
        same = dcol_ref[low : low + size, :] == drow_ref[:, start : start + QB]
        usable = (vcol_ref[low : low + size, :] > 0) | (key == query)
        allowed = same & (key <= query) & usable
        bias_ref[i, :size, :] = jnp.where(allowed, 0.0, -1e30)


def lane_head(shape, head):
    lane = lax.broadcasted_iota(jnp.int32, shape, 1)
    return (lane // HDIM) == head


def attend_kernel(q_ref, k_ref, v_ref, dcol_ref, drow_ref, vcol_ref, ctx_ref, lse_ref, bias_ref):
    length = q_ref.shape[0]

    @pl.when(pl.program_id(0) == 0)
    def _():
        fill_bias(bias_ref, dcol_ref, drow_ref, vcol_ref, length)

    values_t = v_ref[...].astype(f32).T.astype(bf16)
    for i in range(length // QB):
        start = i * QB
        low = max(0, start - REACH)
        size = start + QB - low
        keys = k_ref[low : low + size, :]
        query = q_ref[start : start + QB, :]
        parts = []
        for head in range(2):
            masked = jnp.where(lane_head(query.shape, head), query, jnp.zeros_like(query))
            scores = mm_nt(keys, masked) + bias_ref[i, :size, :]
            largest = jnp.max(scores, axis=0, keepdims=True)
            raised = jnp.exp(scores - largest)
            total = jnp.sum(raised, axis=0, keepdims=True)
            part = mm(
                values_t[head * HDIM : (head + 1) * HDIM, low : low + size], raised.astype(bf16)
            )
            parts.append(part * (1.0 / total))
            lse_ref[0, head : head + 1, start : start + QB] = largest + jnp.log(total)
        ctx_ref[start : start + QB, :] = jnp.concatenate(parts, axis=0).T.astype(bf16)


def attend_call(q, k, v, dcol, drow, vcol):
    length = q.shape[0]
    pairs = HEADS // 2
    column = pl.BlockSpec((length, LANES), lambda p: (0, p))
    return pl.pallas_call(
        attend_kernel,
        grid=(pairs,),
        in_specs=[column, column, column, whole(dcol.shape), whole(drow.shape), whole(vcol.shape)],
        out_specs=[column, pl.BlockSpec((1, 2, length), lambda p: (p, 0, 0))],
        out_shape=[
            jax.ShapeDtypeStruct((length, D), bf16),
            jax.ShapeDtypeStruct((pairs, 2, length), f32),
        ],
        scratch_shapes=[pltpu.VMEM((length // QB, REACH + QB, QB), f32)],
        compiler_params=params(),
        cost_estimate=cost(20e9, 8 * length * D),
        name="attend",
    )(q, k, v, dcol, drow, vcol)


def attend_back_kernel(
    q_ref,
    k_ref,
    v_ref,
    g_ref,
    lse_ref,
    dcol_ref,
    drow_ref,
    vcol_ref,
    cos_ref,
    sin_ref,
    dq_ref,
    dk_ref,
    dv_ref,
    bias_ref,
    gk_ref,
    gv_ref,
    gq_ref,
):
    length = q_ref.shape[0]

    @pl.when(pl.program_id(0) == 0)
    def _():
        fill_bias(bias_ref, dcol_ref, drow_ref, vcol_ref, length)

    gk_ref[...] = jnp.zeros_like(gk_ref)
    gv_ref[...] = jnp.zeros_like(gv_ref)
    keys_t = k_ref[...].astype(f32).T.astype(bf16)
    for i in range(length // QB):
        start = i * QB
        low = max(0, start - REACH)
        size = start + QB - low
        span = slice(low, low + size)
        keys = k_ref[span, :]
        values = v_ref[span, :]
        query = q_ref[start : start + QB, :]
        grads = g_ref[start : start + QB, :]
        for head in range(2):
            own = lane_head(query.shape, head)
            query_h = jnp.where(own, query, jnp.zeros_like(query))
            grads_h = jnp.where(own, grads, jnp.zeros_like(grads))
            scores = mm_nt(keys, query_h) + bias_ref[i, :size, :]
            probs = jnp.exp(scores - lse_ref[0, head : head + 1, start : start + QB])
            grad_probs = mm_nt(values, grads_h)
            inner = jnp.sum(probs * grad_probs, axis=0, keepdims=True)
            grad_scores = (probs * (grad_probs - inner)).astype(bf16)
            gv_ref[span, :] += mm(probs.astype(bf16), grads_h)
            gk_ref[span, :] += mm(grad_scores, query_h)
            gq_ref[head * HDIM : (head + 1) * HDIM, start : start + QB] = mm(
                keys_t[head * HDIM : (head + 1) * HDIM, span], grad_scores
            )
    cosine, sine = cos_ref[...], sin_ref[...]
    grad_q = gq_ref[...].T * HDIM**-0.5
    grad_k = gk_ref[...]
    dq_ref[...] = (grad_q * cosine - swap_halves(grad_q) * sine).astype(bf16)
    dk_ref[...] = (grad_k * cosine - swap_halves(grad_k) * sine).astype(bf16)
    dv_ref[...] = gv_ref[...].astype(bf16)


def attend_back_call(q, k, v, g, lse, dcol, drow, vcol, cosine, sine):
    length = q.shape[0]
    pairs = HEADS // 2
    column = pl.BlockSpec((length, LANES), lambda p: (0, p))
    return pl.pallas_call(
        attend_back_kernel,
        grid=(pairs,),
        in_specs=[column] * 4
        + [pl.BlockSpec((1, 2, length), lambda p: (p, 0, 0))]
        + [whole(a.shape) for a in (dcol, drow, vcol, cosine, sine)],
        out_specs=[column] * 3,
        out_shape=[jax.ShapeDtypeStruct((length, D), bf16)] * 3,
        scratch_shapes=[
            pltpu.VMEM((length // QB, REACH + QB, QB), f32),
            pltpu.VMEM((length, LANES), f32),
            pltpu.VMEM((length, LANES), f32),
            pltpu.VMEM((LANES, length), f32),
        ],
        compiler_params=params(),
        cost_estimate=cost(45e9, 14 * length * D),
        name="attend_back",
    )(q, k, v, g, lse, dcol, drow, vcol, cosine, sine)


def lanes_of(shape):
    return lax.broadcasted_iota(jnp.int32, shape, 1)


def partner(v, lane):
    return jnp.where(lane % 2 == 0, pltpu.roll(v, LANES - 1, 1), pltpu.roll(v, 1, 1))


def after_kernel(
    ctx_ref,
    x_ref,
    dy_ref,
    proj_ref,
    gain_ref,
    wsmall_ref,
    cvec_ref,
    crow_ref,
    prev_ref,
    pmix_ref,
    sel_ref,
    res_ref,
    h_ref,
    base_ref,
    one_ref,
    two_ref,
):
    res = x_ref[...].astype(f32) + mm(ctx_ref[...], proj_ref[...])
    res_ref[...] = res
    inverse = lax.rsqrt(jnp.mean(res * res, axis=-1, keepdims=True) + EPS)
    spread = res * inverse * gain_ref[...]
    low = spread.astype(bf16)
    h_ref[...] = low
    small = mm(low, wsmall_ref[...])
    logits = small + mm(prev_ref[...], pmix_ref[...])
    lane = lanes_of(small.shape)
    choice = lane < NCH
    top = jnp.max(jnp.where(choice, logits, -1e30), axis=-1, keepdims=True)
    raised = jnp.where(choice, jnp.exp(jnp.where(choice, logits - top, 0.0)), 0.0)
    gates = raised / jnp.sum(raised, axis=-1, keepdims=True)
    other = partner(small, lane)
    mixing = 1.0 / (1.0 + jnp.exp(other - small))
    is_mix = (lane >= NCH) & (lane < NCH + 4)
    taken = gates * sel_ref[...]
    dy = dy_ref[...]
    dyf = dy.astype(f32)
    hd = jnp.sum(spread * dyf, axis=-1, keepdims=True)
    cd = mm(dy, cvec_ref[...])
    one_ref[...] = jnp.where(choice, gates, jnp.where(is_mix, mixing, 0.0))
    gate_copy = taken[:, EXPERTS + 1 : EXPERTS + 2]
    coef = gate_copy
    grads = jnp.where(lane == EXPERTS + 1, hd, 0.0)
    mix_grads = jnp.zeros_like(small)
    base = res
    for m in range(2):
        gate = taken[:, EXPERTS + 2 + m : EXPERTS + 3 + m]
        a0 = mixing[:, NCH + 2 * m : NCH + 2 * m + 1]
        a1 = mixing[:, NCH + 2 * m + 1 : NCH + 2 * m + 2]
        dot = cd[:, NCH + 2 * m + 1 : NCH + 2 * m + 2]
        coef = coef + gate * a0
        base = base + (gate * a1) * crow_ref[m : m + 1, :]
        grads = jnp.where(lane == EXPERTS + 2 + m, a0 * hd + a1 * dot, grads)
        mix_grads = jnp.where(lane == NCH + 2 * m, gate * hd, mix_grads)
        mix_grads = jnp.where(lane == NCH + 2 * m + 1, gate * dot, mix_grads)
    base_ref[...] = base + coef * spread
    grads = grads * sel_ref[...]
    two = jnp.where(choice, grads, jnp.where(is_mix, mix_grads, 0.0))
    two = jnp.where(lane == 16, coef, two)
    two = jnp.where(lane == 17, inverse, two)
    two_ref[...] = two


def after_call(ctx, x, dy, proj, gain, wsmall, cvec, crow, prev, pmix, sel):
    rows = x.shape[0]
    block = 256
    narrow = jax.ShapeDtypeStruct((rows, LANES), f32)
    return pl.pallas_call(
        after_kernel,
        grid=(rows // block,),
        in_specs=[rows_of(block, D)] * 3
        + [whole(a.shape) for a in (proj, gain, wsmall, cvec, crow)]
        + [rows_of(block, LANES), whole(pmix.shape), rows_of(block, LANES)],
        out_specs=[rows_of(block, D)] * 3 + [rows_of(block, LANES)] * 2,
        out_shape=[
            jax.ShapeDtypeStruct((rows, D), f32),
            jax.ShapeDtypeStruct((rows, D), bf16),
            jax.ShapeDtypeStruct((rows, D), f32),
            narrow,
            narrow,
        ],
        compiler_params=params(),
        cost_estimate=cost(2 * rows * D * D, 16 * rows * D),
        name="after_attention",
    )(ctx, x, dy, proj, gain, wsmall, cvec, crow, prev, pmix, sel)


def expert_kernel(tiles, first, last, *refs):
    refs = list(refs)
    x_refs, refs = refs[:EXPERTS], refs[EXPERTS:]
    y_refs, refs = refs[:EXPERTS], refs[EXPERTS:]
    gate_ref, wg_ref, wu_ref, wo_ref = refs[:4]
    refs = refs[4:]
    if not first:
        ret_in, dx_in = refs[:2]
        refs = refs[2:]
    dwg_ref, dwu_ref, dwo_ref, ret_out, dx_out = refs[:5]
    refs = refs[5:]
    if last:
        dgate_ref = refs[0]
        refs = refs[1:]
    xs, ds, xt, ret_acc, dx_acc, ag, au, ao = refs
    t = pl.program_id(0)
    b = pl.program_id(1)
    for k in range(EXPERTS):

        @pl.when((t == 0) & (b == k))
        def _(k=k):
            x = x_refs[k][...]
            xs[k] = x
            xt[k] = x.astype(f32).T.astype(bf16)
            ds[k] = (y_refs[k][...].astype(f32) * gate_ref[k]).astype(bf16)
            if first:
                ret_acc[k] = jnp.zeros(x.shape, f32)
                dx_acc[k] = jnp.zeros(x.shape, f32)
            else:
                ret_acc[k] = ret_in[k]
                dx_acc[k] = dx_in[k]

    @pl.when(b == 0)
    def _():
        ag[...] = jnp.zeros_like(ag)
        au[...] = jnp.zeros_like(au)
        ao[...] = jnp.zeros_like(ao)

    x, d = xs[b], ds[b]
    wg, wu, wo = wg_ref[...], wu_ref[...], wo_ref[...]
    gate = mm(x, wg)
    up = mm(x, wu)
    grad_act = mm_nt(d, wo)
    sig = 1.0 / (1.0 + jnp.exp(-gate))
    silu = gate * sig
    act = (silu * up).astype(bf16)
    grad_up = (grad_act * silu).astype(bf16)
    grad_gate = (grad_act * up * (sig + silu * (1.0 - sig))).astype(bf16)
    ret_acc[b] += mm(act, wo)
    dx_acc[b] += mm_nt(grad_gate, wg) + mm_nt(grad_up, wu)
    ag[...] += mm(xt[b], grad_gate)
    au[...] += mm(xt[b], grad_up)
    ao[...] += mm_tn(act, d)

    @pl.when(b == EXPERTS - 1)
    def _():
        dwg_ref[...] = ag[...].astype(bf16)
        dwu_ref[...] = au[...].astype(bf16)
        dwo_ref[...] = ao[...].astype(bf16)

    if not last:

        @pl.when(t == tiles - 1)
        def _():
            ret_out[0] = ret_acc[b]
            dx_out[0] = dx_acc[b]

    else:
        for k in range(EXPERTS):

            @pl.when((t == tiles - 1) & (b == k))
            def _(k=k):
                ret = ret_acc[k]
                ret_out[0] = (ret * gate_ref[k]).astype(bf16)
                dx_out[0] = dx_acc[k].astype(bf16)
                dgate_ref[0] = jnp.sum(ret * y_refs[k][...].astype(f32), axis=-1, keepdims=True)


def expert_call(xs, ys, gate, w_in, w_out, carried, last):
    cap = xs[0].shape[0]
    width = w_out.shape[0]
    tile = min(256, width)
    tiles = width // tile
    first = carried is None

    def at_end(t, b):
        return (jnp.where(t == tiles - 1, b, 0), 0, 0)

    in_specs = [whole((cap, D))] * (2 * EXPERTS) + [
        whole(gate.shape),
        pl.BlockSpec((D, tile), lambda t, b: (0, t)),
        pl.BlockSpec((D, tile), lambda t, b: (0, t + tiles)),
        pl.BlockSpec((tile, D), lambda t, b: (t, 0)),
    ]
    operands = list(xs) + list(ys) + [gate, w_in, w_in, w_out]
    if not first:
        in_specs += [whole((EXPERTS, cap, D))] * 2
        operands += list(carried)
    kind = bf16 if last else f32
    out_specs = [
        pl.BlockSpec((D, tile), lambda t, b: (0, t)),
        pl.BlockSpec((D, tile), lambda t, b: (0, t)),
        pl.BlockSpec((tile, D), lambda t, b: (t, 0)),
        pl.BlockSpec((1, cap, D), at_end),
        pl.BlockSpec((1, cap, D), at_end),
    ]
    out_shape = [
        jax.ShapeDtypeStruct((D, width), bf16),
        jax.ShapeDtypeStruct((D, width), bf16),
        jax.ShapeDtypeStruct((width, D), bf16),
        jax.ShapeDtypeStruct((EXPERTS, cap, D), kind),
        jax.ShapeDtypeStruct((EXPERTS, cap, D), kind),
    ]
    if last:
        out_specs.append(pl.BlockSpec((1, cap, 1), at_end))
        out_shape.append(jax.ShapeDtypeStruct((EXPERTS, cap, 1), f32))
    return pl.pallas_call(
        partial(expert_kernel, tiles, first, last),
        grid=(tiles, EXPERTS),
        in_specs=in_specs,
        out_specs=out_specs,
        out_shape=out_shape,
        scratch_shapes=[
            pltpu.VMEM((EXPERTS, cap, D), bf16),
            pltpu.VMEM((EXPERTS, cap, D), bf16),
            pltpu.VMEM((EXPERTS, D, cap), bf16),
            pltpu.VMEM((EXPERTS, cap, D), f32),
            pltpu.VMEM((EXPERTS, cap, D), f32),
            pltpu.VMEM((D, tile), f32),
            pltpu.VMEM((D, tile), f32),
            pltpu.VMEM((tile, D), f32),
        ],
        compiler_params=params(2),
        cost_estimate=cost(18 * EXPERTS * cap * D * width, 12 * D * width),
        name="experts",
    )(*operands)


def back_kernel(
    res_ref,
    h_ref,
    dy_ref,
    one_ref,
    two_ref,
    sel_ref,
    place_ref,
    choice_ref,
    prev_ref,
    dx_ref,
    dg_ref,
    gain_ref,
    wsmall_ref,
    proj_ref,
    dres_ref,
    branch_ref,
    dctx_ref,
    dsmall_ref,
    gain_out,
    prev_out,
    cvec_out,
):
    step = pl.program_id(0)

    @pl.when(step == 0)
    def _():
        gain_out[...] = jnp.zeros_like(gain_out)
        prev_out[...] = jnp.zeros_like(prev_out)
        cvec_out[...] = jnp.zeros_like(cvec_out)
        dsmall_ref[...] = jnp.zeros_like(dsmall_ref)

    res = res_ref[...]
    rows = res.shape[0]
    cap = dx_ref.shape[1]
    one, two, sel = one_ref[...], two_ref[...], sel_ref[...]
    lane = lanes_of(one.shape)
    slot = lax.broadcasted_iota(jnp.int32, (rows, EXPERTS * cap), 1)
    grads = two
    hits = []
    for column in range(2):
        place = place_ref[:, column : column + 1]
        hit = slot == place
        hits.append(hit)
        dgate = jnp.sum(jnp.where(hit, dg_ref[...], 0.0), axis=-1, keepdims=True)
        named = (lane == choice_ref[:, column : column + 1]) & (lane < EXPERTS)
        grads = jnp.where(named, dgate, grads)
    spots = jnp.where(hits[0] | hits[1], 1.0, 0.0).astype(bf16)
    moved = jnp.zeros(res.shape, f32)
    for k in range(EXPERTS):
        moved = moved + mm(spots[:, k * cap : (k + 1) * cap], dx_ref[k])
    choice = lane < NCH
    is_mix = (lane >= NCH) & (lane < NCH + 4)
    dp = jnp.where(choice, grads, 0.0)
    weighted = one * grads
    mean_choice = jnp.sum(jnp.where(choice, weighted, 0.0), axis=-1, keepdims=True)
    d_logits = jnp.where(choice, one * (dp - mean_choice), 0.0)
    pair_sum = weighted + partner(weighted, lane)
    d_mix = one * (grads - pair_sum)
    d_small = jnp.where(choice, d_logits, jnp.where(is_mix, d_mix, 0.0))
    low = d_small.astype(bf16)
    coef = two[:, 16:17]
    inverse = two[:, 17:18]
    dy = dy_ref[...]
    dyf = dy.astype(f32)
    spread_grad = moved + mm_nt(low, wsmall_ref[...]) + coef * dyf
    scaled = spread_grad * gain_ref[...]
    mean_dot = jnp.mean(res * scaled, axis=-1, keepdims=True)
    d_res = dyf + inverse * scaled - res * (inverse * inverse * inverse * mean_dot)
    dres_ref[...] = d_res
    gain_out[...] += jnp.sum(spread_grad * res * inverse, axis=0, keepdims=True)
    branch = d_res.astype(bf16)
    branch_ref[...] = branch
    dctx_ref[...] = mm_nt(branch, proj_ref[...]).astype(bf16)
    dsmall_ref[...] += mm_tn(low, h_ref[...])
    high = d_logits.astype(bf16)
    rest = (d_logits - high.astype(f32)).astype(bf16)
    prev = prev_ref[...]
    prev_out[...] += mm_tn(prev, high) + mm_tn(prev, rest)
    taken = one * sel
    made = jnp.zeros_like(one)
    for m in range(2):
        a1 = one[:, NCH + 2 * m + 1 : NCH + 2 * m + 2]
        gate = taken[:, EXPERTS + 2 + m : EXPERTS + 3 + m]
        made = jnp.where(lane == m, gate * a1, made)
    high = made.astype(bf16)
    rest = (made - high.astype(f32)).astype(bf16)
    cvec_out[...] += mm_tn(high, dy) + mm_tn(rest, dy)


def back_call(res, h, dy, one, two, sel, places, choices, prev, dx, dg, gain, wsmall, proj):
    rows = res.shape[0]
    block = 256
    tall = jax.ShapeDtypeStruct((LANES, D), f32)
    return pl.pallas_call(
        back_kernel,
        grid=(rows // block,),
        in_specs=[rows_of(block, D)] * 3
        + [rows_of(block, LANES)] * 3
        + [rows_of(block, 2)] * 2
        + [rows_of(block, LANES)]
        + [whole(a.shape) for a in (dx, dg, gain, wsmall, proj)],
        out_specs=[rows_of(block, D)] * 3
        + [whole((LANES, D)), whole((1, D)), whole((LANES, LANES)), whole((LANES, D))],
        out_shape=[
            jax.ShapeDtypeStruct((rows, D), f32),
            jax.ShapeDtypeStruct((rows, D), bf16),
            jax.ShapeDtypeStruct((rows, D), bf16),
            tall,
            jax.ShapeDtypeStruct((1, D), f32),
            jax.ShapeDtypeStruct((LANES, LANES), f32),
            tall,
        ],
        compiler_params=params(),
        cost_estimate=cost(2 * rows * D * (D + 2048), 24 * rows * D),
        name="combine_back",
    )(res, h, dy, one, two, sel, places, choices, prev, dx, dg, gain, wsmall, proj)


def last_kernel(dq_ref, dk_ref, dv_ref, x_ref, dres_ref, gain_ref, w_ref, out_ref, gain_out):
    @pl.when(pl.program_id(0) == 0)
    def _():
        gain_out[...] = jnp.zeros_like(gain_out)

    grad = mm_nt(dq_ref[...], w_ref[:, :D])
    grad = grad + mm_nt(dk_ref[...], w_ref[:, D : 2 * D])
    grad = grad + mm_nt(dv_ref[...], w_ref[:, 2 * D :])
    x = x_ref[...].astype(f32)
    inverse = lax.rsqrt(jnp.mean(x * x, axis=-1, keepdims=True) + EPS)
    scaled = grad * gain_ref[...]
    mean_dot = jnp.mean(x * scaled, axis=-1, keepdims=True)
    d_x = inverse * scaled - x * (inverse * inverse * inverse * mean_dot)
    out_ref[...] = (dres_ref[...] + d_x).astype(bf16)
    gain_out[...] += jnp.sum(grad * x * inverse, axis=0, keepdims=True)


def last_call(dq, dk, dv, x, dres, gain, w):
    rows = x.shape[0]
    block = 256
    return pl.pallas_call(
        last_kernel,
        grid=(rows // block,),
        in_specs=[rows_of(block, D)] * 5 + [whole(gain.shape), whole(w.shape)],
        out_specs=[rows_of(block, D), whole((1, D))],
        out_shape=[jax.ShapeDtypeStruct((rows, D), bf16), jax.ShapeDtypeStruct((1, D), f32)],
        compiler_params=params(),
        cost_estimate=cost(6 * rows * D * D, 14 * rows * D),
        name="input_grad",
    )(dq, dk, dv, x, dres, gain, w)


def body(
    replicas,
    shards,
    tokens,
    prev_logits,
    out_grad,
    routes,
    doc_ids,
    valid_mask,
    qkv_weight,
    proj_weight,
    gain_attn,
    gain_ffn,
    router,
    const_mix,
    prev_mix,
    const_vec,
    expert_in,
    expert_out,
):
    me = lax.axis_index("rep")
    zi = lax.axis_index("fsdp")
    copies = replicas // EXPERTS
    mine = me // copies
    part = me % copies
    rows = tokens.shape[0]
    shard = qkv_weight.shape[0]
    hidden = expert_in.shape[2] // 2
    seg = hidden // (shards * copies)
    quarter = shard // EXPERTS

    def to_expert(a, k):
        return lax.ppermute(a, "rep", [(i, i ^ (k * copies)) for i in range(replicas)])

    def to_part(a, m):
        return lax.ppermute(a, "rep", [(i, i ^ m) for i in range(replicas)])

    def spin(a, k):
        return lax.ppermute(a, "fsdp", [(i, (i + k) % shards) for i in range(shards)])

    def by_shard(pieces, axis=0):
        size = pieces[0].shape[axis]
        shape = list(pieces[0].shape)
        shape[axis] = size * shards
        full = jnp.zeros(shape, pieces[0].dtype)
        for k, piece in enumerate(pieces):
            at = lax.rem(zi + shards - k, shards) * size
            full = lax.dynamic_update_slice_in_dim(full, piece, at, axis)
        return full

    def by_xor(pieces, own, axis):
        size = pieces[0].shape[axis]
        shape = list(pieces[0].shape)
        shape[axis] = size * len(pieces)
        full = jnp.zeros(shape, pieces[0].dtype)
        for k, piece in enumerate(pieces):
            full = lax.dynamic_update_slice_in_dim(full, piece, (own ^ k) * size, axis)
        return full

    def gather_dense(weight):
        width = weight.shape[1] // copies
        piece = lax.dynamic_slice(weight, (mine * quarter, part * width), (quarter, width))
        piece = piece[None, None]
        piece = by_shard([piece] + [spin(piece, k) for k in range(1, shards)], 0)
        piece = by_xor([piece] + [to_expert(piece, k) for k in range(1, EXPERTS)], mine, 1)
        piece = piece.reshape(shards * shard, width)
        return by_xor([piece] + [to_part(piece, m) for m in range(1, copies)], part, 1)

    def sum_dense(grad):
        width = grad.shape[1] // copies

        def columns(index):
            return lax.dynamic_slice_in_dim(grad, index * width, width, 1)

        total = columns(part).astype(f32)
        for m in range(1, copies):
            total = total + to_part(columns(part ^ m), m).astype(f32)
        total = total.astype(bf16).reshape(shards, EXPERTS, quarter, width)

        def quarters(index):
            return lax.dynamic_slice_in_dim(total, index, 1, 1)[:, 0]

        total2 = quarters(mine).astype(f32)
        for k in range(1, EXPERTS):
            total2 = total2 + to_expert(quarters(mine ^ k), k).astype(f32)
        total2 = total2.astype(bf16)

        def bands(index):
            return lax.dynamic_slice_in_dim(total2, index, 1, 0)[0]

        total3 = bands(zi).astype(f32)
        for k in range(1, shards):
            total3 = total3 + spin(bands(lax.rem(zi + k, shards)), k).astype(f32)
        total3 = total3.astype(bf16)
        full = by_xor([total3] + [to_expert(total3, k) for k in range(1, EXPERTS)], mine, 0)
        full = by_xor([full] + [to_part(full, m) for m in range(1, copies)], part, 1)
        return full.astype(f32)

    packed = jnp.concatenate(
        [
            gain_attn,
            gain_ffn,
            router.reshape(-1),
            const_mix.reshape(-1),
            const_vec.reshape(-1),
            prev_mix.reshape(-1),
        ]
    )
    packed = packed[None]
    packed = by_shard([packed] + [spin(packed, k) for k in range(1, shards)], 0)
    offsets = [0]
    for piece in (gain_attn, gain_ffn, router, const_mix, const_vec, prev_mix):
        offsets.append(offsets[-1] + piece.size)

    def unpacked(index, width):
        return packed[:, offsets[index] : offsets[index + 1]].reshape(-1, width)

    gain_a = unpacked(0, D).astype(f32)
    gain_f = unpacked(1, D).astype(f32)
    router_full = unpacked(2, NCH)
    mix_full = unpacked(3, 4)
    cvec_full = unpacked(4, 2)
    pmix_full = unpacked(5, NCH)

    qkv_full = gather_dense(qkv_weight)
    proj_full = gather_dense(proj_weight)

    own_in = lax.dynamic_index_in_dim(expert_in, mine, 1, keepdims=False)
    own_in = jnp.concatenate(
        [
            lax.dynamic_slice_in_dim(own_in, (j * copies + part) * seg, seg, 1)
            for j in range(2 * shards)
        ],
        axis=1,
    )
    own_out = lax.dynamic_slice(expert_out, (part * seg, mine, 0), (seg, 1, D))[:, 0]
    own_in = by_shard([own_in] + [spin(own_in, k) for k in range(1, shards)], 0)
    own_out = by_shard([own_out] + [spin(own_out, k) for k in range(1, shards)], 0)
    parts_in = [own_in] + [to_part(own_in, m) for m in range(1, copies)]
    parts_out = [own_out] + [to_part(own_out, m) for m in range(1, copies)]

    docs = doc_ids.reshape(-1)
    drow = docs[None, :]
    dcol = docs[:, None]
    vcol = valid_mask.reshape(-1)[:, None]
    first_place = jnp.sum((drow < dcol).astype(jnp.int32), axis=1)
    offset = (jnp.arange(rows, dtype=jnp.int32) - first_place).astype(f32)
    frequency = jnp.exp(
        jnp.arange(HDIM // 2, dtype=f32) * (-2.0 * math.log(10000.0) / HDIM)
    )
    angles = offset[:, None] * frequency[None, :]
    cosine, sine = jnp.cos(angles), jnp.sin(angles)
    cosine = jnp.concatenate([cosine] * 4, axis=1)
    sine = jnp.concatenate([-sine, sine, -sine, sine], axis=1)

    chosen = jnp.where(routes < EXPERTS, routes ^ mine, routes)
    named = jnp.any(
        chosen[:, :, None] == jnp.arange(EXPERTS, dtype=jnp.int32)[None, None, :], axis=1
    )
    earlier = jnp.tril(jnp.ones((rows, rows), bf16), -1)
    rank = mm(earlier, named.astype(bf16)).astype(jnp.int32)
    spot = jnp.where(named, rank, CAP)
    slots = jnp.arange(CAP, dtype=jnp.int32)
    onehot = (spot.T[:, None, :] == slots[None, :, None]).astype(bf16)
    safe = jnp.minimum(chosen, EXPERTS - 1)
    places = jnp.where(
        chosen < EXPERTS, safe * CAP + jnp.take_along_axis(rank, safe, axis=1), -1
    )
    sel = jnp.any(
        routes[:, :, None] == jnp.arange(LANES, dtype=jnp.int32)[None, None, :], axis=1
    ).astype(f32)

    def dispatched(values):
        blocks = [mm(onehot[k], values).astype(bf16) for k in range(EXPERTS)]
        return [blocks[0]] + [to_expert(blocks[k], k) for k in range(1, EXPERTS)]

    ys = dispatched(out_grad)

    h1, q, k, v = qkv_call(tokens, gain_a, qkv_full, cosine, sine)
    ctx, lse = attend_call(q, k, v, dcol, drow, vcol)
    wsmall = jnp.concatenate(
        [router_full, mix_full, jnp.zeros((D, LANES - NCH - 4), bf16)], axis=1
    )
    zero = jnp.zeros((D, 1), bf16)
    cvec = jnp.concatenate(
        [
            jnp.zeros((D, NCH + 1), bf16),
            cvec_full[:, :1],
            zero,
            cvec_full[:, 1:],
            jnp.zeros((D, LANES - NCH - 4), bf16),
        ],
        axis=1,
    )
    crow = cvec_full.astype(f32).T
    prev = jnp.pad(prev_logits, ((0, 0), (0, LANES - NCH)))
    pmix = jnp.pad(pmix_full, ((0, LANES - NCH), (0, LANES - NCH)))
    res, h2, base, one, two = after_call(
        ctx, tokens, out_grad, proj_full, gain_f, wsmall, cvec, crow, prev, pmix, sel
    )

    xs = dispatched(h2)
    gates = jnp.take(one[:, :EXPERTS], mine ^ jnp.arange(EXPERTS, dtype=jnp.int32), axis=1)
    gate_slots = jnp.sum(
        jnp.where(onehot > 0, gates.T[:, None, :], 0.0), axis=-1, keepdims=True
    )
    gate = jnp.stack(
        [gate_slots[0]] + [to_expert(gate_slots[k], k) for k in range(1, EXPERTS)]
    )
    order = list(range(1, copies)) + [0]
    carried = None
    pieces = {}
    for m in order:
        made = expert_call(xs, ys, gate, parts_in[m], parts_out[m], carried, m == 0)
        pieces[m] = made[:3]
        carried = made[3:5]
    ret, dx = carried
    dgate = made[5]

    def returned(blocks):
        return jnp.stack([blocks[0]] + [to_expert(blocks[k], k) for k in range(1, EXPERTS)])

    dx = returned(dx)
    dgate = returned(dgate.reshape(EXPERTS, CAP)).reshape(1, EXPERTS * CAP)
    ret = returned(ret)

    def sum_parts(index):
        total = pieces[0][index].astype(f32)
        for m in range(1, copies):
            total = total + to_part(pieces[m][index], m).astype(f32)
        return total.astype(bf16)

    grad_in = jnp.concatenate([sum_parts(0), sum_parts(1)], axis=1)
    grad_out = sum_parts(2)

    def sum_shards(grad, size):
        def band(index):
            return lax.dynamic_slice_in_dim(grad, index * size, size, 0)

        total = band(zi).astype(f32)
        for k in range(1, shards):
            total = total + spin(band(lax.rem(zi + k, shards)), k).astype(f32)
        return total.astype(bf16)

    grad_in = sum_shards(grad_in, shard)
    grad_out = sum_shards(grad_out, seg)

    def spread_out(piece):
        piece = by_xor(
            [piece[None]] + [to_expert(piece, k)[None] for k in range(1, EXPERTS)], mine, 0
        )
        return by_xor(
            [piece[:, :, None]] + [to_part(piece, m)[:, :, None] for m in range(1, copies)], part, 2
        )

    full_in = spread_out(grad_in.reshape(shard, 2 * shards, seg).swapaxes(0, 1).reshape(2 * shards * shard, seg))
    full_in = full_in.reshape(EXPERTS, 2 * shards, shard, copies * seg)
    full_in = full_in.transpose(2, 0, 1, 3).reshape(shard, EXPERTS, 2 * hidden).astype(f32)
    full_out = spread_out(grad_out[None])
    full_out = full_out.reshape(EXPERTS, copies * seg, D).swapaxes(0, 1).astype(f32)

    dres, branch, dctx, dsmall, gain_f_grad, prev_grad, cvec_grad = back_call(
        res,
        h2,
        out_grad,
        one,
        two,
        sel,
        places,
        routes,
        prev,
        dx,
        dgate,
        gain_f,
        wsmall,
        proj_full,
    )
    proj_grad = sum_dense(mm_tn(ctx, branch).astype(bf16))
    dq, dk, dv = attend_back_call(q, k, v, dctx, lse, dcol, drow, vcol, cosine, sine)
    input_grad, gain_a_grad = last_call(dq, dk, dv, tokens, dres, gain_a, qkv_full)
    owned = prev_mix.shape[0]
    prev_block = jnp.pad(
        prev_grad[:NCH, :NCH].reshape(shards, owned, NCH), ((0, 0), (0, shard - owned), (0, 0))
    ).reshape(D, NCH)
    smalls = jnp.concatenate(
        [
            gain_a_grad.T,
            gain_f_grad.T,
            dsmall[: NCH + 4].T,
            cvec_grad[:2].T,
            prev_block,
        ],
        axis=1,
    )
    smalls = jnp.pad(smalls, ((0, 0), (0, 2 * LANES - smalls.shape[1]))).astype(bf16)
    tail = jnp.concatenate(
        [
            mm_tn(h1, dq).astype(bf16),
            mm_tn(h1, dk).astype(bf16),
            mm_tn(h1, dv).astype(bf16),
            smalls,
        ],
        axis=1,
    )
    tail = sum_dense(tail)
    small = tail[:, 3 * D :]

    gathered = base
    for k in range(EXPERTS):
        gathered = gathered + mm_tn(onehot[k], ret[k])
    return (
        gathered.astype(bf16),
        input_grad,
        tail[:, : 3 * D],
        proj_grad,
        small[:, 0],
        small[:, 1],
        small[:, 2 : 2 + NCH],
        small[:, 2 + NCH : 6 + NCH],
        small[:owned, 8 + NCH : 8 + 2 * NCH],
        small[:, 6 + NCH : 8 + NCH],
        full_in,
        full_out,
    )


def solution(mesh):
    replicas, shards = mesh.shape["rep"], mesh.shape["fsdp"]
    split = P(("rep", "fsdp"), None)
    matrix = P("fsdp", None)
    cube = P("fsdp", None, None)
    in_specs = (split,) * 6 + (matrix, matrix, P("fsdp"), P("fsdp")) + (matrix,) * 4 + (cube, cube)
    out_specs = (split, split, matrix, matrix, P("fsdp"), P("fsdp")) + (matrix,) * 4 + (cube, cube)
    return jax.shard_map(
        partial(body, replicas, shards),
        mesh=mesh,
        in_specs=in_specs,
        out_specs=out_specs,
        check_vma=False,
    )
```

```python
from functools import partial
import math

import jax
import jax.numpy as jnp
from jax import lax
from jax.experimental import pallas as pl
from jax.experimental.pallas import tpu as pltpu
from jax.sharding import PartitionSpec as P

D = 768
HEADS = 12
HDIM = 64
EXPERTS = 4
NCH = 8
CAP = 384
LANES = 128
QB = 256
REACH = 512
VMEM_BYTES = 58 * 1024 * 1024
EPS = 1e-06
COST_SCALE = 0.02
f32 = jnp.float32
bf16 = jnp.bfloat16

NT = (((1,), (1,)), ((), ()))
TN = (((0,), (0,)), ((), ()))


def mm(a, b):
    return jnp.dot(a, b, preferred_element_type=f32)


def mm_nt(a, b):
    return lax.dot_general(a, b, NT, preferred_element_type=f32)


def mm_tn(a, b):
    return lax.dot_general(a, b, TN, preferred_element_type=f32)


def params(steps=1):
    return pltpu.CompilerParams(
        dimension_semantics=("arbitrary",) * steps, vmem_limit_bytes=VMEM_BYTES
    )


def cost(flops, nbytes):
    return pl.CostEstimate(
        flops=int(flops * COST_SCALE), bytes_accessed=int(nbytes * COST_SCALE), transcendentals=0
    )


def launch(kernel, operands, in_specs, out_specs, out_shape, after=(), **kw):
    n, skip = len(operands), len(after)

    def run(*refs):
        kernel(*refs[:n], *refs[n + skip :])

    kw.setdefault("compiler_params", pltpu.CompilerParams(vmem_limit_bytes=VMEM_BYTES))
    return pl.pallas_call(
        run,
        in_specs=list(in_specs) + [pl.BlockSpec(memory_space=pl.ANY)] * skip,
        out_specs=out_specs,
        out_shape=out_shape,
        **kw,
    )(*operands, *after)


def tie(value, *others):
    return lax.optimization_barrier((value, others))[0]


VM = pl.BlockSpec(memory_space=pltpu.VMEM)
SMEM = pl.BlockSpec(memory_space=pltpu.SMEM)
CVEC, GAIN_A, GAIN_F = NCH + 4, NCH + 6, NCH + 7


def row_of(ref, row):
    return ref[:16, :].astype(f32)[row : row + 1]


def whole(shape):
    return pl.BlockSpec(shape, lambda *_: (0,) * len(shape), pipeline_mode=pl.Buffered(1))


def rows_of(block, width):
    return pl.BlockSpec((block, width), lambda i: (i, 0))


def swap_halves(v):
    lane = lax.broadcasted_iota(jnp.int32, v.shape, 1)
    half = HDIM // 2
    ahead = pltpu.roll(v, LANES - half, 1)
    behind = pltpu.roll(v, half, 1)
    return jnp.where(lane % HDIM < half, ahead, behind)


def lay_columns(full_ref, pieces, part):
    width = pieces[0].shape[1]
    for p in range(len(pieces)):
        chosen = pieces[0][...]
        for m in range(1, len(pieces)):
            chosen = jnp.where(part == (p ^ m), pieces[m][...], chosen)
        full_ref[:, p * width : (p + 1) * width] = chosen


def qkv_kernel(count, part_ref, x_ref, small_ref, cos_ref, sin_ref, *refs):
    pieces = refs[:count]
    h_ref, q_ref, k_ref, v_ref, w_ref = refs[count:]

    @pl.when(pl.program_id(0) == 0)
    def _():
        lay_columns(w_ref, pieces, part_ref[0])

    x = x_ref[...].astype(f32)
    inverse = lax.rsqrt(jnp.mean(x * x, axis=-1, keepdims=True) + EPS)
    h = (x * inverse * row_of(small_ref, GAIN_A)).astype(bf16)
    h_ref[...] = h
    cosine, sine = cos_ref[...], sin_ref[...]
    mixed = mm(h, w_ref[...])
    for out_ref, base, scale in ((q_ref, 0, HDIM**-0.5), (k_ref, D, 1.0)):
        for c in range(0, D, LANES):
            v = mixed[:, base + c : base + c + LANES]
            turned = v * cosine + swap_halves(v) * sine
            out_ref[:, c : c + LANES] = (turned.astype(bf16).astype(f32) * scale).astype(bf16)
    v_ref[...] = mixed[:, 2 * D :].astype(bf16)


def qkv_call(part, x, small, cosine, sine, pieces, after):
    rows = x.shape[0]
    block = 256
    wide = jax.ShapeDtypeStruct((rows, D), bf16)
    return launch(
        partial(qkv_kernel, len(pieces)),
        [part, x, small, cosine, sine, *pieces],
        [
            SMEM,
            rows_of(block, D),
            whole(small.shape),
            rows_of(block, LANES),
            rows_of(block, LANES),
        ]
        + [whole(p.shape) for p in pieces],
        [rows_of(block, D)] * 4,
        [wide] * 4,
        after,
        grid=(rows // block,),
        scratch_shapes=[pltpu.VMEM((D, 3 * D), bf16)],
        compiler_params=params(),
        cost_estimate=cost(2 * rows * D * 3 * D, 2 * (5 * rows * D + 3 * D * D)),
        name="qkv_rope",
    )


def fill_bias(bias_ref, dcol_ref, drow_ref, vcol_ref, length):
    for i in range(length // QB):
        start = i * QB
        low = max(0, start - REACH)
        size = start + QB - low
        key = low + lax.broadcasted_iota(jnp.int32, (size, QB), 0)
        query = start + lax.broadcasted_iota(jnp.int32, (size, QB), 1)
        same = dcol_ref[low : low + size, :] == drow_ref[:, start : start + QB]
        usable = (vcol_ref[low : low + size, :] > 0) | (key == query)
        allowed = same & (key <= query) & usable
        bias_ref[i, :size, :] = jnp.where(allowed, 0.0, -1e30)


def lane_head(shape, head):
    lane = lax.broadcasted_iota(jnp.int32, shape, 1)
    return (lane // HDIM) == head


def attend_kernel(q_ref, k_ref, v_ref, dcol_ref, drow_ref, vcol_ref, ctx_ref, lse_ref, bias_ref):
    length = q_ref.shape[0]

    @pl.when(pl.program_id(0) == 0)
    def _():
        fill_bias(bias_ref, dcol_ref, drow_ref, vcol_ref, length)

    values_t = v_ref[...].astype(f32).T.astype(bf16)
    for i in range(length // QB):
        start = i * QB
        low = max(0, start - REACH)
        size = start + QB - low
        keys = k_ref[low : low + size, :]
        query = q_ref[start : start + QB, :]
        parts = []
        for head in range(2):
            masked = jnp.where(lane_head(query.shape, head), query, jnp.zeros_like(query))
            scores = mm_nt(keys, masked) + bias_ref[i, :size, :]
            largest = jnp.max(scores, axis=0, keepdims=True)
            raised = jnp.exp(scores - largest)
            total = jnp.sum(raised, axis=0, keepdims=True)
            part = mm(
                values_t[head * HDIM : (head + 1) * HDIM, low : low + size], raised.astype(bf16)
            )
            parts.append(part * (1.0 / total))
            lse_ref[0, head : head + 1, start : start + QB] = largest + jnp.log(total)
        ctx_ref[start : start + QB, :] = jnp.concatenate(parts, axis=0).T.astype(bf16)


def attend_call(q, k, v, dcol, drow, vcol, after):
    length = q.shape[0]
    pairs = HEADS // 2
    column = pl.BlockSpec((length, LANES), lambda p: (0, p))
    return launch(
        attend_kernel,
        [q, k, v, dcol, drow, vcol],
        [column, column, column, whole(dcol.shape), whole(drow.shape), whole(vcol.shape)],
        [column, pl.BlockSpec((1, 2, length), lambda p: (p, 0, 0))],
        [
            jax.ShapeDtypeStruct((length, D), bf16),
            jax.ShapeDtypeStruct((pairs, 2, length), f32),
        ],
        after,
        grid=(pairs,),
        scratch_shapes=[pltpu.VMEM((length // QB, REACH + QB, QB), f32)],
        compiler_params=params(),
        cost_estimate=cost(20e9, 8 * length * D),
        name="attend",
    )


def attend_back_kernel(
    q_ref,
    k_ref,
    v_ref,
    g_ref,
    lse_ref,
    dcol_ref,
    drow_ref,
    vcol_ref,
    cos_ref,
    sin_ref,
    dq_ref,
    dk_ref,
    dv_ref,
    bias_ref,
    gk_ref,
    gv_ref,
    gq_ref,
):
    length = q_ref.shape[0]

    @pl.when(pl.program_id(0) == 0)
    def _():
        fill_bias(bias_ref, dcol_ref, drow_ref, vcol_ref, length)

    gk_ref[...] = jnp.zeros_like(gk_ref)
    gv_ref[...] = jnp.zeros_like(gv_ref)
    keys_t = k_ref[...].astype(f32).T.astype(bf16)
    for i in range(length // QB):
        start = i * QB
        low = max(0, start - REACH)
        size = start + QB - low
        span = slice(low, low + size)
        keys = k_ref[span, :]
        values = v_ref[span, :]
        query = q_ref[start : start + QB, :]
        grads = g_ref[start : start + QB, :]
        for head in range(2):
            own = lane_head(query.shape, head)
            query_h = jnp.where(own, query, jnp.zeros_like(query))
            grads_h = jnp.where(own, grads, jnp.zeros_like(grads))
            scores = mm_nt(keys, query_h) + bias_ref[i, :size, :]
            probs = jnp.exp(scores - lse_ref[0, head : head + 1, start : start + QB])
            grad_probs = mm_nt(values, grads_h)
            inner = jnp.sum(probs * grad_probs, axis=0, keepdims=True)
            grad_scores = (probs * (grad_probs - inner)).astype(bf16)
            gv_ref[span, :] += mm(probs.astype(bf16), grads_h)
            gk_ref[span, :] += mm(grad_scores, query_h)
            gq_ref[head * HDIM : (head + 1) * HDIM, start : start + QB] = mm(
                keys_t[head * HDIM : (head + 1) * HDIM, span], grad_scores
            )
    cosine, sine = cos_ref[...], sin_ref[...]
    grad_q = gq_ref[...].T * HDIM**-0.5
    grad_k = gk_ref[...]
    dq_ref[...] = (grad_q * cosine - swap_halves(grad_q) * sine).astype(bf16)
    dk_ref[...] = (grad_k * cosine - swap_halves(grad_k) * sine).astype(bf16)
    dv_ref[...] = gv_ref[...].astype(bf16)


def attend_back_call(q, k, v, g, lse, dcol, drow, vcol, cosine, sine, after):
    length = q.shape[0]
    pairs = HEADS // 2
    column = pl.BlockSpec((length, LANES), lambda p: (0, p))
    return launch(
        attend_back_kernel,
        [q, k, v, g, lse, dcol, drow, vcol, cosine, sine],
        [column] * 4
        + [pl.BlockSpec((1, 2, length), lambda p: (p, 0, 0))]
        + [whole(a.shape) for a in (dcol, drow, vcol, cosine, sine)],
        [column] * 3,
        [jax.ShapeDtypeStruct((length, D), bf16)] * 3,
        after,
        grid=(pairs,),
        scratch_shapes=[
            pltpu.VMEM((length // QB, REACH + QB, QB), f32),
            pltpu.VMEM((length, LANES), f32),
            pltpu.VMEM((length, LANES), f32),
            pltpu.VMEM((LANES, length), f32),
        ],
        compiler_params=params(),
        cost_estimate=cost(45e9, 14 * length * D),
        name="attend_back",
    )


def cut_dense_kernel(quarter, widths, who_ref, qkv_ref, proj_ref, small_ref, out_ref, token_ref):
    token_ref[0] = who_ref[0]
    row = pl.multiple_of(who_ref[0] * quarter, quarter)
    start = 0
    for ref, width in zip((qkv_ref, proj_ref), widths, strict=True):
        column = pl.multiple_of(who_ref[1] * width, LANES)
        out_ref[:quarter, start : start + width] = ref[pl.ds(row, quarter), pl.ds(column, width)]
        start += width
    shard = small_ref.shape[1]
    out_ref[quarter:, :] = jnp.zeros((16, start), bf16)
    out_ref[quarter:, :shard] = small_ref[:16, :]
    out_ref[quarter:, 2 * LANES : 3 * LANES] = small_ref[16:, :LANES]


def cut_dense(who, qkv, proj, small, copies):
    shard = qkv.shape[0]
    quarter = shard // EXPERTS
    widths = (qkv.shape[1] // copies, proj.shape[1] // copies)
    total = sum(widths)
    if quarter % 16 == 0 and all(w % LANES == 0 for w in widths):
        return launch(
            partial(cut_dense_kernel, quarter, widths),
            [who, qkv, proj, small],
            [SMEM, VM, VM, VM],
            [VM, SMEM],
            [
                jax.ShapeDtypeStruct((quarter + 16, total), bf16),
                jax.ShapeDtypeStruct((1,), jnp.int32),
            ],
            name="cut_dense",
        )
    row = who[0] * quarter
    cuts = [
        lax.dynamic_slice(w, (row, who[1] * width), (quarter, width))
        for w, width in zip((qkv, proj), widths, strict=True)
    ]
    spare = total - 3 * LANES
    below = jnp.concatenate(
        [
            jnp.pad(small[:16], ((0, 0), (0, 2 * LANES - shard))),
            jnp.pad(small[16:], ((0, 0), (0, 2 * LANES - shard)))[:, :LANES],
            jnp.zeros((16, spare), bf16),
        ],
        axis=1,
    )
    return jnp.concatenate([jnp.concatenate(cuts, axis=1), below]), who[:1]


def lay_shards_kernel(count, shard, quarter, width, zi_ref, *refs):
    pieces = refs[:count]
    qkv_ref, small_ref, prev_ref = refs[count:]
    for k in range(count):
        at = lax.rem(zi_ref[0] + count - k, count)
        qkv_ref[at] = pieces[k][:quarter, :width]
        prev_ref[at] = pieces[k][quarter:, 2 * LANES : 3 * LANES]
    small_ref[16:, :] = jnp.zeros((LANES - 16, D), bf16)
    for z in range(count):
        chosen = pieces[0][quarter:, : 2 * LANES].astype(f32)
        for k in range(1, count):
            here = lax.rem(zi_ref[0] + count - k, count) == z
            chosen = jnp.where(here, pieces[k][quarter:, : 2 * LANES].astype(f32), chosen)
        small_ref[:16, z * shard : (z + 1) * shard] = chosen[:, :shard].astype(bf16)


def lay_shards(zi, pieces, shard, quarter, width, after):
    count = len(pieces)
    return launch(
        partial(lay_shards_kernel, count, shard, quarter, width),
        [zi, *pieces],
        [SMEM] + [VM] * count,
        [VM] * 3,
        [
            jax.ShapeDtypeStruct((count, quarter, width), bf16),
            jax.ShapeDtypeStruct((LANES, D), bf16),
            jax.ShapeDtypeStruct((count, 16, LANES), bf16),
        ],
        after,
        name="lay_shards",
    )


def lay_proj_kernel(count, quarter, width, zi_ref, *refs):
    pieces, out = refs[:count], refs[count]
    for k in range(count):
        at = lax.rem(zi_ref[0] + count - k, count)
        out[at] = pieces[k][:quarter, width:]


def lay_proj(zi, pieces, quarter, width, after):
    count = len(pieces)
    rest = pieces[0].shape[1] - width
    return launch(
        partial(lay_proj_kernel, count, quarter, width),
        [zi, *pieces],
        [SMEM] + [VM] * count,
        VM,
        jax.ShapeDtypeStruct((count, quarter, rest), bf16),
        after,
        name="lay_proj",
    )


def lay_xor_kernel(count, own_ref, *refs):
    pieces, out = refs[:count], refs[count]
    for k in range(count):
        out[:, own_ref[0] ^ k] = pieces[k][...]


def lay_xor(own, pieces, after=()):
    count = len(pieces)
    first, rows, columns = pieces[0].shape
    return launch(
        partial(lay_xor_kernel, count),
        [own, *pieces],
        [SMEM] + [VM] * count,
        VM,
        jax.ShapeDtypeStruct((first, count, rows, columns), bf16),
        after,
        name="lay_xor",
    )


def lanes_of(shape):
    return lax.broadcasted_iota(jnp.int32, shape, 1)


def partner(v, lane):
    return jnp.where(lane % 2 == 0, pltpu.roll(v, LANES - 1, 1), pltpu.roll(v, 1, 1))


def selected(choice_ref, lane):
    return (lane == choice_ref[:, 0:1]) | (lane == choice_ref[:, 1:2])


def after_kernel(
    count, part_ref, ctx_ref, x_ref, wsmall_ref, prev_ref, pmix_ref, choice_ref, *refs
):
    pieces = refs[:count]
    res_ref, h_ref, one_ref, gate_ref, w_ref = refs[count:]

    @pl.when(pl.program_id(0) == 0)
    def _():
        lay_columns(w_ref, pieces, part_ref[0])

    res = x_ref[...].astype(f32) + mm(ctx_ref[...], w_ref[...])
    res_ref[...] = res
    inverse = lax.rsqrt(jnp.mean(res * res, axis=-1, keepdims=True) + EPS)
    low = (res * inverse * row_of(wsmall_ref, GAIN_F)).astype(bf16)
    h_ref[...] = low
    small = mm_nt(low, wsmall_ref[...])
    logits = small + mm_tn(prev_ref[...], pmix_ref[...])
    lane = lanes_of(small.shape)
    choice = lane < NCH
    top = jnp.max(jnp.where(choice, logits, -1e30), axis=-1, keepdims=True)
    raised = jnp.where(choice, jnp.exp(jnp.where(choice, logits - top, 0.0)), 0.0)
    gates = raised / jnp.sum(raised, axis=-1, keepdims=True)
    mixing = 1.0 / (1.0 + jnp.exp(partner(small, lane) - small))
    is_mix = (lane >= NCH) & (lane < NCH + 4)
    one_ref[...] = jnp.where(choice, gates, jnp.where(is_mix, mixing, 0.0))
    taken = jnp.where(selected(choice_ref, lane), gates, 0.0).T[:NCH]
    high = taken.astype(bf16).astype(f32)
    gate_ref[...] = jnp.concatenate([high, taken - high], axis=0).astype(bf16)


def after_call(part, ctx, x, small, prev, pmix, choices, pieces):
    rows = x.shape[0]
    block = 256
    return launch(
        partial(after_kernel, len(pieces)),
        [part, ctx, x, small, prev, pmix, choices, *pieces],
        [SMEM]
        + [rows_of(block, D)] * 2
        + [
            whole(small.shape),
            pl.BlockSpec((NCH, block), lambda i: (0, i)),
            whole(pmix.shape),
            rows_of(block, 2),
        ]
        + [whole(p.shape) for p in pieces],
        [rows_of(block, D)] * 2
        + [rows_of(block, LANES), pl.BlockSpec((2 * NCH, block), lambda i: (0, i))],
        [
            jax.ShapeDtypeStruct((rows, D), f32),
            jax.ShapeDtypeStruct((rows, D), bf16),
            jax.ShapeDtypeStruct((rows, LANES), f32),
            jax.ShapeDtypeStruct((2 * NCH, rows), bf16),
        ],
        grid=(rows // block,),
        scratch_shapes=[pltpu.VMEM((D, D), bf16)],
        compiler_params=params(),
        cost_estimate=cost(2 * rows * D * D, 10 * rows * D),
        name="after_attention",
    )


EXTRA = 16


def dispatch_kernel(gated, mine_ref, spot_ref, v_ref, *refs):
    if gated:
        gate_ref, refs = refs[0], refs[1:]
    rows = v_ref.shape[0]
    slot = lax.broadcasted_iota(jnp.int32, (CAP, rows), 0)
    for k in range(EXPERTS):
        hits = jnp.where(slot == spot_ref[k : k + 1, :], 1.0, 0.0).astype(bf16)
        refs[k][:CAP, :] = mm(hits, v_ref[...]).astype(bf16)
        if gated:
            moved = mm_nt(gate_ref[...], hits)
            row = lax.broadcasted_iota(jnp.int32, moved.shape, 0) % NCH
            moved = jnp.where(row == (mine_ref[0] ^ k), moved, 0.0)
            high = jnp.sum(moved[:NCH], axis=0, keepdims=True)
            rest = jnp.sum(moved[NCH:], axis=0, keepdims=True)
            tail = jnp.concatenate(
                [high, rest, jnp.zeros((EXTRA - 2, CAP), f32)], axis=0
            ).astype(bf16)
            refs[k][CAP:, :CAP] = tail
            refs[k][CAP:, CAP:] = jnp.zeros((EXTRA, D - CAP), bf16)


def dispatch_call(mine, spot, values, gates=None, after=()):
    size = CAP + (0 if gates is None else EXTRA)
    operands = [mine, spot, values] + ([] if gates is None else [gates])
    rows = values.shape[0]
    return launch(
        partial(dispatch_kernel, gates is not None),
        operands,
        [SMEM] + [VM] * (len(operands) - 1),
        [VM] * EXPERTS,
        [jax.ShapeDtypeStruct((size, D), bf16)] * EXPERTS,
        after,
        cost_estimate=cost(2 * rows * D * CAP * EXPERTS, 2 * rows * D + 2 * EXPERTS * CAP * D),
        name="dispatch",
    )


class Plan:
    def __init__(self, replicas, shards, shard, hidden, chunks):
        self.copies = replicas // EXPERTS
        self.shards = shards
        self.shard = shard
        self.hidden = hidden
        self.chunks = chunks
        self.seg = hidden // (shards * self.copies * chunks)
        self.width = self.seg * shards
        self.wide = min(256, self.width)
        self.tiles = self.width // self.wide
        self.spans = self.wide // self.seg
        self.downs = D // self.wide
        self.rows = 2 * self.tiles * shard + self.downs * self.seg

    def column(self, half, tile, span, part, chunk):
        z = tile * self.spans + span
        base = half * self.hidden + z * (self.hidden // self.shards)
        return base + (part * self.chunks + chunk) * self.seg

    def down_row(self, part, chunk):
        return (part * self.chunks + chunk) * self.seg


def pack_kernel(plan, part_ref, in_ref, out_ref, *packs):
    part = part_ref[0]
    seg, shard = plan.seg, plan.shard
    for chunk in range(plan.chunks):
        pack = packs[chunk]
        for half in range(2):
            for tile in range(plan.tiles):
                row = (half * plan.tiles + tile) * shard
                for span in range(plan.spans):
                    at = pl.multiple_of(plan.column(half, tile, span, part, chunk), LANES)
                    pack[row : row + shard, span * seg : (span + 1) * seg] = in_ref[
                        :, pl.ds(at, seg)
                    ]
        row = 2 * plan.tiles * shard
        at = pl.multiple_of(plan.down_row(part, chunk), seg)
        for down in range(plan.downs):
            pack[row + down * seg : row + (down + 1) * seg, :] = out_ref[
                pl.ds(at, seg), down * plan.wide : (down + 1) * plan.wide
            ]


def pack_pieces(plan, part, own_in, own_out):
    if plan.seg % LANES == 0:
        vmem = pl.BlockSpec(memory_space=pltpu.VMEM)
        return pl.pallas_call(
            partial(pack_kernel, plan),
            in_specs=[SMEM, vmem, vmem],
            out_specs=[vmem] * plan.chunks,
            out_shape=[jax.ShapeDtypeStruct((plan.rows, plan.wide), bf16)] * plan.chunks,
            compiler_params=pltpu.CompilerParams(vmem_limit_bytes=VMEM_BYTES),
            name="pack",
        )(part, own_in, own_out)
    packs = []
    for chunk in range(plan.chunks):
        blocks = []
        for half in range(2):
            for tile in range(plan.tiles):
                spans = [
                    lax.dynamic_slice_in_dim(
                        own_in, plan.column(half, tile, span, part[0], chunk), plan.seg, 1
                    )
                    for span in range(plan.spans)
                ]
                blocks.append(jnp.concatenate(spans, axis=1))
        rows = lax.dynamic_slice_in_dim(own_out, plan.down_row(part[0], chunk), plan.seg, 0)
        blocks += [rows[:, d * plan.wide : (d + 1) * plan.wide] for d in range(plan.downs)]
        packs.append(jnp.concatenate(blocks, axis=0))
    return packs


def unpack_kernel(plan, begun, who_ref, *refs):
    copies, seg = plan.copies, plan.seg
    ins, downs = refs[:copies], refs[copies : 2 * copies]
    in_out, down_out = refs[2 * copies + 2 * begun :]
    mine, part = who_ref[0], who_ref[1]
    step = pl.program_id(0)
    p = step % copies
    z = (step // copies) % plan.shards
    for j in range(EXPERTS):
        chosen = ins[0][j ^ mine].astype(f32)
        for m in range(1, copies):
            chosen = jnp.where(part == (p ^ m), ins[m][j ^ mine].astype(f32), chosen)
        piece = chosen[:, :seg]
        for span in range(1, plan.spans):
            here = z % plan.spans == span
            piece = jnp.where(here, chosen[:, span * seg : (span + 1) * seg], piece)
        in_out[:, j, :] = piece

    @pl.when(step < copies)
    def _():
        for j in range(EXPERTS):
            for down in range(plan.downs):
                rows = slice(down * seg, (down + 1) * seg)
                chosen = downs[0][j ^ mine, rows, :].astype(f32)
                for m in range(1, copies):
                    chosen = jnp.where(
                        part == (p ^ m), downs[m][j ^ mine, rows, :].astype(f32), chosen
                    )
                down_out[:, j, down * plan.wide : (down + 1) * plan.wide] = chosen


def unpack_chunk(plan, who, chunk, sums, begun):
    copies, shards = plan.copies, plan.shards
    per = plan.hidden // shards
    start = 2 * plan.tiles * plan.shard
    down_rows = plan.downs * plan.seg

    def in_block(i):
        half, z = i // (shards * copies), (i // copies) % shards
        return (0, half * plan.tiles + z // plan.spans, 0)

    def down_block(i):
        return (jnp.minimum(i, copies - 1) * plan.chunks + chunk, 0, 0)

    hbm = pl.BlockSpec(memory_space=pl.ANY)
    operands = [who, *sums, *[s[:, start:, :] for s in sums], *begun]
    return launch(
        partial(unpack_kernel, plan, len(begun) // 2),
        operands,
        [SMEM]
        + [pl.BlockSpec((EXPERTS, plan.shard, plan.wide), in_block)] * copies
        + [whole((EXPERTS, down_rows, plan.wide))] * copies
        + [hbm] * len(begun),
        [
            pl.BlockSpec((plan.shard, EXPERTS, plan.seg), lambda i: (0, 0, i * plan.chunks + chunk)),
            pl.BlockSpec((plan.seg, EXPERTS, D), down_block),
        ],
        [
            jax.ShapeDtypeStruct((plan.shard, EXPERTS, 2 * plan.hidden), f32),
            jax.ShapeDtypeStruct((per, EXPERTS, D), f32),
        ],
        grid=(2 * shards * copies,),
        input_output_aliases={len(operands) - 2 + i: i for i in range(len(begun))},
        compiler_params=params(),
        cost_estimate=cost(0, 12 * plan.shard * plan.hidden * EXPERTS),
        name="unpack",
    )


def unpack_grads(plan, who, sums, begun):
    if begun:
        for chunk in range(1, plan.chunks):
            begun = unpack_chunk(plan, who, chunk, sums[chunk], begun)
        return begun
    mine, part = who[0], who[1]
    ins, outs = [], []
    for j in range(EXPERTS):
        columns = {}
        rows = []
        for p in range(plan.copies):
            for chunk in range(plan.chunks):
                stacked = jnp.stack(sums[chunk])
                piece = lax.dynamic_index_in_dim(stacked, part ^ p, 0, keepdims=False)
                piece = lax.dynamic_index_in_dim(piece, mine ^ j, 0, keepdims=False)
                for half in range(2):
                    for tile in range(plan.tiles):
                        row = (half * plan.tiles + tile) * plan.shard
                        for span in range(plan.spans):
                            columns[plan.column(half, tile, span, p, chunk)] = piece[
                                row : row + plan.shard, span * plan.seg : (span + 1) * plan.seg
                            ]
                row = 2 * plan.tiles * plan.shard
                rows.append(
                    jnp.concatenate(
                        [
                            piece[row + d * plan.seg : row + (d + 1) * plan.seg]
                            for d in range(plan.downs)
                        ],
                        axis=1,
                    )
                )
        ins.append(jnp.concatenate([columns[c] for c in sorted(columns)], axis=1))
        outs.append(jnp.concatenate(rows, axis=0))
    return jnp.stack(ins, axis=1).astype(f32), jnp.stack(outs, axis=1).astype(f32)


def expert_kernel(plan, first, last, *refs):
    refs = list(refs)

    def take(n):
        out = refs[:n]
        del refs[:n]
        return out

    copies = plan.copies
    x_refs, y_refs = take(EXPERTS), take(EXPERTS)
    w_refs = take(copies)
    carry_in = [] if first else take(2)
    grad_outs = take(copies)
    if last:
        dx_outs, ret_outs = take(EXPERTS), take(EXPERTS)
        carry_out = []
    else:
        carry_out = take(2)
    xs, ds, xt, gcol, ret_acc, dx_acc, wg, wu, wo, act_s, dg_s, du_s, grads, sems = refs
    rows = EXPERTS * CAP
    shard, seg, wide, tiles = plan.shard, plan.seg, plan.wide, plan.tiles

    carries = [
        pltpu.make_async_copy(src, dst, sems.at[i])
        for i, (src, dst) in enumerate(zip(carry_in, (ret_acc, dx_acc)))
    ]
    for copy in carries:
        copy.start()
    for k in range(EXPERTS):
        span = slice(k * CAP, (k + 1) * CAP)
        x = x_refs[k][:CAP, :]
        xs[span, :] = x
        xt[:, span] = x.astype(f32).T.astype(bf16)
        extra = x_refs[k][CAP:, :CAP].astype(f32)
        gate = (extra[0:1] + extra[1:2]).T
        gcol[span, :] = jnp.broadcast_to(gate, (CAP, LANES))
        ds[span, :] = (y_refs[k][...].astype(f32) * gate).astype(bf16)
    if first:
        ret_acc[...] = jnp.zeros_like(ret_acc)
        dx_acc[...] = jnp.zeros_like(dx_acc)
    for copy in carries:
        copy.wait()

    sends = []
    for m in range(copies):
        w = w_refs[m]
        for z in range(plan.shards):
            for tile in range(tiles):
                for half, target in ((0, wg), (1, wu)):
                    row = (half * tiles + tile) * shard
                    target[z * shard : (z + 1) * shard, tile * wide : (tile + 1) * wide] = w[
                        z, row : row + shard, :
                    ]
            for down in range(plan.downs):
                row = 2 * tiles * shard + down * seg
                wo[z * seg : (z + 1) * seg, down * wide : (down + 1) * wide] = w[
                    z, row : row + seg, :
                ]

        def block(b, _):
            span = pl.ds(pl.multiple_of(b * CAP, CAP), CAP)
            x, d = xs[span, :], ds[span, :]
            gate = mm(x, wg[...])
            up = mm(x, wu[...])
            grad_act = mm_nt(d, wo[...])
            sig = 1.0 / (1.0 + jnp.exp(-gate))
            silu = gate * sig
            act = (silu * up).astype(bf16)
            grad_up = (grad_act * silu).astype(bf16)
            grad_gate = (grad_act * up * (sig + silu * (1.0 - sig))).astype(bf16)
            act_s[span, :] = act
            du_s[span, :] = grad_up
            dg_s[span, :] = grad_gate
            ret_acc[span, :] += mm(act, wo[...])
            dx_acc[span, :] += mm_nt(grad_gate, wg[...]) + mm_nt(grad_up, wu[...])
            return 0

        lax.fori_loop(0, EXPERTS, block, 0)
        if m == copies - 1 and not last:
            for i, (src, dst) in enumerate(zip((ret_acc, dx_acc), carry_out, strict=True)):
                copy = pltpu.make_async_copy(src, dst, sems.at[2 + i])
                copy.start()
                sends.append(copy)
        if m == copies - 1 and last:
            for k in range(EXPERTS):
                span = slice(k * CAP, (k + 1) * CAP)
                ret = ret_acc[span, :]
                dgate = jnp.sum(ret * y_refs[k][...].astype(f32), axis=-1, keepdims=True)
                dgate = jnp.broadcast_to(dgate, (CAP, LANES)).T[:1]
                ret_outs[k][...] = (ret * gcol[span, :1]).astype(bf16)
                dx_outs[k][:CAP, :] = dx_acc[span, :].astype(bf16)
                high = dgate.astype(bf16).astype(f32)
                tail = jnp.concatenate(
                    [high, dgate - high, jnp.zeros((EXTRA - 2, CAP), f32)], axis=0
                ).astype(bf16)
                dx_outs[k][CAP:, :CAP] = tail
                dx_outs[k][CAP:, CAP:] = jnp.zeros((EXTRA, D - CAP), bf16)
        for half, source in ((0, dg_s), (1, du_s)):
            for tile in range(tiles):
                made = mm(xt[...], source[:, tile * wide : (tile + 1) * wide]).astype(bf16)
                row = (half * tiles + tile) * shard
                for z in range(plan.shards):
                    grads[m, z, row : row + shard, :] = made[z * shard : (z + 1) * shard, :]
        for tile in range(tiles):
            made = mm_tn(act_s[:, tile * wide : (tile + 1) * wide], ds[...]).astype(bf16)
            for span in range(plan.spans):
                z = tile * plan.spans + span
                for down in range(plan.downs):
                    row = 2 * tiles * shard + down * seg
                    grads[m, z, row : row + seg, :] = made[
                        span * seg : (span + 1) * seg, down * wide : (down + 1) * wide
                    ]
        copy = pltpu.make_async_copy(grads.at[m], grad_outs[m], sems.at[4 + m])
        copy.start()
        sends.append(copy)
    for copy in sends:
        copy.wait()


def expert_call(plan, xs, ys, weights, carried, last):
    first = carried is None
    rows = EXPERTS * CAP
    vmem = pl.BlockSpec(memory_space=pltpu.VMEM)
    hbm = pl.BlockSpec(memory_space=pl.ANY)
    copies = plan.copies
    in_specs = [vmem] * (2 * EXPERTS + copies)
    operands = list(xs) + list(ys) + list(weights)
    if not first:
        in_specs += [hbm] * 2
        operands += list(carried)
    out_specs = [hbm] * copies
    out_shape = [jax.ShapeDtypeStruct((plan.shards, plan.rows, plan.wide), bf16)] * copies
    if last:
        out_specs += [vmem] * (2 * EXPERTS)
        out_shape += [jax.ShapeDtypeStruct((CAP + EXTRA, D), bf16)] * EXPERTS
        out_shape += [jax.ShapeDtypeStruct((CAP, D), bf16)] * EXPERTS
    else:
        out_specs += [hbm] * 2
        out_shape += [jax.ShapeDtypeStruct((rows, D), f32)] * 2
    made = pl.pallas_call(
        partial(expert_kernel, plan, first, last),
        in_specs=in_specs,
        out_specs=out_specs,
        out_shape=out_shape,
        scratch_shapes=[
            pltpu.VMEM((rows, D), bf16),
            pltpu.VMEM((rows, D), bf16),
            pltpu.VMEM((D, rows), bf16),
            pltpu.VMEM((rows, LANES), f32),
            pltpu.VMEM((rows, D), f32),
            pltpu.VMEM((rows, D), f32),
            pltpu.VMEM((D, plan.width), bf16),
            pltpu.VMEM((D, plan.width), bf16),
            pltpu.VMEM((plan.width, D), bf16),
            pltpu.VMEM((rows, plan.width), bf16),
            pltpu.VMEM((rows, plan.width), bf16),
            pltpu.VMEM((rows, plan.width), bf16),
            pltpu.VMEM((copies, plan.shards, plan.rows, plan.wide), bf16),
            pltpu.SemaphoreType.DMA((4 + copies,)),
        ],
        compiler_params=pltpu.CompilerParams(vmem_limit_bytes=VMEM_BYTES),
        cost_estimate=cost(
            18 * rows * D * plan.width * copies, 12 * D * plan.width * copies + 12 * rows * D
        ),
        name="experts",
    )(*operands)
    return made[:copies], made[copies:]


def spots_of(place_ref, rows):
    slot = lax.broadcasted_iota(jnp.int32, (rows, EXPERTS * CAP), 1)
    hit = (slot == place_ref[:, 0:1]) | (slot == place_ref[:, 1:2])
    return jnp.where(hit, 1.0, 0.0).astype(bf16)


def constant_gates(one, chosen, m):
    a0 = one[:, NCH + 2 * m : NCH + 2 * m + 1]
    a1 = one[:, NCH + 2 * m + 1 : NCH + 2 * m + 2]
    gate = chosen[:, EXPERTS + 2 + m : EXPERTS + 3 + m]
    return gate, a0, a1


def back_kernel(
    count,
    who_ref,
    res_ref,
    h_ref,
    dy_ref,
    one_ref,
    place_ref,
    choice_ref,
    prev_ref,
    wsmall_ref,
    *refs,
):
    dx_refs, refs = refs[:EXPERTS], refs[EXPERTS:]
    pieces, refs = refs[:count], refs[count:]
    (
        dres_ref,
        branch_ref,
        dctx_ref,
        dsmall_ref,
        gain_out,
        prev_out,
        cvec_out,
        w_ref,
        dg_ref,
    ) = refs

    @pl.when(pl.program_id(0) == 0)
    def _():
        gain_out[...] = jnp.zeros_like(gain_out)
        prev_out[...] = jnp.zeros_like(prev_out)
        cvec_out[...] = jnp.zeros_like(cvec_out)
        dsmall_ref[...] = jnp.zeros_like(dsmall_ref)
        lay_columns(w_ref, pieces, who_ref[1])
        lane = lanes_of((CAP, LANES))
        for k in range(EXPERTS):
            columns = dx_refs[k][CAP:, :CAP].astype(f32).T
            at = who_ref[0] ^ k
            made = jnp.where(lane == at, columns[:, 0:1], 0.0)
            made = jnp.where(lane == at + 16, columns[:, 1:2], made)
            dg_ref[k * CAP : (k + 1) * CAP, :] = made.astype(bf16)

    res = res_ref[...]
    rows = res.shape[0]
    one = one_ref[...]
    lane = lanes_of(one.shape)
    chosen = jnp.where(selected(choice_ref, lane), one, 0.0)
    choice = lane < NCH
    is_mix = (lane >= NCH) & (lane < NCH + 4)
    spots = spots_of(place_ref, rows)
    moved = jnp.zeros(res.shape, f32)
    for k in range(EXPERTS):
        moved = moved + mm(spots[:, k * CAP : (k + 1) * CAP], dx_refs[k][:CAP, :])
    from_experts = mm(spots, dg_ref[...])
    from_experts = from_experts + pltpu.roll(from_experts, LANES - 16, 1)

    inverse = lax.rsqrt(jnp.mean(res * res, axis=-1, keepdims=True) + EPS)
    dy = dy_ref[...]
    dyf = dy.astype(f32)
    gain = row_of(wsmall_ref, GAIN_F)
    spread = res * inverse * gain
    hd = jnp.sum(spread * dyf, axis=-1, keepdims=True)
    cd = mm_nt(dy, wsmall_ref[...])
    coef = chosen[:, EXPERTS + 1 : EXPERTS + 2]
    grads = jnp.where(lane < EXPERTS, from_experts, 0.0)
    grads = jnp.where(lane == EXPERTS + 1, hd, grads)
    made = jnp.zeros_like(one)
    for m in range(2):
        gate, a0, a1 = constant_gates(one, chosen, m)
        dot = cd[:, CVEC + m : CVEC + m + 1]
        coef = coef + gate * a0
        grads = jnp.where(lane == EXPERTS + 2 + m, a0 * hd + a1 * dot, grads)
        grads = jnp.where(lane == NCH + 2 * m, gate * hd, grads)
        grads = jnp.where(lane == NCH + 2 * m + 1, gate * dot, grads)
        made = jnp.where(lane == m, gate * a1, made)
    grads = jnp.where(is_mix | selected(choice_ref, lane), grads, 0.0)
    weighted = one * grads
    mean_choice = jnp.sum(jnp.where(choice, weighted, 0.0), axis=-1, keepdims=True)
    d_logits = jnp.where(choice, one * (grads - mean_choice), 0.0)
    d_mix = one * (grads - (weighted + partner(weighted, lane)))
    d_small = jnp.where(choice, d_logits, jnp.where(is_mix, d_mix, 0.0))
    low = d_small.astype(bf16)
    spread_grad = moved + mm(low, wsmall_ref[...]) + coef * dyf
    scaled = spread_grad * gain
    mean_dot = jnp.mean(res * scaled, axis=-1, keepdims=True)
    d_res = dyf + inverse * scaled - res * (inverse * inverse * inverse * mean_dot)
    dres_ref[...] = d_res
    gain_out[...] += jnp.sum(spread_grad * res * inverse, axis=0, keepdims=True)
    branch = d_res.astype(bf16)
    branch_ref[...] = branch
    dctx_ref[...] = mm_nt(branch, w_ref[...]).astype(bf16)
    dsmall_ref[...] += mm_tn(low, h_ref[...])
    high = d_logits.astype(bf16)
    rest = (d_logits - high.astype(f32)).astype(bf16)
    prev = prev_ref[...]
    prev_out[...] += mm(prev, high) + mm(prev, rest)
    high = made.astype(bf16)
    rest = (made - high.astype(f32)).astype(bf16)
    cvec_out[...] += mm_tn(high, dy) + mm_tn(rest, dy)


def back_call(who, res, h, dy, one, places, choices, prev, small, dx, pieces, after):
    rows = res.shape[0]
    block = 256
    tall = jax.ShapeDtypeStruct((LANES, D), f32)
    return launch(
        partial(back_kernel, len(pieces)),
        [who, res, h, dy, one, places, choices, prev, small, *dx, *pieces],
        [SMEM]
        + [rows_of(block, D)] * 3
        + [rows_of(block, LANES)]
        + [rows_of(block, 2)] * 2
        + [pl.BlockSpec((NCH, block), lambda i: (0, i))]
        + [whole(a.shape) for a in (small, *dx, *pieces)],
        [rows_of(block, D)] * 3
        + [whole((LANES, D)), whole((1, D)), whole((NCH, LANES)), whole((LANES, D))],
        [
            jax.ShapeDtypeStruct((rows, D), f32),
            jax.ShapeDtypeStruct((rows, D), bf16),
            jax.ShapeDtypeStruct((rows, D), bf16),
            tall,
            jax.ShapeDtypeStruct((1, D), f32),
            jax.ShapeDtypeStruct((NCH, LANES), f32),
            tall,
        ],
        after,
        grid=(rows // block,),
        scratch_shapes=[pltpu.VMEM((D, D), bf16), pltpu.VMEM((EXPERTS * CAP, LANES), bf16)],
        compiler_params=params(),
        cost_estimate=cost(2 * rows * D * (D + 2048), 20 * rows * D),
        name="combine_back",
    )


def finish_kernel(res_ref, one_ref, place_ref, choice_ref, small_ref, *refs):
    ret_refs, out_ref = refs[:EXPERTS], refs[EXPERTS]
    res = res_ref[...]
    one = one_ref[...]
    lane = lanes_of(one.shape)
    chosen = jnp.where(selected(choice_ref, lane), one, 0.0)
    inverse = lax.rsqrt(jnp.mean(res * res, axis=-1, keepdims=True) + EPS)
    total = res
    coef = chosen[:, EXPERTS + 1 : EXPERTS + 2]
    for m in range(2):
        gate, a0, a1 = constant_gates(one, chosen, m)
        coef = coef + gate * a0
        total = total + (gate * a1) * row_of(small_ref, CVEC + m)
    total = total + (coef * inverse) * res * row_of(small_ref, GAIN_F)
    spots = spots_of(place_ref, res.shape[0])
    for k in range(EXPERTS):
        total = total + mm(spots[:, k * CAP : (k + 1) * CAP], ret_refs[k][...])
    out_ref[...] = total.astype(bf16)


def finish_call(res, one, places, choices, small, ret, after):
    rows = res.shape[0]
    block = 256
    return launch(
        finish_kernel,
        [res, one, places, choices, small, *ret],
        [rows_of(block, D), rows_of(block, LANES)]
        + [rows_of(block, 2)] * 2
        + [whole(a.shape) for a in (small, *ret)],
        rows_of(block, D),
        jax.ShapeDtypeStruct((rows, D), bf16),
        after,
        grid=(rows // block,),
        compiler_params=params(),
        cost_estimate=cost(2 * rows * D * 1536, 10 * rows * D),
        name="layer_out",
    )


def dense_kernel(copies, h_ref, ctx_ref, dq_ref, dk_ref, dv_ref, branch_ref, *outs):
    cut = 4 * D // copies
    ht = h_ref[...].astype(f32).T.astype(bf16)
    ct = ctx_ref[...].astype(f32).T.astype(bf16)
    step = 384
    for index, (left, right) in enumerate(
        ((ht, dq_ref), (ht, dk_ref), (ht, dv_ref), (ct, branch_ref))
    ):
        for c in range(0, D, step):
            made = mm(left, right[:, c : c + step]).astype(bf16)
            at = index * D + c
            done = 0
            while done < step:
                owner, column = (at + done) // cut, (at + done) % cut
                size = min(step - done, cut - column)
                outs[owner][:, column : column + size] = made[:, done : done + size]
                done += size


def dense_call(copies, h, ctx, dq, dk, dv, branch, after):
    rows = h.shape[0]
    return launch(
        partial(dense_kernel, copies),
        [h, ctx, dq, dk, dv, branch],
        [VM] * 6,
        [VM] * copies,
        [jax.ShapeDtypeStruct((D, 4 * D // copies), bf16)] * copies,
        after,
        cost_estimate=cost(8 * rows * D * D, 12 * rows * D + 8 * D * D),
        name="dense_grads",
    )


def fold_parts_kernel(copies, who_ref, *refs):
    dense, got = refs[:copies], refs[copies : 2 * copies - 1]
    small, outs = refs[2 * copies - 1], refs[2 * copies :]
    cut = dense[0].shape[-1]
    for k in range(EXPERTS):
        at = who_ref[0] ^ k
        own = dense[0][:, at].astype(f32)
        for p in range(1, copies):
            own = jnp.where(who_ref[1] == p, dense[p][:, at].astype(f32), own)
        for piece in got:
            own = own + piece[:, at].astype(f32)
        outs[k][:, :, :cut] = own.astype(bf16)
        outs[k][:, :, cut:] = small[:, at]


def fold_parts(who, dense, got, small, shards):
    copies = len(dense)
    cut = dense[0].shape[1]
    quarter = D // (shards * EXPERTS)
    shape = (shards, EXPERTS, quarter, cut)
    operands = [who] + [a.reshape(shape) for a in (*dense, *got)]
    operands.append(small.reshape(shards, EXPERTS, quarter, LANES))
    return launch(
        partial(fold_parts_kernel, copies),
        operands,
        [SMEM] + [VM] * (len(operands) - 1),
        [VM] * EXPERTS,
        [jax.ShapeDtypeStruct((shards, quarter, cut + LANES), bf16)] * EXPERTS,
        name="fold_parts",
    )


def fold_quarters_kernel(count, zi_ref, *refs):
    pieces, outs = refs[:count], refs[count:]
    for k, out in enumerate(outs):
        at = lax.rem(zi_ref[0] + k, len(outs))
        total = pieces[0][at].astype(f32)
        for piece in pieces[1:]:
            total = total + piece[at].astype(f32)
        out[...] = total.astype(bf16)


def fold_quarters(zi, pieces, after=()):
    shards, rows, columns = pieces[0].shape
    return launch(
        partial(fold_quarters_kernel, len(pieces)),
        [zi, *pieces],
        [SMEM] + [VM] * len(pieces),
        [VM] * shards,
        [jax.ShapeDtypeStruct((rows, columns), bf16)] * shards,
        after,
        name="fold_quarters",
    )


def fold_copies(pieces):
    shape = pieces[0].shape
    block = pl.BlockSpec((1,) + shape[1:], lambda i: (i, 0, 0))
    return launch(
        fold_shards_kernel,
        pieces,
        [block] * len(pieces),
        block,
        jax.ShapeDtypeStruct(shape, bf16),
        grid=(shape[0],),
        compiler_params=params(),
        cost_estimate=cost(0, 0),
        name="fold_copies",
    )


def fold_shards_kernel(*refs):
    total = refs[0][...].astype(f32)
    for ref in refs[1:-1]:
        total = total + ref[...].astype(f32)
    refs[-1][...] = total.astype(bf16)


def fold_shards(pieces):
    return launch(
        fold_shards_kernel,
        pieces,
        [VM] * len(pieces),
        VM,
        jax.ShapeDtypeStruct(pieces[0].shape, bf16),
        name="fold_shards",
    )


def unpack_dense_kernel(count, part_ref, *refs):
    pieces, (qkv_ref, proj_ref, small_ref) = refs[:count], refs[count:]
    cut = pieces[0].shape[1] - LANES
    small = pieces[0][:, cut:].astype(f32)
    for piece in pieces[1:]:
        small = small + piece[:, cut:].astype(f32)
    small_ref[...] = small
    for p in range(count):
        chosen = pieces[0][:, :cut].astype(f32)
        for m in range(1, count):
            chosen = jnp.where(part_ref[0] == (p ^ m), pieces[m][:, :cut].astype(f32), chosen)
        start = p * cut
        in_qkv = max(0, min(cut, 3 * D - start))
        if in_qkv:
            qkv_ref[:, start : start + in_qkv] = chosen[:, :in_qkv]
        if in_qkv < cut:
            at = start + in_qkv - 3 * D
            proj_ref[:, at : at + cut - in_qkv] = chosen[:, in_qkv:]


def unpack_dense(part, pieces):
    rows = pieces[0].shape[0]
    return launch(
        partial(unpack_dense_kernel, len(pieces)),
        [part, *pieces],
        [SMEM] + [VM] * len(pieces),
        [VM] * 3,
        [
            jax.ShapeDtypeStruct((rows, 3 * D), f32),
            jax.ShapeDtypeStruct((rows, D), f32),
            jax.ShapeDtypeStruct((rows, LANES), f32),
        ],
        name="unpack_dense",
    )


def last_kernel(
    count,
    shards,
    part_ref,
    dq_ref,
    dk_ref,
    dv_ref,
    x_ref,
    dres_ref,
    small_ref,
    dsmall_ref,
    gain_f_ref,
    prev_ref,
    cvec_ref,
    *refs,
):
    pieces = refs[:count]
    out_ref, small_out, w_ref, gain_ref = refs[count:]

    @pl.when(pl.program_id(0) == 0)
    def _():
        gain_ref[...] = jnp.zeros_like(gain_ref)
        lay_columns(w_ref, pieces, part_ref[0])

    grad = mm_nt(dq_ref[...], w_ref[:, :D])
    grad = grad + mm_nt(dk_ref[...], w_ref[:, D : 2 * D])
    grad = grad + mm_nt(dv_ref[...], w_ref[:, 2 * D :])
    x = x_ref[...].astype(f32)
    inverse = lax.rsqrt(jnp.mean(x * x, axis=-1, keepdims=True) + EPS)
    scaled = grad * row_of(small_ref, GAIN_A)
    mean_dot = jnp.mean(x * scaled, axis=-1, keepdims=True)
    d_x = inverse * scaled - x * (inverse * inverse * inverse * mean_dot)
    out_ref[...] = (dres_ref[...] + d_x).astype(bf16)
    gain_ref[...] += jnp.sum(grad * x * inverse, axis=0, keepdims=True)

    @pl.when(pl.program_id(0) == pl.num_programs(0) - 1)
    def _():
        row = lax.broadcasted_iota(jnp.int32, (LANES, D), 0)
        total = jnp.where(row < CVEC, dsmall_ref[...], 0.0)
        for m in range(2):
            total = jnp.where(row == CVEC + m, cvec_ref[m : m + 1, :], total)
        total = jnp.where(row == GAIN_A, gain_ref[...], total)
        total = jnp.where(row == GAIN_F, gain_f_ref[...], total)
        total = total.T
        owned = NCH // shards
        shard = D // shards
        row = lax.broadcasted_iota(jnp.int32, total.shape, 0)
        lane = lanes_of((NCH, LANES))
        prev = pltpu.roll(jnp.where(lane < NCH, prev_ref[...], 0.0), 16, 1)
        for index in range(NCH):
            at = (index // owned) * shard + index % owned
            total = jnp.where(row == at, total + prev[index : index + 1, :], total)
        small_out[...] = total.astype(bf16)


def last_call(part, shards, dq, dk, dv, x, dres, small, smalls, pieces, after):
    rows = x.shape[0]
    block = 256
    return launch(
        partial(last_kernel, len(pieces), shards),
        [part, dq, dk, dv, x, dres, small, *smalls, *pieces],
        [SMEM]
        + [rows_of(block, D)] * 5
        + [whole(a.shape) for a in (small, *smalls, *pieces)],
        [rows_of(block, D), whole((D, LANES))],
        [jax.ShapeDtypeStruct((rows, D), bf16), jax.ShapeDtypeStruct((D, LANES), bf16)],
        after,
        grid=(rows // block,),
        scratch_shapes=[pltpu.VMEM((D, 3 * D), bf16), pltpu.VMEM((1, D), f32)],
        compiler_params=params(),
        cost_estimate=cost(6 * rows * D * D, 14 * rows * D),
        name="input_grad",
    )


def body(
    replicas,
    shards,
    tokens,
    prev_logits,
    out_grad,
    routes,
    doc_ids,
    valid_mask,
    qkv_weight,
    proj_weight,
    gain_attn,
    gain_ffn,
    router,
    const_mix,
    prev_mix,
    const_vec,
    expert_in,
    expert_out,
):
    me = lax.axis_index("rep")
    zi = lax.axis_index("fsdp")
    copies = replicas // EXPERTS
    mine = me // copies
    part = me % copies
    rows = tokens.shape[0]
    shard = qkv_weight.shape[0]
    hidden = expert_in.shape[2] // 2
    quarter = shard // EXPERTS
    plan = Plan(replicas, shards, shard, hidden, 2)
    zi_s = zi.reshape(1).astype(jnp.int32)
    mine_s = mine.reshape(1).astype(jnp.int32)
    part_s = part.reshape(1).astype(jnp.int32)
    who = jnp.concatenate([mine_s, part_s])

    def to_expert(a, k):
        return lax.ppermute(a, "rep", [(i, i ^ (k * copies)) for i in range(replicas)])

    def to_part(a, m):
        return lax.ppermute(a, "rep", [(i, i ^ m) for i in range(replicas)])

    def spin(a, k):
        return lax.ppermute(a, "fsdp", [(i, (i + k) % shards) for i in range(shards)])

    def by_xor(pieces, own, axis):
        size = pieces[0].shape[axis]
        shape = list(pieces[0].shape)
        shape[axis] = size * len(pieces)
        full = jnp.zeros(shape, pieces[0].dtype)
        for k, piece in enumerate(pieces):
            full = lax.dynamic_update_slice_in_dim(full, piece, (own ^ k) * size, axis)
        return full

    width = 3 * D // copies
    owned = prev_mix.shape[0]
    smalls = jnp.concatenate(
        [
            router.T,
            const_mix.T,
            const_vec.T,
            gain_attn[None],
            gain_ffn[None],
            jnp.pad(prev_mix, ((0, 16 - owned), (0, shard - NCH))),
        ]
    )
    piece, mine_late = cut_dense(who, qkv_weight, proj_weight, smalls, copies)
    spun = [piece] + [spin(piece, k) for k in range(1, shards)]

    own_in = lax.dynamic_index_in_dim(expert_in, mine_late[0], 1, keepdims=False)
    own_out = lax.dynamic_index_in_dim(expert_out, mine_late[0], 1, keepdims=False)
    packs = pack_pieces(plan, part_s, own_in, own_out)
    gathered = [lax.all_gather(p, "fsdp", axis=0, tiled=False) for p in packs]

    def weights_after(chunk, done):
        full = tie(gathered[chunk], done)
        return [full] + [to_part(full, m) for m in range(1, copies)]

    docs = doc_ids.reshape(-1)
    drow = docs[None, :]
    dcol = docs[:, None]
    vcol = valid_mask.reshape(-1)[:, None]
    first_place = jnp.sum((drow < dcol).astype(jnp.int32), axis=1)
    offset = (jnp.arange(rows, dtype=jnp.int32) - first_place).astype(f32)
    frequency = jnp.exp(
        jnp.arange(HDIM // 2, dtype=f32) * (-2.0 * math.log(10000.0) / HDIM)
    )
    angles = offset[:, None] * frequency[None, :]
    cosine, sine = jnp.cos(angles), jnp.sin(angles)
    cosine = jnp.concatenate([cosine] * 4, axis=1)
    sine = jnp.concatenate([-sine, sine, -sine, sine], axis=1)

    routes_t = routes.T
    chosen = jnp.where(routes_t < EXPERTS, routes_t ^ mine, routes_t)
    kinds = jnp.arange(EXPERTS, dtype=jnp.int32)
    named = jnp.any(chosen[:, None, :] == kinds[None, :, None], axis=0)
    later = jnp.triu(jnp.ones((rows, rows), bf16), 1)
    rank = mm(named.astype(bf16), later).astype(jnp.int32)
    spot = jnp.where(named, rank, CAP)
    hit = chosen[:, None, :] == kinds[None, :, None]
    places = jnp.sum(jnp.where(hit, (kinds[:, None] * CAP + rank)[None], 0), axis=1)
    places = jnp.where(chosen < EXPERTS, places, -1).T

    qkv_part, small, prevs = lay_shards(
        zi_s, spun, shard, quarter, width, (packs[0],)
    )
    pmix = prevs[:, :owned].reshape(NCH, LANES)

    def exchanged(blocks):
        return [blocks[0]] + [to_expert(blocks[k], k) for k in range(1, EXPERTS)]

    def over_parts(half):
        half = half.reshape(D, half.shape[3])
        pieces = [half] + [to_part(half, m) for m in range(1, copies)]
        if half.shape[1] % LANES == 0:
            return pieces
        return [by_xor(pieces, part, 1)]

    qkv_half = lay_xor(
        mine_s, exchanged([qkv_part] * EXPERTS), (cosine, sine, spot, dcol, vcol, places)
    )
    qkv_pieces = over_parts(qkv_half)
    part_q = part_s if len(qkv_pieces) == copies else jnp.zeros_like(part_s)
    ys = dispatch_call(mine_s, spot, out_grad, after=(qkv_half,))
    proj_part = lay_proj(zi_s, spun, quarter, width, (ys[0],))

    prev = prev_logits.T
    h1, q, k, v = qkv_call(
        part_q, tokens, small, cosine, sine, qkv_pieces, (ys[0], proj_part)
    )
    proj_half = lay_xor(mine_s, exchanged([proj_part] * EXPERTS), (h1,))
    proj_pieces = over_parts(proj_half)
    part_p = part_s if len(proj_pieces) == copies else jnp.zeros_like(part_s)
    ctx, lse = attend_call(q, k, v, dcol, drow, vcol, (proj_half,))
    ys = exchanged(ys)
    ctx = tie(ctx, ys)
    res, h2, one, gates = after_call(
        part_p, ctx, tokens, small, prev, pmix, routes, proj_pieces
    )

    xs = dispatch_call(mine_s, spot, h2, gates)
    weights = [weights_after(0, ctx)] + [
        weights_after(c, xs[0]) for c in range(1, plan.chunks)
    ]
    xs = exchanged(xs)
    carried = None
    chunk_grads = []
    for chunk in range(plan.chunks):
        grads, carried = expert_call(
            plan, xs, ys, weights[chunk], carried, chunk == plan.chunks - 1
        )
        chunk_grads.append(grads)
    dx = exchanged(carried[:EXPERTS])

    totals = [
        fold_copies([grads[0]] + [to_part(grads[m], m) for m in range(1, copies)])
        for grads in chunk_grads
    ]
    summed = [lax.psum_scatter(t, "fsdp", scatter_dimension=0, tiled=False) for t in totals]

    who_p = jnp.concatenate([mine_s, part_p])
    dres, branch, dctx, dsmall, gain_f_grad, prev_grad, cvec_grad = back_call(
        who_p,
        res,
        h2,
        out_grad,
        one,
        places,
        routes,
        prev,
        small,
        dx,
        proj_pieces,
        totals,
    )
    ret = exchanged(tie(carried[EXPERTS:], branch))
    dq, dk, dv = attend_back_call(q, k, v, dctx, lse, dcol, drow, vcol, cosine, sine, ())
    spread = [exchanged([tie(summed[0], dq)] * EXPERTS)]
    dense = dense_call(copies, h1, ctx, tie(dq, ret), dk, dv, branch, ())

    def columns(index):
        if copies == 2:
            return jnp.where(index == 0, dense[0], dense[1])
        return lax.dynamic_index_in_dim(jnp.stack(dense), index, 0, keepdims=False)

    got = [to_part(columns(part ^ m), m) for m in range(1, copies)]
    input_grad, smalls = last_call(
        part_q,
        shards,
        dq,
        dk,
        dv,
        tokens,
        dres,
        small,
        (dsmall, gain_f_grad, prev_grad, cvec_grad),
        qkv_pieces,
        (dense[0],),
    )
    quarters = fold_parts(who, dense, got, smalls, shards)
    quarters = tie(quarters, spread[0])

    def over_copies(pieces):
        stacked = jnp.stack(pieces)
        return [stacked] + [to_part(stacked, m) for m in range(1, copies)]

    spread[0] = over_copies(tie(spread[0], quarters))
    begun = ()
    if plan.seg % LANES == 0:
        begun = unpack_chunk(plan, who, 0, spread[0], begun)
    bands = fold_quarters(zi_s, exchanged(quarters), begun)
    spread += [exchanged([tie(piece, bands)] * EXPERTS) for piece in summed[1:]]
    out = finish_call(res, one, places, routes, small, tie(ret, bands), ())
    tail = fold_shards(
        [bands[0]] + tie([spin(bands[k], k) for k in range(1, shards)], out)
    )
    spread[1:] = [over_copies(tie(pieces, tail)) for pieces in spread[1:]]
    tail = lay_xor(mine_s, [t[None] for t in exchanged([tail] * EXPERTS)])
    tail = tail.reshape(shard, tail.shape[3])
    tails = [tail] + [to_part(tail, m) for m in range(1, copies)]
    qkv_grad, proj_grad, small_grad = unpack_dense(part_s, tails)

    full_in, full_out = unpack_grads(plan, who, spread, begun)
    return (
        out,
        input_grad,
        qkv_grad,
        proj_grad,
        small_grad[:, GAIN_A],
        small_grad[:, GAIN_F],
        small_grad[:, :NCH],
        small_grad[:, NCH : NCH + 4],
        small_grad[:owned, 16 : 16 + NCH],
        small_grad[:, CVEC : CVEC + 2],
        full_in,
        full_out,
    )


def solution(mesh):
    replicas, shards = mesh.shape["rep"], mesh.shape["fsdp"]
    split = P(("rep", "fsdp"), None)
    matrix = P("fsdp", None)
    cube = P("fsdp", None, None)
    in_specs = (split,) * 6 + (matrix, matrix, P("fsdp"), P("fsdp")) + (matrix,) * 4 + (cube, cube)
    out_specs = (split, split, matrix, matrix, P("fsdp"), P("fsdp")) + (matrix,) * 4 + (cube, cube)
    return jax.shard_map(
        partial(body, replicas, shards),
        mesh=mesh,
        in_specs=in_specs,
        out_specs=out_specs,
        check_vma=False,
    )
```

```python
from functools import partial
import math

import jax
import jax.numpy as jnp
from jax import lax
from jax.experimental import pallas as pl
from jax.experimental.pallas import tpu as pltpu
from jax.sharding import PartitionSpec as P

D = 768
HEADS = 12
HDIM = 64
EXPERTS = 4
NCH = 8
CAP = 384
LANES = 128
QB = 256
REACH = 512
VMEM_BYTES = 58 * 1024 * 1024
EPS = 1e-06
COST_SCALE = 0.02
f32 = jnp.float32
bf16 = jnp.bfloat16

NT = (((1,), (1,)), ((), ()))
TN = (((0,), (0,)), ((), ()))


def mm(a, b):
    return jnp.dot(a, b, preferred_element_type=f32)


def mm_nt(a, b):
    return lax.dot_general(a, b, NT, preferred_element_type=f32)


def mm_tn(a, b):
    return lax.dot_general(a, b, TN, preferred_element_type=f32)


def params(steps=1):
    return pltpu.CompilerParams(
        dimension_semantics=("arbitrary",) * steps, vmem_limit_bytes=VMEM_BYTES
    )


def cost(flops, nbytes):
    return pl.CostEstimate(
        flops=int(flops * COST_SCALE), bytes_accessed=int(nbytes * COST_SCALE), transcendentals=0
    )


def launch(kernel, operands, in_specs, out_specs, out_shape, after=(), **kw):
    n, skip = len(operands), len(after)

    def run(*refs):
        kernel(*refs[:n], *refs[n + skip :])

    kw.setdefault("compiler_params", pltpu.CompilerParams(vmem_limit_bytes=VMEM_BYTES))
    return pl.pallas_call(
        run,
        in_specs=list(in_specs) + [pl.BlockSpec(memory_space=pl.ANY)] * skip,
        out_specs=out_specs,
        out_shape=out_shape,
        **kw,
    )(*operands, *after)


def tie(value, *others):
    return lax.optimization_barrier((value, others))[0]


VM = pl.BlockSpec(memory_space=pltpu.VMEM)
SMEM = pl.BlockSpec(memory_space=pltpu.SMEM)
CVEC, GAIN_A, GAIN_F = NCH + 4, NCH + 6, NCH + 7


def row_of(ref, row):
    return ref[:16, :].astype(f32)[row : row + 1]


def whole(shape):
    return pl.BlockSpec(shape, lambda *_: (0,) * len(shape), pipeline_mode=pl.Buffered(1))


def rows_of(block, width):
    return pl.BlockSpec((block, width), lambda i: (i, 0))


def swap_halves(v):
    lane = lax.broadcasted_iota(jnp.int32, v.shape, 1)
    half = HDIM // 2
    ahead = pltpu.roll(v, LANES - half, 1)
    behind = pltpu.roll(v, half, 1)
    return jnp.where(lane % HDIM < half, ahead, behind)


def lay_columns(full_ref, pieces, part):
    width = pieces[0].shape[1]
    for p in range(len(pieces)):
        chosen = pieces[0][...]
        for m in range(1, len(pieces)):
            chosen = jnp.where(part == (p ^ m), pieces[m][...], chosen)
        full_ref[:, p * width : (p + 1) * width] = chosen


def qkv_kernel(count, part_ref, x_ref, small_ref, cos_ref, sin_ref, *refs):
    pieces = refs[:count]
    h_ref, q_ref, k_ref, v_ref, w_ref = refs[count:]

    @pl.when(pl.program_id(0) == 0)
    def _():
        lay_columns(w_ref, pieces, part_ref[0])

    x = x_ref[...].astype(f32)
    inverse = lax.rsqrt(jnp.mean(x * x, axis=-1, keepdims=True) + EPS)
    h = (x * inverse * row_of(small_ref, GAIN_A)).astype(bf16)
    h_ref[...] = h
    cosine, sine = cos_ref[...], sin_ref[...]
    mixed = mm(h, w_ref[...])
    for out_ref, base, scale in ((q_ref, 0, HDIM**-0.5), (k_ref, D, 1.0)):
        for c in range(0, D, LANES):
            v = mixed[:, base + c : base + c + LANES]
            turned = v * cosine + swap_halves(v) * sine
            out_ref[:, c : c + LANES] = (turned.astype(bf16).astype(f32) * scale).astype(bf16)
    v_ref[...] = mixed[:, 2 * D :].astype(bf16)


def qkv_call(part, x, small, cosine, sine, pieces, after):
    rows = x.shape[0]
    block = 256
    wide = jax.ShapeDtypeStruct((rows, D), bf16)
    return launch(
        partial(qkv_kernel, len(pieces)),
        [part, x, small, cosine, sine, *pieces],
        [
            SMEM,
            rows_of(block, D),
            whole(small.shape),
            rows_of(block, LANES),
            rows_of(block, LANES),
        ]
        + [whole(p.shape) for p in pieces],
        [rows_of(block, D)] * 4,
        [wide] * 4,
        after,
        grid=(rows // block,),
        scratch_shapes=[pltpu.VMEM((D, 3 * D), bf16)],
        compiler_params=params(),
        cost_estimate=cost(2 * rows * D * 3 * D, 2 * (5 * rows * D + 3 * D * D)),
        name="qkv_rope",
    )


def fill_bias(bias_ref, dcol_ref, drow_ref, vcol_ref, length):
    for i in range(length // QB):
        start = i * QB
        low = max(0, start - REACH)
        size = start + QB - low
        key = low + lax.broadcasted_iota(jnp.int32, (size, QB), 0)
        query = start + lax.broadcasted_iota(jnp.int32, (size, QB), 1)
        same = dcol_ref[low : low + size, :] == drow_ref[:, start : start + QB]
        usable = (vcol_ref[low : low + size, :] > 0) | (key == query)
        allowed = same & (key <= query) & usable
        bias_ref[i, :size, :] = jnp.where(allowed, 0.0, -1e30)


def lane_head(shape, head):
    lane = lax.broadcasted_iota(jnp.int32, shape, 1)
    return (lane // HDIM) == head


def attend_kernel(q_ref, k_ref, v_ref, dcol_ref, drow_ref, vcol_ref, ctx_ref, lse_ref, bias_ref):
    length = q_ref.shape[0]

    @pl.when(pl.program_id(0) == 0)
    def _():
        fill_bias(bias_ref, dcol_ref, drow_ref, vcol_ref, length)

    values_t = v_ref[...].astype(f32).T.astype(bf16)
    for i in range(length // QB):
        start = i * QB
        low = max(0, start - REACH)
        size = start + QB - low
        keys = k_ref[low : low + size, :]
        query = q_ref[start : start + QB, :]
        parts = []
        for head in range(2):
            masked = jnp.where(lane_head(query.shape, head), query, jnp.zeros_like(query))
            scores = mm_nt(keys, masked) + bias_ref[i, :size, :]
            largest = jnp.max(scores, axis=0, keepdims=True)
            raised = jnp.exp(scores - largest)
            total = jnp.sum(raised, axis=0, keepdims=True)
            part = mm(
                values_t[head * HDIM : (head + 1) * HDIM, low : low + size], raised.astype(bf16)
            )
            parts.append(part * (1.0 / total))
            lse_ref[0, head : head + 1, start : start + QB] = largest + jnp.log(total)
        ctx_ref[start : start + QB, :] = jnp.concatenate(parts, axis=0).T.astype(bf16)


def attend_call(q, k, v, dcol, drow, vcol, after):
    length = q.shape[0]
    pairs = HEADS // 2
    column = pl.BlockSpec((length, LANES), lambda p: (0, p))
    return launch(
        attend_kernel,
        [q, k, v, dcol, drow, vcol],
        [column, column, column, whole(dcol.shape), whole(drow.shape), whole(vcol.shape)],
        [column, pl.BlockSpec((1, 2, length), lambda p: (p, 0, 0))],
        [
            jax.ShapeDtypeStruct((length, D), bf16),
            jax.ShapeDtypeStruct((pairs, 2, length), f32),
        ],
        after,
        grid=(pairs,),
        scratch_shapes=[pltpu.VMEM((length // QB, REACH + QB, QB), f32)],
        compiler_params=params(),
        cost_estimate=cost(20e9, 8 * length * D),
        name="attend",
    )


def attend_back_kernel(
    q_ref,
    k_ref,
    v_ref,
    g_ref,
    lse_ref,
    dcol_ref,
    drow_ref,
    vcol_ref,
    cos_ref,
    sin_ref,
    dq_ref,
    dk_ref,
    dv_ref,
    bias_ref,
    gk_ref,
    gv_ref,
    gq_ref,
):
    length = q_ref.shape[0]

    @pl.when(pl.program_id(0) == 0)
    def _():
        fill_bias(bias_ref, dcol_ref, drow_ref, vcol_ref, length)

    gk_ref[...] = jnp.zeros_like(gk_ref)
    gv_ref[...] = jnp.zeros_like(gv_ref)
    keys_t = k_ref[...].astype(f32).T.astype(bf16)
    for i in range(length // QB):
        start = i * QB
        low = max(0, start - REACH)
        size = start + QB - low
        span = slice(low, low + size)
        keys = k_ref[span, :]
        values = v_ref[span, :]
        query = q_ref[start : start + QB, :]
        grads = g_ref[start : start + QB, :]
        for head in range(2):
            own = lane_head(query.shape, head)
            query_h = jnp.where(own, query, jnp.zeros_like(query))
            grads_h = jnp.where(own, grads, jnp.zeros_like(grads))
            scores = mm_nt(keys, query_h) + bias_ref[i, :size, :]
            probs = jnp.exp(scores - lse_ref[0, head : head + 1, start : start + QB])
            grad_probs = mm_nt(values, grads_h)
            inner = jnp.sum(probs * grad_probs, axis=0, keepdims=True)
            grad_scores = (probs * (grad_probs - inner)).astype(bf16)
            gv_ref[span, :] += mm(probs.astype(bf16), grads_h)
            gk_ref[span, :] += mm(grad_scores, query_h)
            gq_ref[head * HDIM : (head + 1) * HDIM, start : start + QB] = mm(
                keys_t[head * HDIM : (head + 1) * HDIM, span], grad_scores
            )
    cosine, sine = cos_ref[...], sin_ref[...]
    grad_q = gq_ref[...].T * HDIM**-0.5
    grad_k = gk_ref[...]
    dq_ref[...] = (grad_q * cosine - swap_halves(grad_q) * sine).astype(bf16)
    dk_ref[...] = (grad_k * cosine - swap_halves(grad_k) * sine).astype(bf16)
    dv_ref[...] = gv_ref[...].astype(bf16)


def attend_back_call(q, k, v, g, lse, dcol, drow, vcol, cosine, sine, after):
    length = q.shape[0]
    pairs = HEADS // 2
    column = pl.BlockSpec((length, LANES), lambda p: (0, p))
    return launch(
        attend_back_kernel,
        [q, k, v, g, lse, dcol, drow, vcol, cosine, sine],
        [column] * 4
        + [pl.BlockSpec((1, 2, length), lambda p: (p, 0, 0))]
        + [whole(a.shape) for a in (dcol, drow, vcol, cosine, sine)],
        [column] * 3,
        [jax.ShapeDtypeStruct((length, D), bf16)] * 3,
        after,
        grid=(pairs,),
        scratch_shapes=[
            pltpu.VMEM((length // QB, REACH + QB, QB), f32),
            pltpu.VMEM((length, LANES), f32),
            pltpu.VMEM((length, LANES), f32),
            pltpu.VMEM((LANES, length), f32),
        ],
        compiler_params=params(),
        cost_estimate=cost(45e9, 14 * length * D),
        name="attend_back",
    )


def cut_dense_kernel(quarter, widths, who_ref, qkv_ref, proj_ref, small_ref, out_ref, token_ref):
    token_ref[0] = who_ref[0]
    row = pl.multiple_of(who_ref[0] * quarter, quarter)
    start = 0
    for ref, width in zip((qkv_ref, proj_ref), widths, strict=True):
        column = pl.multiple_of(who_ref[1] * width, LANES)
        out_ref[:quarter, start : start + width] = ref[pl.ds(row, quarter), pl.ds(column, width)]
        start += width
    shard = small_ref.shape[1]
    out_ref[quarter:, :] = jnp.zeros((16, start), bf16)
    out_ref[quarter:, :shard] = small_ref[:16, :]
    out_ref[quarter:, 2 * LANES : 3 * LANES] = small_ref[16:, :LANES]


def cut_dense(who, qkv, proj, small, copies):
    shard = qkv.shape[0]
    quarter = shard // EXPERTS
    widths = (qkv.shape[1] // copies, proj.shape[1] // copies)
    total = sum(widths)
    if quarter % 16 == 0 and all(w % LANES == 0 for w in widths):
        return launch(
            partial(cut_dense_kernel, quarter, widths),
            [who, qkv, proj, small],
            [SMEM, VM, VM, VM],
            [VM, SMEM],
            [
                jax.ShapeDtypeStruct((quarter + 16, total), bf16),
                jax.ShapeDtypeStruct((1,), jnp.int32),
            ],
            name="cut_dense",
        )
    row = who[0] * quarter
    cuts = [
        lax.dynamic_slice(w, (row, who[1] * width), (quarter, width))
        for w, width in zip((qkv, proj), widths, strict=True)
    ]
    spare = total - 3 * LANES
    below = jnp.concatenate(
        [
            jnp.pad(small[:16], ((0, 0), (0, 2 * LANES - shard))),
            jnp.pad(small[16:], ((0, 0), (0, 2 * LANES - shard)))[:, :LANES],
            jnp.zeros((16, spare), bf16),
        ],
        axis=1,
    )
    return jnp.concatenate([jnp.concatenate(cuts, axis=1), below]), who[:1]


def lay_shards_kernel(count, shard, quarter, width, zi_ref, *refs):
    pieces = refs[:count]
    qkv_ref, proj_ref, small_ref, prev_ref = refs[count:]
    for k in range(count):
        at = lax.rem(zi_ref[0] + count - k, count)
        qkv_ref[at] = pieces[k][:quarter, :width]
        proj_ref[at] = pieces[k][:quarter, width:]
        prev_ref[at] = pieces[k][quarter:, 2 * LANES : 3 * LANES]
    small_ref[16:, :] = jnp.zeros((LANES - 16, D), bf16)
    for z in range(count):
        chosen = pieces[0][quarter:, : 2 * LANES].astype(f32)
        for k in range(1, count):
            here = lax.rem(zi_ref[0] + count - k, count) == z
            chosen = jnp.where(here, pieces[k][quarter:, : 2 * LANES].astype(f32), chosen)
        small_ref[:16, z * shard : (z + 1) * shard] = chosen[:, :shard].astype(bf16)


def lay_shards(zi, pieces, shard, quarter, width, after):
    count = len(pieces)
    return launch(
        partial(lay_shards_kernel, count, shard, quarter, width),
        [zi, *pieces],
        [SMEM] + [VM] * count,
        [VM] * 4,
        [
            jax.ShapeDtypeStruct((count, quarter, width), bf16),
            jax.ShapeDtypeStruct((count, quarter, pieces[0].shape[1] - width), bf16),
            jax.ShapeDtypeStruct((LANES, D), bf16),
            jax.ShapeDtypeStruct((count, 16, LANES), bf16),
        ],
        after,
        name="lay_shards",
    )


def lay_xor_kernel(count, own_ref, *refs):
    pieces, out = refs[:count], refs[count]
    for k in range(count):
        out[:, own_ref[0] ^ k] = pieces[k][...]


def lay_xor(own, pieces, after=()):
    count = len(pieces)
    first, rows, columns = pieces[0].shape
    return launch(
        partial(lay_xor_kernel, count),
        [own, *pieces],
        [SMEM] + [VM] * count,
        VM,
        jax.ShapeDtypeStruct((first, count, rows, columns), bf16),
        after,
        name="lay_xor",
    )


def lay_riders_kernel(shape, own_ref, *refs):
    pieces, out = refs[:-1], refs[-1]
    shards, quarter, width = shape
    per = D // width
    for k, piece in enumerate(pieces):
        for z in range(shards):
            row, column = z // per * quarter, z % per * width
            out[z, own_ref[0] ^ k] = piece[CAP + row : CAP + row + quarter, column : column + width]


def lay_riders(own, blocks, shape, after):
    shards, quarter, width = shape
    return launch(
        partial(lay_riders_kernel, shape),
        [own, *blocks],
        [SMEM] + [VM] * len(blocks),
        VM,
        jax.ShapeDtypeStruct((shards, len(blocks), quarter, width), bf16),
        after,
        name="lay_riders",
    )


def lanes_of(shape):
    return lax.broadcasted_iota(jnp.int32, shape, 1)


def partner(v, lane):
    return jnp.where(lane % 2 == 0, pltpu.roll(v, LANES - 1, 1), pltpu.roll(v, 1, 1))


def selected(choice_ref, lane):
    return (lane == choice_ref[:, 0:1]) | (lane == choice_ref[:, 1:2])


def after_kernel(
    count, part_ref, ctx_ref, x_ref, wsmall_ref, prev_ref, pmix_ref, choice_ref, *refs
):
    pieces = refs[:count]
    res_ref, h_ref, one_ref, gate_ref, w_ref = refs[count:]

    @pl.when(pl.program_id(0) == 0)
    def _():
        lay_columns(w_ref, pieces, part_ref[0])

    res = x_ref[...].astype(f32) + mm(ctx_ref[...], w_ref[...])
    res_ref[...] = res
    inverse = lax.rsqrt(jnp.mean(res * res, axis=-1, keepdims=True) + EPS)
    low = (res * inverse * row_of(wsmall_ref, GAIN_F)).astype(bf16)
    h_ref[...] = low
    small = mm_nt(low, wsmall_ref[...])
    logits = small + mm_tn(prev_ref[...], pmix_ref[...])
    lane = lanes_of(small.shape)
    choice = lane < NCH
    top = jnp.max(jnp.where(choice, logits, -1e30), axis=-1, keepdims=True)
    raised = jnp.where(choice, jnp.exp(jnp.where(choice, logits - top, 0.0)), 0.0)
    gates = raised / jnp.sum(raised, axis=-1, keepdims=True)
    mixing = 1.0 / (1.0 + jnp.exp(partner(small, lane) - small))
    is_mix = (lane >= NCH) & (lane < NCH + 4)
    one_ref[...] = jnp.where(choice, gates, jnp.where(is_mix, mixing, 0.0))
    taken = jnp.where(selected(choice_ref, lane), gates, 0.0).T[:NCH]
    high = taken.astype(bf16).astype(f32)
    gate_ref[...] = jnp.concatenate([high, taken - high], axis=0).astype(bf16)


def after_call(part, ctx, x, small, prev, pmix, choices, pieces):
    rows = x.shape[0]
    block = 256
    return launch(
        partial(after_kernel, len(pieces)),
        [part, ctx, x, small, prev, pmix, choices, *pieces],
        [SMEM]
        + [rows_of(block, D)] * 2
        + [
            whole(small.shape),
            pl.BlockSpec((NCH, block), lambda i: (0, i)),
            whole(pmix.shape),
            rows_of(block, 2),
        ]
        + [whole(p.shape) for p in pieces],
        [rows_of(block, D)] * 2
        + [rows_of(block, LANES), pl.BlockSpec((2 * NCH, block), lambda i: (0, i))],
        [
            jax.ShapeDtypeStruct((rows, D), f32),
            jax.ShapeDtypeStruct((rows, D), bf16),
            jax.ShapeDtypeStruct((rows, LANES), f32),
            jax.ShapeDtypeStruct((2 * NCH, rows), bf16),
        ],
        grid=(rows // block,),
        scratch_shapes=[pltpu.VMEM((D, D), bf16)],
        compiler_params=params(),
        cost_estimate=cost(2 * rows * D * D, 10 * rows * D),
        name="after_attention",
    )


EXTRA = 16


def dispatch_kernel(gated, mine_ref, spot_ref, v_ref, *refs):
    if gated:
        gate_ref, refs = refs[0], refs[1:]
    else:
        rider, refs = refs[0], refs[1:]
    rows = v_ref.shape[0]
    slot = lax.broadcasted_iota(jnp.int32, (CAP, rows), 0)
    for k in range(EXPERTS):
        hits = jnp.where(slot == spot_ref[k : k + 1, :], 1.0, 0.0).astype(bf16)
        refs[k][:CAP, :] = mm(hits, v_ref[...]).astype(bf16)
        if gated:
            moved = mm_nt(gate_ref[...], hits)
            row = lax.broadcasted_iota(jnp.int32, moved.shape, 0) % NCH
            moved = jnp.where(row == (mine_ref[0] ^ k), moved, 0.0)
            high = jnp.sum(moved[:NCH], axis=0, keepdims=True)
            rest = jnp.sum(moved[NCH:], axis=0, keepdims=True)
            tail = jnp.concatenate(
                [high, rest, jnp.zeros((EXTRA - 2, CAP), f32)], axis=0
            ).astype(bf16)
            refs[k][CAP:, :CAP] = tail
            refs[k][CAP:, CAP:] = jnp.zeros((EXTRA, D - CAP), bf16)
        else:
            refs[k][CAP:, :] = rider[...]


def dispatch_call(mine, spot, values, gates=None, rider=None, after=()):
    size = CAP + (EXTRA if rider is None else rider.shape[0])
    operands = [mine, spot, values] + [rider if gates is None else gates]
    rows = values.shape[0]
    return launch(
        partial(dispatch_kernel, gates is not None),
        operands,
        [SMEM] + [VM] * (len(operands) - 1),
        [VM] * EXPERTS,
        [jax.ShapeDtypeStruct((size, D), bf16)] * EXPERTS,
        after,
        cost_estimate=cost(2 * rows * D * CAP * EXPERTS, 2 * rows * D + 2 * EXPERTS * CAP * D),
        name="dispatch",
    )


class Plan:
    def __init__(self, replicas, shards, shard, hidden, chunks):
        self.copies = replicas // EXPERTS
        self.shards = shards
        self.shard = shard
        self.hidden = hidden
        self.chunks = chunks
        self.seg = hidden // (shards * self.copies * chunks)
        self.width = self.seg * shards
        self.wide = min(256, self.width)
        self.tiles = self.width // self.wide
        self.spans = self.wide // self.seg
        self.downs = D // self.wide
        self.rows = 2 * self.tiles * shard + self.downs * self.seg

    def column(self, half, tile, span, part, chunk):
        z = tile * self.spans + span
        base = half * self.hidden + z * (self.hidden // self.shards)
        return base + (part * self.chunks + chunk) * self.seg

    def down_row(self, part, chunk):
        return (part * self.chunks + chunk) * self.seg


def pack_kernel(plan, part_ref, in_ref, out_ref, *packs):
    part = part_ref[0]
    seg, shard = plan.seg, plan.shard
    for chunk in range(plan.chunks):
        pack = packs[chunk]
        for half in range(2):
            for tile in range(plan.tiles):
                row = (half * plan.tiles + tile) * shard
                for span in range(plan.spans):
                    at = pl.multiple_of(plan.column(half, tile, span, part, chunk), LANES)
                    pack[row : row + shard, span * seg : (span + 1) * seg] = in_ref[
                        :, pl.ds(at, seg)
                    ]
        row = 2 * plan.tiles * shard
        at = pl.multiple_of(plan.down_row(part, chunk), seg)
        for down in range(plan.downs):
            pack[row + down * seg : row + (down + 1) * seg, :] = out_ref[
                pl.ds(at, seg), down * plan.wide : (down + 1) * plan.wide
            ]


def pack_pieces(plan, part, own_in, own_out):
    if plan.seg % LANES == 0:
        vmem = pl.BlockSpec(memory_space=pltpu.VMEM)
        return pl.pallas_call(
            partial(pack_kernel, plan),
            in_specs=[SMEM, vmem, vmem],
            out_specs=[vmem] * plan.chunks,
            out_shape=[jax.ShapeDtypeStruct((plan.rows, plan.wide), bf16)] * plan.chunks,
            compiler_params=pltpu.CompilerParams(vmem_limit_bytes=VMEM_BYTES),
            name="pack",
        )(part, own_in, own_out)
    packs = []
    for chunk in range(plan.chunks):
        blocks = []
        for half in range(2):
            for tile in range(plan.tiles):
                spans = [
                    lax.dynamic_slice_in_dim(
                        own_in, plan.column(half, tile, span, part[0], chunk), plan.seg, 1
                    )
                    for span in range(plan.spans)
                ]
                blocks.append(jnp.concatenate(spans, axis=1))
        rows = lax.dynamic_slice_in_dim(own_out, plan.down_row(part[0], chunk), plan.seg, 0)
        blocks += [rows[:, d * plan.wide : (d + 1) * plan.wide] for d in range(plan.downs)]
        packs.append(jnp.concatenate(blocks, axis=0))
    return packs


def unpack_kernel(plan, begun, who_ref, *refs):
    copies, seg = plan.copies, plan.seg
    ins, downs = refs[:copies], refs[copies : 2 * copies]
    in_out, down_out = refs[2 * copies + 2 * begun :]
    mine, part = who_ref[0], who_ref[1]
    step = pl.program_id(0)
    p = step % copies
    z = (step // copies) % plan.shards
    for j in range(EXPERTS):
        chosen = ins[0][j ^ mine].astype(f32)
        for m in range(1, copies):
            chosen = jnp.where(part == (p ^ m), ins[m][j ^ mine].astype(f32), chosen)
        piece = chosen[:, :seg]
        for span in range(1, plan.spans):
            here = z % plan.spans == span
            piece = jnp.where(here, chosen[:, span * seg : (span + 1) * seg], piece)
        in_out[:, j, :] = piece

    @pl.when(step < copies)
    def _():
        for j in range(EXPERTS):
            for down in range(plan.downs):
                rows = slice(down * seg, (down + 1) * seg)
                chosen = downs[0][j ^ mine, rows, :].astype(f32)
                for m in range(1, copies):
                    chosen = jnp.where(
                        part == (p ^ m), downs[m][j ^ mine, rows, :].astype(f32), chosen
                    )
                down_out[:, j, down * plan.wide : (down + 1) * plan.wide] = chosen


def unpack_chunk(plan, who, chunk, sums, begun):
    copies, shards = plan.copies, plan.shards
    per = plan.hidden // shards
    start = 2 * plan.tiles * plan.shard
    down_rows = plan.downs * plan.seg

    def in_block(i):
        half, z = i // (shards * copies), (i // copies) % shards
        return (0, half * plan.tiles + z // plan.spans, 0)

    def down_block(i):
        return (jnp.minimum(i, copies - 1) * plan.chunks + chunk, 0, 0)

    hbm = pl.BlockSpec(memory_space=pl.ANY)
    operands = [who, *sums, *[s[:, start:, :] for s in sums], *begun]
    return launch(
        partial(unpack_kernel, plan, len(begun) // 2),
        operands,
        [SMEM]
        + [pl.BlockSpec((EXPERTS, plan.shard, plan.wide), in_block)] * copies
        + [whole((EXPERTS, down_rows, plan.wide))] * copies
        + [hbm] * len(begun),
        [
            pl.BlockSpec((plan.shard, EXPERTS, plan.seg), lambda i: (0, 0, i * plan.chunks + chunk)),
            pl.BlockSpec((plan.seg, EXPERTS, D), down_block),
        ],
        [
            jax.ShapeDtypeStruct((plan.shard, EXPERTS, 2 * plan.hidden), f32),
            jax.ShapeDtypeStruct((per, EXPERTS, D), f32),
        ],
        grid=(2 * shards * copies,),
        input_output_aliases={len(operands) - 2 + i: i for i in range(len(begun))},
        compiler_params=params(),
        cost_estimate=cost(0, 12 * plan.shard * plan.hidden * EXPERTS),
        name="unpack",
    )


def unpack_grads(plan, who, sums, begun):
    if begun:
        for chunk in range(1, plan.chunks):
            begun = unpack_chunk(plan, who, chunk, sums[chunk], begun)
        return begun
    mine, part = who[0], who[1]
    ins, outs = [], []
    for j in range(EXPERTS):
        columns = {}
        rows = []
        for p in range(plan.copies):
            for chunk in range(plan.chunks):
                stacked = jnp.stack(sums[chunk])
                piece = lax.dynamic_index_in_dim(stacked, part ^ p, 0, keepdims=False)
                piece = lax.dynamic_index_in_dim(piece, mine ^ j, 0, keepdims=False)
                for half in range(2):
                    for tile in range(plan.tiles):
                        row = (half * plan.tiles + tile) * plan.shard
                        for span in range(plan.spans):
                            columns[plan.column(half, tile, span, p, chunk)] = piece[
                                row : row + plan.shard, span * plan.seg : (span + 1) * plan.seg
                            ]
                row = 2 * plan.tiles * plan.shard
                rows.append(
                    jnp.concatenate(
                        [
                            piece[row + d * plan.seg : row + (d + 1) * plan.seg]
                            for d in range(plan.downs)
                        ],
                        axis=1,
                    )
                )
        ins.append(jnp.concatenate([columns[c] for c in sorted(columns)], axis=1))
        outs.append(jnp.concatenate(rows, axis=0))
    return jnp.stack(ins, axis=1).astype(f32), jnp.stack(outs, axis=1).astype(f32)


def expert_kernel(plan, first, last, *refs):
    refs = list(refs)

    def take(n):
        out = refs[:n]
        del refs[:n]
        return out

    copies = plan.copies
    x_refs, y_refs = take(EXPERTS), take(EXPERTS)
    w_refs = take(copies)
    carry_in = [] if first else take(2)
    grad_outs = take(copies)
    if last:
        dx_outs, ret_outs = take(EXPERTS), take(EXPERTS)
        carry_out = []
    else:
        carry_out = take(2)
    xs, ds, xt, gcol, ret_acc, dx_acc, wg, wu, wo, act_s, dg_s, du_s, grads, sems = refs
    rows = EXPERTS * CAP
    shard, seg, wide, tiles = plan.shard, plan.seg, plan.wide, plan.tiles

    carries = [
        pltpu.make_async_copy(src, dst, sems.at[i])
        for i, (src, dst) in enumerate(zip(carry_in, (ret_acc, dx_acc)))
    ]
    for copy in carries:
        copy.start()
    for k in range(EXPERTS):
        span = slice(k * CAP, (k + 1) * CAP)
        x = x_refs[k][:CAP, :]
        xs[span, :] = x
        xt[:, span] = x.astype(f32).T.astype(bf16)
        extra = x_refs[k][CAP:, :CAP].astype(f32)
        gate = (extra[0:1] + extra[1:2]).T
        gcol[span, :] = jnp.broadcast_to(gate, (CAP, LANES))
        ds[span, :] = (y_refs[k][:CAP, :].astype(f32) * gate).astype(bf16)
    if first:
        ret_acc[...] = jnp.zeros_like(ret_acc)
        dx_acc[...] = jnp.zeros_like(dx_acc)
    for copy in carries:
        copy.wait()

    sends = []
    for m in range(copies):
        w = w_refs[m]
        for z in range(plan.shards):
            for tile in range(tiles):
                for half, target in ((0, wg), (1, wu)):
                    row = (half * tiles + tile) * shard
                    target[z * shard : (z + 1) * shard, tile * wide : (tile + 1) * wide] = w[
                        z, row : row + shard, :
                    ]
            for down in range(plan.downs):
                row = 2 * tiles * shard + down * seg
                wo[z * seg : (z + 1) * seg, down * wide : (down + 1) * wide] = w[
                    z, row : row + seg, :
                ]

        def block(b, _):
            span = pl.ds(pl.multiple_of(b * CAP, CAP), CAP)
            x, d = xs[span, :], ds[span, :]
            gate = mm(x, wg[...])
            up = mm(x, wu[...])
            grad_act = mm_nt(d, wo[...])
            sig = 1.0 / (1.0 + jnp.exp(-gate))
            silu = gate * sig
            act = (silu * up).astype(bf16)
            grad_up = (grad_act * silu).astype(bf16)
            grad_gate = (grad_act * up * (sig + silu * (1.0 - sig))).astype(bf16)
            act_s[span, :] = act
            du_s[span, :] = grad_up
            dg_s[span, :] = grad_gate
            ret_acc[span, :] += mm(act, wo[...])
            dx_acc[span, :] += mm_nt(grad_gate, wg[...]) + mm_nt(grad_up, wu[...])
            return 0

        lax.fori_loop(0, EXPERTS, block, 0)
        if m == copies - 1 and not last:
            for i, (src, dst) in enumerate(zip((ret_acc, dx_acc), carry_out, strict=True)):
                copy = pltpu.make_async_copy(src, dst, sems.at[2 + i])
                copy.start()
                sends.append(copy)
        if m == copies - 1 and last:
            for k in range(EXPERTS):
                span = slice(k * CAP, (k + 1) * CAP)
                ret = ret_acc[span, :]
                dgate = jnp.sum(ret * y_refs[k][:CAP, :].astype(f32), axis=-1, keepdims=True)
                dgate = jnp.broadcast_to(dgate, (CAP, LANES)).T[:1]
                ret_outs[k][...] = (ret * gcol[span, :1]).astype(bf16)
                dx_outs[k][:CAP, :] = dx_acc[span, :].astype(bf16)
                high = dgate.astype(bf16).astype(f32)
                tail = jnp.concatenate(
                    [high, dgate - high, jnp.zeros((EXTRA - 2, CAP), f32)], axis=0
                ).astype(bf16)
                dx_outs[k][CAP:, :CAP] = tail
                dx_outs[k][CAP:, CAP:] = jnp.zeros((EXTRA, D - CAP), bf16)
        for half, source in ((0, dg_s), (1, du_s)):
            for tile in range(tiles):
                made = mm(xt[...], source[:, tile * wide : (tile + 1) * wide]).astype(bf16)
                row = (half * tiles + tile) * shard
                for z in range(plan.shards):
                    grads[m, z, row : row + shard, :] = made[z * shard : (z + 1) * shard, :]
        for tile in range(tiles):
            made = mm_tn(act_s[:, tile * wide : (tile + 1) * wide], ds[...]).astype(bf16)
            for span in range(plan.spans):
                z = tile * plan.spans + span
                for down in range(plan.downs):
                    row = 2 * tiles * shard + down * seg
                    grads[m, z, row : row + seg, :] = made[
                        span * seg : (span + 1) * seg, down * wide : (down + 1) * wide
                    ]
        copy = pltpu.make_async_copy(grads.at[m], grad_outs[m], sems.at[4 + m])
        copy.start()
        sends.append(copy)
    for copy in sends:
        copy.wait()


def expert_call(plan, xs, ys, weights, carried, last):
    first = carried is None
    rows = EXPERTS * CAP
    vmem = pl.BlockSpec(memory_space=pltpu.VMEM)
    hbm = pl.BlockSpec(memory_space=pl.ANY)
    copies = plan.copies
    in_specs = [vmem] * (2 * EXPERTS + copies)
    operands = list(xs) + list(ys) + list(weights)
    if not first:
        in_specs += [hbm] * 2
        operands += list(carried)
    out_specs = [hbm] * copies
    out_shape = [jax.ShapeDtypeStruct((plan.shards, plan.rows, plan.wide), bf16)] * copies
    if last:
        out_specs += [vmem] * (2 * EXPERTS)
        out_shape += [jax.ShapeDtypeStruct((CAP + EXTRA, D), bf16)] * EXPERTS
        out_shape += [jax.ShapeDtypeStruct((CAP, D), bf16)] * EXPERTS
    else:
        out_specs += [hbm] * 2
        out_shape += [jax.ShapeDtypeStruct((rows, D), f32)] * 2
    made = pl.pallas_call(
        partial(expert_kernel, plan, first, last),
        in_specs=in_specs,
        out_specs=out_specs,
        out_shape=out_shape,
        scratch_shapes=[
            pltpu.VMEM((rows, D), bf16),
            pltpu.VMEM((rows, D), bf16),
            pltpu.VMEM((D, rows), bf16),
            pltpu.VMEM((rows, LANES), f32),
            pltpu.VMEM((rows, D), f32),
            pltpu.VMEM((rows, D), f32),
            pltpu.VMEM((D, plan.width), bf16),
            pltpu.VMEM((D, plan.width), bf16),
            pltpu.VMEM((plan.width, D), bf16),
            pltpu.VMEM((rows, plan.width), bf16),
            pltpu.VMEM((rows, plan.width), bf16),
            pltpu.VMEM((rows, plan.width), bf16),
            pltpu.VMEM((copies, plan.shards, plan.rows, plan.wide), bf16),
            pltpu.SemaphoreType.DMA((4 + copies,)),
        ],
        compiler_params=pltpu.CompilerParams(vmem_limit_bytes=VMEM_BYTES),
        cost_estimate=cost(
            18 * rows * D * plan.width * copies, 12 * D * plan.width * copies + 12 * rows * D
        ),
        name="experts",
    )(*operands)
    return made[:copies], made[copies:]


def spots_of(place_ref, rows):
    slot = lax.broadcasted_iota(jnp.int32, (rows, EXPERTS * CAP), 1)
    hit = (slot == place_ref[:, 0:1]) | (slot == place_ref[:, 1:2])
    return jnp.where(hit, 1.0, 0.0).astype(bf16)


def constant_gates(one, chosen, m):
    a0 = one[:, NCH + 2 * m : NCH + 2 * m + 1]
    a1 = one[:, NCH + 2 * m + 1 : NCH + 2 * m + 2]
    gate = chosen[:, EXPERTS + 2 + m : EXPERTS + 3 + m]
    return gate, a0, a1


def back_kernel(
    count,
    who_ref,
    res_ref,
    h_ref,
    dy_ref,
    one_ref,
    place_ref,
    choice_ref,
    prev_ref,
    wsmall_ref,
    *refs,
):
    dx_refs, refs = refs[:EXPERTS], refs[EXPERTS:]
    pieces, refs = refs[:count], refs[count:]
    (
        dres_ref,
        branch_ref,
        dctx_ref,
        dsmall_ref,
        gain_out,
        prev_out,
        cvec_out,
        w_ref,
        dg_ref,
    ) = refs

    @pl.when(pl.program_id(0) == 0)
    def _():
        gain_out[...] = jnp.zeros_like(gain_out)
        prev_out[...] = jnp.zeros_like(prev_out)
        cvec_out[...] = jnp.zeros_like(cvec_out)
        dsmall_ref[...] = jnp.zeros_like(dsmall_ref)
        lay_columns(w_ref, pieces, who_ref[1])
        lane = lanes_of((CAP, LANES))
        for k in range(EXPERTS):
            columns = dx_refs[k][CAP:, :CAP].astype(f32).T
            at = who_ref[0] ^ k
            made = jnp.where(lane == at, columns[:, 0:1], 0.0)
            made = jnp.where(lane == at + 16, columns[:, 1:2], made)
            dg_ref[k * CAP : (k + 1) * CAP, :] = made.astype(bf16)

    res = res_ref[...]
    rows = res.shape[0]
    one = one_ref[...]
    lane = lanes_of(one.shape)
    chosen = jnp.where(selected(choice_ref, lane), one, 0.0)
    choice = lane < NCH
    is_mix = (lane >= NCH) & (lane < NCH + 4)
    spots = spots_of(place_ref, rows)
    moved = jnp.zeros(res.shape, f32)
    for k in range(EXPERTS):
        moved = moved + mm(spots[:, k * CAP : (k + 1) * CAP], dx_refs[k][:CAP, :])
    from_experts = mm(spots, dg_ref[...])
    from_experts = from_experts + pltpu.roll(from_experts, LANES - 16, 1)

    inverse = lax.rsqrt(jnp.mean(res * res, axis=-1, keepdims=True) + EPS)
    dy = dy_ref[...]
    dyf = dy.astype(f32)
    gain = row_of(wsmall_ref, GAIN_F)
    spread = res * inverse * gain
    hd = jnp.sum(spread * dyf, axis=-1, keepdims=True)
    cd = mm_nt(dy, wsmall_ref[...])
    coef = chosen[:, EXPERTS + 1 : EXPERTS + 2]
    grads = jnp.where(lane < EXPERTS, from_experts, 0.0)
    grads = jnp.where(lane == EXPERTS + 1, hd, grads)
    made = jnp.zeros_like(one)
    for m in range(2):
        gate, a0, a1 = constant_gates(one, chosen, m)
        dot = cd[:, CVEC + m : CVEC + m + 1]
        coef = coef + gate * a0
        grads = jnp.where(lane == EXPERTS + 2 + m, a0 * hd + a1 * dot, grads)
        grads = jnp.where(lane == NCH + 2 * m, gate * hd, grads)
        grads = jnp.where(lane == NCH + 2 * m + 1, gate * dot, grads)
        made = jnp.where(lane == m, gate * a1, made)
    grads = jnp.where(is_mix | selected(choice_ref, lane), grads, 0.0)
    weighted = one * grads
    mean_choice = jnp.sum(jnp.where(choice, weighted, 0.0), axis=-1, keepdims=True)
    d_logits = jnp.where(choice, one * (grads - mean_choice), 0.0)
    d_mix = one * (grads - (weighted + partner(weighted, lane)))
    d_small = jnp.where(choice, d_logits, jnp.where(is_mix, d_mix, 0.0))
    low = d_small.astype(bf16)
    spread_grad = moved + mm(low, wsmall_ref[...]) + coef * dyf
    scaled = spread_grad * gain
    mean_dot = jnp.mean(res * scaled, axis=-1, keepdims=True)
    d_res = dyf + inverse * scaled - res * (inverse * inverse * inverse * mean_dot)
    dres_ref[...] = d_res
    gain_out[...] += jnp.sum(spread_grad * res * inverse, axis=0, keepdims=True)
    branch = d_res.astype(bf16)
    branch_ref[...] = branch
    dctx_ref[...] = mm_nt(branch, w_ref[...]).astype(bf16)
    dsmall_ref[...] += mm_tn(low, h_ref[...])
    high = d_logits.astype(bf16)
    rest = (d_logits - high.astype(f32)).astype(bf16)
    prev = prev_ref[...]
    prev_out[...] += mm(prev, high) + mm(prev, rest)
    high = made.astype(bf16)
    rest = (made - high.astype(f32)).astype(bf16)
    cvec_out[...] += mm_tn(high, dy) + mm_tn(rest, dy)


def back_call(who, res, h, dy, one, places, choices, prev, small, dx, pieces, after):
    rows = res.shape[0]
    block = 256
    tall = jax.ShapeDtypeStruct((LANES, D), f32)
    return launch(
        partial(back_kernel, len(pieces)),
        [who, res, h, dy, one, places, choices, prev, small, *dx, *pieces],
        [SMEM]
        + [rows_of(block, D)] * 3
        + [rows_of(block, LANES)]
        + [rows_of(block, 2)] * 2
        + [pl.BlockSpec((NCH, block), lambda i: (0, i))]
        + [whole(a.shape) for a in (small, *dx, *pieces)],
        [rows_of(block, D)] * 3
        + [whole((LANES, D)), whole((1, D)), whole((NCH, LANES)), whole((LANES, D))],
        [
            jax.ShapeDtypeStruct((rows, D), f32),
            jax.ShapeDtypeStruct((rows, D), bf16),
            jax.ShapeDtypeStruct((rows, D), bf16),
            tall,
            jax.ShapeDtypeStruct((1, D), f32),
            jax.ShapeDtypeStruct((NCH, LANES), f32),
            tall,
        ],
        after,
        grid=(rows // block,),
        scratch_shapes=[pltpu.VMEM((D, D), bf16), pltpu.VMEM((EXPERTS * CAP, LANES), bf16)],
        compiler_params=params(),
        cost_estimate=cost(2 * rows * D * (D + 2048), 20 * rows * D),
        name="combine_back",
    )


def finish_kernel(res_ref, one_ref, place_ref, choice_ref, small_ref, *refs):
    ret_refs, out_ref = refs[:EXPERTS], refs[EXPERTS]
    res = res_ref[...]
    one = one_ref[...]
    lane = lanes_of(one.shape)
    chosen = jnp.where(selected(choice_ref, lane), one, 0.0)
    inverse = lax.rsqrt(jnp.mean(res * res, axis=-1, keepdims=True) + EPS)
    total = res
    coef = chosen[:, EXPERTS + 1 : EXPERTS + 2]
    for m in range(2):
        gate, a0, a1 = constant_gates(one, chosen, m)
        coef = coef + gate * a0
        total = total + (gate * a1) * row_of(small_ref, CVEC + m)
    total = total + (coef * inverse) * res * row_of(small_ref, GAIN_F)
    spots = spots_of(place_ref, res.shape[0])
    for k in range(EXPERTS):
        total = total + mm(spots[:, k * CAP : (k + 1) * CAP], ret_refs[k][...])
    out_ref[...] = total.astype(bf16)


def finish_call(res, one, places, choices, small, ret, after):
    rows = res.shape[0]
    block = 256
    return launch(
        finish_kernel,
        [res, one, places, choices, small, *ret],
        [rows_of(block, D), rows_of(block, LANES)]
        + [rows_of(block, 2)] * 2
        + [whole(a.shape) for a in (small, *ret)],
        rows_of(block, D),
        jax.ShapeDtypeStruct((rows, D), bf16),
        after,
        grid=(rows // block,),
        compiler_params=params(),
        cost_estimate=cost(2 * rows * D * 1536, 10 * rows * D),
        name="layer_out",
    )


def dense_kernel(copies, part_ref, h_ref, ctx_ref, dq_ref, dk_ref, dv_ref, branch_ref, *outs):
    cut = 4 * D // copies
    ht = h_ref[...].astype(f32).T.astype(bf16)
    ct = ctx_ref[...].astype(f32).T.astype(bf16)
    step = 384
    for index, (left, right) in enumerate(
        ((ht, dq_ref), (ht, dk_ref), (ht, dv_ref), (ct, branch_ref))
    ):
        for c in range(0, D, step):
            made = mm(left, right[:, c : c + step]).astype(bf16)
            at = index * D + c
            done = 0
            while done < step:
                owner, column = (at + done) // cut, (at + done) % cut
                size = min(step - done, cut - column)
                for m in range(copies):

                    @pl.when(part_ref[0] == (owner ^ m))
                    def _(m=m, column=column, size=size, piece=made[:, done : done + size]):
                        outs[m][:, column : column + size] = piece

                done += size


def dense_call(copies, part, h, ctx, dq, dk, dv, branch, after):
    rows = h.shape[0]
    return launch(
        partial(dense_kernel, copies),
        [part, h, ctx, dq, dk, dv, branch],
        [SMEM] + [VM] * 6,
        [VM] * copies,
        [jax.ShapeDtypeStruct((D, 4 * D // copies), bf16)] * copies,
        after,
        cost_estimate=cost(8 * rows * D * D, 12 * rows * D + 8 * D * D),
        name="dense_grads",
    )


def fold_parts_kernel(who_ref, *refs):
    pieces, outs = refs[:-EXPERTS], refs[-EXPERTS:]
    for k in range(EXPERTS):
        at = who_ref[0] ^ k
        total = pieces[0][:, at].astype(f32)
        for piece in pieces[1:]:
            total = total + piece[:, at].astype(f32)
        outs[k][...] = total.astype(bf16)


def fold_parts(who, pieces, shards):
    cut = pieces[0].shape[1]
    quarter = D // (shards * EXPERTS)
    shape = (shards, EXPERTS, quarter, cut)
    operands = [who] + [a.reshape(shape) for a in pieces]
    return launch(
        fold_parts_kernel,
        operands,
        [SMEM] + [VM] * len(pieces),
        [VM] * EXPERTS,
        [jax.ShapeDtypeStruct((shards, quarter, cut), bf16)] * EXPERTS,
        name="fold_parts",
    )


def fold_quarters_kernel(count, zi_ref, small_ref, *refs):
    pieces, outs = refs[:count], refs[count:]
    rows, cut = pieces[0].shape[1:]
    spare = outs[0].shape[0] - rows
    for k, out in enumerate(outs):
        at = lax.rem(zi_ref[0] + k, len(outs))
        total = pieces[0][at].astype(f32)
        for piece in pieces[1:]:
            total = total + piece[at].astype(f32)
        out[:rows, :] = total.astype(bf16)
        for c in range(cut // LANES):
            out[rows:, c * LANES : (c + 1) * LANES] = small_ref[at, c * spare : (c + 1) * spare, :]


def fold_quarters(zi, small, pieces, after=()):
    shards, rows, cut = pieces[0].shape
    spare = D // shards * LANES // cut
    return launch(
        partial(fold_quarters_kernel, len(pieces)),
        [zi, small.reshape(shards, D // shards, LANES), *pieces],
        [SMEM] + [VM] * (len(pieces) + 1),
        [VM] * shards,
        [jax.ShapeDtypeStruct((rows + spare, cut), bf16)] * shards,
        after,
        name="fold_quarters",
    )


def lay_tail_kernel(count, rows, own_ref, *refs):
    pieces, out = refs[:count], refs[count]
    total = pieces[0][rows:, :].astype(f32)
    for k in range(count):
        at = pl.multiple_of((own_ref[0] ^ k) * rows, rows)
        out[pl.ds(at, rows), :] = pieces[k][:rows, :]
        if k:
            total = total + pieces[k][rows:, :].astype(f32)
    out[count * rows :, :] = total.astype(bf16)


def lay_tail(own, pieces, rows, after):
    count = len(pieces)
    size, cut = pieces[0].shape
    return launch(
        partial(lay_tail_kernel, count, rows),
        [own, *pieces],
        [SMEM] + [VM] * count,
        VM,
        jax.ShapeDtypeStruct((count * rows + size - rows, cut), bf16),
        after,
        name="lay_tail",
    )


def fold_copies(pieces):
    shards, rows, wide = pieces[0].shape
    block = pl.BlockSpec((1, rows // 2, wide), lambda i: (i // 2, i % 2, 0))
    return launch(
        fold_shards_kernel,
        pieces,
        [block] * len(pieces),
        block,
        jax.ShapeDtypeStruct(pieces[0].shape, bf16),
        grid=(2 * shards,),
        compiler_params=params(),
        cost_estimate=cost(0, 0),
        name="fold_copies",
    )


def fold_shards_kernel(*refs):
    total = refs[0][...].astype(f32)
    for ref in refs[1:-1]:
        total = total + ref[...].astype(f32)
    refs[-1][...] = total.astype(bf16)


def fold_shards(pieces):
    return launch(
        fold_shards_kernel,
        pieces,
        [VM] * len(pieces),
        VM,
        jax.ShapeDtypeStruct(pieces[0].shape, bf16),
        name="fold_shards",
    )


def unpack_dense_kernel(count, rows, part_ref, *refs):
    pieces, (qkv_ref, proj_ref, small_ref) = refs[:count], refs[count:]
    cut = pieces[0].shape[1]
    small = pieces[0][rows:, :].astype(f32)
    for piece in pieces[1:]:
        small = small + piece[rows:, :].astype(f32)
    spare = small.shape[0]
    for c in range(cut // LANES):
        small_ref[c * spare : (c + 1) * spare, :] = small[:, c * LANES : (c + 1) * LANES]
    for p in range(count):
        chosen = pieces[0][:rows, :].astype(f32)
        for m in range(1, count):
            chosen = jnp.where(part_ref[0] == (p ^ m), pieces[m][:rows, :].astype(f32), chosen)
        start = p * cut
        in_qkv = max(0, min(cut, 3 * D - start))
        if in_qkv:
            qkv_ref[:, start : start + in_qkv] = chosen[:, :in_qkv]
        if in_qkv < cut:
            at = start + in_qkv - 3 * D
            proj_ref[:, at : at + cut - in_qkv] = chosen[:, in_qkv:]


def unpack_dense(part, pieces, rows):
    return launch(
        partial(unpack_dense_kernel, len(pieces), rows),
        [part, *pieces],
        [SMEM] + [VM] * len(pieces),
        [VM] * 3,
        [
            jax.ShapeDtypeStruct((rows, 3 * D), f32),
            jax.ShapeDtypeStruct((rows, D), f32),
            jax.ShapeDtypeStruct((rows, LANES), f32),
        ],
        name="unpack_dense",
    )


def last_kernel(
    count,
    shards,
    part_ref,
    dq_ref,
    dk_ref,
    dv_ref,
    x_ref,
    dres_ref,
    small_ref,
    dsmall_ref,
    gain_f_ref,
    prev_ref,
    cvec_ref,
    *refs,
):
    pieces = refs[:count]
    out_ref, small_out, w_ref, gain_ref = refs[count:]

    @pl.when(pl.program_id(0) == 0)
    def _():
        gain_ref[...] = jnp.zeros_like(gain_ref)
        lay_columns(w_ref, pieces, part_ref[0])

    grad = mm_nt(dq_ref[...], w_ref[:, :D])
    grad = grad + mm_nt(dk_ref[...], w_ref[:, D : 2 * D])
    grad = grad + mm_nt(dv_ref[...], w_ref[:, 2 * D :])
    x = x_ref[...].astype(f32)
    inverse = lax.rsqrt(jnp.mean(x * x, axis=-1, keepdims=True) + EPS)
    scaled = grad * row_of(small_ref, GAIN_A)
    mean_dot = jnp.mean(x * scaled, axis=-1, keepdims=True)
    d_x = inverse * scaled - x * (inverse * inverse * inverse * mean_dot)
    out_ref[...] = (dres_ref[...] + d_x).astype(bf16)
    gain_ref[...] += jnp.sum(grad * x * inverse, axis=0, keepdims=True)

    @pl.when(pl.program_id(0) == pl.num_programs(0) - 1)
    def _():
        row = lax.broadcasted_iota(jnp.int32, (LANES, D), 0)
        total = jnp.where(row < CVEC, dsmall_ref[...], 0.0)
        for m in range(2):
            total = jnp.where(row == CVEC + m, cvec_ref[m : m + 1, :], total)
        total = jnp.where(row == GAIN_A, gain_ref[...], total)
        total = jnp.where(row == GAIN_F, gain_f_ref[...], total)
        total = total.T
        owned = NCH // shards
        shard = D // shards
        row = lax.broadcasted_iota(jnp.int32, total.shape, 0)
        lane = lanes_of((NCH, LANES))
        prev = pltpu.roll(jnp.where(lane < NCH, prev_ref[...], 0.0), 16, 1)
        for index in range(NCH):
            at = (index // owned) * shard + index % owned
            total = jnp.where(row == at, total + prev[index : index + 1, :], total)
        small_out[...] = total.astype(bf16)


def last_call(part, shards, dq, dk, dv, x, dres, small, smalls, pieces, after):
    rows = x.shape[0]
    block = 256
    return launch(
        partial(last_kernel, len(pieces), shards),
        [part, dq, dk, dv, x, dres, small, *smalls, *pieces],
        [SMEM]
        + [rows_of(block, D)] * 5
        + [whole(a.shape) for a in (small, *smalls, *pieces)],
        [rows_of(block, D), whole((D, LANES))],
        [jax.ShapeDtypeStruct((rows, D), bf16), jax.ShapeDtypeStruct((D, LANES), bf16)],
        after,
        grid=(rows // block,),
        scratch_shapes=[pltpu.VMEM((D, 3 * D), bf16), pltpu.VMEM((1, D), f32)],
        compiler_params=params(),
        cost_estimate=cost(6 * rows * D * D, 14 * rows * D),
        name="input_grad",
    )


def body(
    replicas,
    shards,
    tokens,
    prev_logits,
    out_grad,
    routes,
    doc_ids,
    valid_mask,
    qkv_weight,
    proj_weight,
    gain_attn,
    gain_ffn,
    router,
    const_mix,
    prev_mix,
    const_vec,
    expert_in,
    expert_out,
):
    me = lax.axis_index("rep")
    zi = lax.axis_index("fsdp")
    copies = replicas // EXPERTS
    mine = me // copies
    part = me % copies
    rows = tokens.shape[0]
    shard = qkv_weight.shape[0]
    hidden = expert_in.shape[2] // 2
    quarter = shard // EXPERTS
    plan = Plan(replicas, shards, shard, hidden, 2)
    zi_s = zi.reshape(1).astype(jnp.int32)
    mine_s = mine.reshape(1).astype(jnp.int32)
    part_s = part.reshape(1).astype(jnp.int32)
    who = jnp.concatenate([mine_s, part_s])

    def to_expert(a, k):
        return lax.ppermute(a, "rep", [(i, i ^ (k * copies)) for i in range(replicas)])

    def to_part(a, m):
        return lax.ppermute(a, "rep", [(i, i ^ m) for i in range(replicas)])

    def spin(a, k):
        return lax.ppermute(a, "fsdp", [(i, (i + k) % shards) for i in range(shards)])

    def by_xor(pieces, own, axis):
        size = pieces[0].shape[axis]
        shape = list(pieces[0].shape)
        shape[axis] = size * len(pieces)
        full = jnp.zeros(shape, pieces[0].dtype)
        for k, piece in enumerate(pieces):
            full = lax.dynamic_update_slice_in_dim(full, piece, (own ^ k) * size, axis)
        return full

    width = 3 * D // copies
    owned = prev_mix.shape[0]
    smalls = jnp.concatenate(
        [
            router.T,
            const_mix.T,
            const_vec.T,
            gain_attn[None],
            gain_ffn[None],
            jnp.pad(prev_mix, ((0, 16 - owned), (0, shard - NCH))),
        ]
    )
    piece, mine_late = cut_dense(who, qkv_weight, proj_weight, smalls, copies)
    spun = [piece] + [spin(piece, k) for k in range(1, shards)]

    own_in = lax.dynamic_index_in_dim(expert_in, mine_late[0], 1, keepdims=False)
    own_out = lax.dynamic_index_in_dim(expert_out, mine_late[0], 1, keepdims=False)
    packs = pack_pieces(plan, part_s, own_in, own_out)
    gathered = [lax.all_gather(p, "fsdp", axis=0, tiled=False) for p in packs]

    def weights_after(chunk, done):
        full = tie(gathered[chunk], done)
        return [full] + [to_part(full, m) for m in range(1, copies)]

    docs = doc_ids.reshape(-1)
    drow = docs[None, :]
    dcol = docs[:, None]
    vcol = valid_mask.reshape(-1)[:, None]
    first_place = jnp.sum((drow < dcol).astype(jnp.int32), axis=1)
    offset = (jnp.arange(rows, dtype=jnp.int32) - first_place).astype(f32)
    frequency = jnp.exp(
        jnp.arange(HDIM // 2, dtype=f32) * (-2.0 * math.log(10000.0) / HDIM)
    )
    angles = offset[:, None] * frequency[None, :]
    cosine, sine = jnp.cos(angles), jnp.sin(angles)
    cosine = jnp.concatenate([cosine] * 4, axis=1)
    sine = jnp.concatenate([-sine, sine, -sine, sine], axis=1)

    routes_t = routes.T
    chosen = jnp.where(routes_t < EXPERTS, routes_t ^ mine, routes_t)
    kinds = jnp.arange(EXPERTS, dtype=jnp.int32)
    named = jnp.any(chosen[:, None, :] == kinds[None, :, None], axis=0)
    later = jnp.triu(jnp.ones((rows, rows), bf16), 1)
    rank = mm(named.astype(bf16), later).astype(jnp.int32)
    spot = jnp.where(named, rank, CAP)
    hit = chosen[:, None, :] == kinds[None, :, None]
    places = jnp.sum(jnp.where(hit, (kinds[:, None] * CAP + rank)[None], 0), axis=1)
    places = jnp.where(chosen < EXPERTS, places, -1).T

    qkv_part, proj_part, small, prevs = lay_shards(
        zi_s, spun, shard, quarter, width, (packs[0],)
    )
    pmix = prevs[:, :owned].reshape(NCH, LANES)

    def exchanged(blocks):
        return [blocks[0]] + [to_expert(blocks[k], k) for k in range(1, EXPERTS)]

    def over_parts(half):
        half = half.reshape(D, half.shape[3])
        pieces = [half] + [to_part(half, m) for m in range(1, copies)]
        if half.shape[1] % LANES == 0:
            return pieces
        return [by_xor(pieces, part, 1)]

    qkv_half = lay_xor(
        mine_s, exchanged([qkv_part] * EXPERTS), (cosine, sine, spot, dcol, vcol, places)
    )
    qkv_pieces = over_parts(qkv_half)
    part_q = part_s if len(qkv_pieces) == copies else jnp.zeros_like(part_s)
    per = D // proj_part.shape[2]
    rider = proj_part.reshape(-1, per, quarter, D // per).transpose(0, 2, 1, 3)
    rider = rider.reshape(-1, D)
    rider = jnp.pad(rider, ((0, -rider.shape[0] % 16), (0, 0)))
    ys = dispatch_call(mine_s, spot, out_grad, rider=rider, after=(qkv_half,))

    prev = prev_logits.T
    h1, q, k, v = qkv_call(part_q, tokens, small, cosine, sine, qkv_pieces, (ys[0],))
    ys = exchanged(ys)
    ctx, lse = attend_call(q, k, v, dcol, drow, vcol, ())
    proj_half = lay_riders(mine_s, ys, proj_part.shape, (ctx,))
    proj_pieces = over_parts(proj_half)
    part_p = part_s if len(proj_pieces) == copies else jnp.zeros_like(part_s)
    res, h2, one, gates = after_call(
        part_p, ctx, tokens, small, prev, pmix, routes, proj_pieces
    )

    xs = dispatch_call(mine_s, spot, h2, gates)
    weights = [weights_after(0, ctx)] + [
        weights_after(c, xs[0]) for c in range(1, plan.chunks)
    ]
    xs = exchanged(xs)
    carried = None
    chunk_grads = []
    for chunk in range(plan.chunks):
        grads, carried = expert_call(
            plan,
            xs,
            ys,
            weights[chunk] if chunk else tie(weights[0], weights[1:]),
            carried,
            chunk == plan.chunks - 1,
        )
        chunk_grads.append(grads)
    dx = exchanged(carried[:EXPERTS])

    chunk_grads = [
        [grads[0]] + [to_part(grads[m], m) for m in range(1, copies)] for grads in chunk_grads
    ]
    total = fold_copies(chunk_grads[0])

    def over_shards(t):
        return lax.psum_scatter(t, "fsdp", scatter_dimension=0, tiled=False)

    who_p = jnp.concatenate([mine_s, part_p])
    dres, branch, dctx, dsmall, gain_f_grad, prev_grad, cvec_grad = back_call(
        who_p,
        res,
        h2,
        out_grad,
        one,
        places,
        routes,
        prev,
        small,
        dx,
        proj_pieces,
        (total,),
    )
    summed = [over_shards(total)]
    summed += [over_shards(fold_copies(tie(grads, branch))) for grads in chunk_grads[1:]]
    ret = exchanged(tie(carried[EXPERTS:], branch))
    first = tie(summed[0], branch)
    spread = [[first] + [to_expert(first, k) for k in range(1, EXPERTS - 1)]]
    dq, dk, dv = attend_back_call(q, k, v, dctx, lse, dcol, drow, vcol, cosine, sine, ())
    dense = dense_call(
        copies, part_s, h1, ctx, tie(dq, ret, spread[0]), dk, dv, branch, ()
    )
    spread[0].append(to_expert(tie(first, dq), EXPERTS - 1))
    dense = tie(list(dense), summed[1:])
    dense = [dense[0]] + [to_part(dense[m], m) for m in range(1, copies)]
    quarters = tie(fold_parts(who, dense, shards), spread[0])

    def over_copies(pieces):
        stacked = jnp.stack(pieces)
        return [stacked] + [to_part(stacked, m) for m in range(1, copies)]

    spread[0] = over_copies(tie(spread[0], quarters))
    input_grad, smalls = last_call(
        part_q,
        shards,
        dq,
        dk,
        dv,
        tokens,
        tie(dres, quarters),
        small,
        (dsmall, gain_f_grad, prev_grad, cvec_grad),
        qkv_pieces,
        (),
    )
    begun = ()
    if plan.seg % LANES == 0:
        begun = unpack_chunk(plan, who, 0, spread[0], begun)
    out = finish_call(res, one, places, routes, small, tie(ret, quarters), ())
    bands = fold_quarters(zi_s, smalls, exchanged(quarters), (*begun, out))
    tail = fold_shards([bands[0]] + [spin(bands[k], k) for k in range(1, shards)])
    for piece in summed[1:]:
        piece = tie(piece, bands)
        late = [to_expert(tie(piece, tail), k) for k in range(EXPERTS - 1, EXPERTS)]
        spread.append([piece] + [to_expert(piece, k) for k in range(1, EXPERTS - 1)] + late)
    tail = lay_tail(mine_s, exchanged([tail] * EXPERTS), quarter, ())
    spread[1:] = [over_copies(tie(pieces, tail)) for pieces in spread[1:]]
    tails = [tail] + [to_part(tail, m) for m in range(1, copies)]
    qkv_grad, proj_grad, small_grad = unpack_dense(part_s, tails, shard)

    full_in, full_out = unpack_grads(plan, who, spread, begun)
    return (
        out,
        input_grad,
        qkv_grad,
        proj_grad,
        small_grad[:, GAIN_A],
        small_grad[:, GAIN_F],
        small_grad[:, :NCH],
        small_grad[:, NCH : NCH + 4],
        small_grad[:owned, 16 : 16 + NCH],
        small_grad[:, CVEC : CVEC + 2],
        full_in,
        full_out,
    )


def solution(mesh):
    replicas, shards = mesh.shape["rep"], mesh.shape["fsdp"]
    split = P(("rep", "fsdp"), None)
    matrix = P("fsdp", None)
    cube = P("fsdp", None, None)
    in_specs = (split,) * 6 + (matrix, matrix, P("fsdp"), P("fsdp")) + (matrix,) * 4 + (cube, cube)
    out_specs = (split, split, matrix, matrix, P("fsdp"), P("fsdp")) + (matrix,) * 4 + (cube, cube)
    return jax.shard_map(
        partial(body, replicas, shards),
        mesh=mesh,
        in_specs=in_specs,
        out_specs=out_specs,
        check_vma=False,
    )
```

```python
from functools import partial
import math

import jax
import jax.numpy as jnp
from jax import lax
from jax.experimental import pallas as pl
from jax.experimental.pallas import tpu as pltpu
from jax.sharding import PartitionSpec as P

D = 768
HEADS = 12
HDIM = 64
EXPERTS = 4
NCH = 8
CAP = 384
LANES = 128
QB = 256
REACH = 512
VMEM_BYTES = 58 * 1024 * 1024
EPS = 1e-06
COST_SCALE = 0.02
ATT = 100
f32 = jnp.float32
bf16 = jnp.bfloat16

NT = (((1,), (1,)), ((), ()))
TN = (((0,), (0,)), ((), ()))


def mm(a, b):
    return jnp.dot(a, b, preferred_element_type=f32)


def mm_nt(a, b):
    return lax.dot_general(a, b, NT, preferred_element_type=f32)


def mm_tn(a, b):
    return lax.dot_general(a, b, TN, preferred_element_type=f32)


def params(steps=1):
    return pltpu.CompilerParams(
        dimension_semantics=("arbitrary",) * steps, vmem_limit_bytes=VMEM_BYTES
    )


def cost(flops, nbytes):
    return pl.CostEstimate(
        flops=int(flops * COST_SCALE), bytes_accessed=int(nbytes * COST_SCALE), transcendentals=0
    )


def launch(kernel, operands, in_specs, out_specs, out_shape, after=(), **kw):
    n, skip = len(operands), len(after)

    def run(*refs):
        kernel(*refs[:n], *refs[n + skip :])

    kw.setdefault("compiler_params", pltpu.CompilerParams(vmem_limit_bytes=VMEM_BYTES))
    return pl.pallas_call(
        run,
        in_specs=list(in_specs) + [pl.BlockSpec(memory_space=pl.ANY)] * skip,
        out_specs=out_specs,
        out_shape=out_shape,
        **kw,
    )(*operands, *after)


def tie(value, *others):
    return lax.optimization_barrier((value, others))[0]


VM = pl.BlockSpec(memory_space=pltpu.VMEM)
SMEM = pl.BlockSpec(memory_space=pltpu.SMEM)
CVEC, GAIN_A, GAIN_F = NCH + 4, NCH + 6, NCH + 7


def row_of(ref, row):
    return ref[:16, :].astype(f32)[row : row + 1]


def whole(shape):
    return pl.BlockSpec(shape, lambda *_: (0,) * len(shape), pipeline_mode=pl.Buffered(1))


def rows_of(block, width):
    return pl.BlockSpec((block, width), lambda i: (i, 0))


def swap_halves(v):
    lane = lax.broadcasted_iota(jnp.int32, v.shape, 1)
    half = HDIM // 2
    ahead = pltpu.roll(v, LANES - half, 1)
    behind = pltpu.roll(v, half, 1)
    return jnp.where(lane % HDIM < half, ahead, behind)


def lay_columns(full_ref, pieces, part):
    width = pieces[0].shape[1]
    for p in range(len(pieces)):
        chosen = pieces[0][...]
        for m in range(1, len(pieces)):
            chosen = jnp.where(part == (p ^ m), pieces[m][...], chosen)
        full_ref[:, p * width : (p + 1) * width] = chosen


def qkv_kernel(count, part_ref, x_ref, small_ref, cos_ref, sin_ref, *refs):
    pieces = refs[:count]
    h_ref, q_ref, k_ref, v_ref, w_ref = refs[count:]

    @pl.when(pl.program_id(0) == 0)
    def _():
        lay_columns(w_ref, pieces, part_ref[0])

    x = x_ref[...].astype(f32)
    inverse = lax.rsqrt(jnp.mean(x * x, axis=-1, keepdims=True) + EPS)
    h = (x * inverse * row_of(small_ref, GAIN_A)).astype(bf16)
    h_ref[...] = h
    cosine, sine = cos_ref[...], sin_ref[...]
    mixed = mm(h, w_ref[...])
    for out_ref, base, scale in ((q_ref, 0, HDIM**-0.5), (k_ref, D, 1.0)):
        for c in range(0, D, LANES):
            v = mixed[:, base + c : base + c + LANES]
            turned = v * cosine + swap_halves(v) * sine
            out_ref[:, c : c + LANES] = (turned.astype(bf16).astype(f32) * scale).astype(bf16)
    v_ref[...] = mixed[:, 2 * D :].astype(bf16)


def qkv_call(part, x, small, cosine, sine, pieces, after):
    rows = x.shape[0]
    block = 256
    wide = jax.ShapeDtypeStruct((rows, D), bf16)
    return launch(
        partial(qkv_kernel, len(pieces)),
        [part, x, small, cosine, sine, *pieces],
        [
            SMEM,
            rows_of(block, D),
            whole(small.shape),
            rows_of(block, LANES),
            rows_of(block, LANES),
        ]
        + [whole(p.shape) for p in pieces],
        [rows_of(block, D)] * 4,
        [wide] * 4,
        after,
        grid=(rows // block,),
        scratch_shapes=[pltpu.VMEM((D, 3 * D), bf16)],
        compiler_params=params(),
        cost_estimate=cost(2 * rows * D * 3 * D, 2 * (5 * rows * D + 3 * D * D)),
        name="qkv_rope",
    )


def fill_bias(bias_ref, dcol_ref, drow_ref, vcol_ref, length):
    for i in range(length // QB):
        start = i * QB
        low = max(0, start - REACH)
        size = start + QB - low
        key = low + lax.broadcasted_iota(jnp.int32, (size, QB), 0)
        query = start + lax.broadcasted_iota(jnp.int32, (size, QB), 1)
        same = dcol_ref[low : low + size, :] == drow_ref[:, start : start + QB]
        usable = (vcol_ref[low : low + size, :] > 0) | (key == query)
        allowed = same & (key <= query) & usable
        bias_ref[i, :size, :] = jnp.where(allowed, 0.0, -1e30)


def lane_head(shape, head):
    lane = lax.broadcasted_iota(jnp.int32, shape, 1)
    return (lane // HDIM) == head


def attend_kernel(q_ref, k_ref, v_ref, dcol_ref, drow_ref, vcol_ref, ctx_ref, lse_ref, bias_ref):
    length = q_ref.shape[0]

    @pl.when(pl.program_id(0) == 0)
    def _():
        fill_bias(bias_ref, dcol_ref, drow_ref, vcol_ref, length)

    values_t = v_ref[...].astype(f32).T.astype(bf16)
    for i in range(length // QB):
        start = i * QB
        low = max(0, start - REACH)
        size = start + QB - low
        keys = k_ref[low : low + size, :]
        query = q_ref[start : start + QB, :]
        parts = []
        for head in range(2):
            masked = jnp.where(lane_head(query.shape, head), query, jnp.zeros_like(query))
            scores = mm_nt(keys, masked) + bias_ref[i, :size, :]
            largest = jnp.max(scores, axis=0, keepdims=True)
            raised = jnp.exp(scores - largest)
            total = jnp.sum(raised, axis=0, keepdims=True)
            part = mm(
                values_t[head * HDIM : (head + 1) * HDIM, low : low + size], raised.astype(bf16)
            )
            parts.append(part * (1.0 / total))
            lse_ref[0, head : head + 1, start : start + QB] = largest + jnp.log(total)
        ctx_ref[start : start + QB, :] = jnp.concatenate(parts, axis=0).T.astype(bf16)


def attend_call(q, k, v, dcol, drow, vcol, after):
    length = q.shape[0]
    pairs = HEADS // 2
    column = pl.BlockSpec((length, LANES), lambda p: (0, p))
    return launch(
        attend_kernel,
        [q, k, v, dcol, drow, vcol],
        [column, column, column, whole(dcol.shape), whole(drow.shape), whole(vcol.shape)],
        [column, pl.BlockSpec((1, 2, length), lambda p: (p, 0, 0))],
        [
            jax.ShapeDtypeStruct((length, D), bf16),
            jax.ShapeDtypeStruct((pairs, 2, length), f32),
        ],
        after,
        grid=(pairs,),
        scratch_shapes=[pltpu.VMEM((length // QB, REACH + QB, QB), f32)],
        compiler_params=params(),
        cost_estimate=cost(ATT * 20e9, ATT * 8 * length * D),
        name="attend",
    )


def attend_back_kernel(
    q_ref,
    k_ref,
    v_ref,
    g_ref,
    lse_ref,
    dcol_ref,
    drow_ref,
    vcol_ref,
    cos_ref,
    sin_ref,
    dq_ref,
    dk_ref,
    dv_ref,
    bias_ref,
    gk_ref,
    gv_ref,
    gq_ref,
):
    length = q_ref.shape[0]

    @pl.when(pl.program_id(0) == 0)
    def _():
        fill_bias(bias_ref, dcol_ref, drow_ref, vcol_ref, length)

    gk_ref[...] = jnp.zeros_like(gk_ref)
    gv_ref[...] = jnp.zeros_like(gv_ref)
    keys_t = k_ref[...].astype(f32).T.astype(bf16)
    for i in range(length // QB):
        start = i * QB
        low = max(0, start - REACH)
        size = start + QB - low
        span = slice(low, low + size)
        keys = k_ref[span, :]
        values = v_ref[span, :]
        query = q_ref[start : start + QB, :]
        grads = g_ref[start : start + QB, :]
        for head in range(2):
            own = lane_head(query.shape, head)
            query_h = jnp.where(own, query, jnp.zeros_like(query))
            grads_h = jnp.where(own, grads, jnp.zeros_like(grads))
            scores = mm_nt(keys, query_h) + bias_ref[i, :size, :]
            probs = jnp.exp(scores - lse_ref[0, head : head + 1, start : start + QB])
            grad_probs = mm_nt(values, grads_h)
            inner = jnp.sum(probs * grad_probs, axis=0, keepdims=True)
            grad_scores = (probs * (grad_probs - inner)).astype(bf16)
            gv_ref[span, :] += mm(probs.astype(bf16), grads_h)
            gk_ref[span, :] += mm(grad_scores, query_h)
            gq_ref[head * HDIM : (head + 1) * HDIM, start : start + QB] = mm(
                keys_t[head * HDIM : (head + 1) * HDIM, span], grad_scores
            )
    cosine, sine = cos_ref[...], sin_ref[...]
    grad_q = gq_ref[...].T * HDIM**-0.5
    grad_k = gk_ref[...]
    dq_ref[...] = (grad_q * cosine - swap_halves(grad_q) * sine).astype(bf16)
    dk_ref[...] = (grad_k * cosine - swap_halves(grad_k) * sine).astype(bf16)
    dv_ref[...] = gv_ref[...].astype(bf16)


def attend_back_call(q, k, v, g, lse, dcol, drow, vcol, cosine, sine, after):
    length = q.shape[0]
    pairs = HEADS // 2
    column = pl.BlockSpec((length, LANES), lambda p: (0, p))
    return launch(
        attend_back_kernel,
        [q, k, v, g, lse, dcol, drow, vcol, cosine, sine],
        [column] * 4
        + [pl.BlockSpec((1, 2, length), lambda p: (p, 0, 0))]
        + [whole(a.shape) for a in (dcol, drow, vcol, cosine, sine)],
        [column] * 3,
        [jax.ShapeDtypeStruct((length, D), bf16)] * 3,
        after,
        grid=(pairs,),
        scratch_shapes=[
            pltpu.VMEM((length // QB, REACH + QB, QB), f32),
            pltpu.VMEM((length, LANES), f32),
            pltpu.VMEM((length, LANES), f32),
            pltpu.VMEM((LANES, length), f32),
        ],
        compiler_params=params(),
        cost_estimate=cost(45e9, 14 * length * D),
        name="attend_back",
    )


def cut_dense_kernel(quarter, widths, who_ref, qkv_ref, proj_ref, *refs):
    smalls, out_ref, mark_ref = refs[:-2], refs[-2], refs[-1]
    mark_ref[...] = qkv_ref[:16, :LANES]
    row = pl.multiple_of(who_ref[0] * quarter, quarter)
    start = 0
    for ref, width in zip((qkv_ref, proj_ref), widths, strict=True):
        column = pl.multiple_of(who_ref[1] * width, LANES)
        out_ref[:quarter, start : start + width] = ref[pl.ds(row, quarter), pl.ds(column, width)]
        start += width
    shard = qkv_ref.shape[0]
    out_ref[quarter:, :] = jnp.zeros((16, start), bf16)
    rows = jnp.concatenate([ref[...].astype(f32) for ref in smalls[:-1]], axis=0)
    out_ref[quarter:, :shard] = rows.astype(bf16)
    prev = smalls[-1]
    out_ref[quarter : quarter + prev.shape[0], 2 * LANES : 2 * LANES + NCH] = prev[...]


def cut_dense(who, qkv, proj, smalls, copies):
    shard = qkv.shape[0]
    quarter = shard // EXPERTS
    widths = (qkv.shape[1] // copies, proj.shape[1] // copies)
    total = sum(widths)
    if quarter % 16 == 0 and all(w % LANES == 0 for w in widths):
        return launch(
            partial(cut_dense_kernel, quarter, widths),
            [who, qkv, proj, *smalls],
            [SMEM] + [VM] * (2 + len(smalls)),
            [VM, VM],
            [
                jax.ShapeDtypeStruct((quarter + 16, total), bf16),
                jax.ShapeDtypeStruct((16, LANES), bf16),
            ],
            name="cut_dense",
        )
    row = who[0] * quarter
    cuts = [
        lax.dynamic_slice(w, (row, who[1] * width), (quarter, width))
        for w, width in zip((qkv, proj), widths, strict=True)
    ]
    prev = smalls[-1]
    below = jnp.concatenate(
        [
            jnp.pad(jnp.concatenate(smalls[:-1]), ((0, 0), (0, 2 * LANES - shard))),
            jnp.pad(prev, ((0, 16 - prev.shape[0]), (0, total - 2 * LANES - NCH))),
        ],
        axis=1,
    )
    piece = jnp.concatenate([jnp.concatenate(cuts, axis=1), below])
    return piece, piece[:16, :LANES]


def lay_shards_kernel(count, shard, quarter, width, zi_ref, *refs):
    pieces = refs[:count]
    qkv_ref, proj_ref, small_ref, prev_ref = refs[count:]
    for k in range(count):
        at = lax.rem(zi_ref[0] + count - k, count)
        qkv_ref[at] = pieces[k][:quarter, :width]
        proj_ref[at] = pieces[k][:quarter, width:]
        prev_ref[at] = pieces[k][quarter:, 2 * LANES : 3 * LANES]
    small_ref[16:, :] = jnp.zeros((LANES - 16, D), bf16)
    for z in range(count):
        chosen = pieces[0][quarter:, : 2 * LANES].astype(f32)
        for k in range(1, count):
            here = lax.rem(zi_ref[0] + count - k, count) == z
            chosen = jnp.where(here, pieces[k][quarter:, : 2 * LANES].astype(f32), chosen)
        small_ref[:16, z * shard : (z + 1) * shard] = chosen[:, :shard].astype(bf16)


def lay_shards(zi, pieces, shard, quarter, width, after):
    count = len(pieces)
    return launch(
        partial(lay_shards_kernel, count, shard, quarter, width),
        [zi, *pieces],
        [SMEM] + [VM] * count,
        [VM] * 4,
        [
            jax.ShapeDtypeStruct((count, quarter, width), bf16),
            jax.ShapeDtypeStruct((count, quarter, pieces[0].shape[1] - width), bf16),
            jax.ShapeDtypeStruct((LANES, D), bf16),
            jax.ShapeDtypeStruct((count, 16, LANES), bf16),
        ],
        after,
        name="lay_shards",
    )


def lay_xor_kernel(count, own_ref, *refs):
    pieces, out = refs[:count], refs[count]
    for k in range(count):
        out[:, own_ref[0] ^ k] = pieces[k][...]


def lay_xor(own, pieces, after=()):
    count = len(pieces)
    first, rows, columns = pieces[0].shape
    return launch(
        partial(lay_xor_kernel, count),
        [own, *pieces],
        [SMEM] + [VM] * count,
        VM,
        jax.ShapeDtypeStruct((first, count, rows, columns), bf16),
        after,
        name="lay_xor",
    )


def lay_riders_kernel(shape, own_ref, *refs):
    pieces, out = refs[:-1], refs[-1]
    shards, quarter, width = shape
    per = D // width
    for k, piece in enumerate(pieces):
        for z in range(shards):
            row, column = z // per * quarter, z % per * width
            out[z, own_ref[0] ^ k] = piece[CAP + row : CAP + row + quarter, column : column + width]


def lay_riders(own, blocks, shape, after):
    shards, quarter, width = shape
    return launch(
        partial(lay_riders_kernel, shape),
        [own, *blocks],
        [SMEM] + [VM] * len(blocks),
        VM,
        jax.ShapeDtypeStruct((shards, len(blocks), quarter, width), bf16),
        after,
        name="lay_riders",
    )


def lanes_of(shape):
    return lax.broadcasted_iota(jnp.int32, shape, 1)


def partner(v, lane):
    return jnp.where(lane % 2 == 0, pltpu.roll(v, LANES - 1, 1), pltpu.roll(v, 1, 1))


def selected(choice_ref, lane):
    return (lane == choice_ref[:, 0:1]) | (lane == choice_ref[:, 1:2])


def after_kernel(
    count, part_ref, ctx_ref, x_ref, wsmall_ref, prev_ref, pmix_ref, choice_ref, *refs
):
    pieces = refs[:count]
    res_ref, h_ref, one_ref, gate_ref, w_ref = refs[count:]

    @pl.when(pl.program_id(0) == 0)
    def _():
        lay_columns(w_ref, pieces, part_ref[0])

    res = x_ref[...].astype(f32) + mm(ctx_ref[...], w_ref[...])
    res_ref[...] = res
    inverse = lax.rsqrt(jnp.mean(res * res, axis=-1, keepdims=True) + EPS)
    low = (res * inverse * row_of(wsmall_ref, GAIN_F)).astype(bf16)
    h_ref[...] = low
    small = mm_nt(low, wsmall_ref[...])
    logits = small + mm_tn(prev_ref[...], pmix_ref[...])
    lane = lanes_of(small.shape)
    choice = lane < NCH
    top = jnp.max(jnp.where(choice, logits, -1e30), axis=-1, keepdims=True)
    raised = jnp.where(choice, jnp.exp(jnp.where(choice, logits - top, 0.0)), 0.0)
    gates = raised / jnp.sum(raised, axis=-1, keepdims=True)
    mixing = 1.0 / (1.0 + jnp.exp(partner(small, lane) - small))
    is_mix = (lane >= NCH) & (lane < NCH + 4)
    one_ref[...] = jnp.where(choice, gates, jnp.where(is_mix, mixing, 0.0))
    taken = jnp.where(selected(choice_ref, lane), gates, 0.0).T[:NCH]
    high = taken.astype(bf16).astype(f32)
    gate_ref[...] = jnp.concatenate([high, taken - high], axis=0).astype(bf16)


def after_call(part, ctx, x, small, prev, pmix, choices, pieces):
    rows = x.shape[0]
    block = 256
    return launch(
        partial(after_kernel, len(pieces)),
        [part, ctx, x, small, prev, pmix, choices, *pieces],
        [SMEM]
        + [rows_of(block, D)] * 2
        + [
            whole(small.shape),
            pl.BlockSpec((NCH, block), lambda i: (0, i)),
            whole(pmix.shape),
            rows_of(block, 2),
        ]
        + [whole(p.shape) for p in pieces],
        [rows_of(block, D)] * 2
        + [rows_of(block, LANES), pl.BlockSpec((2 * NCH, block), lambda i: (0, i))],
        [
            jax.ShapeDtypeStruct((rows, D), f32),
            jax.ShapeDtypeStruct((rows, D), bf16),
            jax.ShapeDtypeStruct((rows, LANES), f32),
            jax.ShapeDtypeStruct((2 * NCH, rows), bf16),
        ],
        grid=(rows // block,),
        scratch_shapes=[pltpu.VMEM((D, D), bf16)],
        compiler_params=params(),
        cost_estimate=cost(2 * rows * D * D, 10 * rows * D),
        name="after_attention",
    )


EXTRA = 16


def dispatch_kernel(gated, mine_ref, spot_ref, v_ref, *refs):
    if gated:
        gate_ref, refs = refs[0], refs[1:]
    else:
        rider, refs = refs[0], refs[1:]
    rows = v_ref.shape[0]
    slot = lax.broadcasted_iota(jnp.int32, (CAP, rows), 0)
    for k in range(EXPERTS):
        hits = jnp.where(slot == spot_ref[k : k + 1, :], 1.0, 0.0).astype(bf16)
        refs[k][:CAP, :] = mm(hits, v_ref[...]).astype(bf16)
        if gated:
            moved = mm_nt(gate_ref[...], hits)
            row = lax.broadcasted_iota(jnp.int32, moved.shape, 0) % NCH
            moved = jnp.where(row == (mine_ref[0] ^ k), moved, 0.0)
            high = jnp.sum(moved[:NCH], axis=0, keepdims=True)
            rest = jnp.sum(moved[NCH:], axis=0, keepdims=True)
            tail = jnp.concatenate(
                [high, rest, jnp.zeros((EXTRA - 2, CAP), f32)], axis=0
            ).astype(bf16)
            refs[k][CAP:, :CAP] = tail
            refs[k][CAP:, CAP:] = jnp.zeros((EXTRA, D - CAP), bf16)
        else:
            refs[k][CAP:, :] = rider[...]


def dispatch_call(mine, spot, values, gates=None, rider=None, after=()):
    size = CAP + (EXTRA if rider is None else rider.shape[0])
    operands = [mine, spot, values] + [rider if gates is None else gates]
    rows = values.shape[0]
    return launch(
        partial(dispatch_kernel, gates is not None),
        operands,
        [SMEM] + [VM] * (len(operands) - 1),
        [VM] * EXPERTS,
        [jax.ShapeDtypeStruct((size, D), bf16)] * EXPERTS,
        after,
        cost_estimate=cost(2 * rows * D * CAP * EXPERTS, 2 * rows * D + 2 * EXPERTS * CAP * D),
        name="dispatch",
    )


class Plan:
    def __init__(self, replicas, shards, shard, hidden, chunks):
        self.copies = replicas // EXPERTS
        self.shards = shards
        self.shard = shard
        self.hidden = hidden
        self.chunks = chunks
        self.seg = hidden // (shards * self.copies * chunks)
        self.width = self.seg * shards
        self.wide = min(256, self.width)
        self.tiles = self.width // self.wide
        self.spans = self.wide // self.seg
        self.downs = D // self.wide
        self.rows = 2 * self.tiles * shard + self.downs * self.seg

    def column(self, half, tile, span, part, chunk):
        z = tile * self.spans + span
        base = half * self.hidden + z * (self.hidden // self.shards)
        return base + (part * self.chunks + chunk) * self.seg

    def down_row(self, part, chunk):
        return (part * self.chunks + chunk) * self.seg


def pack_kernel(plan, who_ref, in_ref, out_ref, pack):
    mine, part = who_ref[0], who_ref[1]
    seg, shard = plan.seg, plan.shard
    step = pl.program_id(0)
    half, z = step // plan.shards, step % plan.shards
    row = pl.multiple_of((half * plan.tiles + z // plan.spans) * shard, shard)
    column = pl.multiple_of(z % plan.spans * seg, seg)
    for e in range(EXPERTS):

        @pl.when(mine == e)
        def _(e=e):
            value = in_ref[:, e, :]
            for chunk in range(plan.chunks):
                piece = value[:, chunk * seg : (chunk + 1) * seg]
                for p in range(1, plan.copies):
                    at = (p * plan.chunks + chunk) * seg
                    piece = jnp.where(part == p, value[:, at : at + seg], piece)
                at = pl.multiple_of(chunk * plan.rows + row, 16)
                pack[pl.ds(at, shard), pl.ds(column, seg)] = piece

        @pl.when((mine == e) & (step == 0))
        def _(e=e):
            for chunk in range(plan.chunks):
                start = chunk * plan.rows + 2 * plan.tiles * shard
                at = pl.multiple_of(plan.down_row(part, chunk), seg)
                value = out_ref[pl.ds(at, seg), e, :]
                for down in range(plan.downs):
                    pack[start + down * seg : start + (down + 1) * seg, :] = value[
                        :, down * plan.wide : (down + 1) * plan.wide
                    ]


def pack_pieces(plan, who, expert_in, expert_out, after):
    if plan.seg % LANES == 0:
        per = plan.hidden // plan.shards
        return launch(
            partial(pack_kernel, plan),
            [who, expert_in, expert_out],
            [
                SMEM,
                pl.BlockSpec((plan.shard, EXPERTS, per), lambda i: (0, 0, i)),
                whole(expert_out.shape),
            ],
            whole((plan.chunks * plan.rows, plan.wide)),
            jax.ShapeDtypeStruct((plan.chunks * plan.rows, plan.wide), bf16),
            after,
            grid=(2 * plan.shards,),
            compiler_params=params(),
            cost_estimate=cost(0, 0),
            name="pack",
        )
    mine, part = who[0], who[1:]
    own_in = lax.dynamic_index_in_dim(expert_in, mine, 1, keepdims=False)
    own_out = lax.dynamic_index_in_dim(expert_out, mine, 1, keepdims=False)
    packs = []
    for chunk in range(plan.chunks):
        blocks = []
        for half in range(2):
            for tile in range(plan.tiles):
                spans = [
                    lax.dynamic_slice_in_dim(
                        own_in, plan.column(half, tile, span, part[0], chunk), plan.seg, 1
                    )
                    for span in range(plan.spans)
                ]
                blocks.append(jnp.concatenate(spans, axis=1))
        rows = lax.dynamic_slice_in_dim(own_out, plan.down_row(part[0], chunk), plan.seg, 0)
        blocks += [rows[:, d * plan.wide : (d + 1) * plan.wide] for d in range(plan.downs)]
        packs.append(jnp.concatenate(blocks, axis=0))
    return jnp.concatenate(packs, axis=0)


def unpack_kernel(plan, begun, who_ref, *refs):
    copies, seg = plan.copies, plan.seg
    ins, downs = refs[:copies], refs[copies : 2 * copies]
    in_out, down_out = refs[2 * copies + 2 * begun :]
    mine, part = who_ref[0], who_ref[1]
    step = pl.program_id(0)
    p = step % copies
    z = (step // copies) % plan.shards
    for j in range(EXPERTS):
        chosen = ins[0][j ^ mine].astype(f32)
        for m in range(1, copies):
            chosen = jnp.where(part == (p ^ m), ins[m][j ^ mine].astype(f32), chosen)
        piece = chosen[:, :seg]
        for span in range(1, plan.spans):
            here = z % plan.spans == span
            piece = jnp.where(here, chosen[:, span * seg : (span + 1) * seg], piece)
        in_out[:, j, :] = piece

    @pl.when(step < copies)
    def _():
        for j in range(EXPERTS):
            for down in range(plan.downs):
                rows = slice(down * seg, (down + 1) * seg)
                chosen = downs[0][j ^ mine, rows, :].astype(f32)
                for m in range(1, copies):
                    chosen = jnp.where(
                        part == (p ^ m), downs[m][j ^ mine, rows, :].astype(f32), chosen
                    )
                down_out[:, j, down * plan.wide : (down + 1) * plan.wide] = chosen


def unpack_chunk(plan, who, chunk, sums, begun):
    copies, shards = plan.copies, plan.shards
    per = plan.hidden // shards
    start = 2 * plan.tiles * plan.shard
    down_rows = plan.downs * plan.seg

    def in_block(i):
        half, z = i // (shards * copies), (i // copies) % shards
        return (0, half * plan.tiles + z // plan.spans, 0)

    def down_block(i):
        return (jnp.minimum(i, copies - 1) * plan.chunks + chunk, 0, 0)

    hbm = pl.BlockSpec(memory_space=pl.ANY)
    operands = [who, *sums, *[s[:, start:, :] for s in sums], *begun]
    return launch(
        partial(unpack_kernel, plan, len(begun) // 2),
        operands,
        [SMEM]
        + [pl.BlockSpec((EXPERTS, plan.shard, plan.wide), in_block)] * copies
        + [whole((EXPERTS, down_rows, plan.wide))] * copies
        + [hbm] * len(begun),
        [
            pl.BlockSpec((plan.shard, EXPERTS, plan.seg), lambda i: (0, 0, i * plan.chunks + chunk)),
            pl.BlockSpec((plan.seg, EXPERTS, D), down_block),
        ],
        [
            jax.ShapeDtypeStruct((plan.shard, EXPERTS, 2 * plan.hidden), f32),
            jax.ShapeDtypeStruct((per, EXPERTS, D), f32),
        ],
        grid=(2 * shards * copies,),
        input_output_aliases={len(operands) - 2 + i: i for i in range(len(begun))},
        compiler_params=params(),
        cost_estimate=cost(0, 12 * plan.shard * plan.hidden * EXPERTS),
        name="unpack",
    )


def unpack_grads(plan, who, sums, begun):
    if begun:
        for chunk in range(1, plan.chunks):
            begun = unpack_chunk(plan, who, chunk, sums[chunk], begun)
        return begun
    mine, part = who[0], who[1]
    ins, outs = [], []
    for j in range(EXPERTS):
        columns = {}
        rows = []
        for p in range(plan.copies):
            for chunk in range(plan.chunks):
                stacked = jnp.stack(sums[chunk])
                piece = lax.dynamic_index_in_dim(stacked, part ^ p, 0, keepdims=False)
                piece = lax.dynamic_index_in_dim(piece, mine ^ j, 0, keepdims=False)
                for half in range(2):
                    for tile in range(plan.tiles):
                        row = (half * plan.tiles + tile) * plan.shard
                        for span in range(plan.spans):
                            columns[plan.column(half, tile, span, p, chunk)] = piece[
                                row : row + plan.shard, span * plan.seg : (span + 1) * plan.seg
                            ]
                row = 2 * plan.tiles * plan.shard
                rows.append(
                    jnp.concatenate(
                        [
                            piece[row + d * plan.seg : row + (d + 1) * plan.seg]
                            for d in range(plan.downs)
                        ],
                        axis=1,
                    )
                )
        ins.append(jnp.concatenate([columns[c] for c in sorted(columns)], axis=1))
        outs.append(jnp.concatenate(rows, axis=0))
    return jnp.stack(ins, axis=1).astype(f32), jnp.stack(outs, axis=1).astype(f32)


def expert_kernel(plan, first, last, *refs):
    refs = list(refs)

    def take(n):
        out = refs[:n]
        del refs[:n]
        return out

    copies = plan.copies
    x_refs, y_refs = take(EXPERTS), take(EXPERTS)
    w_refs = take(copies)
    carry_in = [] if first else take(2)
    grad_outs = take(copies)
    if last:
        dx_outs, ret_outs = take(EXPERTS), take(EXPERTS)
        carry_out = []
    else:
        carry_out = take(2)
    xs, ds, xt, gcol, ret_acc, dx_acc, wg, wu, wo, act_s, dg_s, du_s, grads, sems = refs
    rows = EXPERTS * CAP
    shard, seg, wide, tiles = plan.shard, plan.seg, plan.wide, plan.tiles

    carries = [
        pltpu.make_async_copy(src, dst, sems.at[i])
        for i, (src, dst) in enumerate(zip(carry_in, (ret_acc, dx_acc)))
    ]
    for copy in carries:
        copy.start()
    for k in range(EXPERTS):
        span = slice(k * CAP, (k + 1) * CAP)
        x = x_refs[k][:CAP, :]
        xs[span, :] = x
        xt[:, span] = x.astype(f32).T.astype(bf16)
        extra = x_refs[k][CAP:, :CAP].astype(f32)
        gate = (extra[0:1] + extra[1:2]).T
        gcol[span, :] = jnp.broadcast_to(gate, (CAP, LANES))
        ds[span, :] = (y_refs[k][:CAP, :].astype(f32) * gate).astype(bf16)
    if first:
        ret_acc[...] = jnp.zeros_like(ret_acc)
        dx_acc[...] = jnp.zeros_like(dx_acc)
    for copy in carries:
        copy.wait()

    sends = []
    for m in range(copies):
        w = w_refs[m]
        for z in range(plan.shards):
            for tile in range(tiles):
                for half, target in ((0, wg), (1, wu)):
                    row = (half * tiles + tile) * shard
                    target[z * shard : (z + 1) * shard, tile * wide : (tile + 1) * wide] = w[
                        z, row : row + shard, :
                    ]
            for down in range(plan.downs):
                row = 2 * tiles * shard + down * seg
                wo[z * seg : (z + 1) * seg, down * wide : (down + 1) * wide] = w[
                    z, row : row + seg, :
                ]

        def block(b, _):
            span = pl.ds(pl.multiple_of(b * CAP, CAP), CAP)
            x, d = xs[span, :], ds[span, :]
            gate = mm(x, wg[...])
            up = mm(x, wu[...])
            grad_act = mm_nt(d, wo[...])
            sig = 1.0 / (1.0 + jnp.exp(-gate))
            silu = gate * sig
            act = (silu * up).astype(bf16)
            grad_up = (grad_act * silu).astype(bf16)
            grad_gate = (grad_act * up * (sig + silu * (1.0 - sig))).astype(bf16)
            act_s[span, :] = act
            du_s[span, :] = grad_up
            dg_s[span, :] = grad_gate
            ret_acc[span, :] += mm(act, wo[...])
            dx_acc[span, :] += mm_nt(grad_gate, wg[...]) + mm_nt(grad_up, wu[...])
            return 0

        lax.fori_loop(0, EXPERTS, block, 0)
        if m == copies - 1 and not last:
            for i, (src, dst) in enumerate(zip((ret_acc, dx_acc), carry_out, strict=True)):
                copy = pltpu.make_async_copy(src, dst, sems.at[2 + i])
                copy.start()
                sends.append(copy)
        if m == copies - 1 and last:
            for k in range(EXPERTS):
                span = slice(k * CAP, (k + 1) * CAP)
                ret = ret_acc[span, :]
                dgate = jnp.sum(ret * y_refs[k][:CAP, :].astype(f32), axis=-1, keepdims=True)
                dgate = jnp.broadcast_to(dgate, (CAP, LANES)).T[:1]
                ret_outs[k][...] = (ret * gcol[span, :1]).astype(bf16)
                dx_outs[k][:CAP, :] = dx_acc[span, :].astype(bf16)
                high = dgate.astype(bf16).astype(f32)
                tail = jnp.concatenate(
                    [high, dgate - high, jnp.zeros((EXTRA - 2, CAP), f32)], axis=0
                ).astype(bf16)
                dx_outs[k][CAP:, :CAP] = tail
                dx_outs[k][CAP:, CAP:] = jnp.zeros((EXTRA, D - CAP), bf16)
        for half, source in ((0, dg_s), (1, du_s)):
            for tile in range(tiles):
                made = mm(xt[...], source[:, tile * wide : (tile + 1) * wide]).astype(bf16)
                row = (half * tiles + tile) * shard
                for z in range(plan.shards):
                    grads[m, z, row : row + shard, :] = made[z * shard : (z + 1) * shard, :]
        for tile in range(tiles):
            made = mm_tn(act_s[:, tile * wide : (tile + 1) * wide], ds[...]).astype(bf16)
            for span in range(plan.spans):
                z = tile * plan.spans + span
                for down in range(plan.downs):
                    row = 2 * tiles * shard + down * seg
                    grads[m, z, row : row + seg, :] = made[
                        span * seg : (span + 1) * seg, down * wide : (down + 1) * wide
                    ]
        copy = pltpu.make_async_copy(grads.at[m], grad_outs[m], sems.at[4 + m])
        copy.start()
        sends.append(copy)
    for copy in sends:
        copy.wait()


def expert_call(plan, xs, ys, weights, chunk, carried):
    first, last = chunk == 0, chunk == plan.chunks - 1
    rows = EXPERTS * CAP
    hbm = pl.BlockSpec(memory_space=pl.ANY)
    copies = plan.copies
    block = pl.BlockSpec(
        (plan.shards, plan.rows, plan.wide),
        lambda i: (0, chunk, 0),
        pipeline_mode=pl.Buffered(1),
    )
    in_specs = [whole(a.shape) for a in (*xs, *ys)] + [block] * copies
    operands = list(xs) + list(ys) + list(weights)
    if not first:
        in_specs += [hbm] * 2
        operands += list(carried)
    out_specs = [hbm] * copies
    out_shape = [jax.ShapeDtypeStruct((plan.shards, plan.rows, plan.wide), bf16)] * copies
    if last:
        out_specs += [whole((CAP + EXTRA, D))] * EXPERTS
        out_specs += [whole((CAP, D))] * EXPERTS
        out_shape += [jax.ShapeDtypeStruct((CAP + EXTRA, D), bf16)] * EXPERTS
        out_shape += [jax.ShapeDtypeStruct((CAP, D), bf16)] * EXPERTS
    else:
        out_specs += [hbm] * 2
        out_shape += [jax.ShapeDtypeStruct((rows, D), f32)] * 2
    made = pl.pallas_call(
        partial(expert_kernel, plan, first, last),
        in_specs=in_specs,
        out_specs=out_specs,
        out_shape=out_shape,
        scratch_shapes=[
            pltpu.VMEM((rows, D), bf16),
            pltpu.VMEM((rows, D), bf16),
            pltpu.VMEM((D, rows), bf16),
            pltpu.VMEM((rows, LANES), f32),
            pltpu.VMEM((rows, D), f32),
            pltpu.VMEM((rows, D), f32),
            pltpu.VMEM((D, plan.width), bf16),
            pltpu.VMEM((D, plan.width), bf16),
            pltpu.VMEM((plan.width, D), bf16),
            pltpu.VMEM((rows, plan.width), bf16),
            pltpu.VMEM((rows, plan.width), bf16),
            pltpu.VMEM((rows, plan.width), bf16),
            pltpu.VMEM((copies, plan.shards, plan.rows, plan.wide), bf16),
            pltpu.SemaphoreType.DMA((4 + copies,)),
        ],
        grid=(1,),
        compiler_params=params(),
        cost_estimate=cost(
            18 * rows * D * plan.width * copies, 12 * D * plan.width * copies + 12 * rows * D
        ),
        name="experts",
    )(*operands)
    return made[:copies], made[copies:]


def spots_of(place_ref, rows):
    slot = lax.broadcasted_iota(jnp.int32, (rows, EXPERTS * CAP), 1)
    hit = (slot == place_ref[:, 0:1]) | (slot == place_ref[:, 1:2])
    return jnp.where(hit, 1.0, 0.0).astype(bf16)


def constant_gates(one, chosen, m):
    a0 = one[:, NCH + 2 * m : NCH + 2 * m + 1]
    a1 = one[:, NCH + 2 * m + 1 : NCH + 2 * m + 2]
    gate = chosen[:, EXPERTS + 2 + m : EXPERTS + 3 + m]
    return gate, a0, a1


def back_kernel(
    count,
    who_ref,
    res_ref,
    h_ref,
    dy_ref,
    one_ref,
    place_ref,
    choice_ref,
    prev_ref,
    wsmall_ref,
    *refs,
):
    dx_refs, refs = refs[:EXPERTS], refs[EXPERTS:]
    pieces, refs = refs[:count], refs[count:]
    (
        dres_ref,
        branch_ref,
        dctx_ref,
        dsmall_ref,
        gain_out,
        prev_out,
        cvec_out,
        w_ref,
        dg_ref,
    ) = refs

    @pl.when(pl.program_id(0) == 0)
    def _():
        gain_out[...] = jnp.zeros_like(gain_out)
        prev_out[...] = jnp.zeros_like(prev_out)
        cvec_out[...] = jnp.zeros_like(cvec_out)
        dsmall_ref[...] = jnp.zeros_like(dsmall_ref)
        lay_columns(w_ref, pieces, who_ref[1])
        lane = lanes_of((CAP, LANES))
        for k in range(EXPERTS):
            columns = dx_refs[k][CAP:, :CAP].astype(f32).T
            at = who_ref[0] ^ k
            made = jnp.where(lane == at, columns[:, 0:1], 0.0)
            made = jnp.where(lane == at + 16, columns[:, 1:2], made)
            dg_ref[k * CAP : (k + 1) * CAP, :] = made.astype(bf16)

    res = res_ref[...]
    rows = res.shape[0]
    one = one_ref[...]
    lane = lanes_of(one.shape)
    chosen = jnp.where(selected(choice_ref, lane), one, 0.0)
    choice = lane < NCH
    is_mix = (lane >= NCH) & (lane < NCH + 4)
    spots = spots_of(place_ref, rows)
    moved = jnp.zeros(res.shape, f32)
    for k in range(EXPERTS):
        moved = moved + mm(spots[:, k * CAP : (k + 1) * CAP], dx_refs[k][:CAP, :])
    from_experts = mm(spots, dg_ref[...])
    from_experts = from_experts + pltpu.roll(from_experts, LANES - 16, 1)

    inverse = lax.rsqrt(jnp.mean(res * res, axis=-1, keepdims=True) + EPS)
    dy = dy_ref[...]
    dyf = dy.astype(f32)
    gain = row_of(wsmall_ref, GAIN_F)
    spread = res * inverse * gain
    hd = jnp.sum(spread * dyf, axis=-1, keepdims=True)
    cd = mm_nt(dy, wsmall_ref[...])
    coef = chosen[:, EXPERTS + 1 : EXPERTS + 2]
    grads = jnp.where(lane < EXPERTS, from_experts, 0.0)
    grads = jnp.where(lane == EXPERTS + 1, hd, grads)
    made = jnp.zeros_like(one)
    for m in range(2):
        gate, a0, a1 = constant_gates(one, chosen, m)
        dot = cd[:, CVEC + m : CVEC + m + 1]
        coef = coef + gate * a0
        grads = jnp.where(lane == EXPERTS + 2 + m, a0 * hd + a1 * dot, grads)
        grads = jnp.where(lane == NCH + 2 * m, gate * hd, grads)
        grads = jnp.where(lane == NCH + 2 * m + 1, gate * dot, grads)
        made = jnp.where(lane == m, gate * a1, made)
    grads = jnp.where(is_mix | selected(choice_ref, lane), grads, 0.0)
    weighted = one * grads
    mean_choice = jnp.sum(jnp.where(choice, weighted, 0.0), axis=-1, keepdims=True)
    d_logits = jnp.where(choice, one * (grads - mean_choice), 0.0)
    d_mix = one * (grads - (weighted + partner(weighted, lane)))
    d_small = jnp.where(choice, d_logits, jnp.where(is_mix, d_mix, 0.0))
    low = d_small.astype(bf16)
    spread_grad = moved + mm(low, wsmall_ref[...]) + coef * dyf
    scaled = spread_grad * gain
    mean_dot = jnp.mean(res * scaled, axis=-1, keepdims=True)
    d_res = dyf + inverse * scaled - res * (inverse * inverse * inverse * mean_dot)
    dres_ref[...] = d_res
    gain_out[...] += jnp.sum(spread_grad * res * inverse, axis=0, keepdims=True)
    branch = d_res.astype(bf16)
    branch_ref[...] = branch
    dctx_ref[...] = mm_nt(branch, w_ref[...]).astype(bf16)
    dsmall_ref[...] += mm_tn(low, h_ref[...])
    high = d_logits.astype(bf16)
    rest = (d_logits - high.astype(f32)).astype(bf16)
    prev = prev_ref[...]
    prev_out[...] += mm(prev, high) + mm(prev, rest)
    high = made.astype(bf16)
    rest = (made - high.astype(f32)).astype(bf16)
    cvec_out[...] += mm_tn(high, dy) + mm_tn(rest, dy)


def back_call(who, res, h, dy, one, places, choices, prev, small, dx, pieces, after):
    rows = res.shape[0]
    block = 256
    tall = jax.ShapeDtypeStruct((LANES, D), f32)
    return launch(
        partial(back_kernel, len(pieces)),
        [who, res, h, dy, one, places, choices, prev, small, *dx, *pieces],
        [SMEM]
        + [rows_of(block, D)] * 3
        + [rows_of(block, LANES)]
        + [rows_of(block, 2)] * 2
        + [pl.BlockSpec((NCH, block), lambda i: (0, i))]
        + [whole(a.shape) for a in (small, *dx, *pieces)],
        [rows_of(block, D)] * 3
        + [whole((LANES, D)), whole((1, D)), whole((NCH, LANES)), whole((LANES, D))],
        [
            jax.ShapeDtypeStruct((rows, D), f32),
            jax.ShapeDtypeStruct((rows, D), bf16),
            jax.ShapeDtypeStruct((rows, D), bf16),
            tall,
            jax.ShapeDtypeStruct((1, D), f32),
            jax.ShapeDtypeStruct((NCH, LANES), f32),
            tall,
        ],
        after,
        grid=(rows // block,),
        scratch_shapes=[pltpu.VMEM((D, D), bf16), pltpu.VMEM((EXPERTS * CAP, LANES), bf16)],
        compiler_params=params(),
        cost_estimate=cost(2 * rows * D * (D + 2048), 20 * rows * D),
        name="combine_back",
    )


def finish_kernel(res_ref, one_ref, place_ref, choice_ref, small_ref, *refs):
    ret_refs, out_ref = refs[:EXPERTS], refs[EXPERTS]
    res = res_ref[...]
    one = one_ref[...]
    lane = lanes_of(one.shape)
    chosen = jnp.where(selected(choice_ref, lane), one, 0.0)
    inverse = lax.rsqrt(jnp.mean(res * res, axis=-1, keepdims=True) + EPS)
    total = res
    coef = chosen[:, EXPERTS + 1 : EXPERTS + 2]
    for m in range(2):
        gate, a0, a1 = constant_gates(one, chosen, m)
        coef = coef + gate * a0
        total = total + (gate * a1) * row_of(small_ref, CVEC + m)
    total = total + (coef * inverse) * res * row_of(small_ref, GAIN_F)
    spots = spots_of(place_ref, res.shape[0])
    for k in range(EXPERTS):
        total = total + mm(spots[:, k * CAP : (k + 1) * CAP], ret_refs[k][...])
    out_ref[...] = total.astype(bf16)


def finish_call(res, one, places, choices, small, ret, after):
    rows = res.shape[0]
    block = 256
    return launch(
        finish_kernel,
        [res, one, places, choices, small, *ret],
        [rows_of(block, D), rows_of(block, LANES)]
        + [rows_of(block, 2)] * 2
        + [whole(a.shape) for a in (small, *ret)],
        rows_of(block, D),
        jax.ShapeDtypeStruct((rows, D), bf16),
        after,
        grid=(rows // block,),
        compiler_params=params(),
        cost_estimate=cost(2 * rows * D * 1536, 10 * rows * D),
        name="layer_out",
    )


def turn_kernel(count, *refs):
    for source, out in zip(refs[:count], refs[count:], strict=True):
        out[...] = source[...].astype(f32).T.astype(bf16)


def turn_call(arrays):
    rows, columns = arrays[0].shape
    return launch(
        partial(turn_kernel, len(arrays)),
        arrays,
        [pl.BlockSpec((rows, 256), lambda i: (0, i))] * len(arrays),
        [pl.BlockSpec((256, rows), lambda i: (i, 0))] * len(arrays),
        [jax.ShapeDtypeStruct((columns, rows), bf16)] * len(arrays),
        grid=(columns // 256,),
        compiler_params=params(),
        cost_estimate=cost(0, 0),
        name="turn",
    )


def dense_kernel(copies, per, part_ref, ht_ref, ct_ref, *refs):
    rights, outs = refs[:4], refs[4:]
    step = pl.program_id(0)
    source = ((step // per) ^ part_ref[0]) * per + step % per
    for index, right in enumerate(rights):
        left = ct_ref if index == 3 else ht_ref
        for m in range(copies):

            @pl.when((source // 2 == index) & (step // per == m))
            def _(left=left, right=right, m=m):
                outs[m][...] = mm(left[...], right[...]).astype(bf16)


def dense_call(copies, part, ht, ct, dq, dk, dv, branch):
    rows = ht.shape[1]
    half = D // 2
    per = 8 // copies

    def right_block(index):
        def block(i, part_ref):
            source = ((i // per) ^ part_ref[0]) * per + i % per
            return (0, jnp.clip(source - 2 * index, 0, 1))

        return block

    def out_block(m):
        return lambda i, part_ref: (0, jnp.clip(i - m * per, 0, per - 1))

    def fixed(shape):
        return pl.BlockSpec(shape, lambda i, part_ref: (0, 0), pipeline_mode=pl.Buffered(1))

    return pl.pallas_call(
        partial(dense_kernel, copies, per),
        grid_spec=pltpu.PrefetchScalarGridSpec(
            num_scalar_prefetch=1,
            grid=(8,),
            in_specs=[fixed(ht.shape), fixed(ct.shape)]
            + [pl.BlockSpec((rows, half), right_block(index)) for index in range(4)],
            out_specs=[pl.BlockSpec((D, half), out_block(m)) for m in range(copies)],
        ),
        out_shape=[jax.ShapeDtypeStruct((D, 4 * D // copies), bf16)] * copies,
        compiler_params=params(),
        cost_estimate=cost(8 * rows * D * D, 12 * rows * D + 8 * D * D),
        name="dense_grads",
    )(part, ht, ct, dq, dk, dv, branch)


def fold_parts_kernel(who_ref, *refs):
    pieces, outs = refs[:-EXPERTS], refs[-EXPERTS:]
    for k in range(EXPERTS):
        at = who_ref[0] ^ k
        total = pieces[0][0, at].astype(f32)
        for piece in pieces[1:]:
            total = total + piece[0, at].astype(f32)
        outs[k][0] = total.astype(bf16)


def fold_parts(who, pieces, shards):
    cut = pieces[0].shape[1]
    quarter = D // (shards * EXPERTS)
    shape = (shards, EXPERTS, quarter, cut)
    operands = [who] + [a.reshape(shape) for a in pieces]
    return launch(
        fold_parts_kernel,
        operands,
        [SMEM] + [pl.BlockSpec((1, EXPERTS, quarter, cut), lambda i: (i, 0, 0, 0))] * len(pieces),
        [pl.BlockSpec((1, quarter, cut), lambda i: (i, 0, 0))] * EXPERTS,
        [jax.ShapeDtypeStruct((shards, quarter, cut), bf16)] * EXPERTS,
        grid=(shards,),
        compiler_params=params(),
        name="fold_parts",
    )


def fold_quarters_kernel(count, zi_ref, small_ref, *refs):
    pieces, outs = refs[:count], refs[count:]
    rows, cut = pieces[0].shape[1:]
    spare = outs[0].shape[0] - rows
    for k, out in enumerate(outs):
        at = lax.rem(zi_ref[0] + k, len(outs))
        total = pieces[0][at].astype(f32)
        for piece in pieces[1:]:
            total = total + piece[at].astype(f32)
        out[:rows, :] = total.astype(bf16)
        for c in range(cut // LANES):
            out[rows:, c * LANES : (c + 1) * LANES] = small_ref[at, c * spare : (c + 1) * spare, :]


def fold_quarters(zi, small, pieces, after=()):
    shards, rows, cut = pieces[0].shape
    spare = D // shards * LANES // cut
    return launch(
        partial(fold_quarters_kernel, len(pieces)),
        [zi, small.reshape(shards, D // shards, LANES), *pieces],
        [SMEM] + [VM] * (len(pieces) + 1),
        [VM] * shards,
        [jax.ShapeDtypeStruct((rows + spare, cut), bf16)] * shards,
        after,
        name="fold_quarters",
    )


def lay_tail_kernel(count, rows, own_ref, *refs):
    pieces, out = refs[:count], refs[count]
    total = pieces[0][rows:, :].astype(f32)
    for k in range(count):
        at = pl.multiple_of((own_ref[0] ^ k) * rows, rows)
        out[pl.ds(at, rows), :] = pieces[k][:rows, :]
        if k:
            total = total + pieces[k][rows:, :].astype(f32)
    out[count * rows :, :] = total.astype(bf16)


def lay_tail(own, pieces, rows, after):
    count = len(pieces)
    size, cut = pieces[0].shape
    return launch(
        partial(lay_tail_kernel, count, rows),
        [own, *pieces],
        [SMEM] + [VM] * count,
        VM,
        jax.ShapeDtypeStruct((count * rows + size - rows, cut), bf16),
        after,
        name="lay_tail",
    )


def fold_copies(pieces):
    total = pieces[0].astype(f32)
    for piece in pieces[1:]:
        total = total + piece.astype(f32)
    return total.astype(bf16)


def fold_shards_kernel(*refs):
    total = refs[0][...].astype(f32)
    for ref in refs[1:-1]:
        total = total + ref[...].astype(f32)
    refs[-1][...] = total.astype(bf16)


def fold_shards(pieces):
    return launch(
        fold_shards_kernel,
        pieces,
        [VM] * len(pieces),
        VM,
        jax.ShapeDtypeStruct(pieces[0].shape, bf16),
        name="fold_shards",
    )


def unpack_dense_kernel(count, rows, part_ref, *refs):
    pieces = refs[:count]
    qkv_ref, proj_ref, router_ref, mix_ref, cvec_ref, gain_a_ref, gain_f_ref, prev_ref = refs[count:-1]
    small_ref = refs[-1]
    cut = pieces[0].shape[1]
    small = pieces[0][rows:, :].astype(f32)
    for piece in pieces[1:]:
        small = small + piece[rows:, :].astype(f32)
    spare = small.shape[0]
    for c in range(cut // LANES):
        small_ref[c * spare : (c + 1) * spare, :] = small[:, c * LANES : (c + 1) * LANES]
    turned = small_ref[...].T
    router_ref[...] = turned[:NCH]
    mix_ref[...] = turned[NCH:CVEC]
    cvec_ref[...] = turned[CVEC:GAIN_A]
    gain_a_ref[...] = turned[GAIN_A:GAIN_F]
    gain_f_ref[...] = turned[GAIN_F : GAIN_F + 1]
    prev_ref[...] = small_ref[: prev_ref.shape[0], 16 : 16 + NCH]
    for p in range(count):
        chosen = pieces[0][:rows, :].astype(f32)
        for m in range(1, count):
            chosen = jnp.where(part_ref[0] == (p ^ m), pieces[m][:rows, :].astype(f32), chosen)
        start = p * cut
        in_qkv = max(0, min(cut, 3 * D - start))
        if in_qkv:
            qkv_ref[:, start : start + in_qkv] = chosen[:, :in_qkv]
        if in_qkv < cut:
            at = start + in_qkv - 3 * D
            proj_ref[:, at : at + cut - in_qkv] = chosen[:, in_qkv:]


def unpack_dense(part, pieces, rows, owned):
    heights = (NCH, 4, 2, 1, 1)
    return launch(
        partial(unpack_dense_kernel, len(pieces), rows),
        [part, *pieces],
        [SMEM] + [VM] * len(pieces),
        [VM] * 8,
        [jax.ShapeDtypeStruct((rows, 3 * D), f32), jax.ShapeDtypeStruct((rows, D), f32)]
        + [jax.ShapeDtypeStruct((height, rows), f32) for height in heights]
        + [jax.ShapeDtypeStruct((owned, NCH), f32)],
        scratch_shapes=[pltpu.VMEM((rows, LANES), f32)],
        name="unpack_dense",
    )


def last_kernel(
    count,
    shards,
    part_ref,
    dq_ref,
    dk_ref,
    dv_ref,
    x_ref,
    dres_ref,
    small_ref,
    dsmall_ref,
    gain_f_ref,
    prev_ref,
    cvec_ref,
    *refs,
):
    pieces = refs[:count]
    out_ref, small_out, w_ref, gain_ref = refs[count:]

    @pl.when(pl.program_id(0) == 0)
    def _():
        gain_ref[...] = jnp.zeros_like(gain_ref)
        lay_columns(w_ref, pieces, part_ref[0])

    grad = mm_nt(dq_ref[...], w_ref[:, :D])
    grad = grad + mm_nt(dk_ref[...], w_ref[:, D : 2 * D])
    grad = grad + mm_nt(dv_ref[...], w_ref[:, 2 * D :])
    x = x_ref[...].astype(f32)
    inverse = lax.rsqrt(jnp.mean(x * x, axis=-1, keepdims=True) + EPS)
    scaled = grad * row_of(small_ref, GAIN_A)
    mean_dot = jnp.mean(x * scaled, axis=-1, keepdims=True)
    d_x = inverse * scaled - x * (inverse * inverse * inverse * mean_dot)
    out_ref[...] = (dres_ref[...] + d_x).astype(bf16)
    gain_ref[...] += jnp.sum(grad * x * inverse, axis=0, keepdims=True)

    @pl.when(pl.program_id(0) == pl.num_programs(0) - 1)
    def _():
        row = lax.broadcasted_iota(jnp.int32, (LANES, D), 0)
        total = jnp.where(row < CVEC, dsmall_ref[...], 0.0)
        for m in range(2):
            total = jnp.where(row == CVEC + m, cvec_ref[m : m + 1, :], total)
        total = jnp.where(row == GAIN_A, gain_ref[...], total)
        total = jnp.where(row == GAIN_F, gain_f_ref[...], total)
        total = total.T
        owned = NCH // shards
        shard = D // shards
        row = lax.broadcasted_iota(jnp.int32, total.shape, 0)
        lane = lanes_of((NCH, LANES))
        prev = pltpu.roll(jnp.where(lane < NCH, prev_ref[...], 0.0), 16, 1)
        for index in range(NCH):
            at = (index // owned) * shard + index % owned
            total = jnp.where(row == at, total + prev[index : index + 1, :], total)
        small_out[...] = total.astype(bf16)


def last_call(part, shards, dq, dk, dv, x, dres, small, smalls, pieces, after):
    rows = x.shape[0]
    block = 256
    return launch(
        partial(last_kernel, len(pieces), shards),
        [part, dq, dk, dv, x, dres, small, *smalls, *pieces],
        [SMEM]
        + [rows_of(block, D)] * 5
        + [whole(a.shape) for a in (small, *smalls, *pieces)],
        [rows_of(block, D), whole((D, LANES))],
        [jax.ShapeDtypeStruct((rows, D), bf16), jax.ShapeDtypeStruct((D, LANES), bf16)],
        after,
        grid=(rows // block,),
        scratch_shapes=[pltpu.VMEM((D, 3 * D), bf16), pltpu.VMEM((1, D), f32)],
        compiler_params=params(),
        cost_estimate=cost(6 * rows * D * D, 14 * rows * D),
        name="input_grad",
    )


def body(
    replicas,
    shards,
    tokens,
    prev_logits,
    out_grad,
    routes,
    doc_ids,
    valid_mask,
    qkv_weight,
    proj_weight,
    gain_attn,
    gain_ffn,
    router,
    const_mix,
    prev_mix,
    const_vec,
    expert_in,
    expert_out,
):
    me = lax.axis_index("rep")
    zi = lax.axis_index("fsdp")
    copies = replicas // EXPERTS
    mine = me // copies
    part = me % copies
    rows = tokens.shape[0]
    shard = qkv_weight.shape[0]
    hidden = expert_in.shape[2] // 2
    quarter = shard // EXPERTS
    plan = Plan(replicas, shards, shard, hidden, 2)
    zi_s = zi.reshape(1).astype(jnp.int32)
    mine_s = mine.reshape(1).astype(jnp.int32)
    part_s = part.reshape(1).astype(jnp.int32)
    who = jnp.concatenate([mine_s, part_s])

    def to_expert(a, k):
        return lax.ppermute(a, "rep", [(i, i ^ (k * copies)) for i in range(replicas)])

    def to_part(a, m):
        return lax.ppermute(a, "rep", [(i, i ^ m) for i in range(replicas)])

    def spin(a, k):
        return lax.ppermute(a, "fsdp", [(i, (i + k) % shards) for i in range(shards)])

    def by_xor(pieces, own, axis):
        size = pieces[0].shape[axis]
        shape = list(pieces[0].shape)
        shape[axis] = size * len(pieces)
        full = jnp.zeros(shape, pieces[0].dtype)
        for k, piece in enumerate(pieces):
            full = lax.dynamic_update_slice_in_dim(full, piece, (own ^ k) * size, axis)
        return full

    width = 3 * D // copies
    owned = prev_mix.shape[0]
    smalls = [router.T, const_mix.T, const_vec.T, gain_attn[None], gain_ffn[None], prev_mix]
    piece, mark = cut_dense(who, qkv_weight, proj_weight, smalls, copies)
    spun = [piece] + [spin(piece, k) for k in range(1, shards)]

    docs = doc_ids.reshape(-1)
    drow = docs[None, :]
    dcol = docs[:, None]
    vcol = valid_mask.reshape(-1)[:, None]
    first_place = jnp.sum((drow < dcol).astype(jnp.int32), axis=1)
    offset = (jnp.arange(rows, dtype=jnp.int32) - first_place).astype(f32)
    frequency = jnp.exp(
        jnp.arange(HDIM // 2, dtype=f32) * (-2.0 * math.log(10000.0) / HDIM)
    )
    angles = offset[:, None] * frequency[None, :]
    cosine, sine = jnp.cos(angles), jnp.sin(angles)
    cosine = jnp.concatenate([cosine] * 4, axis=1)
    sine = jnp.concatenate([-sine, sine, -sine, sine], axis=1)

    routes_t = routes.T
    chosen = jnp.where(routes_t < EXPERTS, routes_t ^ mine, routes_t)
    kinds = jnp.arange(EXPERTS, dtype=jnp.int32)
    named = jnp.any(chosen[:, None, :] == kinds[None, :, None], axis=0)
    later = jnp.triu(jnp.ones((rows, rows), bf16), 1)
    rank = mm(named.astype(bf16), later).astype(jnp.int32)
    spot = jnp.where(named, rank, CAP)
    hit = chosen[:, None, :] == kinds[None, :, None]
    places = jnp.sum(jnp.where(hit, (kinds[:, None] * CAP + rank)[None], 0), axis=1)
    places = jnp.where(chosen < EXPERTS, places, -1).T

    tables = (cosine, sine, spot, dcol, vcol, places)
    packed = pack_pieces(plan, who, expert_in, expert_out, (to_part(mark, 1),))
    gathered = lax.all_gather(packed, "fsdp", axis=0, tiled=False)
    qkv_part, proj_part, small, prevs = lay_shards(
        zi_s, spun, shard, quarter, width, (packed,)
    )
    pmix = prevs[:, :owned].reshape(NCH, LANES)

    def exchanged(blocks):
        return [blocks[0]] + [to_expert(blocks[k], k) for k in range(1, EXPERTS)]

    def over_parts(half):
        half = half.reshape(D, half.shape[3])
        pieces = [half] + [to_part(half, m) for m in range(1, copies)]
        if half.shape[1] % LANES == 0:
            return pieces
        return [by_xor(pieces, part, 1)]

    qkv_half = lay_xor(
        mine_s, exchanged([qkv_part] * EXPERTS), tables
    )
    qkv_pieces = over_parts(qkv_half)
    part_q = part_s if len(qkv_pieces) == copies else jnp.zeros_like(part_s)
    per = D // proj_part.shape[2]
    rider = proj_part.reshape(-1, per, quarter, D // per).transpose(0, 2, 1, 3)
    rider = rider.reshape(-1, D)
    rider = jnp.pad(rider, ((0, -rider.shape[0] % 16), (0, 0)))
    ys = dispatch_call(mine_s, spot, out_grad, rider=rider, after=(qkv_half,))

    prev = prev_logits.T
    h1, q, k, v = qkv_call(part_q, tokens, small, cosine, sine, qkv_pieces, (ys[0],))
    ys = exchanged(ys)
    ctx, lse = attend_call(q, k, v, dcol, drow, vcol, ())
    proj_half = lay_riders(mine_s, ys, proj_part.shape, (ctx,))
    proj_pieces = over_parts(proj_half)
    part_p = part_s if len(proj_pieces) == copies else jnp.zeros_like(part_s)
    res, h2, one, gates = after_call(
        part_p, ctx, tokens, small, prev, pmix, routes, proj_pieces
    )

    xs = dispatch_call(mine_s, spot, h2, gates)
    gathered = tie(gathered, xs[0])
    weights = [gathered] + [to_part(gathered, m) for m in range(1, copies)]
    h1_t, ctx_t = turn_call([tie(h1, xs[0]), ctx])
    xs = exchanged(xs)
    weights[0] = tie(weights[0], h1_t)
    carried = None
    chunk_grads = []
    for chunk in range(plan.chunks):
        grads, carried = expert_call(
            plan,
            xs,
            ys,
            weights,
            chunk,
            carried,
        )
        chunk_grads.append(grads)
    dx = exchanged(carried[:EXPERTS])

    chunk_grads = [
        [grads[0]] + [to_part(grads[m], m) for m in range(1, copies)] for grads in chunk_grads
    ]
    total = fold_copies(tie(chunk_grads[0], carried[0]))

    def over_shards(t):
        return lax.psum_scatter(t, "fsdp", scatter_dimension=0, tiled=False)

    who_p = jnp.concatenate([mine_s, part_p])
    dres, branch, dctx, dsmall, gain_f_grad, prev_grad, cvec_grad = back_call(
        who_p,
        res,
        h2,
        out_grad,
        one,
        places,
        routes,
        prev,
        small,
        dx,
        proj_pieces,
        (total,),
    )
    summed = [over_shards(total)]
    summed += [over_shards(fold_copies(tie(grads, branch))) for grads in chunk_grads[1:]]
    ret = exchanged(tie(carried[EXPERTS:], branch))
    first = tie(summed[0], branch)
    spread = [[first] + [to_expert(first, k) for k in range(1, EXPERTS - 1)]]
    dq, dk, dv = attend_back_call(q, k, v, dctx, lse, dcol, drow, vcol, cosine, sine, ())
    dense = dense_call(
        copies, part_s, h1_t, ctx_t, tie(dq, ret, spread[0]), dk, dv, branch
    )
    spread[0].append(to_expert(tie(first, dq), EXPERTS - 1))
    dense = tie(list(dense), summed[1:])
    for piece in summed[1:]:
        piece = tie(piece, dense[0])
        spread.append([piece] + [to_expert(piece, k) for k in range(1, EXPERTS - 1)])
    dense = [dense[0]] + [to_part(dense[m], m) for m in range(1, copies)]
    quarters = fold_parts(who, dense, shards)

    def over_copies(pieces):
        stacked = jnp.stack(pieces)
        return [stacked] + [to_part(stacked, m) for m in range(1, copies)]

    spread[0] = over_copies(tie(spread[0], quarters))
    input_grad, smalls = last_call(
        part_q,
        shards,
        dq,
        dk,
        dv,
        tokens,
        tie(dres, quarters),
        small,
        (dsmall, gain_f_grad, prev_grad, cvec_grad),
        qkv_pieces,
        (),
    )
    begun = ()
    if plan.seg % LANES == 0:
        begun = unpack_chunk(plan, who, 0, spread[0], begun)
    out = finish_call(res, one, places, routes, small, tie(ret, quarters), ())
    near = [pieces[1:] for pieces in spread[1:]]
    bands = fold_quarters(zi_s, smalls, exchanged(quarters), (*begun, out, *near[0]))
    for pieces in spread[1:]:
        pieces.append(to_expert(tie(pieces[0], bands), EXPERTS - 1))
    spun = [bands[0]] + [spin(bands[k], k) for k in range(1, shards)]
    spread[1:] = [over_copies(tie(pieces, spun)) for pieces in spread[1:]]
    tail = fold_shards(spun)
    full_in, full_out = unpack_grads(plan, who, spread, begun)
    tail = lay_tail(mine_s, exchanged([tail] * EXPERTS), quarter, (full_out,))
    tails = [tail] + [to_part(tail, m) for m in range(1, copies)]
    qkv_grad, proj_grad, router_t, mix_t, cvec_t, gain_a, gain_f, prev_out = unpack_dense(
        part_s, tails, shard, owned
    )

    return (
        out,
        input_grad,
        qkv_grad,
        proj_grad,
        gain_a[0],
        gain_f[0],
        router_t.T,
        mix_t.T,
        prev_out,
        cvec_t.T,
        full_in,
        full_out,
    )


def solution(mesh):
    replicas, shards = mesh.shape["rep"], mesh.shape["fsdp"]
    split = P(("rep", "fsdp"), None)
    matrix = P("fsdp", None)
    cube = P("fsdp", None, None)
    in_specs = (split,) * 6 + (matrix, matrix, P("fsdp"), P("fsdp")) + (matrix,) * 4 + (cube, cube)
    out_specs = (split, split, matrix, matrix, P("fsdp"), P("fsdp")) + (matrix,) * 4 + (cube, cube)
    return jax.shard_map(
        partial(body, replicas, shards),
        mesh=mesh,
        in_specs=in_specs,
        out_specs=out_specs,
        check_vma=False,
    )
```

```python
from functools import partial
import math

import jax
import jax.numpy as jnp
from jax import lax
from jax.experimental import pallas as pl
from jax.experimental.pallas import tpu as pltpu
from jax.sharding import PartitionSpec as P

D = 768
HEADS = 12
HDIM = 64
EXPERTS = 4
NCH = 8
CAP = 384
LANES = 128
QB = 256
REACH = 512
VMEM_BYTES = 58 * 1024 * 1024
EPS = 1e-06
COST_SCALE = 0.02
ATT = 100
BACK = 400
f32 = jnp.float32
bf16 = jnp.bfloat16

NT = (((1,), (1,)), ((), ()))
TN = (((0,), (0,)), ((), ()))


def mm(a, b):
    return jnp.dot(a, b, preferred_element_type=f32)


def mm_nt(a, b):
    return lax.dot_general(a, b, NT, preferred_element_type=f32)


def mm_tn(a, b):
    return lax.dot_general(a, b, TN, preferred_element_type=f32)


def params(steps=1):
    return pltpu.CompilerParams(
        dimension_semantics=("arbitrary",) * steps, vmem_limit_bytes=VMEM_BYTES
    )


def cost(flops, nbytes):
    return pl.CostEstimate(
        flops=int(flops * COST_SCALE), bytes_accessed=int(nbytes * COST_SCALE), transcendentals=0
    )


def launch(kernel, operands, in_specs, out_specs, out_shape, after=(), **kw):
    n, skip = len(operands), len(after)

    def run(*refs):
        kernel(*refs[:n], *refs[n + skip :])

    kw.setdefault("compiler_params", pltpu.CompilerParams(vmem_limit_bytes=VMEM_BYTES))
    return pl.pallas_call(
        run,
        in_specs=list(in_specs) + [pl.BlockSpec(memory_space=pl.ANY)] * skip,
        out_specs=out_specs,
        out_shape=out_shape,
        **kw,
    )(*operands, *after)


def tie(value, *others):
    return lax.optimization_barrier((value, others))[0]


VM = pl.BlockSpec(memory_space=pltpu.VMEM)
SMEM = pl.BlockSpec(memory_space=pltpu.SMEM)
CVEC, GAIN_A, GAIN_F = NCH + 4, NCH + 6, NCH + 7


def row_of(ref, row):
    return ref[:16, :].astype(f32)[row : row + 1]


def whole(shape):
    return pl.BlockSpec(shape, lambda *_: (0,) * len(shape), pipeline_mode=pl.Buffered(1))


def rows_of(block, width):
    return pl.BlockSpec((block, width), lambda i: (i, 0))


def swap_halves(v):
    lane = lax.broadcasted_iota(jnp.int32, v.shape, 1)
    half = HDIM // 2
    ahead = pltpu.roll(v, LANES - half, 1)
    behind = pltpu.roll(v, half, 1)
    return jnp.where(lane % HDIM < half, ahead, behind)


def lay_columns(full_ref, pieces, part):
    width = pieces[0].shape[1]
    for p in range(len(pieces)):
        chosen = pieces[0][...]
        for m in range(1, len(pieces)):
            chosen = jnp.where(part == (p ^ m), pieces[m][...], chosen)
        full_ref[:, p * width : (p + 1) * width] = chosen


def qkv_kernel(count, part_ref, x_ref, small_ref, cos_ref, sin_ref, *refs):
    pieces = refs[:count]
    h_ref, q_ref, k_ref, v_ref, w_ref = refs[count:]

    @pl.when(pl.program_id(0) == 0)
    def _():
        lay_columns(w_ref, pieces, part_ref[0])

    x = x_ref[...].astype(f32)
    inverse = lax.rsqrt(jnp.mean(x * x, axis=-1, keepdims=True) + EPS)
    h = (x * inverse * row_of(small_ref, GAIN_A)).astype(bf16)
    h_ref[...] = h
    cosine, sine = cos_ref[...], sin_ref[...]
    mixed = mm(h, w_ref[...])
    for out_ref, base, scale in ((q_ref, 0, HDIM**-0.5), (k_ref, D, 1.0)):
        for c in range(0, D, LANES):
            v = mixed[:, base + c : base + c + LANES]
            turned = v * cosine + swap_halves(v) * sine
            out_ref[:, c : c + LANES] = (turned.astype(bf16).astype(f32) * scale).astype(bf16)
    v_ref[...] = mixed[:, 2 * D :].astype(bf16)


def qkv_call(part, x, small, cosine, sine, pieces, after):
    rows = x.shape[0]
    block = 256
    wide = jax.ShapeDtypeStruct((rows, D), bf16)
    return launch(
        partial(qkv_kernel, len(pieces)),
        [part, x, small, cosine, sine, *pieces],
        [
            SMEM,
            rows_of(block, D),
            whole(small.shape),
            rows_of(block, LANES),
            rows_of(block, LANES),
        ]
        + [whole(p.shape) for p in pieces],
        [rows_of(block, D)] * 4,
        [wide] * 4,
        after,
        grid=(rows // block,),
        scratch_shapes=[pltpu.VMEM((D, 3 * D), bf16)],
        compiler_params=params(),
        cost_estimate=cost(2 * rows * D * 3 * D, 2 * (5 * rows * D + 3 * D * D)),
        name="qkv_rope",
    )


PAD_LANE = 6


def fill_masks(query_mask, key_mask, key_mask_own, table, dcol_ref, vcol_ref):
    length = dcol_ref.shape[0]
    lane = lax.broadcasted_iota(jnp.int32, (length, LANES), 1) % HDIM
    docs = dcol_ref[...]
    query_mask[...] = jnp.where((lane == docs) | (lane == PAD_LANE), 1.0, 0.0).astype(bf16)
    other = jnp.where((lane < PAD_LANE) & (lane != docs), -1e30, 0.0)
    key_mask_own[...] = other.astype(bf16)
    padded = (lane == PAD_LANE) & (vcol_ref[...] == 0)
    key_mask[...] = jnp.where(padded, -1e30, other).astype(bf16)
    key = lax.broadcasted_iota(jnp.int32, (QB, QB), 0)
    query = lax.broadcasted_iota(jnp.int32, (QB, QB), 1)
    for i in range(length // QB):
        usable = (vcol_ref[i * QB : (i + 1) * QB, :] > 0) | (key == query)
        table[i] = jnp.where((key <= query) & usable, 0.0, -1e30)


def mask_scratch(length):
    return [pltpu.VMEM((length, LANES), bf16)] * 3 + [pltpu.VMEM((length // QB, QB, QB), f32)]


def per_head(inside, outside):
    lane = lax.broadcasted_iota(jnp.int32, inside.shape, 1)
    return [jnp.where(lane // HDIM == head, inside, outside) for head in range(2)]


def key_blocks(i):
    start = i * QB
    return [start] + list(range(max(0, start - REACH), start, QB))


def attend_kernel(
    q_ref, k_ref, v_ref, dcol_ref, vcol_ref, ctx_ref, lse_ref, q_mask, k_mask, k_own, table
):
    length = q_ref.shape[0]

    @pl.when(pl.program_id(0) == 0)
    def _():
        fill_masks(q_mask, k_mask, k_own, table, dcol_ref, vcol_ref)

    values_t = v_ref[...].astype(f32).T.astype(bf16)
    queries = per_head(q_ref[...], q_mask[...])
    keys = per_head(k_ref[...], k_mask[...])
    own_keys = per_head(k_ref[...], k_own[...])

    def scores_of(i, head):
        start = i * QB
        query = queries[head][start : start + QB]
        scores = [mm_nt(own_keys[head][start : start + QB], query) + table[i]]
        for at in key_blocks(i)[1:]:
            scores.append(mm_nt(keys[head][at : at + QB], query))
        return scores

    def weights_of(i, head, scores):
        largest = scores[0]
        for block in scores[1:]:
            largest = jnp.maximum(largest, block)
        largest = jnp.max(largest, axis=0, keepdims=True)
        raised = [jnp.exp(block - largest) for block in scores]
        total = raised[0]
        for block in raised[1:]:
            total = total + block
        total = jnp.sum(total, axis=0, keepdims=True)
        lse_ref[0, head : head + 1, i * QB : (i + 1) * QB] = largest + jnp.log(total)
        return [block.astype(bf16) for block in raised], total

    def context_of(i, head, raised, total):
        context = 0.0
        for at, block in zip(key_blocks(i), raised, strict=True):
            context = context + mm(
                values_t[head * HDIM : (head + 1) * HDIM, at : at + QB], block
            )
        return context * (1.0 / total)

    units = [(i, head) for i in range(length // QB) for head in range(2)]
    ahead = scores_of(*units[0])
    behind, contexts = None, []
    for index in range(len(units) + 1):
        scores = ahead
        if index + 1 < len(units):
            ahead = scores_of(*units[index + 1])
        made = None
        if index < len(units):
            made = (*units[index], *weights_of(*units[index], scores))
        if behind is not None:
            contexts.append(context_of(*behind))
            if len(contexts) == 2:
                i = behind[0]
                ctx_ref[i * QB : (i + 1) * QB, :] = (
                    jnp.concatenate(contexts, axis=0).T.astype(bf16)
                )
                contexts = []
        behind = made


def attend_call(q, k, v, dcol, vcol):
    length = q.shape[0]
    pairs = HEADS // 2
    column = pl.BlockSpec((length, LANES), lambda p: (0, p))
    return launch(
        attend_kernel,
        [q, k, v, dcol, vcol],
        [column, column, column, whole(dcol.shape), whole(vcol.shape)],
        [column, pl.BlockSpec((1, 2, length), lambda p: (p, 0, 0))],
        [
            jax.ShapeDtypeStruct((length, D), bf16),
            jax.ShapeDtypeStruct((pairs, 2, length), f32),
        ],
        grid=(pairs,),
        scratch_shapes=mask_scratch(length),
        compiler_params=params(),
        cost_estimate=cost(ATT * 20e9, ATT * 8 * length * D),
        name="attend",
    )


def attend_back_kernel(
    q_ref,
    k_ref,
    v_ref,
    g_ref,
    lse_ref,
    dcol_ref,
    vcol_ref,
    cos_ref,
    sin_ref,
    dq_ref,
    dk_ref,
    dv_ref,
    q_mask,
    k_mask,
    k_own,
    table,
    gk_ref,
    gv_ref,
    gq_ref,
):
    length = q_ref.shape[0]

    @pl.when(pl.program_id(0) == 0)
    def _():
        fill_masks(q_mask, k_mask, k_own, table, dcol_ref, vcol_ref)

    keys_t = k_ref[...].astype(f32).T.astype(bf16)
    zero = jnp.zeros(q_ref.shape, bf16)
    queries = per_head(q_ref[...], q_mask[...])
    bare = per_head(q_ref[...], zero)
    grads = per_head(g_ref[...], zero)
    keys = per_head(k_ref[...], k_mask[...])
    own_keys = per_head(k_ref[...], k_own[...])
    begun = set()

    def products_of(i, head):
        start = i * QB
        query = queries[head][start : start + QB]
        grad = grads[head][start : start + QB]
        scores, grad_probs = [], []
        for at in key_blocks(i):
            if at == start:
                scores.append(mm_nt(own_keys[head][at : at + QB], query) + table[i])
            else:
                scores.append(mm_nt(keys[head][at : at + QB], query))
            grad_probs.append(mm_nt(v_ref[at : at + QB, :], grad))
        return scores, grad_probs

    def softmax_back(i, head, scores, grad_probs):
        lse = lse_ref[0, head : head + 1, i * QB : (i + 1) * QB]
        probs = [jnp.exp(block - lse) for block in scores]
        inner = probs[0] * grad_probs[0]
        for p, d in zip(probs[1:], grad_probs[1:], strict=True):
            inner = inner + p * d
        inner = jnp.sum(inner, axis=0, keepdims=True)
        grad_scores = [
            (p * (d - inner)).astype(bf16) for p, d in zip(probs, grad_probs, strict=True)
        ]
        return [p.astype(bf16) for p in probs], grad_scores

    def spread_back(i, head, probs, grad_scores):
        start = i * QB
        grad_q = 0.0
        for at, p, s in zip(key_blocks(i), probs, grad_scores, strict=True):
            grad_v = mm(p, grads[head][start : start + QB])
            grad_k = mm(s, bare[head][start : start + QB])
            if at in begun:
                gv_ref[at : at + QB, :] += grad_v
                gk_ref[at : at + QB, :] += grad_k
            else:
                begun.add(at)
                gv_ref[at : at + QB, :] = grad_v
                gk_ref[at : at + QB, :] = grad_k
            grad_q = grad_q + mm(keys_t[head * HDIM : (head + 1) * HDIM, at : at + QB], s)
        gq_ref[head * HDIM : (head + 1) * HDIM, start : start + QB] = grad_q

    units = [(i, head) for i in range(length // QB) for head in range(2)]
    ahead = products_of(*units[0])
    behind = None
    for index in range(len(units) + 1):
        products = ahead
        if index + 1 < len(units):
            ahead = products_of(*units[index + 1])
        made = None
        if index < len(units):
            made = (*units[index], *softmax_back(*units[index], *products))
        if behind is not None:
            spread_back(*behind)
        behind = made
    cosine, sine = cos_ref[...], sin_ref[...]
    grad_q = gq_ref[...].T * HDIM**-0.5
    grad_k = gk_ref[...]
    dq_ref[...] = (grad_q * cosine - swap_halves(grad_q) * sine).astype(bf16)
    dk_ref[...] = (grad_k * cosine - swap_halves(grad_k) * sine).astype(bf16)
    dv_ref[...] = gv_ref[...].astype(bf16)


def attend_back_call(q, k, v, g, lse, dcol, vcol, cosine, sine):
    length = q.shape[0]
    pairs = HEADS // 2
    column = pl.BlockSpec((length, LANES), lambda p: (0, p))
    return launch(
        attend_back_kernel,
        [q, k, v, g, lse, dcol, vcol, cosine, sine],
        [column] * 4
        + [pl.BlockSpec((1, 2, length), lambda p: (p, 0, 0))]
        + [whole(a.shape) for a in (dcol, vcol, cosine, sine)],
        [column] * 3,
        [jax.ShapeDtypeStruct((length, D), bf16)] * 3,
        grid=(pairs,),
        scratch_shapes=mask_scratch(length)
        + [
            pltpu.VMEM((length, LANES), f32),
            pltpu.VMEM((length, LANES), f32),
            pltpu.VMEM((LANES, length), f32),
        ],
        compiler_params=params(),
        cost_estimate=cost(45e9, 14 * length * D),
        name="attend_back",
    )


def cut_dense_kernel(quarter, widths, who_ref, qkv_ref, proj_ref, *refs):
    smalls, out_ref, mark_ref = refs[:-2], refs[-2], refs[-1]
    mark_ref[...] = qkv_ref[:16, :LANES]
    row = pl.multiple_of(who_ref[0] * quarter, quarter)
    start = 0
    for ref, width in zip((qkv_ref, proj_ref), widths, strict=True):
        column = pl.multiple_of(who_ref[1] * width, LANES)
        out_ref[:quarter, start : start + width] = ref[pl.ds(row, quarter), pl.ds(column, width)]
        start += width
    shard = qkv_ref.shape[0]
    out_ref[quarter:, :] = jnp.zeros((16, start), bf16)
    rows = jnp.concatenate([ref[...].astype(f32) for ref in smalls[:-1]], axis=0)
    out_ref[quarter:, :shard] = rows.astype(bf16)
    prev = smalls[-1]
    out_ref[quarter : quarter + prev.shape[0], 2 * LANES : 2 * LANES + NCH] = prev[...]


def cut_dense(who, qkv, proj, smalls, copies):
    shard = qkv.shape[0]
    quarter = shard // EXPERTS
    widths = (qkv.shape[1] // copies, proj.shape[1] // copies)
    total = sum(widths)
    if quarter % 16 == 0 and all(w % LANES == 0 for w in widths):
        return launch(
            partial(cut_dense_kernel, quarter, widths),
            [who, qkv, proj, *smalls],
            [SMEM] + [VM] * (2 + len(smalls)),
            [VM, VM],
            [
                jax.ShapeDtypeStruct((quarter + 16, total), bf16),
                jax.ShapeDtypeStruct((16, LANES), bf16),
            ],
            name="cut_dense",
        )
    row = who[0] * quarter
    cuts = [
        lax.dynamic_slice(w, (row, who[1] * width), (quarter, width))
        for w, width in zip((qkv, proj), widths, strict=True)
    ]
    prev = smalls[-1]
    below = jnp.concatenate(
        [
            jnp.pad(jnp.concatenate(smalls[:-1]), ((0, 0), (0, 2 * LANES - shard))),
            jnp.pad(prev, ((0, 16 - prev.shape[0]), (0, total - 2 * LANES - NCH))),
        ],
        axis=1,
    )
    piece = jnp.concatenate([jnp.concatenate(cuts, axis=1), below])
    return piece, piece[:16, :LANES]


def lay_shards_kernel(count, shard, quarter, width, zi_ref, *refs):
    pieces = refs[:count]
    qkv_ref, proj_ref, small_ref, prev_ref = refs[count:]
    for k in range(count):
        at = lax.rem(zi_ref[0] + count - k, count)
        qkv_ref[at] = pieces[k][:quarter, :width]
        proj_ref[at] = pieces[k][:quarter, width:]
        prev_ref[at] = pieces[k][quarter:, 2 * LANES : 3 * LANES]
    small_ref[16:, :] = jnp.zeros((LANES - 16, D), bf16)
    for z in range(count):
        chosen = pieces[0][quarter:, : 2 * LANES].astype(f32)
        for k in range(1, count):
            here = lax.rem(zi_ref[0] + count - k, count) == z
            chosen = jnp.where(here, pieces[k][quarter:, : 2 * LANES].astype(f32), chosen)
        small_ref[:16, z * shard : (z + 1) * shard] = chosen[:, :shard].astype(bf16)


def lay_shards(zi, pieces, shard, quarter, width, after):
    count = len(pieces)
    return launch(
        partial(lay_shards_kernel, count, shard, quarter, width),
        [zi, *pieces],
        [SMEM] + [VM] * count,
        [VM] * 4,
        [
            jax.ShapeDtypeStruct((count, quarter, width), bf16),
            jax.ShapeDtypeStruct((count, quarter, pieces[0].shape[1] - width), bf16),
            jax.ShapeDtypeStruct((LANES, D), bf16),
            jax.ShapeDtypeStruct((count, 16, LANES), bf16),
        ],
        after,
        name="lay_shards",
    )


def lay_xor_kernel(count, own_ref, *refs):
    pieces, out = refs[:count], refs[count]
    for k in range(count):
        out[:, own_ref[0] ^ k] = pieces[k][...]


def lay_xor(own, pieces, after=()):
    count = len(pieces)
    first, rows, columns = pieces[0].shape
    return launch(
        partial(lay_xor_kernel, count),
        [own, *pieces],
        [SMEM] + [VM] * count,
        VM,
        jax.ShapeDtypeStruct((first, count, rows, columns), bf16),
        after,
        name="lay_xor",
    )


def lanes_of(shape):
    return lax.broadcasted_iota(jnp.int32, shape, 1)


def partner(v, lane):
    return jnp.where(lane % 2 == 0, pltpu.roll(v, LANES - 1, 1), pltpu.roll(v, 1, 1))


def selected(choice_ref, lane):
    return (lane == choice_ref[:, 0:1]) | (lane == choice_ref[:, 1:2])


def after_kernel(
    count, part_ref, ctx_ref, x_ref, wsmall_ref, prev_ref, pmix_ref, choice_ref, *refs
):
    pieces = refs[:count]
    res_ref, h_ref, one_ref, gate_ref, w_ref = refs[count:]

    @pl.when(pl.program_id(0) == 0)
    def _():
        lay_columns(w_ref, pieces, part_ref[0])

    res = x_ref[...].astype(f32) + mm(ctx_ref[...], w_ref[...])
    res_ref[...] = res
    inverse = lax.rsqrt(jnp.mean(res * res, axis=-1, keepdims=True) + EPS)
    low = (res * inverse * row_of(wsmall_ref, GAIN_F)).astype(bf16)
    h_ref[...] = low
    small = mm_nt(low, wsmall_ref[...])
    logits = small + mm_tn(prev_ref[...], pmix_ref[...])
    lane = lanes_of(small.shape)
    choice = lane < NCH
    top = jnp.max(jnp.where(choice, logits, -1e30), axis=-1, keepdims=True)
    raised = jnp.where(choice, jnp.exp(jnp.where(choice, logits - top, 0.0)), 0.0)
    gates = raised / jnp.sum(raised, axis=-1, keepdims=True)
    mixing = 1.0 / (1.0 + jnp.exp(partner(small, lane) - small))
    is_mix = (lane >= NCH) & (lane < NCH + 4)
    one_ref[...] = jnp.where(choice, gates, jnp.where(is_mix, mixing, 0.0))
    taken = jnp.where(selected(choice_ref, lane), gates, 0.0).T[:NCH]
    high = taken.astype(bf16).astype(f32)
    gate_ref[...] = jnp.concatenate([high, taken - high], axis=0).astype(bf16)


def after_call(part, ctx, x, small, prev, pmix, choices, pieces):
    rows = x.shape[0]
    block = 256
    return launch(
        partial(after_kernel, len(pieces)),
        [part, ctx, x, small, prev, pmix, choices, *pieces],
        [SMEM]
        + [rows_of(block, D)] * 2
        + [
            whole(small.shape),
            pl.BlockSpec((NCH, block), lambda i: (0, i)),
            whole(pmix.shape),
            rows_of(block, 2),
        ]
        + [whole(p.shape) for p in pieces],
        [rows_of(block, D)] * 2
        + [rows_of(block, LANES), pl.BlockSpec((2 * NCH, block), lambda i: (0, i))],
        [
            jax.ShapeDtypeStruct((rows, D), f32),
            jax.ShapeDtypeStruct((rows, D), bf16),
            jax.ShapeDtypeStruct((rows, LANES), f32),
            jax.ShapeDtypeStruct((2 * NCH, rows), bf16),
        ],
        grid=(rows // block,),
        scratch_shapes=[pltpu.VMEM((D, D), bf16)],
        compiler_params=params(),
        cost_estimate=cost(2 * rows * D * D, 10 * rows * D),
        name="after_attention",
    )


EXTRA = 16
COEF, INVERSE = 16, 17


def dispatch_kernel(gated, mine_ref, spot_ref, v_ref, *refs):
    if gated:
        gate_ref, refs = refs[0], refs[1:]
    rows = v_ref.shape[0]
    slot = lax.broadcasted_iota(jnp.int32, (CAP, rows), 0)
    for k in range(EXPERTS):
        hits = jnp.where(slot == spot_ref[k : k + 1, :], 1.0, 0.0).astype(bf16)
        refs[k][:CAP, :] = mm(hits, v_ref[...]).astype(bf16)
        if gated:
            moved = mm_nt(gate_ref[...], hits)
            row = lax.broadcasted_iota(jnp.int32, moved.shape, 0) % NCH
            moved = jnp.where(row == (mine_ref[0] ^ k), moved, 0.0)
            high = jnp.sum(moved[:NCH], axis=0, keepdims=True)
            rest = jnp.sum(moved[NCH:], axis=0, keepdims=True)
            tail = jnp.concatenate(
                [high, rest, jnp.zeros((EXTRA - 2, CAP), f32)], axis=0
            ).astype(bf16)
            refs[k][CAP:, :CAP] = tail
            refs[k][CAP:, CAP:] = jnp.zeros((EXTRA, D - CAP), bf16)


def dispatch_call(mine, spot, values, gates=None, after=()):
    size = CAP + (0 if gates is None else EXTRA)
    operands = [mine, spot, values] + ([] if gates is None else [gates])
    rows = values.shape[0]
    return launch(
        partial(dispatch_kernel, gates is not None),
        operands,
        [SMEM] + [VM] * (len(operands) - 1),
        [VM] * EXPERTS,
        [jax.ShapeDtypeStruct((size, D), bf16)] * EXPERTS,
        after,
        cost_estimate=cost(2 * rows * D * CAP * EXPERTS, 2 * rows * D + 2 * EXPERTS * CAP * D),
        name="dispatch",
    )


class Plan:
    def __init__(self, replicas, shards, shard, hidden, chunks):
        self.copies = replicas // EXPERTS
        self.shards = shards
        self.shard = shard
        self.hidden = hidden
        self.chunks = chunks
        self.seg = hidden // (shards * self.copies * chunks)
        self.width = self.seg * shards
        self.wide = min(256, self.width)
        self.tiles = self.width // self.wide
        self.spans = self.wide // self.seg
        self.downs = D // self.wide
        self.rows = 2 * self.tiles * shard + self.downs * self.seg

    def column(self, half, tile, span, part, chunk):
        z = tile * self.spans + span
        base = half * self.hidden + z * (self.hidden // self.shards)
        return base + (chunk * self.copies + part) * self.seg

    def down_row(self, part, chunk):
        return (chunk * self.copies + part) * self.seg


def pack_kernel(plan, who_ref, in_ref, out_ref, pack):
    mine, part = who_ref[0], who_ref[1]
    seg, shard = plan.seg, plan.shard
    step = pl.program_id(0)
    half, z = step // plan.shards, step % plan.shards
    row = pl.multiple_of((half * plan.tiles + z // plan.spans) * shard, shard)
    column = pl.multiple_of(z % plan.spans * seg, seg)
    for e in range(EXPERTS):

        @pl.when(mine == e)
        def _(e=e):
            value = in_ref[:, e, :]
            for chunk in range(plan.chunks):
                at = chunk * plan.copies * seg
                piece = value[:, at : at + seg]
                for p in range(1, plan.copies):
                    at = (chunk * plan.copies + p) * seg
                    piece = jnp.where(part == p, value[:, at : at + seg], piece)
                at = pl.multiple_of(chunk * plan.rows + row, 16)
                pack[pl.ds(at, shard), pl.ds(column, seg)] = piece

        @pl.when((mine == e) & (step == 0))
        def _(e=e):
            for chunk in range(plan.chunks):
                start = chunk * plan.rows + 2 * plan.tiles * shard
                at = pl.multiple_of(plan.down_row(part, chunk), seg)
                value = out_ref[pl.ds(at, seg), e, :]
                for down in range(plan.downs):
                    pack[start + down * seg : start + (down + 1) * seg, :] = value[
                        :, down * plan.wide : (down + 1) * plan.wide
                    ]


def pack_pieces(plan, who, expert_in, expert_out, after):
    if plan.seg % LANES == 0:
        per = plan.hidden // plan.shards
        return launch(
            partial(pack_kernel, plan),
            [who, expert_in, expert_out],
            [
                SMEM,
                pl.BlockSpec((plan.shard, EXPERTS, per), lambda i: (0, 0, i)),
                whole(expert_out.shape),
            ],
            whole((plan.chunks * plan.rows, plan.wide)),
            jax.ShapeDtypeStruct((plan.chunks * plan.rows, plan.wide), bf16),
            after,
            grid=(2 * plan.shards,),
            compiler_params=params(),
            cost_estimate=cost(0, 0),
            name="pack",
        )
    mine, part = who[0], who[1:]
    own_in = lax.dynamic_index_in_dim(expert_in, mine, 1, keepdims=False)
    own_out = lax.dynamic_index_in_dim(expert_out, mine, 1, keepdims=False)
    packs = []
    for chunk in range(plan.chunks):
        blocks = []
        for half in range(2):
            for tile in range(plan.tiles):
                spans = [
                    lax.dynamic_slice_in_dim(
                        own_in, plan.column(half, tile, span, part[0], chunk), plan.seg, 1
                    )
                    for span in range(plan.spans)
                ]
                blocks.append(jnp.concatenate(spans, axis=1))
        rows = lax.dynamic_slice_in_dim(own_out, plan.down_row(part[0], chunk), plan.seg, 0)
        blocks += [rows[:, d * plan.wide : (d + 1) * plan.wide] for d in range(plan.downs)]
        packs.append(jnp.concatenate(blocks, axis=0))
    return jnp.concatenate(packs, axis=0)


def unpack_kernel(plan, begun, who_ref, *refs):
    copies, seg = plan.copies, plan.seg
    ins, downs = refs[:copies], refs[copies : 2 * copies]
    in_out, down_out = refs[2 * copies + 2 * begun :]
    mine, part = who_ref[0], who_ref[1]
    step = pl.program_id(0)
    z = step % plan.shards

    def of_replica(arrays, p, index):
        chosen = arrays[0][index].astype(f32)
        for m in range(1, copies):
            chosen = jnp.where(part == (p ^ m), arrays[m][index].astype(f32), chosen)
        return chosen

    for j in range(EXPERTS):
        for p in range(copies):
            chosen = of_replica(ins, p, j ^ mine)
            piece = chosen[:, :seg]
            for span in range(1, plan.spans):
                here = z % plan.spans == span
                piece = jnp.where(here, chosen[:, span * seg : (span + 1) * seg], piece)
            in_out[:, j, p * seg : (p + 1) * seg] = piece

    @pl.when(step == 0)
    def _():
        for j in range(EXPERTS):
            for p in range(copies):
                chosen = of_replica(downs, p, j ^ mine)
                for down in range(plan.downs):
                    down_out[
                        p * seg : (p + 1) * seg, j, down * plan.wide : (down + 1) * plan.wide
                    ] = chosen[down * seg : (down + 1) * seg]


def unpack_chunk(plan, who, chunk, sums, begun):
    copies, shards = plan.copies, plan.shards
    per = plan.hidden // shards
    start = 2 * plan.tiles * plan.shard
    down_rows = plan.downs * plan.seg
    both = copies * plan.seg

    def in_block(i):
        return (0, i // shards * plan.tiles + i % shards // plan.spans, 0)

    down_in = pl.BlockSpec(
        (EXPERTS, down_rows, plan.wide),
        lambda i: (0, start // down_rows, 0),
        pipeline_mode=pl.Buffered(1),
    )
    hbm = pl.BlockSpec(memory_space=pl.ANY)
    operands = [who, *sums, *sums, *begun]
    return launch(
        partial(unpack_kernel, plan, len(begun) // 2),
        operands,
        [SMEM]
        + [pl.BlockSpec((EXPERTS, plan.shard, plan.wide), in_block)] * copies
        + [down_in] * copies
        + [hbm] * len(begun),
        [
            pl.BlockSpec((plan.shard, EXPERTS, both), lambda i: (0, 0, i * plan.chunks + chunk)),
            pl.BlockSpec((both, EXPERTS, D), lambda i: (chunk, 0, 0)),
        ],
        [
            jax.ShapeDtypeStruct((plan.shard, EXPERTS, 2 * plan.hidden), f32),
            jax.ShapeDtypeStruct((per, EXPERTS, D), f32),
        ],
        grid=(2 * shards,),
        input_output_aliases={len(operands) - 2 + i: i for i in range(len(begun))},
        compiler_params=params(),
        cost_estimate=cost(0, 12 * plan.shard * plan.hidden * EXPERTS),
        name="unpack",
    )


def unpack_grads(plan, who, sums, begun):
    if begun:
        for chunk in range(1, plan.chunks):
            begun = unpack_chunk(plan, who, chunk, sums[chunk], begun)
        return begun
    mine, part = who[0], who[1]
    ins, outs = [], []
    for j in range(EXPERTS):
        columns = {}
        rows = []
        for chunk in range(plan.chunks):
            for p in range(plan.copies):
                stacked = jnp.stack(sums[chunk])
                piece = lax.dynamic_index_in_dim(stacked, part ^ p, 0, keepdims=False)
                piece = lax.dynamic_index_in_dim(piece, mine ^ j, 0, keepdims=False)
                for half in range(2):
                    for tile in range(plan.tiles):
                        row = (half * plan.tiles + tile) * plan.shard
                        for span in range(plan.spans):
                            columns[plan.column(half, tile, span, p, chunk)] = piece[
                                row : row + plan.shard, span * plan.seg : (span + 1) * plan.seg
                            ]
                row = 2 * plan.tiles * plan.shard
                rows.append(
                    jnp.concatenate(
                        [
                            piece[row + d * plan.seg : row + (d + 1) * plan.seg]
                            for d in range(plan.downs)
                        ],
                        axis=1,
                    )
                )
        ins.append(jnp.concatenate([columns[c] for c in sorted(columns)], axis=1))
        outs.append(jnp.concatenate(rows, axis=0))
    return jnp.stack(ins, axis=1).astype(f32), jnp.stack(outs, axis=1).astype(f32)


def weight_grads(plan, part, xt, ds, act, grad_gate, grad_up, grads):
    shard, seg, wide, tiles = plan.shard, plan.seg, plan.wide, plan.tiles
    for half, source in ((0, grad_gate), (1, grad_up)):
        for tile in range(tiles):
            made = mm(xt[...], source[part, :, tile * wide : (tile + 1) * wide]).astype(bf16)
            row = (half * tiles + tile) * shard
            for z in range(plan.shards):
                grads[part, z, row : row + shard, :] = made[z * shard : (z + 1) * shard, :]
    for tile in range(tiles):
        made = mm_tn(act[part, :, tile * wide : (tile + 1) * wide], ds[...]).astype(bf16)
        for span in range(plan.spans):
            z = tile * plan.spans + span
            for down in range(plan.downs):
                row = 2 * tiles * shard + down * seg
                grads[part, z, row : row + seg, :] = made[
                    span * seg : (span + 1) * seg, down * wide : (down + 1) * wide
                ]


def expert_kernel(plan, first, last, *refs):
    refs = list(refs)

    def take(n):
        out = refs[:n]
        del refs[:n]
        return out

    copies = plan.copies
    x_refs, y_refs = take(EXPERTS), take(EXPERTS)
    w_refs = take(copies)
    if first:
        carry_in = []
    else:
        carry_in = take(2)
        (ds,) = take(1)
    if last:
        dx_outs, ret_outs, saved = take(EXPERTS), take(EXPERTS), take(3)
    else:
        grad_outs, carry_out, saved = take(copies), take(2), take(2)
    xs, gcol, ret_acc, dx_acc, act_s, dg_s, du_s = take(7)
    waiting = [take(3), take(3)]
    if last:
        y_held, sems = refs
    else:
        ds, xt, grads, sems = refs
    shard, seg, wide, tiles = plan.shard, plan.seg, plan.wide, plan.tiles
    started = []

    def copy(src, dst):
        made = pltpu.make_async_copy(src, dst, sems.at[len(started)])
        started.append(made)
        made.start()
        return made

    carries = [copy(src, dst) for src, dst in zip(carry_in, (ret_acc, dx_acc))]
    if last:
        held = [
            copy(y_refs[k].at[pl.ds(0, CAP)], y_held.at[pl.ds(k * CAP, CAP)])
            for k in range(EXPERTS)
        ]
    for k in range(EXPERTS):
        span = slice(k * CAP, (k + 1) * CAP)
        x = x_refs[k][:CAP, :]
        xs[span, :] = x
        extra = x_refs[k][CAP:, :CAP].astype(f32)
        gate = (extra[0:1] + extra[1:2]).T
        gcol[span, :] = jnp.broadcast_to(gate, (CAP, LANES))
        if not last:
            xt[:, span] = x.astype(f32).T.astype(bf16)
            ds[span, :] = (y_refs[k][:CAP, :].astype(f32) * gate).astype(bf16)
    sends = []
    if not last:
        sends = [copy(src, dst) for src, dst in zip((xt, ds), saved, strict=True)]
    if first:
        ret_acc[...] = jnp.zeros_like(ret_acc)
        dx_acc[...] = jnp.zeros_like(dx_acc)

    def columns(part, half, tile):
        row = (half * tiles + tile) * shard
        return w_refs[part][:, row : row + shard, :].reshape(D, wide)

    def down_columns(part, down):
        row = 2 * tiles * shard + down * seg
        return w_refs[part][:, row : row + seg, :].reshape(plan.width, wide)

    def products(part, b, held):
        span = slice(b * CAP, (b + 1) * CAP)
        x, d = xs[span, :], ds[span, :]
        for tile in range(tiles):
            at = slice(tile * wide, (tile + 1) * wide)
            held[0][:, at] = mm(x, columns(part, 0, tile))
            held[1][:, at] = mm(x, columns(part, 1, tile))
        grad = 0.0
        for down in range(plan.downs):
            grad = grad + mm_nt(
                d[:, down * wide : (down + 1) * wide], down_columns(part, down)
            )
        held[2][...] = grad

    def gating(part, b, held):
        span = slice(b * CAP, (b + 1) * CAP)
        gate, up, grad_act = held[0][...], held[1][...], held[2][...]
        sig = 1.0 / (1.0 + jnp.exp(-gate))
        silu = gate * sig
        act_s[part, span, :] = (silu * up).astype(bf16)
        du_s[part, span, :] = (grad_act * silu).astype(bf16)
        dg_s[part, span, :] = (grad_act * up * (sig + silu * (1.0 - sig))).astype(bf16)

    def back(part, b):
        span = slice(b * CAP, (b + 1) * CAP)
        act = act_s[part, span, :]
        for down in range(plan.downs):
            ret_acc[span, down * wide : (down + 1) * wide] += mm(act, down_columns(part, down))
        total = 0.0
        for tile in range(tiles):
            at = slice(tile * wide, (tile + 1) * wide)
            total = total + mm_nt(dg_s[part, span, at], columns(part, 0, tile))
            total = total + mm_nt(du_s[part, span, at], columns(part, 1, tile))
        dx_acc[span, :] += total

    for part in range(copies):
        products(part, 0, waiting[0])
        for b in range(EXPERTS):
            if b + 1 < EXPERTS:
                products(part, b + 1, waiting[(b + 1) % 2])
            gating(part, b, waiting[b % 2])
            if b > 0:
                if part == 0 and b == 1:
                    for made in carries:
                        made.wait()
                back(part, b - 1)
        back(part, EXPERTS - 1)
        if last:
            sends += [
                copy(src.at[part], dst.at[part])
                for src, dst in zip((act_s, dg_s, du_s), saved, strict=True)
            ]
        else:
            if part == copies - 1:
                sends += [
                    copy(src, dst) for src, dst in zip((ret_acc, dx_acc), carry_out, strict=True)
                ]
            weight_grads(plan, part, xt, ds, act_s, dg_s, du_s, grads)
            sends.append(copy(grads.at[part], grad_outs[part]))
    if last:
        for made in held:
            made.wait()
        for k in range(EXPERTS):
            span = slice(k * CAP, (k + 1) * CAP)
            ret = ret_acc[span, :]
            dgate = jnp.sum(ret * y_held[span, :].astype(f32), axis=-1, keepdims=True)
            dgate = jnp.broadcast_to(dgate, (CAP, LANES)).T[:1]
            ret_outs[k][...] = (ret * gcol[span, :1]).astype(bf16)
            dx_outs[k][:CAP, :] = dx_acc[span, :].astype(bf16)
            high = dgate.astype(bf16).astype(f32)
            tail = jnp.concatenate(
                [high, dgate - high, jnp.zeros((EXTRA - 2, CAP), f32)], axis=0
            ).astype(bf16)
            dx_outs[k][CAP:, :CAP] = tail
            dx_outs[k][CAP:, CAP:] = jnp.zeros((EXTRA, D - CAP), bf16)
    for made in sends:
        made.wait()


def expert_call(plan, xs, ys, weights, chunk, carried):
    first, last = chunk == 0, chunk == plan.chunks - 1
    rows = EXPERTS * CAP
    hbm = pl.BlockSpec(memory_space=pl.ANY)
    copies = plan.copies
    block = pl.BlockSpec(
        (plan.shards, plan.rows, plan.wide),
        lambda i: (0, chunk, 0),
        pipeline_mode=pl.Buffered(1),
    )
    in_specs = [whole(a.shape) for a in xs]
    in_specs += [hbm if last else whole(a.shape) for a in ys] + [block] * copies
    operands = list(xs) + list(ys) + list(weights)
    if not first:
        in_specs += [hbm] * 2 + [whole((rows, D))]
        operands += list(carried)
    held = jax.ShapeDtypeStruct((copies, rows, plan.width), bf16)
    if last:
        out_specs = [whole((CAP + EXTRA, D))] * EXPERTS + [whole((CAP, D))] * EXPERTS
        out_shape = [jax.ShapeDtypeStruct((CAP + EXTRA, D), bf16)] * EXPERTS
        out_shape += [jax.ShapeDtypeStruct((CAP, D), bf16)] * EXPERTS
        out_specs += [hbm] * 3
        out_shape += [held] * 3
    else:
        out_specs = [hbm] * (copies + 4)
        out_shape = [jax.ShapeDtypeStruct((plan.shards, plan.rows, plan.wide), bf16)] * copies
        out_shape += [jax.ShapeDtypeStruct((rows, D), f32)] * 2
        out_shape += [
            jax.ShapeDtypeStruct((D, rows), bf16),
            jax.ShapeDtypeStruct((rows, D), bf16),
        ]
    scratch = [
        pltpu.VMEM((rows, D), bf16),
        pltpu.VMEM((rows, LANES), f32),
        pltpu.VMEM((rows, D), f32),
        pltpu.VMEM((rows, D), f32),
    ]
    scratch += [pltpu.VMEM((copies, rows, plan.width), bf16)] * 3
    scratch += [pltpu.VMEM((CAP, plan.width), f32)] * 6
    if last:
        scratch.append(pltpu.VMEM((rows, D), bf16))
    else:
        scratch += [
            pltpu.VMEM((rows, D), bf16),
            pltpu.VMEM((D, rows), bf16),
            pltpu.VMEM((copies, plan.shards, plan.rows, plan.wide), bf16),
        ]
    scratch.append(pltpu.SemaphoreType.DMA((6 + 3 * copies,)))
    return pl.pallas_call(
        partial(expert_kernel, plan, first, last),
        grid=(1,),
        in_specs=in_specs,
        out_specs=out_specs,
        out_shape=out_shape,
        scratch_shapes=scratch,
        compiler_params=params(),
        cost_estimate=cost(
            18 * rows * D * plan.width * copies, 12 * D * plan.width * copies + 12 * rows * D
        ),
        name="experts",
    )(*operands)


def expert_grads_kernel(plan, act, grad_gate, grad_up, xt, ds, *refs):
    outs, (grads, sems) = refs[: plan.copies], refs[plan.copies :]
    sends = []
    for part in range(plan.copies):
        weight_grads(plan, part, xt, ds, act, grad_gate, grad_up, grads)
        sends.append(pltpu.make_async_copy(grads.at[part], outs[part], sems.at[part]))
        sends[-1].start()
    for made in sends:
        made.wait()


def expert_grads(plan, held):
    copies = plan.copies
    packed = (plan.shards, plan.rows, plan.wide)
    return launch(
        partial(expert_grads_kernel, plan),
        list(held),
        [whole(a.shape) for a in held],
        [pl.BlockSpec(memory_space=pl.ANY)] * copies,
        [jax.ShapeDtypeStruct(packed, bf16)] * copies,
        grid=(1,),
        scratch_shapes=[
            pltpu.VMEM((copies, *packed), bf16),
            pltpu.SemaphoreType.DMA((copies,)),
        ],
        compiler_params=params(),
        cost_estimate=cost(0, 0),
        name="expert_grads",
    )


def spots_of(place_ref, rows):
    slot = lax.broadcasted_iota(jnp.int32, (rows, EXPERTS * CAP), 1)
    hit = (slot == place_ref[:, 0:1]) | (slot == place_ref[:, 1:2])
    return jnp.where(hit, 1.0, 0.0).astype(bf16)


def constant_gates(one, chosen, m):
    a0 = one[:, NCH + 2 * m : NCH + 2 * m + 1]
    a1 = one[:, NCH + 2 * m + 1 : NCH + 2 * m + 2]
    gate = chosen[:, EXPERTS + 2 + m : EXPERTS + 3 + m]
    return gate, a0, a1


def side_kernel(
    res_ref, dy_ref, one_ref, place_ref, choice_ref, small_ref, two_ref, spots_ref, cvec_out
):
    @pl.when(pl.program_id(0) == 0)
    def _():
        cvec_out[...] = jnp.zeros_like(cvec_out)

    res = res_ref[...]
    one = one_ref[...]
    lane = lanes_of(one.shape)
    named = selected(choice_ref, lane)
    chosen = jnp.where(named, one, 0.0)
    is_mix = (lane >= NCH) & (lane < NCH + 4)
    spots_ref[...] = spots_of(place_ref, res.shape[0])
    inverse = lax.rsqrt(jnp.mean(res * res, axis=-1, keepdims=True) + EPS)
    dy = dy_ref[...]
    spread = res * inverse * row_of(small_ref, GAIN_F)
    hd = jnp.sum(spread * dy.astype(f32), axis=-1, keepdims=True)
    cd = mm_nt(dy, small_ref[...])
    coef = chosen[:, EXPERTS + 1 : EXPERTS + 2]
    grads = jnp.where(lane == EXPERTS + 1, hd, 0.0)
    made = jnp.zeros_like(one)
    for m in range(2):
        gate, a0, a1 = constant_gates(one, chosen, m)
        dot = cd[:, CVEC + m : CVEC + m + 1]
        coef = coef + gate * a0
        grads = jnp.where(lane == EXPERTS + 2 + m, a0 * hd + a1 * dot, grads)
        grads = jnp.where(lane == NCH + 2 * m, gate * hd, grads)
        grads = jnp.where(lane == NCH + 2 * m + 1, gate * dot, grads)
        made = jnp.where(lane == m, gate * a1, made)
    two = jnp.where(is_mix | named, grads, 0.0)
    two = jnp.where(lane == COEF, coef, two)
    two_ref[...] = jnp.where(lane == INVERSE, inverse, two)
    high = made.astype(bf16)
    rest = (made - high.astype(f32)).astype(bf16)
    cvec_out[...] += mm_tn(high, dy) + mm_tn(rest, dy)


def side_call(res, dy, one, places, choices, small):
    rows = res.shape[0]
    block = 256
    return launch(
        side_kernel,
        [res, dy, one, places, choices, small],
        [rows_of(block, D)] * 2
        + [rows_of(block, LANES)]
        + [rows_of(block, 2)] * 2
        + [whole(small.shape)],
        [rows_of(block, LANES), rows_of(block, EXPERTS * CAP), whole((LANES, D))],
        [
            jax.ShapeDtypeStruct((rows, LANES), f32),
            jax.ShapeDtypeStruct((rows, EXPERTS * CAP), bf16),
            jax.ShapeDtypeStruct((LANES, D), f32),
        ],
        grid=(rows // block,),
        compiler_params=params(),
        cost_estimate=cost(0, 0),
        name="side",
    )


def back_kernel(
    count,
    who_ref,
    res_ref,
    h_ref,
    dy_ref,
    one_ref,
    two_ref,
    spots_ref,
    prev_ref,
    wsmall_ref,
    *refs,
):
    dx_refs, refs = refs[:EXPERTS], refs[EXPERTS:]
    pieces, refs = refs[:count], refs[count:]
    (
        dres_ref,
        branch_ref,
        dctx_ref,
        dsmall_ref,
        gain_out,
        prev_out,
        w_ref,
        dg_ref,
    ) = refs

    @pl.when(pl.program_id(0) == 0)
    def _():
        gain_out[...] = jnp.zeros_like(gain_out)
        prev_out[...] = jnp.zeros_like(prev_out)
        dsmall_ref[...] = jnp.zeros_like(dsmall_ref)
        lay_columns(w_ref, pieces, who_ref[1])
        lane = lanes_of((CAP, LANES))
        for k in range(EXPERTS):
            columns = dx_refs[k][CAP:, :CAP].astype(f32).T
            at = who_ref[0] ^ k
            made = jnp.where(lane == at, columns[:, 0:1], 0.0)
            made = jnp.where(lane == at + 16, columns[:, 1:2], made)
            dg_ref[k * CAP : (k + 1) * CAP, :] = made.astype(bf16)

    res = res_ref[...]
    rows = res.shape[0]
    one = one_ref[...]
    lane = lanes_of(one.shape)
    choice = lane < NCH
    is_mix = (lane >= NCH) & (lane < NCH + 4)
    two = two_ref[...]
    spots = spots_ref[...]
    moved = jnp.zeros(res.shape, f32)
    for k in range(EXPERTS):
        moved = moved + mm(spots[:, k * CAP : (k + 1) * CAP], dx_refs[k][:CAP, :])
    from_experts = mm(spots, dg_ref[...])
    from_experts = from_experts + pltpu.roll(from_experts, LANES - 16, 1)
    coef, inverse = two[:, COEF : COEF + 1], two[:, INVERSE : INVERSE + 1]
    dy = dy_ref[...]
    dyf = dy.astype(f32)
    gain = row_of(wsmall_ref, GAIN_F)
    grads = jnp.where(lane < EXPERTS, from_experts, jnp.where(lane < NCH + 4, two, 0.0))
    weighted = one * grads
    mean_choice = jnp.sum(jnp.where(choice, weighted, 0.0), axis=-1, keepdims=True)
    d_logits = jnp.where(choice, one * (grads - mean_choice), 0.0)
    d_mix = one * (grads - (weighted + partner(weighted, lane)))
    d_small = jnp.where(choice, d_logits, jnp.where(is_mix, d_mix, 0.0))
    low = d_small.astype(bf16)
    spread_grad = moved + mm(low, wsmall_ref[...]) + coef * dyf
    scaled = spread_grad * gain
    mean_dot = jnp.mean(res * scaled, axis=-1, keepdims=True)
    d_res = dyf + inverse * scaled - res * (inverse * inverse * inverse * mean_dot)
    dres_ref[...] = d_res
    gain_out[...] += jnp.sum(spread_grad * res * inverse, axis=0, keepdims=True)
    branch = d_res.astype(bf16)
    branch_ref[...] = branch
    dctx_ref[...] = mm_nt(branch, w_ref[...]).astype(bf16)
    dsmall_ref[...] += mm_tn(low, h_ref[...])
    high = d_logits.astype(bf16)
    rest = (d_logits - high.astype(f32)).astype(bf16)
    prev = prev_ref[...]
    prev_out[...] += mm(prev, high) + mm(prev, rest)


def back_call(who, res, h, dy, one, two, spots, prev, small, dx, pieces, after):
    rows = res.shape[0]
    block = 256
    return launch(
        partial(back_kernel, len(pieces)),
        [who, res, h, dy, one, two, spots, prev, small, *dx, *pieces],
        [SMEM]
        + [rows_of(block, D)] * 3
        + [rows_of(block, LANES)] * 2
        + [rows_of(block, EXPERTS * CAP)]
        + [pl.BlockSpec((NCH, block), lambda i: (0, i))]
        + [whole(a.shape) for a in (small, *dx, *pieces)],
        [rows_of(block, D)] * 3
        + [whole((LANES, D)), whole((1, D)), whole((NCH, LANES))],
        [
            jax.ShapeDtypeStruct((rows, D), f32),
            jax.ShapeDtypeStruct((rows, D), bf16),
            jax.ShapeDtypeStruct((rows, D), bf16),
            jax.ShapeDtypeStruct((LANES, D), f32),
            jax.ShapeDtypeStruct((1, D), f32),
            jax.ShapeDtypeStruct((NCH, LANES), f32),
        ],
        after,
        grid=(rows // block,),
        scratch_shapes=[pltpu.VMEM((D, D), bf16), pltpu.VMEM((EXPERTS * CAP, LANES), bf16)],
        compiler_params=params(),
        cost_estimate=cost(BACK * 2 * rows * D * (D + 2048), BACK * 20 * rows * D),
        name="combine_back",
    )


def finish_kernel(res_ref, one_ref, spots_ref, choice_ref, small_ref, *refs):
    ret_refs, out_ref = refs[:EXPERTS], refs[EXPERTS]
    res = res_ref[...]
    one = one_ref[...]
    lane = lanes_of(one.shape)
    chosen = jnp.where(selected(choice_ref, lane), one, 0.0)
    inverse = lax.rsqrt(jnp.mean(res * res, axis=-1, keepdims=True) + EPS)
    total = res
    coef = chosen[:, EXPERTS + 1 : EXPERTS + 2]
    for m in range(2):
        gate, a0, a1 = constant_gates(one, chosen, m)
        coef = coef + gate * a0
        total = total + (gate * a1) * row_of(small_ref, CVEC + m)
    total = total + (coef * inverse) * res * row_of(small_ref, GAIN_F)
    spots = spots_ref[...]
    for k in range(EXPERTS):
        total = total + mm(spots[:, k * CAP : (k + 1) * CAP], ret_refs[k][...])
    out_ref[...] = total.astype(bf16)


def finish_call(res, one, spots, choices, small, ret, after):
    rows = res.shape[0]
    block = 256
    return launch(
        finish_kernel,
        [res, one, spots, choices, small, *ret],
        [rows_of(block, D), rows_of(block, LANES)]
        + [rows_of(block, EXPERTS * CAP), rows_of(block, 2)]
        + [whole(a.shape) for a in (small, *ret)],
        rows_of(block, D),
        jax.ShapeDtypeStruct((rows, D), bf16),
        after,
        grid=(rows // block,),
        compiler_params=params(),
        cost_estimate=cost(2 * rows * D * 1536, 10 * rows * D),
        name="layer_out",
    )


def turn_kernel(count, *refs):
    for source, out in zip(refs[:count], refs[count:], strict=True):
        out[...] = source[...].astype(f32).T.astype(bf16)


def turn_call(arrays):
    rows, columns = arrays[0].shape
    return launch(
        partial(turn_kernel, len(arrays)),
        arrays,
        [pl.BlockSpec((rows, 256), lambda i: (0, i))] * len(arrays),
        [pl.BlockSpec((256, rows), lambda i: (i, 0))] * len(arrays),
        [jax.ShapeDtypeStruct((columns, rows), bf16)] * len(arrays),
        grid=(columns // 256,),
        compiler_params=params(),
        cost_estimate=cost(0, 0),
        name="turn",
    )


def dense_kernel(copies, each, own, part_ref, mine_ref, ht_ref, ct_ref, *refs):
    rights, refs = refs[:4], refs[4:]
    step = pl.program_id(0)
    if own:
        got, outs, total_ref = refs[: copies - 1], refs[copies - 1 : -1], refs[-1]
    else:
        outs = refs
    per = pl.num_programs(0) if own else pl.num_programs(0) // (copies - 1)
    source = (part_ref[0] if own else (step // per + 1) ^ part_ref[0]) * per + step % per
    for index, right in enumerate(rights):
        left = ct_ref if index == 3 else ht_ref

        @pl.when(source // each == index)
        def _(left=left, right=right):
            made = mm(left[...], right[...])
            if own:
                for ref in got:
                    made = made + ref[...].astype(f32)
                total_ref[...] = made.astype(bf16).reshape(total_ref.shape)
            else:
                for m, out in enumerate(outs):
                    if len(outs) == 1:
                        out[...] = made.astype(bf16)
                    else:

                        @pl.when(step // per == m)
                        def _(out=out):
                            out[...] = made.astype(bf16)

    if own:
        for k, out in enumerate(outs):
            out[...] = total_ref[:, mine_ref[0] ^ k]


def dense_call(copies, shards, part, mine, ht, ct, rights, got=None):
    rows = ht.shape[1]
    cut = 4 * D // copies
    step = D // 2 if cut % D == 0 else cut
    per = cut // step
    each = D // step
    quarter = D // (shards * EXPERTS)
    own = got is not None

    def right_block(index):
        def block(i, part_ref, mine_ref):
            replica = part_ref[0] if own else (i // per + 1) ^ part_ref[0]
            return (0, jnp.clip(replica * per + i % per - each * index, 0, each - 1))

        return block

    def other_block(m):
        return lambda i, *_: (0, jnp.clip(i - m * per, 0, per - 1))

    def fixed(shape):
        return pl.BlockSpec(shape, lambda i, *_: (0, 0), pipeline_mode=pl.Buffered(1))

    in_specs = [fixed(ht.shape), fixed(ct.shape)]
    in_specs += [pl.BlockSpec((rows, step), right_block(index)) for index in range(4)]
    if own:
        in_specs += [pl.BlockSpec((D, step), lambda i, *_: (0, i))] * (copies - 1)
        out_specs = [pl.BlockSpec((shards, quarter, step), lambda i, *_: (0, 0, i))] * EXPERTS
        out_shape = [jax.ShapeDtypeStruct((shards, quarter, cut), bf16)] * EXPERTS
        scratch = [pltpu.VMEM((shards, EXPERTS, quarter, step), bf16)]
    else:
        out_specs = [pl.BlockSpec((D, step), other_block(m)) for m in range(copies - 1)]
        out_shape = [jax.ShapeDtypeStruct((D, cut), bf16)] * (copies - 1)
        scratch = []
    return pl.pallas_call(
        partial(dense_kernel, copies, each, own),
        grid_spec=pltpu.PrefetchScalarGridSpec(
            num_scalar_prefetch=2,
            grid=(per if own else per * (copies - 1),),
            in_specs=in_specs,
            out_specs=out_specs,
            scratch_shapes=scratch,
        ),
        out_shape=out_shape,
        compiler_params=params(),
        cost_estimate=cost(8 * rows * D * D, 12 * rows * D + 8 * D * D),
        name="dense_own" if own else "dense_others",
    )(part, mine, ht, ct, *rights, *(got or ()))


def fold_quarters_kernel(count, zi_ref, small_ref, *refs):
    pieces, outs = refs[:count], refs[count:]
    rows, cut = pieces[0].shape[1:]
    spare = outs[0].shape[0] - rows
    for k, out in enumerate(outs):
        at = lax.rem(zi_ref[0] + k, len(outs))
        total = pieces[0][at].astype(f32)
        for piece in pieces[1:]:
            total = total + piece[at].astype(f32)
        out[:rows, :] = total.astype(bf16)
        for c in range(cut // LANES):
            out[rows:, c * LANES : (c + 1) * LANES] = small_ref[at, c * spare : (c + 1) * spare, :]


def fold_quarters(zi, small, pieces, after=()):
    shards, rows, cut = pieces[0].shape
    spare = D // shards * LANES // cut
    return launch(
        partial(fold_quarters_kernel, len(pieces)),
        [zi, small.reshape(shards, D // shards, LANES), *pieces],
        [SMEM] + [VM] * (len(pieces) + 1),
        [VM] * shards,
        [jax.ShapeDtypeStruct((rows + spare, cut), bf16)] * shards,
        after,
        name="fold_quarters",
    )


def lay_tail_kernel(count, rows, own_ref, *refs):
    pieces, out = refs[:count], refs[count]
    total = pieces[0][rows:, :].astype(f32)
    for k in range(count):
        at = pl.multiple_of((own_ref[0] ^ k) * rows, rows)
        out[pl.ds(at, rows), :] = pieces[k][:rows, :]
        if k:
            total = total + pieces[k][rows:, :].astype(f32)
    out[count * rows :, :] = total.astype(bf16)


def lay_tail(own, pieces, rows, after):
    count = len(pieces)
    size, cut = pieces[0].shape
    return launch(
        partial(lay_tail_kernel, count, rows),
        [own, *pieces],
        [SMEM] + [VM] * count,
        VM,
        jax.ShapeDtypeStruct((count * rows + size - rows, cut), bf16),
        after,
        name="lay_tail",
    )


def fold_copies(pieces):
    total = pieces[0].astype(f32)
    for piece in pieces[1:]:
        total = total + piece.astype(f32)
    return total.astype(bf16)


def fold_shards_kernel(*refs):
    total = refs[0][...].astype(f32)
    for ref in refs[1:-1]:
        total = total + ref[...].astype(f32)
    refs[-1][...] = total.astype(bf16)


def fold_shards(pieces):
    return launch(
        fold_shards_kernel,
        pieces,
        [VM] * len(pieces),
        VM,
        jax.ShapeDtypeStruct(pieces[0].shape, bf16),
        name="fold_shards",
    )


def unpack_dense_kernel(count, rows, part_ref, *refs):
    pieces = refs[:count]
    qkv_ref, proj_ref, router_ref, mix_ref, cvec_ref, gain_a_ref, gain_f_ref, prev_ref = refs[count:-1]
    small_ref = refs[-1]
    cut = pieces[0].shape[1]
    small = pieces[0][rows:, :].astype(f32)
    for piece in pieces[1:]:
        small = small + piece[rows:, :].astype(f32)
    spare = small.shape[0]
    for c in range(cut // LANES):
        small_ref[c * spare : (c + 1) * spare, :] = small[:, c * LANES : (c + 1) * LANES]
    turned = small_ref[...].T
    router_ref[...] = turned[:NCH]
    mix_ref[...] = turned[NCH:CVEC]
    cvec_ref[...] = turned[CVEC:GAIN_A]
    gain_a_ref[...] = turned[GAIN_A:GAIN_F]
    gain_f_ref[...] = turned[GAIN_F : GAIN_F + 1]
    prev_ref[...] = small_ref[: prev_ref.shape[0], 16 : 16 + NCH]
    for p in range(count):
        chosen = pieces[0][:rows, :].astype(f32)
        for m in range(1, count):
            chosen = jnp.where(part_ref[0] == (p ^ m), pieces[m][:rows, :].astype(f32), chosen)
        start = p * cut
        in_qkv = max(0, min(cut, 3 * D - start))
        if in_qkv:
            qkv_ref[:, start : start + in_qkv] = chosen[:, :in_qkv]
        if in_qkv < cut:
            at = start + in_qkv - 3 * D
            proj_ref[:, at : at + cut - in_qkv] = chosen[:, in_qkv:]


def unpack_dense(part, pieces, rows, owned):
    heights = (NCH, 4, 2, 1, 1)
    return launch(
        partial(unpack_dense_kernel, len(pieces), rows),
        [part, *pieces],
        [SMEM] + [VM] * len(pieces),
        [VM] * 8,
        [jax.ShapeDtypeStruct((rows, 3 * D), f32), jax.ShapeDtypeStruct((rows, D), f32)]
        + [jax.ShapeDtypeStruct((height, rows), f32) for height in heights]
        + [jax.ShapeDtypeStruct((owned, NCH), f32)],
        scratch_shapes=[pltpu.VMEM((rows, LANES), f32)],
        name="unpack_dense",
    )


def last_kernel(
    count,
    shards,
    part_ref,
    dq_ref,
    dk_ref,
    dv_ref,
    x_ref,
    dres_ref,
    small_ref,
    dsmall_ref,
    gain_f_ref,
    prev_ref,
    cvec_ref,
    *refs,
):
    pieces = refs[:count]
    out_ref, small_out, w_ref, gain_ref = refs[count:]

    @pl.when(pl.program_id(0) == 0)
    def _():
        gain_ref[...] = jnp.zeros_like(gain_ref)
        lay_columns(w_ref, pieces, part_ref[0])

    grad = mm_nt(dq_ref[...], w_ref[:, :D])
    grad = grad + mm_nt(dk_ref[...], w_ref[:, D : 2 * D])
    grad = grad + mm_nt(dv_ref[...], w_ref[:, 2 * D :])
    x = x_ref[...].astype(f32)
    inverse = lax.rsqrt(jnp.mean(x * x, axis=-1, keepdims=True) + EPS)
    scaled = grad * row_of(small_ref, GAIN_A)
    mean_dot = jnp.mean(x * scaled, axis=-1, keepdims=True)
    d_x = inverse * scaled - x * (inverse * inverse * inverse * mean_dot)
    out_ref[...] = (dres_ref[...] + d_x).astype(bf16)
    gain_ref[...] += jnp.sum(grad * x * inverse, axis=0, keepdims=True)

    @pl.when(pl.program_id(0) == pl.num_programs(0) - 1)
    def _():
        row = lax.broadcasted_iota(jnp.int32, (LANES, D), 0)
        total = jnp.where(row < CVEC, dsmall_ref[...], 0.0)
        for m in range(2):
            total = jnp.where(row == CVEC + m, cvec_ref[m : m + 1, :], total)
        total = jnp.where(row == GAIN_A, gain_ref[...], total)
        total = jnp.where(row == GAIN_F, gain_f_ref[...], total)
        total = total.T
        owned = NCH // shards
        shard = D // shards
        row = lax.broadcasted_iota(jnp.int32, total.shape, 0)
        lane = lanes_of((NCH, LANES))
        prev = pltpu.roll(jnp.where(lane < NCH, prev_ref[...], 0.0), 16, 1)
        for index in range(NCH):
            at = (index // owned) * shard + index % owned
            total = jnp.where(row == at, total + prev[index : index + 1, :], total)
        small_out[...] = total.astype(bf16)


def last_call(part, shards, dq, dk, dv, x, dres, small, smalls, pieces, after):
    rows = x.shape[0]
    block = 256
    return launch(
        partial(last_kernel, len(pieces), shards),
        [part, dq, dk, dv, x, dres, small, *smalls, *pieces],
        [SMEM]
        + [rows_of(block, D)] * 5
        + [whole(a.shape) for a in (small, *smalls, *pieces)],
        [rows_of(block, D), whole((D, LANES))],
        [jax.ShapeDtypeStruct((rows, D), bf16), jax.ShapeDtypeStruct((D, LANES), bf16)],
        after,
        grid=(rows // block,),
        scratch_shapes=[pltpu.VMEM((D, 3 * D), bf16), pltpu.VMEM((1, D), f32)],
        compiler_params=params(),
        cost_estimate=cost(6 * rows * D * D, 14 * rows * D),
        name="input_grad",
    )


def body(
    replicas,
    shards,
    tokens,
    prev_logits,
    out_grad,
    routes,
    doc_ids,
    valid_mask,
    qkv_weight,
    proj_weight,
    gain_attn,
    gain_ffn,
    router,
    const_mix,
    prev_mix,
    const_vec,
    expert_in,
    expert_out,
):
    me = lax.axis_index("rep")
    zi = lax.axis_index("fsdp")
    copies = replicas // EXPERTS
    mine = me // copies
    part = me % copies
    rows = tokens.shape[0]
    shard = qkv_weight.shape[0]
    hidden = expert_in.shape[2] // 2
    quarter = shard // EXPERTS
    plan = Plan(replicas, shards, shard, hidden, 2)
    zi_s = zi.reshape(1).astype(jnp.int32)
    mine_s = mine.reshape(1).astype(jnp.int32)
    part_s = part.reshape(1).astype(jnp.int32)
    who = jnp.concatenate([mine_s, part_s])

    def to_expert(a, k):
        return lax.ppermute(a, "rep", [(i, i ^ (k * copies)) for i in range(replicas)])

    def to_part(a, m):
        return lax.ppermute(a, "rep", [(i, i ^ m) for i in range(replicas)])

    def spin(a, k):
        return lax.ppermute(a, "fsdp", [(i, (i + k) % shards) for i in range(shards)])

    def by_xor(pieces, own, axis):
        size = pieces[0].shape[axis]
        shape = list(pieces[0].shape)
        shape[axis] = size * len(pieces)
        full = jnp.zeros(shape, pieces[0].dtype)
        for k, piece in enumerate(pieces):
            full = lax.dynamic_update_slice_in_dim(full, piece, (own ^ k) * size, axis)
        return full

    width = 3 * D // copies
    owned = prev_mix.shape[0]
    smalls = [router.T, const_mix.T, const_vec.T, jnp.stack([gain_attn, gain_ffn]), prev_mix]
    piece, mark = cut_dense(who, qkv_weight, proj_weight, smalls, copies)
    spun = [piece] + [spin(piece, k) for k in range(1, shards)]

    docs = doc_ids.reshape(-1)
    drow = docs[None, :]
    dcol = docs[:, None]
    vcol = valid_mask.reshape(-1)[:, None]
    first_place = jnp.sum((drow < dcol).astype(jnp.int32), axis=1)
    offset = (jnp.arange(rows, dtype=jnp.int32) - first_place).astype(f32)
    frequency = jnp.exp(
        jnp.arange(HDIM // 2, dtype=f32) * (-2.0 * math.log(10000.0) / HDIM)
    )
    angles = offset[:, None] * frequency[None, :]
    cosine, sine = jnp.cos(angles), jnp.sin(angles)
    cosine = jnp.concatenate([cosine] * 4, axis=1)
    sine = jnp.concatenate([-sine, sine, -sine, sine], axis=1)

    routes_t = routes.T
    chosen = jnp.where(routes_t < EXPERTS, routes_t ^ mine, routes_t)
    kinds = jnp.arange(EXPERTS, dtype=jnp.int32)
    named = jnp.any(chosen[:, None, :] == kinds[None, :, None], axis=0)
    later = jnp.triu(jnp.ones((rows, rows), bf16), 1)
    rank = mm(named.astype(bf16), later).astype(jnp.int32)
    spot = jnp.where(named, rank, CAP)
    hit = chosen[:, None, :] == kinds[None, :, None]
    places = jnp.sum(jnp.where(hit, (kinds[:, None] * CAP + rank)[None], 0), axis=1)
    places = jnp.where(chosen < EXPERTS, places, -1).T

    tables = (cosine, sine, spot, dcol, vcol, places)
    packed = pack_pieces(plan, who, expert_in, expert_out, (to_part(mark, 1),))
    gathered = lax.all_gather(packed, "fsdp", axis=0, tiled=False)
    qkv_part, proj_part, small, prevs = lay_shards(
        zi_s, spun, shard, quarter, width, (packed,)
    )
    pmix = prevs[:, :owned].reshape(NCH, LANES)

    def exchanged(blocks):
        return [blocks[0]] + [to_expert(blocks[k], k) for k in range(1, EXPERTS)]

    def over_parts(half):
        half = half.reshape(D, half.shape[3])
        pieces = [half] + [to_part(half, m) for m in range(1, copies)]
        if half.shape[1] % LANES == 0:
            return pieces
        return [by_xor(pieces, part, 1)]

    qkv_half = lay_xor(
        mine_s, exchanged([qkv_part] * EXPERTS), tables
    )
    qkv_pieces = over_parts(qkv_half)
    part_q = part_s if len(qkv_pieces) == copies else jnp.zeros_like(part_s)
    ys = dispatch_call(mine_s, spot, out_grad, after=(qkv_half,))
    proj_half = lay_xor(mine_s, exchanged([tie(proj_part, qkv_half)] * EXPERTS))

    prev = prev_logits.T
    h1, q, k, v = qkv_call(part_q, tokens, small, cosine, sine, qkv_pieces, (ys[0],))
    q, proj_half = tie((q, proj_half), h1)
    q = tie(q, proj_half)
    proj_pieces = over_parts(proj_half)
    part_p = part_s if len(proj_pieces) == copies else jnp.zeros_like(part_s)
    ys = exchanged(tie(ys, h1))
    ctx, lse = attend_call(q, k, v, dcol, vcol)
    res, h2, one, gates = after_call(
        part_p, ctx, tokens, small, prev, pmix, routes, proj_pieces
    )

    xs = dispatch_call(mine_s, spot, tie(h2, ys), gates)
    gathered = tie(gathered, xs[0])
    weights = [gathered] + [to_part(gathered, m) for m in range(1, copies)]
    h1_t, ctx_t = turn_call([tie(h1, xs[0]), ctx])
    two, spots, cvec_grad = side_call(tie(res, xs[0]), out_grad, one, places, routes, small)
    xs = exchanged(xs)
    weights[0] = tie(weights[0], (h1_t, two))
    carried, turned = None, None
    chunk_grads = []
    for chunk in range(plan.chunks):
        made = expert_call(plan, xs, ys, weights, chunk, carried)
        if chunk < plan.chunks - 1:
            chunk_grads.append(made[:copies])
            carried = [*made[copies : copies + 2], made[copies + 3]]
            turned = made[copies + 2]
    dx, returned = exchanged(made[:EXPERTS]), made[EXPERTS : 2 * EXPERTS]
    chunk_grads.append(expert_grads(plan, [*made[2 * EXPERTS :], turned, carried[2]]))

    chunk_grads = [
        [grads[0]] + [to_part(grads[m], m) for m in range(1, copies)] for grads in chunk_grads
    ]
    total = fold_copies(tie(chunk_grads[0], returned[0]))

    def over_shards(t):
        return lax.psum_scatter(t, "fsdp", scatter_dimension=0, tiled=False)

    who_p = jnp.concatenate([mine_s, part_p])
    dres, branch, dctx, dsmall, gain_f_grad, prev_grad = back_call(
        who_p,
        res,
        h2,
        out_grad,
        one,
        two,
        spots,
        prev,
        small,
        dx,
        proj_pieces,
        (total,),
    )
    summed = [over_shards(total)]
    summed += [over_shards(fold_copies(tie(grads, branch))) for grads in chunk_grads[1:]]
    ret = exchanged(tie(returned, dx))
    first = tie(summed[0], branch)
    spread = [[first] + [to_expert(first, k) for k in range(1, EXPERTS - 1)]]
    dq, dk, dv = attend_back_call(q, k, v, dctx, lse, dcol, vcol, cosine, sine)
    rights = [tie(dq, ret, spread[0]), dk, dv, branch]
    others = dense_call(copies, shards, part_s, mine_s, h1_t, ctx_t, rights)
    spread[0].append(to_expert(tie(first, others[0]), EXPERTS - 1))
    out = finish_call(res, one, spots, routes, small, tie(ret, others), ())
    got = [to_part(others[m - 1], m) for m in range(1, copies)]
    got = tie(got, (out, summed[1:]))
    quarters = dense_call(copies, shards, part_s, mine_s, h1_t, ctx_t, rights, got)
    def over_copies(pieces):
        stacked = jnp.stack(pieces)
        return [stacked] + [to_part(stacked, m) for m in range(1, copies)]

    spread[0] = over_copies(tie(spread[0], quarters))
    input_grad, smalls = last_call(
        part_q,
        shards,
        dq,
        dk,
        dv,
        tokens,
        tie(dres, quarters),
        small,
        (dsmall, gain_f_grad, prev_grad, cvec_grad),
        qkv_pieces,
        (),
    )
    for piece in summed[1:]:
        piece = tie(piece, smalls)
        spread.append([piece] + [to_expert(piece, k) for k in range(1, EXPERTS - 1)])
    begun = ()
    if plan.seg % LANES == 0:
        begun = unpack_chunk(plan, who, 0, spread[0], begun)
    bands = fold_quarters(zi_s, smalls, exchanged(quarters), tuple(begun))
    for pieces in spread[1:]:
        pieces.append(to_expert(tie(pieces[0], bands), EXPERTS - 1))
    spun = [bands[0]] + [spin(bands[k], k) for k in range(1, shards)]
    spread[1:] = [over_copies(tie(pieces, spun)) for pieces in spread[1:]]
    tail = fold_shards(spun)
    full_in, full_out = unpack_grads(plan, who, spread, begun)
    tail = lay_tail(mine_s, exchanged([tail] * EXPERTS), quarter, (full_out,))
    tails = [tail] + [to_part(tail, m) for m in range(1, copies)]
    qkv_grad, proj_grad, router_t, mix_t, cvec_t, gain_a, gain_f, prev_out = unpack_dense(
        part_s, tails, shard, owned
    )

    return (
        out,
        input_grad,
        qkv_grad,
        proj_grad,
        gain_a[0],
        gain_f[0],
        router_t.T,
        mix_t.T,
        prev_out,
        cvec_t.T,
        full_in,
        full_out,
    )


def solution(mesh):
    replicas, shards = mesh.shape["rep"], mesh.shape["fsdp"]
    split = P(("rep", "fsdp"), None)
    matrix = P("fsdp", None)
    cube = P("fsdp", None, None)
    in_specs = (split,) * 6 + (matrix, matrix, P("fsdp"), P("fsdp")) + (matrix,) * 4 + (cube, cube)
    out_specs = (split, split, matrix, matrix, P("fsdp"), P("fsdp")) + (matrix,) * 4 + (cube, cube)
    return jax.shard_map(
        partial(body, replicas, shards),
        mesh=mesh,
        in_specs=in_specs,
        out_specs=out_specs,
        check_vma=False,
    )
```

```python
from functools import partial
import math

import jax
import jax.numpy as jnp
from jax import lax
from jax.experimental import pallas as pl
from jax.experimental.pallas import tpu as pltpu
from jax.sharding import PartitionSpec as P

D = 768
HEADS = 12
HDIM = 64
EXPERTS = 4
NCH = 8
CAP = 384
LANES = 128
QB = 256
REACH = 512
VMEM_BYTES = 58 * 1024 * 1024
SMALL_BYTES = 24 * 1024 * 1024
EPS = 1e-06
COST_SCALE = 0.02
ATT = 100
BACK = 400
f32 = jnp.float32
bf16 = jnp.bfloat16

NT = (((1,), (1,)), ((), ()))
TN = (((0,), (0,)), ((), ()))


def mm(a, b):
    return jnp.dot(a, b, preferred_element_type=f32)


def mm_nt(a, b):
    return lax.dot_general(a, b, NT, preferred_element_type=f32)


def mm_tn(a, b):
    return lax.dot_general(a, b, TN, preferred_element_type=f32)


def staged(rows, block, *stages):
    spans = [slice(at, at + block) for at in range(0, rows, block)]
    held = [() for _ in spans]
    for stage in stages:
        held = [stage(span, *values) for span, values in zip(spans, held, strict=True)]
    return held


def params(limit=SMALL_BYTES):
    return pltpu.CompilerParams(dimension_semantics=("arbitrary",), vmem_limit_bytes=limit)


def cost(flops, nbytes):
    return pl.CostEstimate(
        flops=int(flops * COST_SCALE), bytes_accessed=int(nbytes * COST_SCALE), transcendentals=0
    )


def launch(kernel, operands, in_specs, out_specs, out_shape, after=(), **kw):
    n, skip = len(operands), len(after)

    def run(*refs):
        kernel(*refs[:n], *refs[n + skip :])

    kw.setdefault("compiler_params", pltpu.CompilerParams(vmem_limit_bytes=SMALL_BYTES))
    return pl.pallas_call(
        run,
        in_specs=list(in_specs) + [pl.BlockSpec(memory_space=pl.ANY)] * skip,
        out_specs=out_specs,
        out_shape=out_shape,
        **kw,
    )(*operands, *after)


def tie(value, *others):
    return lax.optimization_barrier((value, others))[0]


VM = pl.BlockSpec(memory_space=pltpu.VMEM)
SMEM = pl.BlockSpec(memory_space=pltpu.SMEM)
CVEC, GAIN_A, GAIN_F = NCH + 4, NCH + 6, NCH + 7


def row_of(ref, row):
    return ref[:16, :].astype(f32)[row : row + 1]


def whole(shape):
    return pl.BlockSpec(shape, lambda *_: (0,) * len(shape), pipeline_mode=pl.Buffered(1))


def rows_of(block, width):
    return pl.BlockSpec((block, width), lambda i: (i, 0))


def swap_halves(v):
    lane = lax.broadcasted_iota(jnp.int32, v.shape, 1)
    half = HDIM // 2
    ahead = pltpu.roll(v, LANES - half, 1)
    behind = pltpu.roll(v, half, 1)
    return jnp.where(lane % HDIM < half, ahead, behind)


def lay_columns(full_ref, pieces, part):
    width = pieces[0].shape[1]
    for p in range(len(pieces)):
        chosen = pieces[0][...]
        for m in range(1, len(pieces)):
            chosen = jnp.where(part == (p ^ m), pieces[m][...], chosen)
        full_ref[:, p * width : (p + 1) * width] = chosen


def qkv_kernel(count, part_ref, x_ref, small_ref, cos_ref, sin_ref, *refs):
    pieces = refs[:count]
    h_ref, q_ref, k_ref, v_ref, w_ref = refs[count:]

    @pl.when(pl.program_id(0) == 0)
    def _():
        lay_columns(w_ref, pieces, part_ref[0])

    gain = row_of(small_ref, GAIN_A)

    def norm(span):
        x = x_ref[span, :].astype(f32)
        inverse = lax.rsqrt(jnp.mean(x * x, axis=-1, keepdims=True) + EPS)
        h = (x * inverse * gain).astype(bf16)
        h_ref[span, :] = h
        return (h,)

    def project(span, h):
        return (h, mm(h, w_ref[:, :D]))

    def turn(span, mixed, out_ref, scale):
        cosine, sine = cos_ref[span, :], sin_ref[span, :]
        for c in range(0, D, LANES):
            v = mixed[:, c : c + LANES]
            turned = v * cosine + swap_halves(v) * sine
            out_ref[span, c : c + LANES] = (turned.astype(bf16).astype(f32) * scale).astype(bf16)

    def queries(span, h, mixed):
        keys = mm(h, w_ref[:, D : 2 * D])
        turn(span, mixed, q_ref, HDIM**-0.5)
        return h, keys

    def rest(span, h, keys):
        values = mm(h, w_ref[:, 2 * D :])
        turn(span, keys, k_ref, 1.0)
        v_ref[span, :] = values.astype(bf16)
        return ()

    staged(h_ref.shape[0], SUB, norm, project, queries, rest)


def qkv_call(part, x, small, cosine, sine, pieces, after):
    rows = x.shape[0]
    block = 512
    wide = jax.ShapeDtypeStruct((rows, D), bf16)
    return launch(
        partial(qkv_kernel, len(pieces)),
        [part, x, small, cosine, sine, *pieces],
        [
            SMEM,
            rows_of(block, D),
            whole(small.shape),
            rows_of(block, LANES),
            rows_of(block, LANES),
        ]
        + [whole(p.shape) for p in pieces],
        [rows_of(block, D)] * 4,
        [wide] * 4,
        after,
        grid=(rows // block,),
        scratch_shapes=[pltpu.VMEM((D, 3 * D), bf16)],
        compiler_params=params(),
        cost_estimate=cost(2 * rows * D * 3 * D, 2 * (5 * rows * D + 3 * D * D)),
        name="qkv_rope",
    )


PAD_LANE = 6


def fill_masks(query_mask, key_mask, key_mask_own, table, dcol_ref, vcol_ref):
    length = dcol_ref.shape[0]
    lane = lax.broadcasted_iota(jnp.int32, (length, LANES), 1) % HDIM
    docs = dcol_ref[...]
    query_mask[...] = jnp.where((lane == docs) | (lane == PAD_LANE), 1.0, 0.0).astype(bf16)
    other = jnp.where((lane < PAD_LANE) & (lane != docs), -1e30, 0.0)
    key_mask_own[...] = other.astype(bf16)
    padded = (lane == PAD_LANE) & (vcol_ref[...] == 0)
    key_mask[...] = jnp.where(padded, -1e30, other).astype(bf16)
    key = lax.broadcasted_iota(jnp.int32, (QB, QB), 0)
    query = lax.broadcasted_iota(jnp.int32, (QB, QB), 1)
    for i in range(length // QB):
        usable = (vcol_ref[i * QB : (i + 1) * QB, :] > 0) | (key == query)
        table[i] = jnp.where((key <= query) & usable, 0.0, -1e30)


def mask_scratch(length):
    return [pltpu.VMEM((length, LANES), bf16)] * 3 + [pltpu.VMEM((length // QB, QB, QB), f32)]


def per_head(inside, outside):
    lane = lax.broadcasted_iota(jnp.int32, inside.shape, 1)
    return [jnp.where(lane // HDIM == head, inside, outside) for head in range(2)]


def key_blocks(i):
    start = i * QB
    return [start] + list(range(max(0, start - REACH), start, QB))


def attend_kernel(
    q_ref, k_ref, v_ref, dcol_ref, vcol_ref, ctx_ref, lse_ref, q_mask, k_mask, k_own, table
):
    length = q_ref.shape[0]

    @pl.when(pl.program_id(0) == 0)
    def _():
        fill_masks(q_mask, k_mask, k_own, table, dcol_ref, vcol_ref)

    values_t = v_ref[...].astype(f32).T.astype(bf16)
    queries = per_head(q_ref[...], q_mask[...])
    keys = per_head(k_ref[...], k_mask[...])
    own_keys = per_head(k_ref[...], k_own[...])

    def scores_of(i, head):
        start = i * QB
        query = queries[head][start : start + QB]
        scores = [mm_nt(own_keys[head][start : start + QB], query) + table[i]]
        for at in key_blocks(i)[1:]:
            scores.append(mm_nt(keys[head][at : at + QB], query))
        return scores

    def weights_of(i, head, scores):
        largest = scores[0]
        for block in scores[1:]:
            largest = jnp.maximum(largest, block)
        largest = jnp.max(largest, axis=0, keepdims=True)
        raised = [jnp.exp(block - largest) for block in scores]
        total = raised[0]
        for block in raised[1:]:
            total = total + block
        total = jnp.sum(total, axis=0, keepdims=True)
        lse_ref[0, head : head + 1, i * QB : (i + 1) * QB] = largest + jnp.log(total)
        return [block.astype(bf16) for block in raised], total

    def context_of(i, head, raised, total):
        context = 0.0
        for at, block in zip(key_blocks(i), raised, strict=True):
            context = context + mm(
                values_t[head * HDIM : (head + 1) * HDIM, at : at + QB], block
            )
        return context * (1.0 / total)

    units = [(i, head) for i in range(length // QB) for head in range(2)]
    ahead = scores_of(*units[0])
    behind, contexts = None, []
    for index in range(len(units) + 1):
        scores = ahead
        if index + 1 < len(units):
            ahead = scores_of(*units[index + 1])
        made = None
        if index < len(units):
            made = (*units[index], *weights_of(*units[index], scores))
        if behind is not None:
            contexts.append(context_of(*behind))
            if len(contexts) == 2:
                i = behind[0]
                ctx_ref[i * QB : (i + 1) * QB, :] = (
                    jnp.concatenate(contexts, axis=0).T.astype(bf16)
                )
                contexts = []
        behind = made


def attend_call(q, k, v, dcol, vcol):
    length = q.shape[0]
    pairs = HEADS // 2
    column = pl.BlockSpec((length, LANES), lambda p: (0, p))
    return launch(
        attend_kernel,
        [q, k, v, dcol, vcol],
        [column, column, column, whole(dcol.shape), whole(vcol.shape)],
        [column, pl.BlockSpec((1, 2, length), lambda p: (p, 0, 0))],
        [
            jax.ShapeDtypeStruct((length, D), bf16),
            jax.ShapeDtypeStruct((pairs, 2, length), f32),
        ],
        grid=(pairs,),
        scratch_shapes=mask_scratch(length),
        compiler_params=params(),
        cost_estimate=cost(ATT * 20e9, ATT * 8 * length * D),
        name="attend",
    )


def attend_back_kernel(
    q_ref,
    k_ref,
    v_ref,
    g_ref,
    lse_ref,
    dcol_ref,
    vcol_ref,
    cos_ref,
    sin_ref,
    dq_ref,
    dk_ref,
    dv_ref,
    q_mask,
    k_mask,
    k_own,
    table,
    gk_ref,
    gv_ref,
    gq_ref,
):
    length = q_ref.shape[0]

    @pl.when(pl.program_id(0) == 0)
    def _():
        fill_masks(q_mask, k_mask, k_own, table, dcol_ref, vcol_ref)

    keys_t = k_ref[...].astype(f32).T.astype(bf16)
    zero = jnp.zeros(q_ref.shape, bf16)
    queries = per_head(q_ref[...], q_mask[...])
    bare = per_head(q_ref[...], zero)
    grads = per_head(g_ref[...], zero)
    keys = per_head(k_ref[...], k_mask[...])
    own_keys = per_head(k_ref[...], k_own[...])
    begun = set()

    def products_of(i, head):
        start = i * QB
        query = queries[head][start : start + QB]
        grad = grads[head][start : start + QB]
        scores, grad_probs = [], []
        for at in key_blocks(i):
            if at == start:
                scores.append(mm_nt(own_keys[head][at : at + QB], query) + table[i])
            else:
                scores.append(mm_nt(keys[head][at : at + QB], query))
            grad_probs.append(mm_nt(v_ref[at : at + QB, :], grad))
        return scores, grad_probs

    def softmax_back(i, head, scores, grad_probs):
        lse = lse_ref[0, head : head + 1, i * QB : (i + 1) * QB]
        probs = [jnp.exp(block - lse) for block in scores]
        inner = probs[0] * grad_probs[0]
        for p, d in zip(probs[1:], grad_probs[1:], strict=True):
            inner = inner + p * d
        inner = jnp.sum(inner, axis=0, keepdims=True)
        grad_scores = [
            (p * (d - inner)).astype(bf16) for p, d in zip(probs, grad_probs, strict=True)
        ]
        return [p.astype(bf16) for p in probs], grad_scores

    def spread_back(i, head, probs, grad_scores):
        start = i * QB
        grad_q = 0.0
        for at, p, s in zip(key_blocks(i), probs, grad_scores, strict=True):
            grad_v = mm(p, grads[head][start : start + QB])
            grad_k = mm(s, bare[head][start : start + QB])
            if at in begun:
                gv_ref[at : at + QB, :] += grad_v
                gk_ref[at : at + QB, :] += grad_k
            else:
                begun.add(at)
                gv_ref[at : at + QB, :] = grad_v
                gk_ref[at : at + QB, :] = grad_k
            grad_q = grad_q + mm(keys_t[head * HDIM : (head + 1) * HDIM, at : at + QB], s)
        gq_ref[head * HDIM : (head + 1) * HDIM, start : start + QB] = grad_q

    units = [(i, head) for i in range(length // QB) for head in range(2)]
    ahead = products_of(*units[0])
    behind = None
    for index in range(len(units) + 1):
        products = ahead
        if index + 1 < len(units):
            ahead = products_of(*units[index + 1])
        made = None
        if index < len(units):
            made = (*units[index], *softmax_back(*units[index], *products))
        if behind is not None:
            spread_back(*behind)
        behind = made
    cosine, sine = cos_ref[...], sin_ref[...]
    grad_q = gq_ref[...].T * HDIM**-0.5
    grad_k = gk_ref[...]
    dq_ref[...] = (grad_q * cosine - swap_halves(grad_q) * sine).astype(bf16)
    dk_ref[...] = (grad_k * cosine - swap_halves(grad_k) * sine).astype(bf16)
    dv_ref[...] = gv_ref[...].astype(bf16)


def attend_back_call(q, k, v, g, lse, dcol, vcol, cosine, sine):
    length = q.shape[0]
    pairs = HEADS // 2
    column = pl.BlockSpec((length, LANES), lambda p: (0, p))
    return launch(
        attend_back_kernel,
        [q, k, v, g, lse, dcol, vcol, cosine, sine],
        [column] * 4
        + [pl.BlockSpec((1, 2, length), lambda p: (p, 0, 0))]
        + [whole(a.shape) for a in (dcol, vcol, cosine, sine)],
        [column] * 3,
        [jax.ShapeDtypeStruct((length, D), bf16)] * 3,
        grid=(pairs,),
        scratch_shapes=mask_scratch(length)
        + [
            pltpu.VMEM((length, LANES), f32),
            pltpu.VMEM((length, LANES), f32),
            pltpu.VMEM((LANES, length), f32),
        ],
        compiler_params=params(VMEM_BYTES),
        cost_estimate=cost(45e9, 14 * length * D),
        name="attend_back",
    )


def cut_dense_kernel(quarter, widths, who_ref, qkv_ref, proj_ref, *refs):
    smalls, out_ref, mark_ref = refs[:-2], refs[-2], refs[-1]
    mark_ref[...] = qkv_ref[:16, :LANES]
    row = pl.multiple_of(who_ref[0] * quarter, quarter)
    start = 0
    for ref, width in zip((qkv_ref, proj_ref), widths, strict=True):
        column = pl.multiple_of(who_ref[1] * width, LANES)
        out_ref[:quarter, start : start + width] = ref[pl.ds(row, quarter), pl.ds(column, width)]
        start += width
    shard = qkv_ref.shape[0]
    out_ref[quarter:, :] = jnp.zeros((16, start), bf16)
    rows = jnp.concatenate([ref[...].astype(f32) for ref in smalls[:-1]], axis=0)
    out_ref[quarter:, :shard] = rows.astype(bf16)
    prev = smalls[-1]
    out_ref[quarter : quarter + prev.shape[0], 2 * LANES : 2 * LANES + NCH] = prev[...]


def cut_dense(who, qkv, proj, smalls, copies):
    shard = qkv.shape[0]
    quarter = shard // EXPERTS
    widths = (qkv.shape[1] // copies, proj.shape[1] // copies)
    total = sum(widths)
    if quarter % 16 == 0 and all(w % LANES == 0 for w in widths):
        return launch(
            partial(cut_dense_kernel, quarter, widths),
            [who, qkv, proj, *smalls],
            [SMEM] + [VM] * (2 + len(smalls)),
            [VM, VM],
            [
                jax.ShapeDtypeStruct((quarter + 16, total), bf16),
                jax.ShapeDtypeStruct((16, LANES), bf16),
            ],
            compiler_params=pltpu.CompilerParams(vmem_limit_bytes=VMEM_BYTES),
        name="cut_dense",
        )
    row = who[0] * quarter
    cuts = [
        lax.dynamic_slice(w, (row, who[1] * width), (quarter, width))
        for w, width in zip((qkv, proj), widths, strict=True)
    ]
    prev = smalls[-1]
    below = jnp.concatenate(
        [
            jnp.pad(jnp.concatenate(smalls[:-1]), ((0, 0), (0, 2 * LANES - shard))),
            jnp.pad(prev, ((0, 16 - prev.shape[0]), (0, total - 2 * LANES - NCH))),
        ],
        axis=1,
    )
    piece = jnp.concatenate([jnp.concatenate(cuts, axis=1), below])
    return piece, piece[:16, :LANES]


def lay_shards_kernel(count, shard, quarter, width, zi_ref, *refs):
    pieces = refs[:count]
    qkv_ref, proj_ref, small_ref, prev_ref = refs[count:]
    for k in range(count):
        at = lax.rem(zi_ref[0] + count - k, count)
        qkv_ref[at] = pieces[k][:quarter, :width]
        proj_ref[at] = pieces[k][:quarter, width:]
        prev_ref[at] = pieces[k][quarter:, 2 * LANES : 3 * LANES]
    small_ref[16:, :] = jnp.zeros((LANES - 16, D), bf16)
    for z in range(count):
        chosen = pieces[0][quarter:, : 2 * LANES].astype(f32)
        for k in range(1, count):
            here = lax.rem(zi_ref[0] + count - k, count) == z
            chosen = jnp.where(here, pieces[k][quarter:, : 2 * LANES].astype(f32), chosen)
        small_ref[:16, z * shard : (z + 1) * shard] = chosen[:, :shard].astype(bf16)


def lay_shards(zi, pieces, shard, quarter, width, after):
    count = len(pieces)
    return launch(
        partial(lay_shards_kernel, count, shard, quarter, width),
        [zi, *pieces],
        [SMEM] + [VM] * count,
        [VM] * 4,
        [
            jax.ShapeDtypeStruct((count, quarter, width), bf16),
            jax.ShapeDtypeStruct((count, quarter, pieces[0].shape[1] - width), bf16),
            jax.ShapeDtypeStruct((LANES, D), bf16),
            jax.ShapeDtypeStruct((count, 16, LANES), bf16),
        ],
        after,
        compiler_params=pltpu.CompilerParams(vmem_limit_bytes=VMEM_BYTES),
        name="lay_shards",
    )


def lay_xor_kernel(count, own_ref, *refs):
    pieces, out = refs[:count], refs[count]
    for k in range(count):
        out[:, own_ref[0] ^ k] = pieces[k][...]


def lay_xor(own, pieces, after=()):
    count = len(pieces)
    first, rows, columns = pieces[0].shape
    return launch(
        partial(lay_xor_kernel, count),
        [own, *pieces],
        [SMEM] + [VM] * count,
        VM,
        jax.ShapeDtypeStruct((first, count, rows, columns), bf16),
        after,
        name="lay_xor",
    )


def lanes_of(shape):
    return lax.broadcasted_iota(jnp.int32, shape, 1)


def partner(v, lane):
    return jnp.where(lane % 2 == 0, pltpu.roll(v, LANES - 1, 1), pltpu.roll(v, 1, 1))


def selected(choice_ref, lane):
    return (lane == choice_ref[:, 0:1]) | (lane == choice_ref[:, 1:2])


def after_kernel(
    count, part_ref, ctx_ref, x_ref, wsmall_ref, prev_ref, pmix_ref, choice_ref, *refs
):
    pieces = refs[:count]
    res_ref, h_ref, one_ref, gate_ref, w_ref = refs[count:]

    @pl.when(pl.program_id(0) == 0)
    def _():
        lay_columns(w_ref, pieces, part_ref[0])

    gain = row_of(wsmall_ref, GAIN_F)
    lane = lanes_of((SUB, LANES))
    choice = lane < NCH
    is_mix = (lane >= NCH) & (lane < NCH + 4)

    def project(span):
        return (x_ref[span, :].astype(f32) + mm(ctx_ref[span, :], w_ref[...]),)

    def norm(span, res):
        res_ref[span, :] = res
        inverse = lax.rsqrt(jnp.mean(res * res, axis=-1, keepdims=True) + EPS)
        low = (res * inverse * gain).astype(bf16)
        h_ref[span, :] = low
        small = mm_nt(low, wsmall_ref[...])
        return small, small + mm_tn(prev_ref[:, span], pmix_ref[...])

    def route(span, small, logits):
        top = jnp.max(jnp.where(choice, logits, -1e30), axis=-1, keepdims=True)
        raised = jnp.where(choice, jnp.exp(jnp.where(choice, logits - top, 0.0)), 0.0)
        gates = raised / jnp.sum(raised, axis=-1, keepdims=True)
        mixing = 1.0 / (1.0 + jnp.exp(partner(small, lane) - small))
        one_ref[span, :] = jnp.where(choice, gates, jnp.where(is_mix, mixing, 0.0))
        named = (lane == choice_ref[span, 0:1]) | (lane == choice_ref[span, 1:2])
        taken = jnp.where(named, gates, 0.0).T[:NCH]
        high = taken.astype(bf16).astype(f32)
        gate_ref[:, span] = jnp.concatenate([high, taken - high], axis=0).astype(bf16)
        return ()

    staged(res_ref.shape[0], SUB, project, norm, route)


def after_call(part, ctx, x, small, prev, pmix, choices, pieces):
    rows = x.shape[0]
    block = 512
    return launch(
        partial(after_kernel, len(pieces)),
        [part, ctx, x, small, prev, pmix, choices, *pieces],
        [SMEM]
        + [rows_of(block, D)] * 2
        + [
            whole(small.shape),
            pl.BlockSpec((NCH, block), lambda i: (0, i)),
            whole(pmix.shape),
            rows_of(block, 2),
        ]
        + [whole(p.shape) for p in pieces],
        [rows_of(block, D)] * 2
        + [rows_of(block, LANES), pl.BlockSpec((2 * NCH, block), lambda i: (0, i))],
        [
            jax.ShapeDtypeStruct((rows, D), f32),
            jax.ShapeDtypeStruct((rows, D), bf16),
            jax.ShapeDtypeStruct((rows, LANES), f32),
            jax.ShapeDtypeStruct((2 * NCH, rows), bf16),
        ],
        grid=(rows // block,),
        scratch_shapes=[pltpu.VMEM((D, D), bf16)],
        compiler_params=params(),
        cost_estimate=cost(2 * rows * D * D, 10 * rows * D),
        name="after_attention",
    )


EXTRA = 16
SUB = 256
COEF, INVERSE = 16, 17


def dispatch_kernel(gated, mine_ref, spot_ref, v_ref, *refs):
    if gated:
        gate_ref, refs = refs[0], refs[1:]
    rows = v_ref.shape[0]
    slot = lax.broadcasted_iota(jnp.int32, (CAP, rows), 0)
    all_hits = [
        jnp.where(slot == spot_ref[k : k + 1, :], 1.0, 0.0).astype(bf16) for k in range(EXPERTS)
    ]
    for k in range(EXPERTS):
        hits = all_hits[k]
        refs[k][:CAP, :] = mm(hits, v_ref[...]).astype(bf16)
        if gated:
            moved = mm_nt(gate_ref[...], hits)
            row = lax.broadcasted_iota(jnp.int32, moved.shape, 0) % NCH
            moved = jnp.where(row == (mine_ref[0] ^ k), moved, 0.0)
            high = jnp.sum(moved[:NCH], axis=0, keepdims=True)
            rest = jnp.sum(moved[NCH:], axis=0, keepdims=True)
            tail = jnp.concatenate(
                [high, rest, jnp.zeros((EXTRA - 2, CAP), f32)], axis=0
            ).astype(bf16)
            refs[k][CAP:, :CAP] = tail
            refs[k][CAP:, CAP:] = jnp.zeros((EXTRA, D - CAP), bf16)


def dispatch_call(mine, spot, values, gates=None, after=()):
    size = CAP + (0 if gates is None else EXTRA)
    operands = [mine, spot, values] + ([] if gates is None else [gates])
    rows = values.shape[0]
    return launch(
        partial(dispatch_kernel, gates is not None),
        operands,
        [SMEM] + [VM] * (len(operands) - 1),
        [VM] * EXPERTS,
        [jax.ShapeDtypeStruct((size, D), bf16)] * EXPERTS,
        after,
        cost_estimate=cost(2 * rows * D * CAP * EXPERTS, 2 * rows * D + 2 * EXPERTS * CAP * D),
        name="dispatch",
    )


class Plan:
    def __init__(self, replicas, shards, shard, hidden, chunks):
        self.copies = replicas // EXPERTS
        self.shards = shards
        self.shard = shard
        self.hidden = hidden
        self.chunks = chunks
        self.seg = hidden // (shards * self.copies * chunks)
        self.width = self.seg * shards
        self.wide = min(256, self.width)
        self.tiles = self.width // self.wide
        self.spans = self.wide // self.seg
        self.downs = D // self.wide
        self.rows = 2 * self.tiles * shard + self.downs * self.seg

    def column(self, half, tile, span, part, chunk):
        z = tile * self.spans + span
        base = half * self.hidden + z * (self.hidden // self.shards)
        return base + (chunk * self.copies + part) * self.seg

    def down_row(self, part, chunk):
        return (chunk * self.copies + part) * self.seg


def pack_kernel(plan, who_ref, in_ref, out_ref, *packs):
    mine, part = who_ref[0], who_ref[1]
    seg, shard = plan.seg, plan.shard
    step = pl.program_id(0)
    half, z = step // plan.shards, step % plan.shards
    row = pl.multiple_of((half * plan.tiles + z // plan.spans) * shard, shard)
    column = pl.multiple_of(z % plan.spans * seg, seg)
    for e in range(EXPERTS):

        @pl.when(mine == e)
        def _(e=e):
            value = in_ref[:, e, :]
            for chunk in range(plan.chunks):
                at = chunk * plan.copies * seg
                piece = value[:, at : at + seg]
                for p in range(1, plan.copies):
                    at = (chunk * plan.copies + p) * seg
                    piece = jnp.where(part == p, value[:, at : at + seg], piece)
                packs[chunk][pl.ds(row, shard), pl.ds(column, seg)] = piece

        @pl.when((mine == e) & (step == 0))
        def _(e=e):
            for chunk in range(plan.chunks):
                start = 2 * plan.tiles * shard
                at = pl.multiple_of(plan.down_row(part, chunk), seg)
                value = out_ref[pl.ds(at, seg), e, :]
                for down in range(plan.downs):
                    packs[chunk][start + down * seg : start + (down + 1) * seg, :] = value[
                        :, down * plan.wide : (down + 1) * plan.wide
                    ]


def pack_pieces(plan, who, expert_in, expert_out, after):
    if plan.seg % LANES == 0:
        per = plan.hidden // plan.shards
        return launch(
            partial(pack_kernel, plan),
            [who, expert_in, expert_out],
            [
                SMEM,
                pl.BlockSpec((plan.shard, EXPERTS, per), lambda i: (0, 0, i)),
                whole(expert_out.shape),
            ],
            [whole((plan.rows, plan.wide))] * plan.chunks,
            [jax.ShapeDtypeStruct((plan.rows, plan.wide), bf16)] * plan.chunks,
            after,
            grid=(2 * plan.shards,),
            compiler_params=params(VMEM_BYTES),
            cost_estimate=cost(0, 0),
            name="pack",
        )
    mine, part = who[0], who[1:]
    own_in = lax.dynamic_index_in_dim(expert_in, mine, 1, keepdims=False)
    own_out = lax.dynamic_index_in_dim(expert_out, mine, 1, keepdims=False)
    packs = []
    for chunk in range(plan.chunks):
        blocks = []
        for half in range(2):
            for tile in range(plan.tiles):
                spans = [
                    lax.dynamic_slice_in_dim(
                        own_in, plan.column(half, tile, span, part[0], chunk), plan.seg, 1
                    )
                    for span in range(plan.spans)
                ]
                blocks.append(jnp.concatenate(spans, axis=1))
        rows = lax.dynamic_slice_in_dim(own_out, plan.down_row(part[0], chunk), plan.seg, 0)
        blocks += [rows[:, d * plan.wide : (d + 1) * plan.wide] for d in range(plan.downs)]
        packs.append(jnp.concatenate(blocks, axis=0))
    return packs


def unpack_kernel(plan, begun, who_ref, *refs):
    copies, seg = plan.copies, plan.seg
    ins, downs = refs[:copies], refs[copies : 2 * copies]
    in_out, down_out = refs[2 * copies + 2 * begun :]
    mine, part = who_ref[0], who_ref[1]
    step = pl.program_id(0)
    z = step % plan.shards

    def of_replica(arrays, p, index):
        chosen = arrays[0][index].astype(f32)
        for m in range(1, copies):
            chosen = jnp.where(part == (p ^ m), arrays[m][index].astype(f32), chosen)
        return chosen

    for j in range(EXPERTS):
        for p in range(copies):
            chosen = of_replica(ins, p, j ^ mine)
            piece = chosen[:, :seg]
            for span in range(1, plan.spans):
                here = z % plan.spans == span
                piece = jnp.where(here, chosen[:, span * seg : (span + 1) * seg], piece)
            in_out[:, j, p * seg : (p + 1) * seg] = piece

    @pl.when(step == 0)
    def _():
        for j in range(EXPERTS):
            for p in range(copies):
                chosen = of_replica(downs, p, j ^ mine)
                for down in range(plan.downs):
                    down_out[
                        p * seg : (p + 1) * seg, j, down * plan.wide : (down + 1) * plan.wide
                    ] = chosen[down * seg : (down + 1) * seg]


def unpack_chunk(plan, who, chunk, sums, begun):
    copies, shards = plan.copies, plan.shards
    per = plan.hidden // shards
    start = 2 * plan.tiles * plan.shard
    down_rows = plan.downs * plan.seg
    both = copies * plan.seg

    def in_block(i):
        return (0, i // shards * plan.tiles + i % shards // plan.spans, 0)

    down_in = pl.BlockSpec(
        (EXPERTS, down_rows, plan.wide),
        lambda i: (0, start // down_rows, 0),
        pipeline_mode=pl.Buffered(1),
    )
    hbm = pl.BlockSpec(memory_space=pl.ANY)
    operands = [who, *sums, *sums, *begun]
    return launch(
        partial(unpack_kernel, plan, len(begun) // 2),
        operands,
        [SMEM]
        + [pl.BlockSpec((EXPERTS, plan.shard, plan.wide), in_block)] * copies
        + [down_in] * copies
        + [hbm] * len(begun),
        [
            pl.BlockSpec((plan.shard, EXPERTS, both), lambda i: (0, 0, i * plan.chunks + chunk)),
            pl.BlockSpec((both, EXPERTS, D), lambda i: (chunk, 0, 0)),
        ],
        [
            jax.ShapeDtypeStruct((plan.shard, EXPERTS, 2 * plan.hidden), f32),
            jax.ShapeDtypeStruct((per, EXPERTS, D), f32),
        ],
        grid=(2 * shards,),
        input_output_aliases={len(operands) - 2 + i: i for i in range(len(begun))},
        compiler_params=params(VMEM_BYTES),
        cost_estimate=cost(0, 12 * plan.shard * plan.hidden * EXPERTS),
        name="unpack",
    )


def unpack_grads(plan, who, sums, begun):
    if begun:
        for chunk in range(1, plan.chunks):
            begun = unpack_chunk(plan, who, chunk, sums[chunk], begun)
        return begun
    mine, part = who[0], who[1]
    ins, outs = [], []
    for j in range(EXPERTS):
        columns = {}
        rows = []
        for chunk in range(plan.chunks):
            for p in range(plan.copies):
                stacked = jnp.stack(sums[chunk])
                piece = lax.dynamic_index_in_dim(stacked, part ^ p, 0, keepdims=False)
                piece = lax.dynamic_index_in_dim(piece, mine ^ j, 0, keepdims=False)
                for half in range(2):
                    for tile in range(plan.tiles):
                        row = (half * plan.tiles + tile) * plan.shard
                        for span in range(plan.spans):
                            columns[plan.column(half, tile, span, p, chunk)] = piece[
                                row : row + plan.shard, span * plan.seg : (span + 1) * plan.seg
                            ]
                row = 2 * plan.tiles * plan.shard
                rows.append(
                    jnp.concatenate(
                        [
                            piece[row + d * plan.seg : row + (d + 1) * plan.seg]
                            for d in range(plan.downs)
                        ],
                        axis=1,
                    )
                )
        ins.append(jnp.concatenate([columns[c] for c in sorted(columns)], axis=1))
        outs.append(jnp.concatenate(rows, axis=0))
    return jnp.stack(ins, axis=1).astype(f32), jnp.stack(outs, axis=1).astype(f32)


def weight_grads(plan, part, xt, ds, act, grad_gate, grad_up, grads):
    shard, seg, wide, tiles = plan.shard, plan.seg, plan.wide, plan.tiles
    for half, source in ((0, grad_gate), (1, grad_up)):
        for tile in range(tiles):
            made = mm(xt[...], source[part, :, tile * wide : (tile + 1) * wide]).astype(bf16)
            row = (half * tiles + tile) * shard
            for z in range(plan.shards):
                grads[part, z, row : row + shard, :] = made[z * shard : (z + 1) * shard, :]
    for tile in range(tiles):
        made = mm_tn(act[part, :, tile * wide : (tile + 1) * wide], ds[...]).astype(bf16)
        for span in range(plan.spans):
            z = tile * plan.spans + span
            for down in range(plan.downs):
                row = 2 * tiles * shard + down * seg
                grads[part, z, row : row + seg, :] = made[
                    span * seg : (span + 1) * seg, down * wide : (down + 1) * wide
                ]


def expert_kernel(plan, first, last, *refs):
    refs = list(refs)

    def take(n):
        out = refs[:n]
        del refs[:n]
        return out

    copies = plan.copies
    x_refs, y_refs = take(EXPERTS), take(EXPERTS)
    w_refs = take(copies)
    if first:
        carry_in = []
    else:
        carry_in = take(2)
        (ds,) = take(1)
    if last:
        dx_outs, ret_outs, saved = take(EXPERTS), take(EXPERTS), take(3)
    else:
        grad_outs, carry_out, saved = take(copies), take(2), take(2)
    xs, gcol, ret_acc, dx_acc, act_s, dg_s, du_s = take(7)
    waiting = [take(3), take(3)]
    if last:
        y_held, sems = refs
    else:
        ds, xt, grads, sems = refs
    shard, seg, wide, tiles = plan.shard, plan.seg, plan.wide, plan.tiles
    started = []

    def copy(src, dst):
        made = pltpu.make_async_copy(src, dst, sems.at[len(started)])
        started.append(made)
        made.start()
        return made

    carries = [copy(src, dst) for src, dst in zip(carry_in, (ret_acc, dx_acc))]
    if last:
        held = [
            copy(y_refs[k].at[pl.ds(0, CAP)], y_held.at[pl.ds(k * CAP, CAP)])
            for k in range(EXPERTS)
        ]
    for k in range(EXPERTS):
        span = slice(k * CAP, (k + 1) * CAP)
        x = x_refs[k][:CAP, :]
        xs[span, :] = x
        extra = x_refs[k][CAP:, :CAP].astype(f32)
        gate = (extra[0:1] + extra[1:2]).T
        gcol[span, :] = jnp.broadcast_to(gate, (CAP, LANES))
        if not last:
            xt[:, span] = x.astype(f32).T.astype(bf16)
            ds[span, :] = (y_refs[k][:CAP, :].astype(f32) * gate).astype(bf16)
    sends = []
    if not last:
        sends = [copy(src, dst) for src, dst in zip((xt, ds), saved, strict=True)]
    if first:
        ret_acc[...] = jnp.zeros_like(ret_acc)
        dx_acc[...] = jnp.zeros_like(dx_acc)

    def columns(part, half, tile):
        row = (half * tiles + tile) * shard
        return w_refs[part][:, row : row + shard, :].reshape(D, wide)

    def down_columns(part, down):
        row = 2 * tiles * shard + down * seg
        return w_refs[part][:, row : row + seg, :].reshape(plan.width, wide)

    def products(part, b, held):
        span = slice(b * CAP, (b + 1) * CAP)
        x, d = xs[span, :], ds[span, :]
        for tile in range(tiles):
            at = slice(tile * wide, (tile + 1) * wide)
            held[0][:, at] = mm(x, columns(part, 0, tile))
            held[1][:, at] = mm(x, columns(part, 1, tile))
        grad = 0.0
        for down in range(plan.downs):
            grad = grad + mm_nt(
                d[:, down * wide : (down + 1) * wide], down_columns(part, down)
            )
        held[2][...] = grad

    def gating(part, b, held):
        span = slice(b * CAP, (b + 1) * CAP)
        gate, up, grad_act = held[0][...], held[1][...], held[2][...]
        sig = 1.0 / (1.0 + jnp.exp(-gate))
        silu = gate * sig
        act_s[part, span, :] = (silu * up).astype(bf16)
        du_s[part, span, :] = (grad_act * silu).astype(bf16)
        dg_s[part, span, :] = (grad_act * up * (sig + silu * (1.0 - sig))).astype(bf16)

    def back(part, b):
        span = slice(b * CAP, (b + 1) * CAP)
        act = act_s[part, span, :]
        for down in range(plan.downs):
            ret_acc[span, down * wide : (down + 1) * wide] += mm(act, down_columns(part, down))
        total = 0.0
        for tile in range(tiles):
            at = slice(tile * wide, (tile + 1) * wide)
            total = total + mm_nt(dg_s[part, span, at], columns(part, 0, tile))
            total = total + mm_nt(du_s[part, span, at], columns(part, 1, tile))
        dx_acc[span, :] += total

    for part in range(copies):
        products(part, 0, waiting[0])
        for b in range(EXPERTS):
            if b + 1 < EXPERTS:
                products(part, b + 1, waiting[(b + 1) % 2])
            gating(part, b, waiting[b % 2])
            if b > 0:
                if part == 0 and b == 1:
                    for made in carries:
                        made.wait()
                back(part, b - 1)
        back(part, EXPERTS - 1)
        if last:
            sends += [
                copy(src.at[part], dst.at[part])
                for src, dst in zip((act_s, dg_s, du_s), saved, strict=True)
            ]
        else:
            if part == copies - 1:
                sends += [
                    copy(src, dst) for src, dst in zip((ret_acc, dx_acc), carry_out, strict=True)
                ]
            weight_grads(plan, part, xt, ds, act_s, dg_s, du_s, grads)
            sends.append(copy(grads.at[part], grad_outs[part]))
    if last:
        for made in held:
            made.wait()
        for k in range(EXPERTS):
            span = slice(k * CAP, (k + 1) * CAP)
            ret = ret_acc[span, :]
            dgate = jnp.sum(ret * y_held[span, :].astype(f32), axis=-1, keepdims=True)
            dgate = jnp.broadcast_to(dgate, (CAP, LANES)).T[:1]
            ret_outs[k][...] = (ret * gcol[span, :1]).astype(bf16)
            dx_outs[k][:CAP, :] = dx_acc[span, :].astype(bf16)
            high = dgate.astype(bf16).astype(f32)
            tail = jnp.concatenate(
                [high, dgate - high, jnp.zeros((EXTRA - 2, CAP), f32)], axis=0
            ).astype(bf16)
            dx_outs[k][CAP:, :CAP] = tail
            dx_outs[k][CAP:, CAP:] = jnp.zeros((EXTRA, D - CAP), bf16)
    for made in sends:
        made.wait()


def expert_call(plan, xs, ys, weights, chunk, carried):
    first, last = chunk == 0, chunk == plan.chunks - 1
    rows = EXPERTS * CAP
    hbm = pl.BlockSpec(memory_space=pl.ANY)
    copies = plan.copies
    block = pl.BlockSpec(
        (plan.shards, plan.rows, plan.wide),
        lambda i: (0, 0, 0),
        pipeline_mode=pl.Buffered(1),
    )
    in_specs = [whole(a.shape) for a in xs]
    in_specs += [hbm if last else whole(a.shape) for a in ys] + [block] * copies
    operands = list(xs) + list(ys) + list(weights)
    if not first:
        in_specs += [hbm] * 2 + [whole((rows, D))]
        operands += list(carried)
    held = jax.ShapeDtypeStruct((copies, rows, plan.width), bf16)
    if last:
        out_specs = [whole((CAP + EXTRA, D))] * EXPERTS + [whole((CAP, D))] * EXPERTS
        out_shape = [jax.ShapeDtypeStruct((CAP + EXTRA, D), bf16)] * EXPERTS
        out_shape += [jax.ShapeDtypeStruct((CAP, D), bf16)] * EXPERTS
        out_specs += [hbm] * 3
        out_shape += [held] * 3
    else:
        out_specs = [hbm] * (copies + 4)
        out_shape = [jax.ShapeDtypeStruct((plan.shards, plan.rows, plan.wide), bf16)] * copies
        out_shape += [jax.ShapeDtypeStruct((rows, D), f32)] * 2
        out_shape += [
            jax.ShapeDtypeStruct((D, rows), bf16),
            jax.ShapeDtypeStruct((rows, D), bf16),
        ]
    scratch = [
        pltpu.VMEM((rows, D), bf16),
        pltpu.VMEM((rows, LANES), f32),
        pltpu.VMEM((rows, D), f32),
        pltpu.VMEM((rows, D), f32),
    ]
    scratch += [pltpu.VMEM((copies, rows, plan.width), bf16)] * 3
    scratch += [pltpu.VMEM((CAP, plan.width), f32)] * 6
    if last:
        scratch.append(pltpu.VMEM((rows, D), bf16))
    else:
        scratch += [
            pltpu.VMEM((rows, D), bf16),
            pltpu.VMEM((D, rows), bf16),
            pltpu.VMEM((copies, plan.shards, plan.rows, plan.wide), bf16),
        ]
    scratch.append(pltpu.SemaphoreType.DMA((6 + 3 * copies,)))
    return pl.pallas_call(
        partial(expert_kernel, plan, first, last),
        grid=(1,),
        in_specs=in_specs,
        out_specs=out_specs,
        out_shape=out_shape,
        scratch_shapes=scratch,
        compiler_params=params(VMEM_BYTES),
        cost_estimate=cost(
            18 * rows * D * plan.width * copies, 12 * D * plan.width * copies + 12 * rows * D
        ),
        name="experts",
    )(*operands)


def expert_grads_kernel(plan, act, grad_gate, grad_up, xt, ds, *refs):
    outs, (grads, sems) = refs[: plan.copies], refs[plan.copies :]
    sends = []
    for part in range(plan.copies):
        weight_grads(plan, part, xt, ds, act, grad_gate, grad_up, grads)
        sends.append(pltpu.make_async_copy(grads.at[part], outs[part], sems.at[part]))
        sends[-1].start()
    for made in sends:
        made.wait()


def expert_grads(plan, held):
    copies = plan.copies
    packed = (plan.shards, plan.rows, plan.wide)
    return launch(
        partial(expert_grads_kernel, plan),
        list(held),
        [whole(a.shape) for a in held],
        [pl.BlockSpec(memory_space=pl.ANY)] * copies,
        [jax.ShapeDtypeStruct(packed, bf16)] * copies,
        grid=(1,),
        scratch_shapes=[
            pltpu.VMEM((copies, *packed), bf16),
            pltpu.SemaphoreType.DMA((copies,)),
        ],
        compiler_params=params(VMEM_BYTES),
        cost_estimate=cost(0, 0),
        name="expert_grads",
    )


def spots_of(place_ref, rows):
    slot = lax.broadcasted_iota(jnp.int32, (rows, EXPERTS * CAP), 1)
    hit = (slot == place_ref[:, 0:1]) | (slot == place_ref[:, 1:2])
    return jnp.where(hit, 1.0, 0.0).astype(bf16)


def constant_gates(one, chosen, m):
    a0 = one[:, NCH + 2 * m : NCH + 2 * m + 1]
    a1 = one[:, NCH + 2 * m + 1 : NCH + 2 * m + 2]
    gate = chosen[:, EXPERTS + 2 + m : EXPERTS + 3 + m]
    return gate, a0, a1


def side_kernel(
    res_ref, dy_ref, one_ref, place_ref, choice_ref, small_ref, two_ref, spots_ref, cvec_out
):
    @pl.when(pl.program_id(0) == 0)
    def _():
        cvec_out[...] = jnp.zeros_like(cvec_out)

    res = res_ref[...]
    one = one_ref[...]
    lane = lanes_of(one.shape)
    named = selected(choice_ref, lane)
    chosen = jnp.where(named, one, 0.0)
    is_mix = (lane >= NCH) & (lane < NCH + 4)
    spots_ref[...] = spots_of(place_ref, res.shape[0])
    inverse = lax.rsqrt(jnp.mean(res * res, axis=-1, keepdims=True) + EPS)
    dy = dy_ref[...]
    spread = res * inverse * row_of(small_ref, GAIN_F)
    hd = jnp.sum(spread * dy.astype(f32), axis=-1, keepdims=True)
    cd = mm_nt(dy, small_ref[...])
    coef = chosen[:, EXPERTS + 1 : EXPERTS + 2]
    grads = jnp.where(lane == EXPERTS + 1, hd, 0.0)
    made = jnp.zeros_like(one)
    for m in range(2):
        gate, a0, a1 = constant_gates(one, chosen, m)
        dot = cd[:, CVEC + m : CVEC + m + 1]
        coef = coef + gate * a0
        grads = jnp.where(lane == EXPERTS + 2 + m, a0 * hd + a1 * dot, grads)
        grads = jnp.where(lane == NCH + 2 * m, gate * hd, grads)
        grads = jnp.where(lane == NCH + 2 * m + 1, gate * dot, grads)
        made = jnp.where(lane == m, gate * a1, made)
    two = jnp.where(is_mix | named, grads, 0.0)
    two = jnp.where(lane == COEF, coef, two)
    two_ref[...] = jnp.where(lane == INVERSE, inverse, two)
    high = made.astype(bf16)
    rest = (made - high.astype(f32)).astype(bf16)
    cvec_out[...] += mm_tn(high, dy) + mm_tn(rest, dy)


def side_call(res, dy, one, places, choices, small):
    rows = res.shape[0]
    block = 256
    return launch(
        side_kernel,
        [res, dy, one, places, choices, small],
        [rows_of(block, D)] * 2
        + [rows_of(block, LANES)]
        + [rows_of(block, 2)] * 2
        + [whole(small.shape)],
        [rows_of(block, LANES), rows_of(block, EXPERTS * CAP), whole((LANES, D))],
        [
            jax.ShapeDtypeStruct((rows, LANES), f32),
            jax.ShapeDtypeStruct((rows, EXPERTS * CAP), bf16),
            jax.ShapeDtypeStruct((LANES, D), f32),
        ],
        grid=(rows // block,),
        compiler_params=params(VMEM_BYTES),
        cost_estimate=cost(0, 0),
        name="side",
    )


def back_kernel(
    count,
    who_ref,
    res_ref,
    h_ref,
    dy_ref,
    one_ref,
    two_ref,
    spots_ref,
    prev_ref,
    wsmall_ref,
    *refs,
):
    dx_refs, refs = refs[:EXPERTS], refs[EXPERTS:]
    pieces, refs = refs[:count], refs[count:]
    (
        dres_ref,
        branch_ref,
        dctx_ref,
        dsmall_ref,
        gain_out,
        prev_out,
        w_ref,
        dg_ref,
    ) = refs

    @pl.when(pl.program_id(0) == 0)
    def _():
        gain_out[...] = jnp.zeros_like(gain_out)
        prev_out[...] = jnp.zeros_like(prev_out)
        dsmall_ref[...] = jnp.zeros_like(dsmall_ref)
        lay_columns(w_ref, pieces, who_ref[1])
        lane = lanes_of((CAP, LANES))
        for k in range(EXPERTS):
            columns = dx_refs[k][CAP:, :CAP].astype(f32).T
            at = who_ref[0] ^ k
            made = jnp.where(lane == at, columns[:, 0:1], 0.0)
            made = jnp.where(lane == at + 16, columns[:, 1:2], made)
            dg_ref[k * CAP : (k + 1) * CAP, :] = made.astype(bf16)

    gain = row_of(wsmall_ref, GAIN_F)
    lane = lanes_of((SUB, LANES))
    choice = lane < NCH
    is_mix = (lane >= NCH) & (lane < NCH + 4)

    def gather(span):
        spots = spots_ref[span, :]
        from_experts = mm(spots, dg_ref[...])
        moved = mm(spots[:, :CAP], dx_refs[0][:CAP, :])
        for k in range(1, EXPERTS):
            moved = moved + mm(spots[:, k * CAP : (k + 1) * CAP], dx_refs[k][:CAP, :])
        return from_experts, moved

    def route(span, from_experts, moved):
        one, two = one_ref[span, :], two_ref[span, :]
        from_experts = from_experts + pltpu.roll(from_experts, LANES - 16, 1)
        grads = jnp.where(lane < EXPERTS, from_experts, jnp.where(lane < NCH + 4, two, 0.0))
        weighted = one * grads
        mean_choice = jnp.sum(jnp.where(choice, weighted, 0.0), axis=-1, keepdims=True)
        d_logits = jnp.where(choice, one * (grads - mean_choice), 0.0)
        d_mix = one * (grads - (weighted + partner(weighted, lane)))
        low = jnp.where(choice, d_logits, jnp.where(is_mix, d_mix, 0.0)).astype(bf16)
        high = d_logits.astype(bf16)
        rest = (d_logits - high.astype(f32)).astype(bf16)
        return low, high, rest, moved + mm(low, wsmall_ref[...])

    def norm(span, low, high, rest, moved):
        two = two_ref[span, :]
        coef, inverse = two[:, COEF : COEF + 1], two[:, INVERSE : INVERSE + 1]
        res = res_ref[span, :]
        dyf = dy_ref[span, :].astype(f32)
        spread_grad = moved + coef * dyf
        scaled = spread_grad * gain
        mean_dot = jnp.mean(res * scaled, axis=-1, keepdims=True)
        d_res = dyf + inverse * scaled - res * (inverse * inverse * inverse * mean_dot)
        dres_ref[span, :] = d_res
        branch = d_res.astype(bf16)
        branch_ref[span, :] = branch
        by_gain = jnp.sum(spread_grad * (res * inverse), axis=0, keepdims=True)
        return low, high, rest, branch, by_gain

    def project(span, low, high, rest, branch, by_gain):
        dctx_ref[span, :] = mm_nt(branch, w_ref[...]).astype(bf16)
        prev = prev_ref[:, span]
        by_prev = mm(prev, high) + mm(prev, rest)
        return mm_tn(low, h_ref[span, :]), by_gain, by_prev

    for by_small, by_gain, by_prev in staged(res_ref.shape[0], SUB, gather, route, norm, project):
        dsmall_ref[...] += by_small
        gain_out[...] += by_gain
        prev_out[...] += by_prev


def back_call(who, res, h, dy, one, two, spots, prev, small, dx, pieces, after):
    rows = res.shape[0]
    block = 512
    return launch(
        partial(back_kernel, len(pieces)),
        [who, res, h, dy, one, two, spots, prev, small, *dx, *pieces],
        [SMEM]
        + [rows_of(block, D)] * 3
        + [rows_of(block, LANES)] * 2
        + [rows_of(block, EXPERTS * CAP)]
        + [pl.BlockSpec((NCH, block), lambda i: (0, i))]
        + [whole(a.shape) for a in (small, *dx, *pieces)],
        [rows_of(block, D)] * 3
        + [whole((LANES, D)), whole((1, D)), whole((NCH, LANES))],
        [
            jax.ShapeDtypeStruct((rows, D), f32),
            jax.ShapeDtypeStruct((rows, D), bf16),
            jax.ShapeDtypeStruct((rows, D), bf16),
            jax.ShapeDtypeStruct((LANES, D), f32),
            jax.ShapeDtypeStruct((1, D), f32),
            jax.ShapeDtypeStruct((NCH, LANES), f32),
        ],
        after,
        grid=(rows // block,),
        scratch_shapes=[pltpu.VMEM((D, D), bf16), pltpu.VMEM((EXPERTS * CAP, LANES), bf16)],
        compiler_params=params(VMEM_BYTES),
        cost_estimate=cost(BACK * 2 * rows * D * (D + 2048), BACK * 20 * rows * D),
        name="combine_back",
    )


def finish_kernel(res_ref, one_ref, spots_ref, choice_ref, small_ref, *refs):
    ret_refs, out_ref = refs[:EXPERTS], refs[EXPERTS]
    res = res_ref[...]
    one = one_ref[...]
    lane = lanes_of(one.shape)
    chosen = jnp.where(selected(choice_ref, lane), one, 0.0)
    inverse = lax.rsqrt(jnp.mean(res * res, axis=-1, keepdims=True) + EPS)
    total = res
    coef = chosen[:, EXPERTS + 1 : EXPERTS + 2]
    for m in range(2):
        gate, a0, a1 = constant_gates(one, chosen, m)
        coef = coef + gate * a0
        total = total + (gate * a1) * row_of(small_ref, CVEC + m)
    total = total + (coef * inverse) * res * row_of(small_ref, GAIN_F)
    spots = spots_ref[...]
    for k in range(EXPERTS):
        total = total + mm(spots[:, k * CAP : (k + 1) * CAP], ret_refs[k][...])
    out_ref[...] = total.astype(bf16)


def finish_call(res, one, spots, choices, small, ret, after):
    rows = res.shape[0]
    block = 256
    return launch(
        finish_kernel,
        [res, one, spots, choices, small, *ret],
        [rows_of(block, D), rows_of(block, LANES)]
        + [rows_of(block, EXPERTS * CAP), rows_of(block, 2)]
        + [whole(a.shape) for a in (small, *ret)],
        rows_of(block, D),
        jax.ShapeDtypeStruct((rows, D), bf16),
        after,
        grid=(rows // block,),
        compiler_params=params(VMEM_BYTES),
        cost_estimate=cost(2 * rows * D * 1536, 10 * rows * D),
        name="layer_out",
    )


def turn_kernel(count, *refs):
    for source, out in zip(refs[:count], refs[count:], strict=True):
        out[...] = source[...].astype(f32).T.astype(bf16)


def turn_call(arrays):
    rows, columns = arrays[0].shape
    return launch(
        partial(turn_kernel, len(arrays)),
        arrays,
        [pl.BlockSpec((rows, 256), lambda i: (0, i))] * len(arrays),
        [pl.BlockSpec((256, rows), lambda i: (i, 0))] * len(arrays),
        [jax.ShapeDtypeStruct((columns, rows), bf16)] * len(arrays),
        grid=(columns // 256,),
        compiler_params=params(VMEM_BYTES),
        cost_estimate=cost(0, 0),
        name="turn",
    )


def dense_kernel(copies, each, own, part_ref, mine_ref, ht_ref, ct_ref, *refs):
    rights, refs = refs[:4], refs[4:]
    step = pl.program_id(0)
    if own:
        got, outs, total_ref = refs[: copies - 1], refs[copies - 1 : -1], refs[-1]
    else:
        outs = refs
    per = pl.num_programs(0) if own else pl.num_programs(0) // (copies - 1)
    source = (part_ref[0] if own else (step // per + 1) ^ part_ref[0]) * per + step % per
    for index, right in enumerate(rights):
        left = ct_ref if index == 3 else ht_ref

        @pl.when(source // each == index)
        def _(left=left, right=right):
            made = mm(left[...], right[...])
            if own:
                for ref in got:
                    made = made + ref[...].astype(f32)
                total_ref[...] = made.astype(bf16).reshape(total_ref.shape)
            else:
                for m, out in enumerate(outs):
                    if len(outs) == 1:
                        out[...] = made.astype(bf16)
                    else:

                        @pl.when(step // per == m)
                        def _(out=out):
                            out[...] = made.astype(bf16)

    if own:
        for k, out in enumerate(outs):
            out[...] = total_ref[:, mine_ref[0] ^ k]


def dense_call(copies, shards, part, mine, ht, ct, rights, got=None):
    rows = ht.shape[1]
    cut = 4 * D // copies
    step = D // 2 if cut % D == 0 else cut
    per = cut // step
    each = D // step
    quarter = D // (shards * EXPERTS)
    own = got is not None

    def right_block(index):
        def block(i, part_ref, mine_ref):
            replica = part_ref[0] if own else (i // per + 1) ^ part_ref[0]
            return (0, jnp.clip(replica * per + i % per - each * index, 0, each - 1))

        return block

    def other_block(m):
        return lambda i, *_: (0, jnp.clip(i - m * per, 0, per - 1))

    def fixed(shape):
        return pl.BlockSpec(shape, lambda i, *_: (0, 0), pipeline_mode=pl.Buffered(1))

    in_specs = [fixed(ht.shape), fixed(ct.shape)]
    in_specs += [pl.BlockSpec((rows, step), right_block(index)) for index in range(4)]
    if own:
        in_specs += [pl.BlockSpec((D, step), lambda i, *_: (0, i))] * (copies - 1)
        out_specs = [pl.BlockSpec((shards, quarter, step), lambda i, *_: (0, 0, i))] * EXPERTS
        out_shape = [jax.ShapeDtypeStruct((shards, quarter, cut), bf16)] * EXPERTS
        scratch = [pltpu.VMEM((shards, EXPERTS, quarter, step), bf16)]
    else:
        out_specs = [pl.BlockSpec((D, step), other_block(m)) for m in range(copies - 1)]
        out_shape = [jax.ShapeDtypeStruct((D, cut), bf16)] * (copies - 1)
        scratch = []
    return pl.pallas_call(
        partial(dense_kernel, copies, each, own),
        grid_spec=pltpu.PrefetchScalarGridSpec(
            num_scalar_prefetch=2,
            grid=(per if own else per * (copies - 1),),
            in_specs=in_specs,
            out_specs=out_specs,
            scratch_shapes=scratch,
        ),
        out_shape=out_shape,
        compiler_params=params(VMEM_BYTES),
        cost_estimate=cost(8 * rows * D * D, 12 * rows * D + 8 * D * D),
        name="dense_own" if own else "dense_others",
    )(part, mine, ht, ct, *rights, *(got or ()))


def fold_quarters_kernel(count, zi_ref, small_ref, *refs):
    pieces, outs = refs[:count], refs[count:]
    rows, cut = pieces[0].shape[1:]
    spare = outs[0].shape[0] - rows
    for k, out in enumerate(outs):
        at = lax.rem(zi_ref[0] + k, len(outs))
        total = pieces[0][at].astype(f32)
        for piece in pieces[1:]:
            total = total + piece[at].astype(f32)
        out[:rows, :] = total.astype(bf16)
        for c in range(cut // LANES):
            out[rows:, c * LANES : (c + 1) * LANES] = small_ref[at, c * spare : (c + 1) * spare, :]


def fold_quarters(zi, small, pieces, after=()):
    shards, rows, cut = pieces[0].shape
    spare = D // shards * LANES // cut
    return launch(
        partial(fold_quarters_kernel, len(pieces)),
        [zi, small.reshape(shards, D // shards, LANES), *pieces],
        [SMEM] + [VM] * (len(pieces) + 1),
        [VM] * shards,
        [jax.ShapeDtypeStruct((rows + spare, cut), bf16)] * shards,
        after,
        compiler_params=pltpu.CompilerParams(vmem_limit_bytes=VMEM_BYTES),
        name="fold_quarters",
    )


def lay_tail_kernel(count, rows, own_ref, *refs):
    pieces, out = refs[:count], refs[count]
    total = pieces[0][rows:, :].astype(f32)
    for k in range(count):
        at = pl.multiple_of((own_ref[0] ^ k) * rows, rows)
        out[pl.ds(at, rows), :] = pieces[k][:rows, :]
        if k:
            total = total + pieces[k][rows:, :].astype(f32)
    out[count * rows :, :] = total.astype(bf16)


def lay_tail(own, pieces, rows, after):
    count = len(pieces)
    size, cut = pieces[0].shape
    return launch(
        partial(lay_tail_kernel, count, rows),
        [own, *pieces],
        [SMEM] + [VM] * count,
        VM,
        jax.ShapeDtypeStruct((count * rows + size - rows, cut), bf16),
        after,
        compiler_params=pltpu.CompilerParams(vmem_limit_bytes=VMEM_BYTES),
        name="lay_tail",
    )


def fold_copies(pieces):
    total = pieces[0].astype(f32)
    for piece in pieces[1:]:
        total = total + piece.astype(f32)
    return total.astype(bf16)


def fold_shards_kernel(*refs):
    total = refs[0][...].astype(f32)
    for ref in refs[1:-1]:
        total = total + ref[...].astype(f32)
    refs[-1][...] = total.astype(bf16)


def fold_shards(pieces):
    return launch(
        fold_shards_kernel,
        pieces,
        [VM] * len(pieces),
        VM,
        jax.ShapeDtypeStruct(pieces[0].shape, bf16),
        compiler_params=pltpu.CompilerParams(vmem_limit_bytes=VMEM_BYTES),
        name="fold_shards",
    )


def unpack_dense_kernel(count, rows, part_ref, *refs):
    pieces = refs[:count]
    qkv_ref, proj_ref, router_ref, mix_ref, cvec_ref, gain_a_ref, gain_f_ref, prev_ref = refs[count:-1]
    small_ref = refs[-1]
    cut = pieces[0].shape[1]
    small = pieces[0][rows:, :].astype(f32)
    for piece in pieces[1:]:
        small = small + piece[rows:, :].astype(f32)
    spare = small.shape[0]
    for c in range(cut // LANES):
        small_ref[c * spare : (c + 1) * spare, :] = small[:, c * LANES : (c + 1) * LANES]
    turned = small_ref[...].T
    router_ref[...] = turned[:NCH]
    mix_ref[...] = turned[NCH:CVEC]
    cvec_ref[...] = turned[CVEC:GAIN_A]
    gain_a_ref[...] = turned[GAIN_A:GAIN_F]
    gain_f_ref[...] = turned[GAIN_F : GAIN_F + 1]
    prev_ref[...] = small_ref[: prev_ref.shape[0], 16 : 16 + NCH]
    for p in range(count):
        chosen = pieces[0][:rows, :].astype(f32)
        for m in range(1, count):
            chosen = jnp.where(part_ref[0] == (p ^ m), pieces[m][:rows, :].astype(f32), chosen)
        start = p * cut
        in_qkv = max(0, min(cut, 3 * D - start))
        if in_qkv:
            qkv_ref[:, start : start + in_qkv] = chosen[:, :in_qkv]
        if in_qkv < cut:
            at = start + in_qkv - 3 * D
            proj_ref[:, at : at + cut - in_qkv] = chosen[:, in_qkv:]


def unpack_dense(part, pieces, rows, owned):
    heights = (NCH, 4, 2, 1, 1)
    return launch(
        partial(unpack_dense_kernel, len(pieces), rows),
        [part, *pieces],
        [SMEM] + [VM] * len(pieces),
        [VM] * 8,
        [jax.ShapeDtypeStruct((rows, 3 * D), f32), jax.ShapeDtypeStruct((rows, D), f32)]
        + [jax.ShapeDtypeStruct((height, rows), f32) for height in heights]
        + [jax.ShapeDtypeStruct((owned, NCH), f32)],
        scratch_shapes=[pltpu.VMEM((rows, LANES), f32)],
        compiler_params=pltpu.CompilerParams(vmem_limit_bytes=VMEM_BYTES),
        name="unpack_dense",
    )


def last_kernel(
    count,
    shards,
    part_ref,
    dq_ref,
    dk_ref,
    dv_ref,
    x_ref,
    dres_ref,
    small_ref,
    dsmall_ref,
    gain_f_ref,
    prev_ref,
    cvec_ref,
    *refs,
):
    pieces = refs[:count]
    out_ref, small_out, w_ref, gain_ref = refs[count:]

    @pl.when(pl.program_id(0) == 0)
    def _():
        gain_ref[...] = jnp.zeros_like(gain_ref)
        lay_columns(w_ref, pieces, part_ref[0])

    grad = mm_nt(dq_ref[...], w_ref[:, :D])
    grad = grad + mm_nt(dk_ref[...], w_ref[:, D : 2 * D])
    grad = grad + mm_nt(dv_ref[...], w_ref[:, 2 * D :])
    x = x_ref[...].astype(f32)
    inverse = lax.rsqrt(jnp.mean(x * x, axis=-1, keepdims=True) + EPS)
    scaled = grad * row_of(small_ref, GAIN_A)
    mean_dot = jnp.mean(x * scaled, axis=-1, keepdims=True)
    d_x = inverse * scaled - x * (inverse * inverse * inverse * mean_dot)
    out_ref[...] = (dres_ref[...] + d_x).astype(bf16)
    gain_ref[...] += jnp.sum(grad * x * inverse, axis=0, keepdims=True)

    @pl.when(pl.program_id(0) == pl.num_programs(0) - 1)
    def _():
        row = lax.broadcasted_iota(jnp.int32, (LANES, D), 0)
        total = jnp.where(row < CVEC, dsmall_ref[...], 0.0)
        for m in range(2):
            total = jnp.where(row == CVEC + m, cvec_ref[m : m + 1, :], total)
        total = jnp.where(row == GAIN_A, gain_ref[...], total)
        total = jnp.where(row == GAIN_F, gain_f_ref[...], total)
        total = total.T
        owned = NCH // shards
        shard = D // shards
        row = lax.broadcasted_iota(jnp.int32, total.shape, 0)
        lane = lanes_of((NCH, LANES))
        prev = pltpu.roll(jnp.where(lane < NCH, prev_ref[...], 0.0), 16, 1)
        for index in range(NCH):
            at = (index // owned) * shard + index % owned
            total = jnp.where(row == at, total + prev[index : index + 1, :], total)
        small_out[...] = total.astype(bf16)


def last_call(part, shards, dq, dk, dv, x, dres, small, smalls, pieces, after):
    rows = x.shape[0]
    block = 256
    return launch(
        partial(last_kernel, len(pieces), shards),
        [part, dq, dk, dv, x, dres, small, *smalls, *pieces],
        [SMEM]
        + [rows_of(block, D)] * 5
        + [whole(a.shape) for a in (small, *smalls, *pieces)],
        [rows_of(block, D), whole((D, LANES))],
        [jax.ShapeDtypeStruct((rows, D), bf16), jax.ShapeDtypeStruct((D, LANES), bf16)],
        after,
        grid=(rows // block,),
        scratch_shapes=[pltpu.VMEM((D, 3 * D), bf16), pltpu.VMEM((1, D), f32)],
        compiler_params=params(VMEM_BYTES),
        cost_estimate=cost(6 * rows * D * D, 14 * rows * D),
        name="input_grad",
    )


def body(
    replicas,
    shards,
    tokens,
    prev_logits,
    out_grad,
    routes,
    doc_ids,
    valid_mask,
    qkv_weight,
    proj_weight,
    gain_attn,
    gain_ffn,
    router,
    const_mix,
    prev_mix,
    const_vec,
    expert_in,
    expert_out,
):
    me = lax.axis_index("rep")
    zi = lax.axis_index("fsdp")
    copies = replicas // EXPERTS
    mine = me // copies
    part = me % copies
    rows = tokens.shape[0]
    shard = qkv_weight.shape[0]
    hidden = expert_in.shape[2] // 2
    quarter = shard // EXPERTS
    plan = Plan(replicas, shards, shard, hidden, 2)
    zi_s = zi.reshape(1).astype(jnp.int32)
    mine_s = mine.reshape(1).astype(jnp.int32)
    part_s = part.reshape(1).astype(jnp.int32)
    who = jnp.concatenate([mine_s, part_s])

    def to_expert(a, k):
        return lax.ppermute(a, "rep", [(i, i ^ (k * copies)) for i in range(replicas)])

    def to_part(a, m):
        return lax.ppermute(a, "rep", [(i, i ^ m) for i in range(replicas)])

    def spin(a, k):
        return lax.ppermute(a, "fsdp", [(i, (i + k) % shards) for i in range(shards)])

    def by_xor(pieces, own, axis):
        size = pieces[0].shape[axis]
        shape = list(pieces[0].shape)
        shape[axis] = size * len(pieces)
        full = jnp.zeros(shape, pieces[0].dtype)
        for k, piece in enumerate(pieces):
            full = lax.dynamic_update_slice_in_dim(full, piece, (own ^ k) * size, axis)
        return full

    width = 3 * D // copies
    owned = prev_mix.shape[0]
    smalls = [router.T, const_mix.T, const_vec.T, jnp.stack([gain_attn, gain_ffn]), prev_mix]
    piece, mark = cut_dense(who, qkv_weight, proj_weight, smalls, copies)
    spun = [piece] + [spin(piece, k) for k in range(1, shards)]

    docs = doc_ids.reshape(-1)
    drow = docs[None, :]
    dcol = docs[:, None]
    vcol = valid_mask.reshape(-1)[:, None]
    first_place = jnp.sum((drow < dcol).astype(jnp.int32), axis=1)
    offset = (jnp.arange(rows, dtype=jnp.int32) - first_place).astype(f32)
    frequency = jnp.exp(
        jnp.arange(HDIM // 2, dtype=f32) * (-2.0 * math.log(10000.0) / HDIM)
    )
    angles = offset[:, None] * frequency[None, :]
    cosine, sine = jnp.cos(angles), jnp.sin(angles)
    cosine = jnp.concatenate([cosine] * 4, axis=1)
    sine = jnp.concatenate([-sine, sine, -sine, sine], axis=1)

    routes_t = routes.T
    chosen = jnp.where(routes_t < EXPERTS, routes_t ^ mine, routes_t)
    kinds = jnp.arange(EXPERTS, dtype=jnp.int32)
    named = jnp.any(chosen[:, None, :] == kinds[None, :, None], axis=0)
    later = jnp.triu(jnp.ones((rows, rows), bf16), 1)
    rank = mm(named.astype(bf16), later).astype(jnp.int32)
    spot = jnp.where(named, rank, CAP)
    hit = chosen[:, None, :] == kinds[None, :, None]
    places = jnp.sum(jnp.where(hit, (kinds[:, None] * CAP + rank)[None], 0), axis=1)
    places = jnp.where(chosen < EXPERTS, places, -1).T

    tables = (cosine, sine, spot, dcol, vcol, places)
    packed = pack_pieces(plan, who, expert_in, expert_out, (to_part(mark, 1),))
    gathered = [lax.all_gather(p, "fsdp", axis=0, tiled=False) for p in packed]
    qkv_part, proj_part, small, prevs = lay_shards(
        zi_s, spun, shard, quarter, width, tuple(packed)
    )
    pmix = prevs[:, :owned].reshape(NCH, LANES)

    def exchanged(blocks):
        return [blocks[0]] + [to_expert(blocks[k], k) for k in range(1, EXPERTS)]

    def over_parts(half):
        half = half.reshape(D, half.shape[3])
        pieces = [half] + [to_part(half, m) for m in range(1, copies)]
        if half.shape[1] % LANES == 0:
            return pieces
        return [by_xor(pieces, part, 1)]

    ys = dispatch_call(mine_s, spot, out_grad)
    qkv_half = lay_xor(mine_s, exchanged([qkv_part] * EXPERTS), (*tables, ys[0]))
    qkv_pieces = over_parts(qkv_half)
    part_q = part_s if len(qkv_pieces) == copies else jnp.zeros_like(part_s)
    proj_from = exchanged([tie(proj_part, qkv_half)] * EXPERTS)

    prev = prev_logits.T
    h1, q, k, v = qkv_call(part_q, tokens, small, cosine, sine, qkv_pieces, ())
    proj_half = lay_xor(mine_s, tie(proj_from, h1))
    q = tie(q, proj_half)
    proj_pieces = over_parts(proj_half)
    part_p = part_s if len(proj_pieces) == copies else jnp.zeros_like(part_s)
    ys = exchanged(tie(ys, h1))
    ctx, lse = attend_call(q, k, v, dcol, vcol)
    res, h2, one, gates = after_call(
        part_p, ctx, tokens, small, prev, pmix, routes, proj_pieces
    )

    xs = dispatch_call(mine_s, spot, tie(h2, ys), gates)
    h1_t, ctx_t = turn_call([tie(h1, xs[0]), ctx])
    two, spots, cvec_grad = side_call(tie(res, xs[0]), out_grad, one, places, routes, small)
    sent, xs = xs[0], exchanged(xs)
    weights = []
    for chunk, full in enumerate(gathered):
        full = tie(full, xs if chunk else sent)
        weights.append([full] + [to_part(full, m) for m in range(1, copies)])
    weights[0] = tie(weights[0], (h1_t, two))
    xs = tie(xs, weights[1][0])
    carried, turned = None, None
    chunk_grads = []
    for chunk in range(plan.chunks):
        made = expert_call(plan, xs, ys, weights[chunk], chunk, carried)
        if chunk < plan.chunks - 1:
            chunk_grads.append(made[:copies])
            carried = [*made[copies : copies + 2], made[copies + 3]]
            turned = made[copies + 2]
    dx, returned = exchanged(made[:EXPERTS]), made[EXPERTS : 2 * EXPERTS]
    chunk_grads.append(expert_grads(plan, [*made[2 * EXPERTS :], turned, carried[2]]))

    chunk_grads = [
        [grads[0]] + [to_part(grads[m], m) for m in range(1, copies)] for grads in chunk_grads
    ]
    total = fold_copies(tie(chunk_grads[0], returned[0]))

    def over_shards(t):
        return lax.psum_scatter(t, "fsdp", scatter_dimension=0, tiled=False)

    who_p = jnp.concatenate([mine_s, part_p])
    dres, branch, dctx, dsmall, gain_f_grad, prev_grad = back_call(
        who_p,
        res,
        h2,
        out_grad,
        one,
        two,
        spots,
        prev,
        small,
        dx,
        proj_pieces,
        (total,),
    )
    summed = [over_shards(total)]
    summed += [over_shards(fold_copies(tie(grads, branch))) for grads in chunk_grads[1:]]
    ret = exchanged(tie(returned, dx))
    first = tie(summed[0], branch)
    spread = [[first] + [to_expert(first, k) for k in range(1, EXPERTS - 1)]]
    dq, dk, dv = attend_back_call(q, k, v, dctx, lse, dcol, vcol, cosine, sine)
    rights = [tie(dq, ret, spread[0]), dk, dv, branch]
    others = dense_call(copies, shards, part_s, mine_s, h1_t, ctx_t, rights)
    spread[0].append(to_expert(tie(first, others[0]), EXPERTS - 1))
    out = finish_call(res, one, spots, routes, small, tie(ret, others), ())
    got = [to_part(others[m - 1], m) for m in range(1, copies)]
    got = tie(got, (out, summed[1:]))
    quarters = dense_call(copies, shards, part_s, mine_s, h1_t, ctx_t, rights, got)
    def over_copies(pieces):
        stacked = jnp.stack(pieces)
        return [stacked] + [to_part(stacked, m) for m in range(1, copies)]

    spread[0] = over_copies(tie(spread[0], quarters))
    input_grad, smalls = last_call(
        part_q,
        shards,
        dq,
        dk,
        dv,
        tokens,
        tie(dres, quarters),
        small,
        (dsmall, gain_f_grad, prev_grad, cvec_grad),
        qkv_pieces,
        (),
    )
    for piece in summed[1:]:
        piece = tie(piece, smalls)
        spread.append([piece] + [to_expert(piece, k) for k in range(1, EXPERTS - 1)])
    begun = ()
    if plan.seg % LANES == 0:
        begun = unpack_chunk(plan, who, 0, spread[0], begun)
    bands = fold_quarters(zi_s, smalls, exchanged(quarters), tuple(begun))
    for pieces in spread[1:]:
        pieces.append(to_expert(tie(pieces[0], bands), EXPERTS - 1))
    spun = [bands[0]] + [spin(bands[k], k) for k in range(1, shards)]
    spread[1:] = [over_copies(tie(pieces, spun)) for pieces in spread[1:]]
    tail = fold_shards(spun)
    full_in, full_out = unpack_grads(plan, who, spread, begun)
    tail = lay_tail(mine_s, exchanged([tail] * EXPERTS), quarter, (full_out,))
    tails = [tail] + [to_part(tail, m) for m in range(1, copies)]
    qkv_grad, proj_grad, router_t, mix_t, cvec_t, gain_a, gain_f, prev_out = unpack_dense(
        part_s, tails, shard, owned
    )

    return (
        out,
        input_grad,
        qkv_grad,
        proj_grad,
        gain_a[0],
        gain_f[0],
        router_t.T,
        mix_t.T,
        prev_out,
        cvec_t.T,
        full_in,
        full_out,
    )


def solution(mesh):
    replicas, shards = mesh.shape["rep"], mesh.shape["fsdp"]
    split = P(("rep", "fsdp"), None)
    matrix = P("fsdp", None)
    cube = P("fsdp", None, None)
    in_specs = (split,) * 6 + (matrix, matrix, P("fsdp"), P("fsdp")) + (matrix,) * 4 + (cube, cube)
    out_specs = (split, split, matrix, matrix, P("fsdp"), P("fsdp")) + (matrix,) * 4 + (cube, cube)
    return jax.shard_map(
        partial(body, replicas, shards),
        mesh=mesh,
        in_specs=in_specs,
        out_specs=out_specs,
        check_vma=False,
    )
```

```python
from functools import partial
import math

import jax
import jax.numpy as jnp
from jax import lax
from jax.experimental import pallas as pl
from jax.experimental.pallas import tpu as pltpu
from jax.sharding import PartitionSpec as P

D = 768
HEADS = 12
HDIM = 64
EXPERTS = 4
NCH = 8
CAP = 384
LANES = 128
QB = 256
REACH = 512
VMEM_BYTES = 58 * 1024 * 1024
SMALL_BYTES = 24 * 1024 * 1024
EPS = 1e-06
COST_SCALE = 0.02
ATT = 100
BACK = 400
f32 = jnp.float32
bf16 = jnp.bfloat16

NT = (((1,), (1,)), ((), ()))
TN = (((0,), (0,)), ((), ()))


def mm(a, b):
    return jnp.dot(a, b, preferred_element_type=f32)


def mm_nt(a, b):
    return lax.dot_general(a, b, NT, preferred_element_type=f32)


def mm_tn(a, b):
    return lax.dot_general(a, b, TN, preferred_element_type=f32)


def staged(rows, block, *stages):
    spans = [slice(at, at + block) for at in range(0, rows, block)]
    held = [() for _ in spans]
    for stage in stages:
        held = [stage(span, *values) for span, values in zip(spans, held, strict=True)]
    return held


def params(limit=SMALL_BYTES):
    return pltpu.CompilerParams(dimension_semantics=("arbitrary",), vmem_limit_bytes=limit)


def cost(flops, nbytes):
    return pl.CostEstimate(
        flops=int(flops * COST_SCALE), bytes_accessed=int(nbytes * COST_SCALE), transcendentals=0
    )


def launch(kernel, operands, in_specs, out_specs, out_shape, after=(), **kw):
    n, skip = len(operands), len(after)

    def run(*refs):
        kernel(*refs[:n], *refs[n + skip :])

    kw.setdefault("compiler_params", pltpu.CompilerParams(vmem_limit_bytes=SMALL_BYTES))
    return pl.pallas_call(
        run,
        in_specs=list(in_specs) + [pl.BlockSpec(memory_space=pl.ANY)] * skip,
        out_specs=out_specs,
        out_shape=out_shape,
        **kw,
    )(*operands, *after)


def tie(value, *others):
    return lax.optimization_barrier((value, others))[0]


VM = pl.BlockSpec(memory_space=pltpu.VMEM)
SMEM = pl.BlockSpec(memory_space=pltpu.SMEM)
CVEC, GAIN_A, GAIN_F = NCH + 4, NCH + 6, NCH + 7


def row_of(ref, row):
    return ref[:16, :].astype(f32)[row : row + 1]


def whole(shape):
    return pl.BlockSpec(shape, lambda *_: (0,) * len(shape), pipeline_mode=pl.Buffered(1))


def rows_of(block, width):
    return pl.BlockSpec((block, width), lambda i: (i, 0))


def swap_halves(v):
    lane = lax.broadcasted_iota(jnp.int32, v.shape, 1)
    half = HDIM // 2
    ahead = pltpu.roll(v, LANES - half, 1)
    behind = pltpu.roll(v, half, 1)
    return jnp.where(lane % HDIM < half, ahead, behind)


def lay_columns(full_ref, pieces, part):
    width = pieces[0].shape[1]
    for p in range(len(pieces)):
        chosen = pieces[0][...]
        for m in range(1, len(pieces)):
            chosen = jnp.where(part == (p ^ m), pieces[m][...], chosen)
        full_ref[:, p * width : (p + 1) * width] = chosen


def qkv_kernel(count, part_ref, x_ref, small_ref, cos_ref, sin_ref, *refs):
    pieces = refs[:count]
    h_ref, q_ref, k_ref, v_ref, w_ref = refs[count:]

    @pl.when(pl.program_id(0) == 0)
    def _():
        lay_columns(w_ref, pieces, part_ref[0])

    gain = row_of(small_ref, GAIN_A)

    def norm(span):
        x = x_ref[span, :].astype(f32)
        inverse = lax.rsqrt(jnp.mean(x * x, axis=-1, keepdims=True) + EPS)
        h = (x * inverse * gain).astype(bf16)
        h_ref[span, :] = h
        return (h,)

    def project(span, h):
        return (h, mm(h, w_ref[:, :D]))

    def turn(span, mixed, out_ref, scale):
        cosine, sine = cos_ref[span, :], sin_ref[span, :]
        for c in range(0, D, LANES):
            v = mixed[:, c : c + LANES]
            turned = v * cosine + swap_halves(v) * sine
            out_ref[span, c : c + LANES] = (turned.astype(bf16).astype(f32) * scale).astype(bf16)

    def queries(span, h, mixed):
        keys = mm(h, w_ref[:, D : 2 * D])
        turn(span, mixed, q_ref, HDIM**-0.5)
        return h, keys

    def rest(span, h, keys):
        values = mm(h, w_ref[:, 2 * D :])
        turn(span, keys, k_ref, 1.0)
        v_ref[span, :] = values.astype(bf16)
        return ()

    staged(h_ref.shape[0], SUB, norm, project, queries, rest)


def qkv_call(part, x, small, cosine, sine, pieces, after):
    rows = x.shape[0]
    block = 512
    wide = jax.ShapeDtypeStruct((rows, D), bf16)
    return launch(
        partial(qkv_kernel, len(pieces)),
        [part, x, small, cosine, sine, *pieces],
        [
            SMEM,
            rows_of(block, D),
            whole(small.shape),
            rows_of(block, LANES),
            rows_of(block, LANES),
        ]
        + [whole(p.shape) for p in pieces],
        [rows_of(block, D)] * 4,
        [wide] * 4,
        after,
        grid=(rows // block,),
        scratch_shapes=[pltpu.VMEM((D, 3 * D), bf16)],
        compiler_params=params(),
        cost_estimate=cost(2 * rows * D * 3 * D, 2 * (5 * rows * D + 3 * D * D)),
        name="qkv_rope",
    )


PAD_LANE = 6


def fill_masks(query_mask, key_mask, key_mask_own, table, dcol_ref, vcol_ref):
    length = dcol_ref.shape[0]
    lane = lax.broadcasted_iota(jnp.int32, (length, LANES), 1) % HDIM
    docs = dcol_ref[...]
    query_mask[...] = jnp.where((lane == docs) | (lane == PAD_LANE), 1.0, 0.0).astype(bf16)
    other = jnp.where((lane < PAD_LANE) & (lane != docs), -1e30, 0.0)
    key_mask_own[...] = other.astype(bf16)
    padded = (lane == PAD_LANE) & (vcol_ref[...] == 0)
    key_mask[...] = jnp.where(padded, -1e30, other).astype(bf16)
    key = lax.broadcasted_iota(jnp.int32, (QB, QB), 0)
    query = lax.broadcasted_iota(jnp.int32, (QB, QB), 1)
    for i in range(length // QB):
        usable = (vcol_ref[i * QB : (i + 1) * QB, :] > 0) | (key == query)
        table[i] = jnp.where((key <= query) & usable, 0.0, -1e30)


def mask_scratch(length):
    return [pltpu.VMEM((length, LANES), bf16)] * 3 + [pltpu.VMEM((length // QB, QB, QB), f32)]


def per_head(inside, outside):
    lane = lax.broadcasted_iota(jnp.int32, inside.shape, 1)
    return [jnp.where(lane // HDIM == head, inside, outside) for head in range(2)]


def key_blocks(i):
    start = i * QB
    return [start] + list(range(max(0, start - REACH), start, QB))


def attend_kernel(
    q_ref, k_ref, v_ref, dcol_ref, vcol_ref, ctx_ref, lse_ref, q_mask, k_mask, k_own, table
):
    length = q_ref.shape[0]

    @pl.when(pl.program_id(0) == 0)
    def _():
        fill_masks(q_mask, k_mask, k_own, table, dcol_ref, vcol_ref)

    values_t = v_ref[...].astype(f32).T.astype(bf16)
    queries = per_head(q_ref[...], q_mask[...])
    keys = per_head(k_ref[...], k_mask[...])
    own_keys = per_head(k_ref[...], k_own[...])

    def scores_of(i, head):
        start = i * QB
        query = queries[head][start : start + QB]
        scores = [mm_nt(own_keys[head][start : start + QB], query) + table[i]]
        for at in key_blocks(i)[1:]:
            scores.append(mm_nt(keys[head][at : at + QB], query))
        return scores

    def weights_of(i, head, scores):
        largest = scores[0]
        for block in scores[1:]:
            largest = jnp.maximum(largest, block)
        largest = jnp.max(largest, axis=0, keepdims=True)
        raised = [jnp.exp(block - largest) for block in scores]
        total = raised[0]
        for block in raised[1:]:
            total = total + block
        total = jnp.sum(total, axis=0, keepdims=True)
        lse_ref[0, head : head + 1, i * QB : (i + 1) * QB] = largest + jnp.log(total)
        return [block.astype(bf16) for block in raised], total

    def context_of(i, head, raised, total):
        context = 0.0
        for at, block in zip(key_blocks(i), raised, strict=True):
            context = context + mm(
                values_t[head * HDIM : (head + 1) * HDIM, at : at + QB], block
            )
        return context * (1.0 / total)

    units = [(i, head) for i in range(length // QB) for head in range(2)]
    ahead = scores_of(*units[0])
    behind, contexts = None, []
    for index in range(len(units) + 1):
        scores = ahead
        if index + 1 < len(units):
            ahead = scores_of(*units[index + 1])
        made = None
        if index < len(units):
            made = (*units[index], *weights_of(*units[index], scores))
        if behind is not None:
            contexts.append(context_of(*behind))
            if len(contexts) == 2:
                i = behind[0]
                ctx_ref[i * QB : (i + 1) * QB, :] = (
                    jnp.concatenate(contexts, axis=0).T.astype(bf16)
                )
                contexts = []
        behind = made


def attend_call(q, k, v, dcol, vcol):
    length = q.shape[0]
    pairs = HEADS // 2
    column = pl.BlockSpec((length, LANES), lambda p: (0, p))
    return launch(
        attend_kernel,
        [q, k, v, dcol, vcol],
        [column, column, column, whole(dcol.shape), whole(vcol.shape)],
        [column, pl.BlockSpec((1, 2, length), lambda p: (p, 0, 0))],
        [
            jax.ShapeDtypeStruct((length, D), bf16),
            jax.ShapeDtypeStruct((pairs, 2, length), f32),
        ],
        grid=(pairs,),
        scratch_shapes=mask_scratch(length),
        compiler_params=params(),
        cost_estimate=cost(ATT * 20e9, ATT * 8 * length * D),
        name="attend",
    )


def attend_back_kernel(
    q_ref,
    k_ref,
    v_ref,
    g_ref,
    lse_ref,
    dcol_ref,
    vcol_ref,
    cos_ref,
    sin_ref,
    dq_ref,
    dk_ref,
    dv_ref,
    q_mask,
    k_mask,
    k_own,
    table,
    gk_ref,
    gv_ref,
    gq_ref,
):
    length = q_ref.shape[0]

    @pl.when(pl.program_id(0) == 0)
    def _():
        fill_masks(q_mask, k_mask, k_own, table, dcol_ref, vcol_ref)

    keys_t = k_ref[...].astype(f32).T.astype(bf16)
    zero = jnp.zeros(q_ref.shape, bf16)
    queries = per_head(q_ref[...], q_mask[...])
    bare = per_head(q_ref[...], zero)
    grads = per_head(g_ref[...], zero)
    keys = per_head(k_ref[...], k_mask[...])
    own_keys = per_head(k_ref[...], k_own[...])
    begun = set()

    def products_of(i, head):
        start = i * QB
        query = queries[head][start : start + QB]
        grad = grads[head][start : start + QB]
        scores, grad_probs = [], []
        for at in key_blocks(i):
            if at == start:
                scores.append(mm_nt(own_keys[head][at : at + QB], query) + table[i])
            else:
                scores.append(mm_nt(keys[head][at : at + QB], query))
            grad_probs.append(mm_nt(v_ref[at : at + QB, :], grad))
        return scores, grad_probs

    def softmax_back(i, head, scores, grad_probs):
        lse = lse_ref[0, head : head + 1, i * QB : (i + 1) * QB]
        probs = [jnp.exp(block - lse) for block in scores]
        inner = probs[0] * grad_probs[0]
        for p, d in zip(probs[1:], grad_probs[1:], strict=True):
            inner = inner + p * d
        inner = jnp.sum(inner, axis=0, keepdims=True)
        grad_scores = [
            (p * (d - inner)).astype(bf16) for p, d in zip(probs, grad_probs, strict=True)
        ]
        return [p.astype(bf16) for p in probs], grad_scores

    def spread_back(i, head, probs, grad_scores):
        start = i * QB
        grad_q = 0.0
        for at, p, s in zip(key_blocks(i), probs, grad_scores, strict=True):
            grad_v = mm(p, grads[head][start : start + QB])
            grad_k = mm(s, bare[head][start : start + QB])
            if at in begun:
                gv_ref[at : at + QB, :] += grad_v
                gk_ref[at : at + QB, :] += grad_k
            else:
                begun.add(at)
                gv_ref[at : at + QB, :] = grad_v
                gk_ref[at : at + QB, :] = grad_k
            grad_q = grad_q + mm(keys_t[head * HDIM : (head + 1) * HDIM, at : at + QB], s)
        gq_ref[head * HDIM : (head + 1) * HDIM, start : start + QB] = grad_q

    units = [(i, head) for i in range(length // QB) for head in range(2)]
    ahead = products_of(*units[0])
    behind = None
    for index in range(len(units) + 1):
        products = ahead
        if index + 1 < len(units):
            ahead = products_of(*units[index + 1])
        made = None
        if index < len(units):
            made = (*units[index], *softmax_back(*units[index], *products))
        if behind is not None:
            spread_back(*behind)
        behind = made
    cosine, sine = cos_ref[...], sin_ref[...]
    grad_q = gq_ref[...].T * HDIM**-0.5
    grad_k = gk_ref[...]
    dq_ref[...] = (grad_q * cosine - swap_halves(grad_q) * sine).astype(bf16)
    dk_ref[...] = (grad_k * cosine - swap_halves(grad_k) * sine).astype(bf16)
    dv_ref[...] = gv_ref[...].astype(bf16)


def attend_back_call(q, k, v, g, lse, dcol, vcol, cosine, sine):
    length = q.shape[0]
    pairs = HEADS // 2
    column = pl.BlockSpec((length, LANES), lambda p: (0, p))
    return launch(
        attend_back_kernel,
        [q, k, v, g, lse, dcol, vcol, cosine, sine],
        [column] * 4
        + [pl.BlockSpec((1, 2, length), lambda p: (p, 0, 0))]
        + [whole(a.shape) for a in (dcol, vcol, cosine, sine)],
        [column] * 3,
        [jax.ShapeDtypeStruct((length, D), bf16)] * 3,
        grid=(pairs,),
        scratch_shapes=mask_scratch(length)
        + [
            pltpu.VMEM((length, LANES), f32),
            pltpu.VMEM((length, LANES), f32),
            pltpu.VMEM((LANES, length), f32),
        ],
        compiler_params=params(VMEM_BYTES),
        cost_estimate=cost(45e9, 14 * length * D),
        name="attend_back",
    )


def cut_dense_kernel(quarter, widths, who_ref, qkv_ref, proj_ref, *refs):
    smalls, out_ref, mark_ref = refs[:-2], refs[-2], refs[-1]
    mark_ref[...] = qkv_ref[:16, :LANES]
    row = pl.multiple_of(who_ref[0] * quarter, quarter)
    start = 0
    for ref, width in zip((qkv_ref, proj_ref), widths, strict=True):
        column = pl.multiple_of(who_ref[1] * width, LANES)
        out_ref[:quarter, start : start + width] = ref[pl.ds(row, quarter), pl.ds(column, width)]
        start += width
    shard = qkv_ref.shape[0]
    out_ref[quarter:, :] = jnp.zeros((16, start), bf16)
    rows = jnp.concatenate([ref[...].astype(f32) for ref in smalls[:-1]], axis=0)
    out_ref[quarter:, :shard] = rows.astype(bf16)
    prev = smalls[-1]
    out_ref[quarter : quarter + prev.shape[0], 2 * LANES : 2 * LANES + NCH] = prev[...]


def cut_dense(who, qkv, proj, smalls, copies):
    shard = qkv.shape[0]
    quarter = shard // EXPERTS
    widths = (qkv.shape[1] // copies, proj.shape[1] // copies)
    total = sum(widths)
    if quarter % 16 == 0 and all(w % LANES == 0 for w in widths):
        return launch(
            partial(cut_dense_kernel, quarter, widths),
            [who, qkv, proj, *smalls],
            [SMEM] + [VM] * (2 + len(smalls)),
            [VM, VM],
            [
                jax.ShapeDtypeStruct((quarter + 16, total), bf16),
                jax.ShapeDtypeStruct((16, LANES), bf16),
            ],
            compiler_params=pltpu.CompilerParams(vmem_limit_bytes=VMEM_BYTES),
        name="cut_dense",
        )
    row = who[0] * quarter
    cuts = [
        lax.dynamic_slice(w, (row, who[1] * width), (quarter, width))
        for w, width in zip((qkv, proj), widths, strict=True)
    ]
    prev = smalls[-1]
    below = jnp.concatenate(
        [
            jnp.pad(jnp.concatenate(smalls[:-1]), ((0, 0), (0, 2 * LANES - shard))),
            jnp.pad(prev, ((0, 16 - prev.shape[0]), (0, total - 2 * LANES - NCH))),
        ],
        axis=1,
    )
    piece = jnp.concatenate([jnp.concatenate(cuts, axis=1), below])
    return piece, piece[:16, :LANES]


def lay_shards_kernel(count, shard, quarter, width, zi_ref, *refs):
    pieces = refs[:count]
    qkv_ref, proj_ref, small_ref, prev_ref = refs[count:]
    for k in range(count):
        at = lax.rem(zi_ref[0] + count - k, count)
        qkv_ref[at] = pieces[k][:quarter, :width]
        proj_ref[at] = pieces[k][:quarter, width:]
        prev_ref[at] = pieces[k][quarter:, 2 * LANES : 3 * LANES]
    small_ref[16:, :] = jnp.zeros((LANES - 16, D), bf16)
    for z in range(count):
        chosen = pieces[0][quarter:, : 2 * LANES].astype(f32)
        for k in range(1, count):
            here = lax.rem(zi_ref[0] + count - k, count) == z
            chosen = jnp.where(here, pieces[k][quarter:, : 2 * LANES].astype(f32), chosen)
        small_ref[:16, z * shard : (z + 1) * shard] = chosen[:, :shard].astype(bf16)


def lay_shards(zi, pieces, shard, quarter, width, after):
    count = len(pieces)
    return launch(
        partial(lay_shards_kernel, count, shard, quarter, width),
        [zi, *pieces],
        [SMEM] + [VM] * count,
        [VM] * 4,
        [
            jax.ShapeDtypeStruct((count, quarter, width), bf16),
            jax.ShapeDtypeStruct((count, quarter, pieces[0].shape[1] - width), bf16),
            jax.ShapeDtypeStruct((LANES, D), bf16),
            jax.ShapeDtypeStruct((count, 16, LANES), bf16),
        ],
        after,
        compiler_params=pltpu.CompilerParams(vmem_limit_bytes=VMEM_BYTES),
        name="lay_shards",
    )


def lay_xor_kernel(count, own_ref, *refs):
    pieces, out = refs[:count], refs[count]
    for k in range(count):
        out[:, own_ref[0] ^ k] = pieces[k][...]


def lay_xor(own, pieces, after=()):
    count = len(pieces)
    first, rows, columns = pieces[0].shape
    return launch(
        partial(lay_xor_kernel, count),
        [own, *pieces],
        [SMEM] + [VM] * count,
        VM,
        jax.ShapeDtypeStruct((first, count, rows, columns), bf16),
        after,
        name="lay_xor",
    )


def lanes_of(shape):
    return lax.broadcasted_iota(jnp.int32, shape, 1)


def partner(v, lane):
    return jnp.where(lane % 2 == 0, pltpu.roll(v, LANES - 1, 1), pltpu.roll(v, 1, 1))


def selected(choice_ref, lane):
    return (lane == choice_ref[:, 0:1]) | (lane == choice_ref[:, 1:2])


def after_kernel(
    count, part_ref, ctx_ref, x_ref, wsmall_ref, prev_ref, pmix_ref, choice_ref, *refs
):
    pieces = refs[:count]
    res_ref, h_ref, one_ref, gate_ref, w_ref = refs[count:]

    @pl.when(pl.program_id(0) == 0)
    def _():
        lay_columns(w_ref, pieces, part_ref[0])

    gain = row_of(wsmall_ref, GAIN_F)
    lane = lanes_of((SUB, LANES))
    choice = lane < NCH
    is_mix = (lane >= NCH) & (lane < NCH + 4)

    def project(span):
        return (x_ref[span, :].astype(f32) + mm(ctx_ref[span, :], w_ref[...]),)

    def norm(span, res):
        res_ref[span, :] = res
        inverse = lax.rsqrt(jnp.mean(res * res, axis=-1, keepdims=True) + EPS)
        low = (res * inverse * gain).astype(bf16)
        h_ref[span, :] = low
        small = mm_nt(low, wsmall_ref[...])
        return small, small + mm_tn(prev_ref[:, span], pmix_ref[...])

    def route(span, small, logits):
        top = jnp.max(jnp.where(choice, logits, -1e30), axis=-1, keepdims=True)
        raised = jnp.where(choice, jnp.exp(jnp.where(choice, logits - top, 0.0)), 0.0)
        gates = raised / jnp.sum(raised, axis=-1, keepdims=True)
        mixing = 1.0 / (1.0 + jnp.exp(partner(small, lane) - small))
        one_ref[span, :] = jnp.where(choice, gates, jnp.where(is_mix, mixing, 0.0))
        named = (lane == choice_ref[span, 0:1]) | (lane == choice_ref[span, 1:2])
        taken = jnp.where(named, gates, 0.0).T[:NCH]
        high = taken.astype(bf16).astype(f32)
        gate_ref[:, span] = jnp.concatenate([high, taken - high], axis=0).astype(bf16)
        return ()

    staged(res_ref.shape[0], SUB, project, norm, route)


def after_call(part, ctx, x, small, prev, pmix, choices, pieces):
    rows = x.shape[0]
    block = 512
    return launch(
        partial(after_kernel, len(pieces)),
        [part, ctx, x, small, prev, pmix, choices, *pieces],
        [SMEM]
        + [rows_of(block, D)] * 2
        + [
            whole(small.shape),
            pl.BlockSpec((NCH, block), lambda i: (0, i)),
            whole(pmix.shape),
            rows_of(block, 2),
        ]
        + [whole(p.shape) for p in pieces],
        [rows_of(block, D)] * 2
        + [rows_of(block, LANES), pl.BlockSpec((2 * NCH, block), lambda i: (0, i))],
        [
            jax.ShapeDtypeStruct((rows, D), f32),
            jax.ShapeDtypeStruct((rows, D), bf16),
            jax.ShapeDtypeStruct((rows, LANES), f32),
            jax.ShapeDtypeStruct((2 * NCH, rows), bf16),
        ],
        grid=(rows // block,),
        scratch_shapes=[pltpu.VMEM((D, D), bf16)],
        compiler_params=params(),
        cost_estimate=cost(2 * rows * D * D, 10 * rows * D),
        name="after_attention",
    )


EXTRA = 16
SUB = 256
COEF, INVERSE = 16, 17


def dispatch_kernel(gated, mine_ref, spot_ref, v_ref, *refs):
    if gated:
        gate_ref, refs = refs[0], refs[1:]
    rows = v_ref.shape[0]
    slot = lax.broadcasted_iota(jnp.int32, (CAP, rows), 0)
    all_hits = [
        jnp.where(slot == spot_ref[k : k + 1, :], 1.0, 0.0).astype(bf16) for k in range(EXPERTS)
    ]
    for k in range(EXPERTS):
        hits = all_hits[k]
        refs[k][:CAP, :] = mm(hits, v_ref[...]).astype(bf16)
        if gated:
            moved = mm_nt(gate_ref[...], hits)
            row = lax.broadcasted_iota(jnp.int32, moved.shape, 0) % NCH
            moved = jnp.where(row == (mine_ref[0] ^ k), moved, 0.0)
            high = jnp.sum(moved[:NCH], axis=0, keepdims=True)
            rest = jnp.sum(moved[NCH:], axis=0, keepdims=True)
            tail = jnp.concatenate(
                [high, rest, jnp.zeros((EXTRA - 2, CAP), f32)], axis=0
            ).astype(bf16)
            refs[k][CAP:, :CAP] = tail
            refs[k][CAP:, CAP:] = jnp.zeros((EXTRA, D - CAP), bf16)


def dispatch_call(mine, spot, values, gates=None, after=()):
    size = CAP + (0 if gates is None else EXTRA)
    operands = [mine, spot, values] + ([] if gates is None else [gates])
    rows = values.shape[0]
    return launch(
        partial(dispatch_kernel, gates is not None),
        operands,
        [SMEM] + [VM] * (len(operands) - 1),
        [VM] * EXPERTS,
        [jax.ShapeDtypeStruct((size, D), bf16)] * EXPERTS,
        after,
        cost_estimate=cost(2 * rows * D * CAP * EXPERTS, 2 * rows * D + 2 * EXPERTS * CAP * D),
        name="dispatch",
    )


class Plan:
    def __init__(self, replicas, shards, shard, hidden, chunks):
        self.copies = replicas // EXPERTS
        self.shards = shards
        self.shard = shard
        self.hidden = hidden
        self.chunks = chunks
        self.seg = hidden // (shards * self.copies * chunks)
        self.width = self.seg * shards
        self.wide = min(256, self.width)
        self.tiles = self.width // self.wide
        self.spans = self.wide // self.seg
        self.downs = D // self.wide
        self.rows = 2 * self.tiles * shard + self.downs * self.seg

    def column(self, half, tile, span, part, chunk):
        z = tile * self.spans + span
        base = half * self.hidden + z * (self.hidden // self.shards)
        return base + (chunk * self.copies + part) * self.seg

    def down_row(self, part, chunk):
        return (chunk * self.copies + part) * self.seg


def pack_kernel(plan, who_ref, in_ref, out_ref, *packs):
    mine, part = who_ref[0], who_ref[1]
    seg, shard = plan.seg, plan.shard
    step = pl.program_id(0)
    half, z = step // plan.shards, step % plan.shards
    row = pl.multiple_of((half * plan.tiles + z // plan.spans) * shard, shard)
    column = pl.multiple_of(z % plan.spans * seg, seg)
    for e in range(EXPERTS):

        @pl.when(mine == e)
        def _(e=e):
            value = in_ref[:, e, :]
            for chunk in range(plan.chunks):
                at = chunk * plan.copies * seg
                piece = value[:, at : at + seg]
                for p in range(1, plan.copies):
                    at = (chunk * plan.copies + p) * seg
                    piece = jnp.where(part == p, value[:, at : at + seg], piece)
                packs[chunk][pl.ds(row, shard), pl.ds(column, seg)] = piece

        @pl.when((mine == e) & (step == 0))
        def _(e=e):
            for chunk in range(plan.chunks):
                start = 2 * plan.tiles * shard
                at = pl.multiple_of(plan.down_row(part, chunk), seg)
                value = out_ref[pl.ds(at, seg), e, :]
                for down in range(plan.downs):
                    packs[chunk][start + down * seg : start + (down + 1) * seg, :] = value[
                        :, down * plan.wide : (down + 1) * plan.wide
                    ]


def pack_pieces(plan, who, expert_in, expert_out, after):
    if plan.seg % LANES == 0:
        per = plan.hidden // plan.shards
        return launch(
            partial(pack_kernel, plan),
            [who, expert_in, expert_out],
            [
                SMEM,
                pl.BlockSpec((plan.shard, EXPERTS, per), lambda i: (0, 0, i)),
                whole(expert_out.shape),
            ],
            [whole((plan.rows, plan.wide))] * plan.chunks,
            [jax.ShapeDtypeStruct((plan.rows, plan.wide), bf16)] * plan.chunks,
            after,
            grid=(2 * plan.shards,),
            compiler_params=params(VMEM_BYTES),
            cost_estimate=cost(0, 0),
            name="pack",
        )
    mine, part = who[0], who[1:]
    own_in = lax.dynamic_index_in_dim(expert_in, mine, 1, keepdims=False)
    own_out = lax.dynamic_index_in_dim(expert_out, mine, 1, keepdims=False)
    packs = []
    for chunk in range(plan.chunks):
        blocks = []
        for half in range(2):
            for tile in range(plan.tiles):
                spans = [
                    lax.dynamic_slice_in_dim(
                        own_in, plan.column(half, tile, span, part[0], chunk), plan.seg, 1
                    )
                    for span in range(plan.spans)
                ]
                blocks.append(jnp.concatenate(spans, axis=1))
        rows = lax.dynamic_slice_in_dim(own_out, plan.down_row(part[0], chunk), plan.seg, 0)
        blocks += [rows[:, d * plan.wide : (d + 1) * plan.wide] for d in range(plan.downs)]
        packs.append(jnp.concatenate(blocks, axis=0))
    return packs


def unpack_kernel(plan, begun, who_ref, *refs):
    copies, seg = plan.copies, plan.seg
    ins, downs = refs[:copies], refs[copies : 2 * copies]
    in_out, down_out = refs[2 * copies + 2 * begun :]
    mine, part = who_ref[0], who_ref[1]
    step = pl.program_id(0)
    z = step % plan.shards

    def of_replica(arrays, p, index):
        chosen = arrays[0][index].astype(f32)
        for m in range(1, copies):
            chosen = jnp.where(part == (p ^ m), arrays[m][index].astype(f32), chosen)
        return chosen

    for j in range(EXPERTS):
        for p in range(copies):
            chosen = of_replica(ins, p, j ^ mine)
            piece = chosen[:, :seg]
            for span in range(1, plan.spans):
                here = z % plan.spans == span
                piece = jnp.where(here, chosen[:, span * seg : (span + 1) * seg], piece)
            in_out[:, j, p * seg : (p + 1) * seg] = piece

    rows = down_out.shape[0]
    p, at = step // (seg // rows), step % (seg // rows) * rows
    for j in range(EXPERTS):
        for down in range(plan.downs):
            span = pl.ds(pl.multiple_of(down * seg + at, rows), rows)
            chosen = downs[0][j ^ mine, span, :].astype(f32)
            for m in range(1, copies):
                chosen = jnp.where(
                    part == (p ^ m), downs[m][j ^ mine, span, :].astype(f32), chosen
                )
            down_out[:, j, down * plan.wide : (down + 1) * plan.wide] = chosen


def unpack_chunk(plan, who, chunk, sums, begun):
    copies, shards = plan.copies, plan.shards
    per = plan.hidden // shards
    start = 2 * plan.tiles * plan.shard
    down_rows = plan.downs * plan.seg
    both = copies * plan.seg

    def in_block(i):
        return (0, i // shards * plan.tiles + i % shards // plan.spans, 0)

    down_in = pl.BlockSpec(
        (EXPERTS, down_rows, plan.wide),
        lambda i: (0, start // down_rows, 0),
        pipeline_mode=pl.Buffered(1),
    )
    hbm = pl.BlockSpec(memory_space=pl.ANY)
    operands = [who, *sums, *sums, *begun]
    return launch(
        partial(unpack_kernel, plan, len(begun) // 2),
        operands,
        [SMEM]
        + [pl.BlockSpec((EXPERTS, plan.shard, plan.wide), in_block)] * copies
        + [down_in] * copies
        + [hbm] * len(begun),
        [
            pl.BlockSpec((plan.shard, EXPERTS, both), lambda i: (0, 0, i * plan.chunks + chunk)),
            pl.BlockSpec(
                (both // (2 * shards), EXPERTS, D), lambda i: (chunk * 2 * shards + i, 0, 0)
            ),
        ],
        [
            jax.ShapeDtypeStruct((plan.shard, EXPERTS, 2 * plan.hidden), f32),
            jax.ShapeDtypeStruct((per, EXPERTS, D), f32),
        ],
        grid=(2 * shards,),
        input_output_aliases={len(operands) - 2 + i: i for i in range(len(begun))},
        compiler_params=params(VMEM_BYTES),
        cost_estimate=cost(0, 12 * plan.shard * plan.hidden * EXPERTS),
        name="unpack",
    )


def unpack_grads(plan, who, sums, begun):
    if begun:
        for chunk in range(1, plan.chunks):
            begun = unpack_chunk(plan, who, chunk, sums[chunk], begun)
        return begun
    mine, part = who[0], who[1]
    ins, outs = [], []
    for j in range(EXPERTS):
        columns = {}
        rows = []
        for chunk in range(plan.chunks):
            for p in range(plan.copies):
                stacked = jnp.stack(sums[chunk])
                piece = lax.dynamic_index_in_dim(stacked, part ^ p, 0, keepdims=False)
                piece = lax.dynamic_index_in_dim(piece, mine ^ j, 0, keepdims=False)
                for half in range(2):
                    for tile in range(plan.tiles):
                        row = (half * plan.tiles + tile) * plan.shard
                        for span in range(plan.spans):
                            columns[plan.column(half, tile, span, p, chunk)] = piece[
                                row : row + plan.shard, span * plan.seg : (span + 1) * plan.seg
                            ]
                row = 2 * plan.tiles * plan.shard
                rows.append(
                    jnp.concatenate(
                        [
                            piece[row + d * plan.seg : row + (d + 1) * plan.seg]
                            for d in range(plan.downs)
                        ],
                        axis=1,
                    )
                )
        ins.append(jnp.concatenate([columns[c] for c in sorted(columns)], axis=1))
        outs.append(jnp.concatenate(rows, axis=0))
    return jnp.stack(ins, axis=1).astype(f32), jnp.stack(outs, axis=1).astype(f32)


def weight_grads(plan, part, xt, ds, act, grad_gate, grad_up, grads):
    shard, seg, wide, tiles = plan.shard, plan.seg, plan.wide, plan.tiles
    for half, source in ((0, grad_gate), (1, grad_up)):
        for tile in range(tiles):
            made = mm(xt[...], source[part, :, tile * wide : (tile + 1) * wide]).astype(bf16)
            row = (half * tiles + tile) * shard
            for z in range(plan.shards):
                grads[part, z, row : row + shard, :] = made[z * shard : (z + 1) * shard, :]
    for tile in range(tiles):
        made = mm_tn(act[part, :, tile * wide : (tile + 1) * wide], ds[...]).astype(bf16)
        for span in range(plan.spans):
            z = tile * plan.spans + span
            for down in range(plan.downs):
                row = 2 * tiles * shard + down * seg
                grads[part, z, row : row + seg, :] = made[
                    span * seg : (span + 1) * seg, down * wide : (down + 1) * wide
                ]


def expert_kernel(plan, first, last, *refs):
    refs = list(refs)

    def take(n):
        out = refs[:n]
        del refs[:n]
        return out

    copies = plan.copies
    x_refs, y_refs = take(EXPERTS), take(EXPERTS)
    w_refs = take(copies)
    if first:
        carry_in = []
    else:
        carry_in = take(2)
        (ds,) = take(1)
    if last:
        dx_outs, ret_outs, saved = take(EXPERTS), take(EXPERTS), take(3)
    else:
        grad_outs, carry_out, saved = take(copies), take(2), take(2)
    xs, gcol, ret_acc, dx_acc, act_s, dg_s, du_s = take(7)
    waiting = [take(3), take(3)]
    if last:
        y_held, sems = refs
    else:
        ds, xt, grads, sems = refs
    shard, seg, wide, tiles = plan.shard, plan.seg, plan.wide, plan.tiles
    started = []

    def copy(src, dst):
        made = pltpu.make_async_copy(src, dst, sems.at[len(started)])
        started.append(made)
        made.start()
        return made

    carries = [copy(src, dst) for src, dst in zip(carry_in, (ret_acc, dx_acc))]
    if last:
        held = [
            copy(y_refs[k].at[pl.ds(0, CAP)], y_held.at[pl.ds(k * CAP, CAP)])
            for k in range(EXPERTS)
        ]
    for k in range(EXPERTS):
        span = slice(k * CAP, (k + 1) * CAP)
        x = x_refs[k][:CAP, :]
        xs[span, :] = x
        extra = x_refs[k][CAP:, :CAP].astype(f32)
        gate = (extra[0:1] + extra[1:2]).T
        gcol[span, :] = jnp.broadcast_to(gate, (CAP, LANES))
        if not last:
            xt[:, span] = x.astype(f32).T.astype(bf16)
            ds[span, :] = (y_refs[k][:CAP, :].astype(f32) * gate).astype(bf16)
    sends = []
    if not last:
        sends = [copy(src, dst) for src, dst in zip((xt, ds), saved, strict=True)]
    if first:
        ret_acc[...] = jnp.zeros_like(ret_acc)
        dx_acc[...] = jnp.zeros_like(dx_acc)

    def columns(part, half, tile):
        row = (half * tiles + tile) * shard
        return w_refs[part][:, row : row + shard, :].reshape(D, wide)

    def down_columns(part, down):
        row = 2 * tiles * shard + down * seg
        return w_refs[part][:, row : row + seg, :].reshape(plan.width, wide)

    def products(part, b, held):
        span = slice(b * CAP, (b + 1) * CAP)
        x, d = xs[span, :], ds[span, :]
        for tile in range(tiles):
            at = slice(tile * wide, (tile + 1) * wide)
            held[0][:, at] = mm(x, columns(part, 0, tile))
            held[1][:, at] = mm(x, columns(part, 1, tile))
        grad = 0.0
        for down in range(plan.downs):
            grad = grad + mm_nt(
                d[:, down * wide : (down + 1) * wide], down_columns(part, down)
            )
        held[2][...] = grad

    def gating(part, b, held):
        span = slice(b * CAP, (b + 1) * CAP)
        gate, up, grad_act = held[0][...], held[1][...], held[2][...]
        sig = 1.0 / (1.0 + jnp.exp(-gate))
        silu = gate * sig
        act_s[part, span, :] = (silu * up).astype(bf16)
        du_s[part, span, :] = (grad_act * silu).astype(bf16)
        dg_s[part, span, :] = (grad_act * up * (sig + silu * (1.0 - sig))).astype(bf16)

    def back(part, b):
        span = slice(b * CAP, (b + 1) * CAP)
        act = act_s[part, span, :]
        for down in range(plan.downs):
            ret_acc[span, down * wide : (down + 1) * wide] += mm(act, down_columns(part, down))
        total = 0.0
        for tile in range(tiles):
            at = slice(tile * wide, (tile + 1) * wide)
            total = total + mm_nt(dg_s[part, span, at], columns(part, 0, tile))
            total = total + mm_nt(du_s[part, span, at], columns(part, 1, tile))
        dx_acc[span, :] += total

    for part in range(copies):
        products(part, 0, waiting[0])
        for b in range(EXPERTS):
            if b + 1 < EXPERTS:
                products(part, b + 1, waiting[(b + 1) % 2])
            gating(part, b, waiting[b % 2])
            if b > 0:
                if part == 0 and b == 1:
                    for made in carries:
                        made.wait()
                back(part, b - 1)
        back(part, EXPERTS - 1)
        if last:
            sends += [
                copy(src.at[part], dst.at[part])
                for src, dst in zip((act_s, dg_s, du_s), saved, strict=True)
            ]
        else:
            if part == copies - 1:
                sends += [
                    copy(src, dst) for src, dst in zip((ret_acc, dx_acc), carry_out, strict=True)
                ]
            weight_grads(plan, part, xt, ds, act_s, dg_s, du_s, grads)
            sends.append(copy(grads.at[part], grad_outs[part]))
    if last:
        for made in held:
            made.wait()
        for k in range(EXPERTS):
            span = slice(k * CAP, (k + 1) * CAP)
            ret = ret_acc[span, :]
            dgate = jnp.sum(ret * y_held[span, :].astype(f32), axis=-1, keepdims=True)
            dgate = jnp.broadcast_to(dgate, (CAP, LANES)).T[:1]
            ret_outs[k][...] = (ret * gcol[span, :1]).astype(bf16)
            dx_outs[k][:CAP, :] = dx_acc[span, :].astype(bf16)
            high = dgate.astype(bf16).astype(f32)
            tail = jnp.concatenate(
                [high, dgate - high, jnp.zeros((EXTRA - 2, CAP), f32)], axis=0
            ).astype(bf16)
            dx_outs[k][CAP:, :CAP] = tail
            dx_outs[k][CAP:, CAP:] = jnp.zeros((EXTRA, D - CAP), bf16)
    for made in sends:
        made.wait()


def expert_call(plan, xs, ys, weights, chunk, carried):
    first, last = chunk == 0, chunk == plan.chunks - 1
    rows = EXPERTS * CAP
    hbm = pl.BlockSpec(memory_space=pl.ANY)
    copies = plan.copies
    block = pl.BlockSpec(
        (plan.shards, plan.rows, plan.wide),
        lambda i: (0, 0, 0),
        pipeline_mode=pl.Buffered(1),
    )
    in_specs = [whole(a.shape) for a in xs]
    in_specs += [hbm if last else whole(a.shape) for a in ys] + [block] * copies
    operands = list(xs) + list(ys) + list(weights)
    if not first:
        in_specs += [hbm] * 2 + [whole((rows, D))]
        operands += list(carried)
    held = jax.ShapeDtypeStruct((copies, rows, plan.width), bf16)
    if last:
        out_specs = [whole((CAP + EXTRA, D))] * EXPERTS + [whole((CAP, D))] * EXPERTS
        out_shape = [jax.ShapeDtypeStruct((CAP + EXTRA, D), bf16)] * EXPERTS
        out_shape += [jax.ShapeDtypeStruct((CAP, D), bf16)] * EXPERTS
        out_specs += [hbm] * 3
        out_shape += [held] * 3
    else:
        out_specs = [hbm] * (copies + 4)
        out_shape = [jax.ShapeDtypeStruct((plan.shards, plan.rows, plan.wide), bf16)] * copies
        out_shape += [jax.ShapeDtypeStruct((rows, D), f32)] * 2
        out_shape += [
            jax.ShapeDtypeStruct((D, rows), bf16),
            jax.ShapeDtypeStruct((rows, D), bf16),
        ]
    scratch = [
        pltpu.VMEM((rows, D), bf16),
        pltpu.VMEM((rows, LANES), f32),
        pltpu.VMEM((rows, D), f32),
        pltpu.VMEM((rows, D), f32),
    ]
    scratch += [pltpu.VMEM((copies, rows, plan.width), bf16)] * 3
    scratch += [pltpu.VMEM((CAP, plan.width), f32)] * 6
    if last:
        scratch.append(pltpu.VMEM((rows, D), bf16))
    else:
        scratch += [
            pltpu.VMEM((rows, D), bf16),
            pltpu.VMEM((D, rows), bf16),
            pltpu.VMEM((copies, plan.shards, plan.rows, plan.wide), bf16),
        ]
    scratch.append(pltpu.SemaphoreType.DMA((6 + 3 * copies,)))
    return pl.pallas_call(
        partial(expert_kernel, plan, first, last),
        grid=(1,),
        in_specs=in_specs,
        out_specs=out_specs,
        out_shape=out_shape,
        scratch_shapes=scratch,
        compiler_params=params(VMEM_BYTES),
        cost_estimate=cost(
            18 * rows * D * plan.width * copies, 12 * D * plan.width * copies + 12 * rows * D
        ),
        name="experts",
    )(*operands)


def expert_grads_kernel(plan, act, grad_gate, grad_up, xt, ds, *refs):
    outs, (grads, sems) = refs[: plan.copies], refs[plan.copies :]
    sends = []
    for part in range(plan.copies):
        weight_grads(plan, part, xt, ds, act, grad_gate, grad_up, grads)
        sends.append(pltpu.make_async_copy(grads.at[part], outs[part], sems.at[part]))
        sends[-1].start()
    for made in sends:
        made.wait()


def expert_grads(plan, held):
    copies = plan.copies
    packed = (plan.shards, plan.rows, plan.wide)
    return launch(
        partial(expert_grads_kernel, plan),
        list(held),
        [whole(a.shape) for a in held],
        [pl.BlockSpec(memory_space=pl.ANY)] * copies,
        [jax.ShapeDtypeStruct(packed, bf16)] * copies,
        grid=(1,),
        scratch_shapes=[
            pltpu.VMEM((copies, *packed), bf16),
            pltpu.SemaphoreType.DMA((copies,)),
        ],
        compiler_params=params(VMEM_BYTES),
        cost_estimate=cost(0, 0),
        name="expert_grads",
    )


def spots_of(place_ref, rows):
    slot = lax.broadcasted_iota(jnp.int32, (rows, EXPERTS * CAP), 1)
    hit = (slot == place_ref[:, 0:1]) | (slot == place_ref[:, 1:2])
    return jnp.where(hit, 1.0, 0.0).astype(bf16)


def constant_gates(one, chosen, m):
    a0 = one[:, NCH + 2 * m : NCH + 2 * m + 1]
    a1 = one[:, NCH + 2 * m + 1 : NCH + 2 * m + 2]
    gate = chosen[:, EXPERTS + 2 + m : EXPERTS + 3 + m]
    return gate, a0, a1


def side_kernel(
    res_ref, dy_ref, one_ref, place_ref, choice_ref, small_ref, two_ref, spots_ref, cvec_out
):
    @pl.when(pl.program_id(0) == 0)
    def _():
        cvec_out[...] = jnp.zeros_like(cvec_out)

    res = res_ref[...]
    one = one_ref[...]
    lane = lanes_of(one.shape)
    named = selected(choice_ref, lane)
    chosen = jnp.where(named, one, 0.0)
    is_mix = (lane >= NCH) & (lane < NCH + 4)
    spots_ref[...] = spots_of(place_ref, res.shape[0])
    inverse = lax.rsqrt(jnp.mean(res * res, axis=-1, keepdims=True) + EPS)
    dy = dy_ref[...]
    spread = res * inverse * row_of(small_ref, GAIN_F)
    hd = jnp.sum(spread * dy.astype(f32), axis=-1, keepdims=True)
    cd = mm_nt(dy, small_ref[...])
    coef = chosen[:, EXPERTS + 1 : EXPERTS + 2]
    grads = jnp.where(lane == EXPERTS + 1, hd, 0.0)
    made = jnp.zeros_like(one)
    for m in range(2):
        gate, a0, a1 = constant_gates(one, chosen, m)
        dot = cd[:, CVEC + m : CVEC + m + 1]
        coef = coef + gate * a0
        grads = jnp.where(lane == EXPERTS + 2 + m, a0 * hd + a1 * dot, grads)
        grads = jnp.where(lane == NCH + 2 * m, gate * hd, grads)
        grads = jnp.where(lane == NCH + 2 * m + 1, gate * dot, grads)
        made = jnp.where(lane == m, gate * a1, made)
    two = jnp.where(is_mix | named, grads, 0.0)
    two = jnp.where(lane == COEF, coef, two)
    two_ref[...] = jnp.where(lane == INVERSE, inverse, two)
    high = made.astype(bf16)
    rest = (made - high.astype(f32)).astype(bf16)
    cvec_out[...] += mm_tn(high, dy) + mm_tn(rest, dy)


def side_call(res, dy, one, places, choices, small):
    rows = res.shape[0]
    block = 256
    return launch(
        side_kernel,
        [res, dy, one, places, choices, small],
        [rows_of(block, D)] * 2
        + [rows_of(block, LANES)]
        + [rows_of(block, 2)] * 2
        + [whole(small.shape)],
        [rows_of(block, LANES), rows_of(block, EXPERTS * CAP), whole((LANES, D))],
        [
            jax.ShapeDtypeStruct((rows, LANES), f32),
            jax.ShapeDtypeStruct((rows, EXPERTS * CAP), bf16),
            jax.ShapeDtypeStruct((LANES, D), f32),
        ],
        grid=(rows // block,),
        compiler_params=params(VMEM_BYTES),
        cost_estimate=cost(0, 0),
        name="side",
    )


def back_kernel(
    count,
    who_ref,
    res_ref,
    h_ref,
    dy_ref,
    one_ref,
    two_ref,
    spots_ref,
    prev_ref,
    wsmall_ref,
    *refs,
):
    dx_refs, refs = refs[:EXPERTS], refs[EXPERTS:]
    pieces, refs = refs[:count], refs[count:]
    (
        dres_ref,
        branch_ref,
        dctx_ref,
        dsmall_ref,
        gain_out,
        prev_out,
        w_ref,
        dg_ref,
    ) = refs

    @pl.when(pl.program_id(0) == 0)
    def _():
        gain_out[...] = jnp.zeros_like(gain_out)
        prev_out[...] = jnp.zeros_like(prev_out)
        dsmall_ref[...] = jnp.zeros_like(dsmall_ref)
        lay_columns(w_ref, pieces, who_ref[1])
        lane = lanes_of((CAP, LANES))
        for k in range(EXPERTS):
            columns = dx_refs[k][CAP:, :CAP].astype(f32).T
            at = who_ref[0] ^ k
            made = jnp.where(lane == at, columns[:, 0:1], 0.0)
            made = jnp.where(lane == at + 16, columns[:, 1:2], made)
            dg_ref[k * CAP : (k + 1) * CAP, :] = made.astype(bf16)

    gain = row_of(wsmall_ref, GAIN_F)
    lane = lanes_of((SUB, LANES))
    choice = lane < NCH
    is_mix = (lane >= NCH) & (lane < NCH + 4)

    def gather(span):
        spots = spots_ref[span, :]
        from_experts = mm(spots, dg_ref[...])
        moved = mm(spots[:, :CAP], dx_refs[0][:CAP, :])
        for k in range(1, EXPERTS):
            moved = moved + mm(spots[:, k * CAP : (k + 1) * CAP], dx_refs[k][:CAP, :])
        return from_experts, moved

    def route(span, from_experts, moved):
        one, two = one_ref[span, :], two_ref[span, :]
        from_experts = from_experts + pltpu.roll(from_experts, LANES - 16, 1)
        grads = jnp.where(lane < EXPERTS, from_experts, jnp.where(lane < NCH + 4, two, 0.0))
        weighted = one * grads
        mean_choice = jnp.sum(jnp.where(choice, weighted, 0.0), axis=-1, keepdims=True)
        d_logits = jnp.where(choice, one * (grads - mean_choice), 0.0)
        d_mix = one * (grads - (weighted + partner(weighted, lane)))
        low = jnp.where(choice, d_logits, jnp.where(is_mix, d_mix, 0.0)).astype(bf16)
        high = d_logits.astype(bf16)
        rest = (d_logits - high.astype(f32)).astype(bf16)
        return low, high, rest, moved + mm(low, wsmall_ref[...])

    def norm(span, low, high, rest, moved):
        two = two_ref[span, :]
        coef, inverse = two[:, COEF : COEF + 1], two[:, INVERSE : INVERSE + 1]
        res = res_ref[span, :]
        dyf = dy_ref[span, :].astype(f32)
        spread_grad = moved + coef * dyf
        scaled = spread_grad * gain
        mean_dot = jnp.mean(res * scaled, axis=-1, keepdims=True)
        d_res = dyf + inverse * scaled - res * (inverse * inverse * inverse * mean_dot)
        dres_ref[span, :] = d_res
        branch = d_res.astype(bf16)
        branch_ref[span, :] = branch
        by_gain = jnp.sum(spread_grad * (res * inverse), axis=0, keepdims=True)
        return low, high, rest, branch, by_gain

    def project(span, low, high, rest, branch, by_gain):
        dctx_ref[span, :] = mm_nt(branch, w_ref[...]).astype(bf16)
        prev = prev_ref[:, span]
        by_prev = mm(prev, high) + mm(prev, rest)
        return mm_tn(low, h_ref[span, :]), by_gain, by_prev

    for by_small, by_gain, by_prev in staged(res_ref.shape[0], SUB, gather, route, norm, project):
        dsmall_ref[...] += by_small
        gain_out[...] += by_gain
        prev_out[...] += by_prev


def back_call(who, res, h, dy, one, two, spots, prev, small, dx, pieces, after):
    rows = res.shape[0]
    block = 512
    return launch(
        partial(back_kernel, len(pieces)),
        [who, res, h, dy, one, two, spots, prev, small, *dx, *pieces],
        [SMEM]
        + [rows_of(block, D)] * 3
        + [rows_of(block, LANES)] * 2
        + [rows_of(block, EXPERTS * CAP)]
        + [pl.BlockSpec((NCH, block), lambda i: (0, i))]
        + [whole(a.shape) for a in (small, *dx, *pieces)],
        [rows_of(block, D)] * 3
        + [whole((LANES, D)), whole((1, D)), whole((NCH, LANES))],
        [
            jax.ShapeDtypeStruct((rows, D), f32),
            jax.ShapeDtypeStruct((rows, D), bf16),
            jax.ShapeDtypeStruct((rows, D), bf16),
            jax.ShapeDtypeStruct((LANES, D), f32),
            jax.ShapeDtypeStruct((1, D), f32),
            jax.ShapeDtypeStruct((NCH, LANES), f32),
        ],
        after,
        grid=(rows // block,),
        scratch_shapes=[pltpu.VMEM((D, D), bf16), pltpu.VMEM((EXPERTS * CAP, LANES), bf16)],
        compiler_params=params(VMEM_BYTES),
        cost_estimate=cost(BACK * 2 * rows * D * (D + 2048), BACK * 20 * rows * D),
        name="combine_back",
    )


def finish_kernel(res_ref, one_ref, spots_ref, choice_ref, small_ref, *refs):
    ret_refs, out_ref = refs[:EXPERTS], refs[EXPERTS]
    res = res_ref[...]
    one = one_ref[...]
    lane = lanes_of(one.shape)
    chosen = jnp.where(selected(choice_ref, lane), one, 0.0)
    inverse = lax.rsqrt(jnp.mean(res * res, axis=-1, keepdims=True) + EPS)
    total = res
    coef = chosen[:, EXPERTS + 1 : EXPERTS + 2]
    for m in range(2):
        gate, a0, a1 = constant_gates(one, chosen, m)
        coef = coef + gate * a0
        total = total + (gate * a1) * row_of(small_ref, CVEC + m)
    total = total + (coef * inverse) * res * row_of(small_ref, GAIN_F)
    spots = spots_ref[...]
    for k in range(EXPERTS):
        total = total + mm(spots[:, k * CAP : (k + 1) * CAP], ret_refs[k][...])
    out_ref[...] = total.astype(bf16)


def finish_call(res, one, spots, choices, small, ret, after):
    rows = res.shape[0]
    block = 256
    return launch(
        finish_kernel,
        [res, one, spots, choices, small, *ret],
        [rows_of(block, D), rows_of(block, LANES)]
        + [rows_of(block, EXPERTS * CAP), rows_of(block, 2)]
        + [whole(a.shape) for a in (small, *ret)],
        rows_of(block, D),
        jax.ShapeDtypeStruct((rows, D), bf16),
        after,
        grid=(rows // block,),
        compiler_params=params(VMEM_BYTES),
        cost_estimate=cost(2 * rows * D * 1536, 10 * rows * D),
        name="layer_out",
    )


def turn_kernel(count, *refs):
    for source, out in zip(refs[:count], refs[count:], strict=True):
        out[...] = source[...].astype(f32).T.astype(bf16)


def turn_call(arrays):
    rows, columns = arrays[0].shape
    return launch(
        partial(turn_kernel, len(arrays)),
        arrays,
        [pl.BlockSpec((rows, 256), lambda i: (0, i))] * len(arrays),
        [pl.BlockSpec((256, rows), lambda i: (i, 0))] * len(arrays),
        [jax.ShapeDtypeStruct((columns, rows), bf16)] * len(arrays),
        grid=(columns // 256,),
        compiler_params=params(VMEM_BYTES),
        cost_estimate=cost(0, 0),
        name="turn",
    )


def dense_kernel(copies, each, own, part_ref, mine_ref, ht_ref, ct_ref, *refs):
    rights, refs = refs[:4], refs[4:]
    step = pl.program_id(0)
    if own:
        got, outs, total_ref = refs[: copies - 1], refs[copies - 1 : -1], refs[-1]
    else:
        outs = refs
    per = pl.num_programs(0) if own else pl.num_programs(0) // (copies - 1)
    source = (part_ref[0] if own else (step // per + 1) ^ part_ref[0]) * per + step % per
    for index, right in enumerate(rights):
        left = ct_ref if index == 3 else ht_ref

        @pl.when(source // each == index)
        def _(left=left, right=right):
            made = mm(left[...], right[...])
            if own:
                for ref in got:
                    made = made + ref[...].astype(f32)
                total_ref[...] = made.astype(bf16).reshape(total_ref.shape)
            else:
                for m, out in enumerate(outs):
                    if len(outs) == 1:
                        out[...] = made.astype(bf16)
                    else:

                        @pl.when(step // per == m)
                        def _(out=out):
                            out[...] = made.astype(bf16)

    if own:
        for k, out in enumerate(outs):
            out[...] = total_ref[:, mine_ref[0] ^ k]


def dense_call(copies, shards, part, mine, ht, ct, rights, got=None):
    rows = ht.shape[1]
    cut = 4 * D // copies
    step = D // 2 if cut % D == 0 else cut
    per = cut // step
    each = D // step
    quarter = D // (shards * EXPERTS)
    own = got is not None

    def right_block(index):
        def block(i, part_ref, mine_ref):
            replica = part_ref[0] if own else (i // per + 1) ^ part_ref[0]
            return (0, jnp.clip(replica * per + i % per - each * index, 0, each - 1))

        return block

    def other_block(m):
        return lambda i, *_: (0, jnp.clip(i - m * per, 0, per - 1))

    def fixed(shape):
        return pl.BlockSpec(shape, lambda i, *_: (0, 0), pipeline_mode=pl.Buffered(1))

    in_specs = [fixed(ht.shape), fixed(ct.shape)]
    in_specs += [pl.BlockSpec((rows, step), right_block(index)) for index in range(4)]
    if own:
        in_specs += [pl.BlockSpec((D, step), lambda i, *_: (0, i))] * (copies - 1)
        out_specs = [pl.BlockSpec((shards, quarter, step), lambda i, *_: (0, 0, i))] * EXPERTS
        out_shape = [jax.ShapeDtypeStruct((shards, quarter, cut), bf16)] * EXPERTS
        scratch = [pltpu.VMEM((shards, EXPERTS, quarter, step), bf16)]
    else:
        out_specs = [pl.BlockSpec((D, step), other_block(m)) for m in range(copies - 1)]
        out_shape = [jax.ShapeDtypeStruct((D, cut), bf16)] * (copies - 1)
        scratch = []
    return pl.pallas_call(
        partial(dense_kernel, copies, each, own),
        grid_spec=pltpu.PrefetchScalarGridSpec(
            num_scalar_prefetch=2,
            grid=(per if own else per * (copies - 1),),
            in_specs=in_specs,
            out_specs=out_specs,
            scratch_shapes=scratch,
        ),
        out_shape=out_shape,
        compiler_params=params(VMEM_BYTES),
        cost_estimate=cost(8 * rows * D * D, 12 * rows * D + 8 * D * D),
        name="dense_own" if own else "dense_others",
    )(part, mine, ht, ct, *rights, *(got or ()))


def fold_quarters_kernel(count, zi_ref, small_ref, *refs):
    pieces, outs = refs[:count], refs[count:]
    rows, cut = pieces[0].shape[1:]
    spare = outs[0].shape[0] - rows
    for k, out in enumerate(outs):
        at = lax.rem(zi_ref[0] + k, len(outs))
        total = pieces[0][at].astype(f32)
        for piece in pieces[1:]:
            total = total + piece[at].astype(f32)
        out[:rows, :] = total.astype(bf16)
        for c in range(cut // LANES):
            out[rows:, c * LANES : (c + 1) * LANES] = small_ref[at, c * spare : (c + 1) * spare, :]


def fold_quarters(zi, small, pieces, after=()):
    shards, rows, cut = pieces[0].shape
    spare = D // shards * LANES // cut
    return launch(
        partial(fold_quarters_kernel, len(pieces)),
        [zi, small.reshape(shards, D // shards, LANES), *pieces],
        [SMEM] + [VM] * (len(pieces) + 1),
        [VM] * shards,
        [jax.ShapeDtypeStruct((rows + spare, cut), bf16)] * shards,
        after,
        compiler_params=pltpu.CompilerParams(vmem_limit_bytes=VMEM_BYTES),
        name="fold_quarters",
    )


def lay_tail_kernel(count, rows, own_ref, *refs):
    pieces, out = refs[:count], refs[count]
    total = pieces[0][rows:, :].astype(f32)
    for k in range(count):
        at = pl.multiple_of((own_ref[0] ^ k) * rows, rows)
        out[pl.ds(at, rows), :] = pieces[k][:rows, :]
        if k:
            total = total + pieces[k][rows:, :].astype(f32)
    out[count * rows :, :] = total.astype(bf16)


def lay_tail(own, pieces, rows, after):
    count = len(pieces)
    size, cut = pieces[0].shape
    return launch(
        partial(lay_tail_kernel, count, rows),
        [own, *pieces],
        [SMEM] + [VM] * count,
        VM,
        jax.ShapeDtypeStruct((count * rows + size - rows, cut), bf16),
        after,
        compiler_params=pltpu.CompilerParams(vmem_limit_bytes=VMEM_BYTES),
        name="lay_tail",
    )


def fold_copies(pieces):
    total = pieces[0].astype(f32)
    for piece in pieces[1:]:
        total = total + piece.astype(f32)
    return total.astype(bf16)


def fold_shards_kernel(*refs):
    total = refs[0][...].astype(f32)
    for ref in refs[1:-1]:
        total = total + ref[...].astype(f32)
    refs[-1][...] = total.astype(bf16)


def fold_shards(pieces):
    return launch(
        fold_shards_kernel,
        pieces,
        [VM] * len(pieces),
        VM,
        jax.ShapeDtypeStruct(pieces[0].shape, bf16),
        compiler_params=pltpu.CompilerParams(vmem_limit_bytes=VMEM_BYTES),
        name="fold_shards",
    )


def unpack_dense_kernel(count, rows, part_ref, *refs):
    pieces = refs[:count]
    qkv_ref, proj_ref, router_ref, mix_ref, cvec_ref, gain_a_ref, gain_f_ref, prev_ref = refs[count:-1]
    small_ref = refs[-1]
    cut = pieces[0].shape[1]
    small = pieces[0][rows:, :].astype(f32)
    for piece in pieces[1:]:
        small = small + piece[rows:, :].astype(f32)
    spare = small.shape[0]
    for c in range(cut // LANES):
        small_ref[c * spare : (c + 1) * spare, :] = small[:, c * LANES : (c + 1) * LANES]
    turned = small_ref[...].T
    router_ref[...] = turned[:NCH]
    mix_ref[...] = turned[NCH:CVEC]
    cvec_ref[...] = turned[CVEC:GAIN_A]
    gain_a_ref[...] = turned[GAIN_A:GAIN_F]
    gain_f_ref[...] = turned[GAIN_F : GAIN_F + 1]
    prev_ref[...] = small_ref[: prev_ref.shape[0], 16 : 16 + NCH]
    for p in range(count):
        chosen = pieces[0][:rows, :].astype(f32)
        for m in range(1, count):
            chosen = jnp.where(part_ref[0] == (p ^ m), pieces[m][:rows, :].astype(f32), chosen)
        start = p * cut
        in_qkv = max(0, min(cut, 3 * D - start))
        if in_qkv:
            qkv_ref[:, start : start + in_qkv] = chosen[:, :in_qkv]
        if in_qkv < cut:
            at = start + in_qkv - 3 * D
            proj_ref[:, at : at + cut - in_qkv] = chosen[:, in_qkv:]


def unpack_dense(part, pieces, rows, owned):
    heights = (NCH, 4, 2, 1, 1)
    return launch(
        partial(unpack_dense_kernel, len(pieces), rows),
        [part, *pieces],
        [SMEM] + [VM] * len(pieces),
        [VM] * 8,
        [jax.ShapeDtypeStruct((rows, 3 * D), f32), jax.ShapeDtypeStruct((rows, D), f32)]
        + [jax.ShapeDtypeStruct((height, rows), f32) for height in heights]
        + [jax.ShapeDtypeStruct((owned, NCH), f32)],
        scratch_shapes=[pltpu.VMEM((rows, LANES), f32)],
        compiler_params=pltpu.CompilerParams(vmem_limit_bytes=VMEM_BYTES),
        name="unpack_dense",
    )


def last_kernel(
    count,
    shards,
    part_ref,
    dq_ref,
    dk_ref,
    dv_ref,
    x_ref,
    dres_ref,
    small_ref,
    dsmall_ref,
    gain_f_ref,
    prev_ref,
    cvec_ref,
    *refs,
):
    pieces = refs[:count]
    out_ref, small_out, w_ref, gain_ref = refs[count:]

    @pl.when(pl.program_id(0) == 0)
    def _():
        gain_ref[...] = jnp.zeros_like(gain_ref)
        lay_columns(w_ref, pieces, part_ref[0])

    grad = mm_nt(dq_ref[...], w_ref[:, :D])
    grad = grad + mm_nt(dk_ref[...], w_ref[:, D : 2 * D])
    grad = grad + mm_nt(dv_ref[...], w_ref[:, 2 * D :])
    x = x_ref[...].astype(f32)
    inverse = lax.rsqrt(jnp.mean(x * x, axis=-1, keepdims=True) + EPS)
    scaled = grad * row_of(small_ref, GAIN_A)
    mean_dot = jnp.mean(x * scaled, axis=-1, keepdims=True)
    d_x = inverse * scaled - x * (inverse * inverse * inverse * mean_dot)
    out_ref[...] = (dres_ref[...] + d_x).astype(bf16)
    gain_ref[...] += jnp.sum(grad * x * inverse, axis=0, keepdims=True)

    @pl.when(pl.program_id(0) == pl.num_programs(0) - 1)
    def _():
        row = lax.broadcasted_iota(jnp.int32, (LANES, D), 0)
        total = jnp.where(row < CVEC, dsmall_ref[...], 0.0)
        for m in range(2):
            total = jnp.where(row == CVEC + m, cvec_ref[m : m + 1, :], total)
        total = jnp.where(row == GAIN_A, gain_ref[...], total)
        total = jnp.where(row == GAIN_F, gain_f_ref[...], total)
        total = total.T
        owned = NCH // shards
        shard = D // shards
        row = lax.broadcasted_iota(jnp.int32, total.shape, 0)
        lane = lanes_of((NCH, LANES))
        prev = pltpu.roll(jnp.where(lane < NCH, prev_ref[...], 0.0), 16, 1)
        for index in range(NCH):
            at = (index // owned) * shard + index % owned
            total = jnp.where(row == at, total + prev[index : index + 1, :], total)
        small_out[...] = total.astype(bf16)


def last_call(part, shards, dq, dk, dv, x, dres, small, smalls, pieces, after):
    rows = x.shape[0]
    block = 256
    return launch(
        partial(last_kernel, len(pieces), shards),
        [part, dq, dk, dv, x, dres, small, *smalls, *pieces],
        [SMEM]
        + [rows_of(block, D)] * 5
        + [whole(a.shape) for a in (small, *smalls, *pieces)],
        [rows_of(block, D), whole((D, LANES))],
        [jax.ShapeDtypeStruct((rows, D), bf16), jax.ShapeDtypeStruct((D, LANES), bf16)],
        after,
        grid=(rows // block,),
        scratch_shapes=[pltpu.VMEM((D, 3 * D), bf16), pltpu.VMEM((1, D), f32)],
        compiler_params=params(VMEM_BYTES),
        cost_estimate=cost(6 * rows * D * D, 14 * rows * D),
        name="input_grad",
    )


def body(
    replicas,
    shards,
    tokens,
    prev_logits,
    out_grad,
    routes,
    doc_ids,
    valid_mask,
    qkv_weight,
    proj_weight,
    gain_attn,
    gain_ffn,
    router,
    const_mix,
    prev_mix,
    const_vec,
    expert_in,
    expert_out,
):
    me = lax.axis_index("rep")
    zi = lax.axis_index("fsdp")
    copies = replicas // EXPERTS
    mine = me // copies
    part = me % copies
    rows = tokens.shape[0]
    shard = qkv_weight.shape[0]
    hidden = expert_in.shape[2] // 2
    quarter = shard // EXPERTS
    plan = Plan(replicas, shards, shard, hidden, 2)
    zi_s = zi.reshape(1).astype(jnp.int32)
    mine_s = mine.reshape(1).astype(jnp.int32)
    part_s = part.reshape(1).astype(jnp.int32)
    who = jnp.concatenate([mine_s, part_s])

    def to_expert(a, k):
        return lax.ppermute(a, "rep", [(i, i ^ (k * copies)) for i in range(replicas)])

    def to_part(a, m):
        return lax.ppermute(a, "rep", [(i, i ^ m) for i in range(replicas)])

    def spin(a, k):
        return lax.ppermute(a, "fsdp", [(i, (i + k) % shards) for i in range(shards)])

    def by_xor(pieces, own, axis):
        size = pieces[0].shape[axis]
        shape = list(pieces[0].shape)
        shape[axis] = size * len(pieces)
        full = jnp.zeros(shape, pieces[0].dtype)
        for k, piece in enumerate(pieces):
            full = lax.dynamic_update_slice_in_dim(full, piece, (own ^ k) * size, axis)
        return full

    width = 3 * D // copies
    owned = prev_mix.shape[0]
    smalls = [router.T, const_mix.T, const_vec.T, jnp.stack([gain_attn, gain_ffn]), prev_mix]
    piece, mark = cut_dense(who, qkv_weight, proj_weight, smalls, copies)
    spun = [piece] + [spin(piece, k) for k in range(1, shards)]

    docs = doc_ids.reshape(-1)
    drow = docs[None, :]
    dcol = docs[:, None]
    vcol = valid_mask.reshape(-1)[:, None]
    first_place = jnp.sum((drow < dcol).astype(jnp.int32), axis=1)
    offset = (jnp.arange(rows, dtype=jnp.int32) - first_place).astype(f32)
    frequency = jnp.exp(
        jnp.arange(HDIM // 2, dtype=f32) * (-2.0 * math.log(10000.0) / HDIM)
    )
    angles = offset[:, None] * frequency[None, :]
    cosine, sine = jnp.cos(angles), jnp.sin(angles)
    cosine = jnp.concatenate([cosine] * 4, axis=1)
    sine = jnp.concatenate([-sine, sine, -sine, sine], axis=1)

    routes_t = routes.T
    chosen = jnp.where(routes_t < EXPERTS, routes_t ^ mine, routes_t)
    kinds = jnp.arange(EXPERTS, dtype=jnp.int32)
    named = jnp.any(chosen[:, None, :] == kinds[None, :, None], axis=0)
    later = jnp.triu(jnp.ones((rows, rows), bf16), 1)
    rank = mm(named.astype(bf16), later).astype(jnp.int32)
    spot = jnp.where(named, rank, CAP)
    hit = chosen[:, None, :] == kinds[None, :, None]
    places = jnp.sum(jnp.where(hit, (kinds[:, None] * CAP + rank)[None], 0), axis=1)
    places = jnp.where(chosen < EXPERTS, places, -1).T

    tables = (cosine, sine, spot, dcol, vcol, places)
    packed = pack_pieces(plan, who, expert_in, expert_out, (to_part(mark, 1),))
    gathered = [lax.all_gather(p, "fsdp", axis=0, tiled=False) for p in packed]
    qkv_part, proj_part, small, prevs = lay_shards(
        zi_s, spun, shard, quarter, width, tuple(packed)
    )
    pmix = prevs[:, :owned].reshape(NCH, LANES)

    def exchanged(blocks):
        return [blocks[0]] + [to_expert(blocks[k], k) for k in range(1, EXPERTS)]

    def over_parts(half):
        half = half.reshape(D, half.shape[3])
        pieces = [half] + [to_part(half, m) for m in range(1, copies)]
        if half.shape[1] % LANES == 0:
            return pieces
        return [by_xor(pieces, part, 1)]

    ys = dispatch_call(mine_s, spot, out_grad)
    qkv_half = lay_xor(mine_s, exchanged([qkv_part] * EXPERTS), (*tables, ys[0]))
    qkv_pieces = over_parts(qkv_half)
    part_q = part_s if len(qkv_pieces) == copies else jnp.zeros_like(part_s)
    proj_from = exchanged([tie(proj_part, qkv_half)] * EXPERTS)

    prev = prev_logits.T
    h1, q, k, v = qkv_call(part_q, tokens, small, cosine, sine, qkv_pieces, ())
    proj_half = lay_xor(mine_s, tie(proj_from, h1))
    q = tie(q, proj_half)
    proj_pieces = over_parts(proj_half)
    part_p = part_s if len(proj_pieces) == copies else jnp.zeros_like(part_s)
    ys = exchanged(tie(ys, h1))
    ctx, lse = attend_call(q, k, v, dcol, vcol)
    res, h2, one, gates = after_call(
        part_p, ctx, tokens, small, prev, pmix, routes, proj_pieces
    )

    xs = dispatch_call(mine_s, spot, h2, gates)
    h1_t, ctx_t = turn_call([tie(h1, xs[0]), ctx])
    two, spots, cvec_grad = side_call(tie(res, xs[0]), out_grad, one, places, routes, small)
    sent, xs = xs[0], exchanged(tie(xs, ys))
    weights = []
    for chunk, full in enumerate(gathered):
        full = tie(full, xs if chunk else h1)
        weights.append([full] + [to_part(full, m) for m in range(1, copies)])
    weights[0] = tie(weights[0], (h1_t, two))
    xs = tie(xs, weights[1][0])
    carried, turned = None, None
    chunk_grads = []
    for chunk in range(plan.chunks):
        made = expert_call(plan, xs, ys, weights[chunk], chunk, carried)
        if chunk < plan.chunks - 1:
            chunk_grads.append(made[:copies])
            carried = [*made[copies : copies + 2], made[copies + 3]]
            turned = made[copies + 2]
    dx, returned = exchanged(made[:EXPERTS]), made[EXPERTS : 2 * EXPERTS]
    chunk_grads.append(expert_grads(plan, [*made[2 * EXPERTS :], turned, carried[2]]))

    chunk_grads = [
        [grads[0]] + [to_part(grads[m], m) for m in range(1, copies)] for grads in chunk_grads
    ]
    total = fold_copies(tie(chunk_grads[0], returned[0]))

    def over_shards(t):
        return lax.psum_scatter(t, "fsdp", scatter_dimension=0, tiled=False)

    who_p = jnp.concatenate([mine_s, part_p])
    dres, branch, dctx, dsmall, gain_f_grad, prev_grad = back_call(
        who_p,
        res,
        h2,
        out_grad,
        one,
        two,
        spots,
        prev,
        small,
        dx,
        proj_pieces,
        (total,),
    )
    summed = [over_shards(total)]
    summed += [over_shards(fold_copies(tie(grads, branch))) for grads in chunk_grads[1:]]
    ret = exchanged(tie(returned, dx))
    first = tie(summed[0], branch)
    spread = [[first] + [to_expert(first, k) for k in range(1, EXPERTS - 1)]]
    dq, dk, dv = attend_back_call(q, k, v, dctx, lse, dcol, vcol, cosine, sine)
    rights = [tie(dq, ret, spread[0]), dk, dv, branch]
    others = dense_call(copies, shards, part_s, mine_s, h1_t, ctx_t, rights)
    spread[0].append(to_expert(tie(first, others[0]), EXPERTS - 1))
    out = finish_call(res, one, spots, routes, small, tie(ret, others), ())
    got = [to_part(others[m - 1], m) for m in range(1, copies)]
    got = tie(got, (out, summed[1:]))
    quarters = dense_call(copies, shards, part_s, mine_s, h1_t, ctx_t, rights, got)
    def over_copies(pieces):
        stacked = jnp.stack(pieces)
        return [stacked] + [to_part(stacked, m) for m in range(1, copies)]

    spread[0] = over_copies(tie(spread[0], quarters))
    input_grad, smalls = last_call(
        part_q,
        shards,
        dq,
        dk,
        dv,
        tokens,
        tie(dres, quarters),
        small,
        (dsmall, gain_f_grad, prev_grad, cvec_grad),
        qkv_pieces,
        (),
    )
    for piece in summed[1:]:
        piece = tie(piece, smalls)
        spread.append([piece] + [to_expert(piece, k) for k in range(1, EXPERTS - 1)])
    begun = ()
    if plan.seg % LANES == 0:
        begun = unpack_chunk(plan, who, 0, spread[0], begun)
    bands = fold_quarters(zi_s, smalls, exchanged(quarters), tuple(begun))
    for pieces in spread[1:]:
        pieces.append(to_expert(tie(pieces[0], bands), EXPERTS - 1))
    spun = [bands[0]] + [spin(bands[k], k) for k in range(1, shards)]
    spread[1:] = [over_copies(tie(pieces, spun)) for pieces in spread[1:]]
    tail = fold_shards(spun)
    full_in, full_out = unpack_grads(plan, who, spread, begun)
    tail = lay_tail(mine_s, exchanged([tail] * EXPERTS), quarter, (full_out,))
    tails = [tail] + [to_part(tail, m) for m in range(1, copies)]
    qkv_grad, proj_grad, router_t, mix_t, cvec_t, gain_a, gain_f, prev_out = unpack_dense(
        part_s, tails, shard, owned
    )

    return (
        out,
        input_grad,
        qkv_grad,
        proj_grad,
        gain_a[0],
        gain_f[0],
        router_t.T,
        mix_t.T,
        prev_out,
        cvec_t.T,
        full_in,
        full_out,
    )


def solution(mesh):
    replicas, shards = mesh.shape["rep"], mesh.shape["fsdp"]
    split = P(("rep", "fsdp"), None)
    matrix = P("fsdp", None)
    cube = P("fsdp", None, None)
    in_specs = (split,) * 6 + (matrix, matrix, P("fsdp"), P("fsdp")) + (matrix,) * 4 + (cube, cube)
    out_specs = (split, split, matrix, matrix, P("fsdp"), P("fsdp")) + (matrix,) * 4 + (cube, cube)
    return jax.shard_map(
        partial(body, replicas, shards),
        mesh=mesh,
        in_specs=in_specs,
        out_specs=out_specs,
        check_vma=False,
    )
```

```python
from functools import partial
import math

import jax
import jax.numpy as jnp
from jax import lax
from jax.experimental import pallas as pl
from jax.experimental.pallas import tpu as pltpu
from jax.sharding import PartitionSpec as P

D = 768
HEADS = 12
HDIM = 64
EXPERTS = 4
NCH = 8
CAP = 384
LANES = 128
QB = 256
REACH = 512
VMEM_BYTES = 58 * 1024 * 1024
SMALL_BYTES = 24 * 1024 * 1024
EPS = 1e-06
COST_SCALE = 0.02
ATT = 100
BACK = 400
f32 = jnp.float32
bf16 = jnp.bfloat16

NT = (((1,), (1,)), ((), ()))
TN = (((0,), (0,)), ((), ()))


def mm(a, b):
    return jnp.dot(a, b, preferred_element_type=f32)


def mm_nt(a, b):
    return lax.dot_general(a, b, NT, preferred_element_type=f32)


def mm_tn(a, b):
    return lax.dot_general(a, b, TN, preferred_element_type=f32)


def staged(rows, block, *stages):
    spans = [slice(at, at + block) for at in range(0, rows, block)]
    held = [() for _ in spans]
    for stage in stages:
        held = [stage(span, *values) for span, values in zip(spans, held, strict=True)]
    return held


def params(limit=SMALL_BYTES):
    return pltpu.CompilerParams(dimension_semantics=("arbitrary",), vmem_limit_bytes=limit)


def cost(flops, nbytes):
    return pl.CostEstimate(
        flops=int(flops * COST_SCALE), bytes_accessed=int(nbytes * COST_SCALE), transcendentals=0
    )


def launch(kernel, operands, in_specs, out_specs, out_shape, after=(), **kw):
    n, skip = len(operands), len(after)

    def run(*refs):
        kernel(*refs[:n], *refs[n + skip :])

    kw.setdefault("compiler_params", pltpu.CompilerParams(vmem_limit_bytes=SMALL_BYTES))
    return pl.pallas_call(
        run,
        in_specs=list(in_specs) + [pl.BlockSpec(memory_space=pl.ANY)] * skip,
        out_specs=out_specs,
        out_shape=out_shape,
        **kw,
    )(*operands, *after)


def tie(value, *others):
    return lax.optimization_barrier((value, others))[0]


VM = pl.BlockSpec(memory_space=pltpu.VMEM)
SMEM = pl.BlockSpec(memory_space=pltpu.SMEM)
CVEC, GAIN_A, GAIN_F = NCH + 4, NCH + 6, NCH + 7


def row_of(ref, row):
    return ref[:16, :].astype(f32)[row : row + 1]


def whole(shape):
    return pl.BlockSpec(shape, lambda *_: (0,) * len(shape), pipeline_mode=pl.Buffered(1))


def rows_of(block, width):
    return pl.BlockSpec((block, width), lambda i: (i, 0))


def swap_halves(v):
    lane = lax.broadcasted_iota(jnp.int32, v.shape, 1)
    half = HDIM // 2
    ahead = pltpu.roll(v, LANES - half, 1)
    behind = pltpu.roll(v, half, 1)
    return jnp.where(lane % HDIM < half, ahead, behind)


def lay_columns(full_ref, pieces, part):
    width = pieces[0].shape[1]
    for p in range(len(pieces)):
        chosen = pieces[0][...]
        for m in range(1, len(pieces)):
            chosen = jnp.where(part == (p ^ m), pieces[m][...], chosen)
        full_ref[:, p * width : (p + 1) * width] = chosen


def qkv_kernel(count, part_ref, x_ref, small_ref, cos_ref, sin_ref, *refs):
    pieces = refs[:count]
    h_ref, q_ref, k_ref, v_ref, w_ref = refs[count:]

    @pl.when(pl.program_id(0) == 0)
    def _():
        lay_columns(w_ref, pieces, part_ref[0])

    gain = row_of(small_ref, GAIN_A)

    def norm(span):
        x = x_ref[span, :].astype(f32)
        inverse = lax.rsqrt(jnp.mean(x * x, axis=-1, keepdims=True) + EPS)
        h = (x * inverse * gain).astype(bf16)
        h_ref[span, :] = h
        return (h,)

    def project(span, h):
        return (h, mm(h, w_ref[:, :D]))

    def turn(span, mixed, out_ref, scale):
        cosine, sine = cos_ref[span, :], sin_ref[span, :]
        for c in range(0, D, LANES):
            v = mixed[:, c : c + LANES]
            turned = v * cosine + swap_halves(v) * sine
            out_ref[span, c : c + LANES] = (turned.astype(bf16).astype(f32) * scale).astype(bf16)

    def queries(span, h, mixed):
        keys = mm(h, w_ref[:, D : 2 * D])
        turn(span, mixed, q_ref, HDIM**-0.5)
        return h, keys

    def rest(span, h, keys):
        values = mm(h, w_ref[:, 2 * D :])
        turn(span, keys, k_ref, 1.0)
        v_ref[span, :] = values.astype(bf16)
        return ()

    staged(h_ref.shape[0], SUB, norm, project, queries, rest)


def qkv_call(part, x, small, cosine, sine, pieces, after):
    rows = x.shape[0]
    block = 512
    wide = jax.ShapeDtypeStruct((rows, D), bf16)
    return launch(
        partial(qkv_kernel, len(pieces)),
        [part, x, small, cosine, sine, *pieces],
        [
            SMEM,
            rows_of(block, D),
            whole(small.shape),
            rows_of(block, LANES),
            rows_of(block, LANES),
        ]
        + [whole(p.shape) for p in pieces],
        [rows_of(block, D)] * 4,
        [wide] * 4,
        after,
        grid=(rows // block,),
        scratch_shapes=[pltpu.VMEM((D, 3 * D), bf16)],
        compiler_params=params(VMEM_BYTES),
        cost_estimate=cost(2 * rows * D * 3 * D, 2 * (5 * rows * D + 3 * D * D)),
        name="qkv_rope",
    )


PAD_LANE = 6


def fill_masks(query_mask, key_mask, key_mask_own, table, dcol_ref, vcol_ref):
    length = dcol_ref.shape[0]
    lane = lax.broadcasted_iota(jnp.int32, (length, LANES), 1) % HDIM
    docs = dcol_ref[...]
    query_mask[...] = jnp.where((lane == docs) | (lane == PAD_LANE), 1.0, 0.0).astype(bf16)
    other = jnp.where((lane < PAD_LANE) & (lane != docs), -1e30, 0.0)
    key_mask_own[...] = other.astype(bf16)
    padded = (lane == PAD_LANE) & (vcol_ref[...] == 0)
    key_mask[...] = jnp.where(padded, -1e30, other).astype(bf16)
    key = lax.broadcasted_iota(jnp.int32, (QB, QB), 0)
    query = lax.broadcasted_iota(jnp.int32, (QB, QB), 1)
    for i in range(length // QB):
        usable = (vcol_ref[i * QB : (i + 1) * QB, :] > 0) | (key == query)
        table[i] = jnp.where((key <= query) & usable, 0.0, -1e30)


def mask_scratch(length):
    return [pltpu.VMEM((length, LANES), bf16)] * 3 + [pltpu.VMEM((length // QB, QB, QB), f32)]


def per_head(inside, outside):
    lane = lax.broadcasted_iota(jnp.int32, inside.shape, 1)
    return [jnp.where(lane // HDIM == head, inside, outside) for head in range(2)]


def key_blocks(i):
    start = i * QB
    return [start] + list(range(max(0, start - REACH), start, QB))


def attend_kernel(
    q_ref, k_ref, v_ref, dcol_ref, vcol_ref, ctx_ref, lse_ref, q_mask, k_mask, k_own, table
):
    length = q_ref.shape[0]

    @pl.when(pl.program_id(0) == 0)
    def _():
        fill_masks(q_mask, k_mask, k_own, table, dcol_ref, vcol_ref)

    values_t = v_ref[...].astype(f32).T.astype(bf16)
    queries = per_head(q_ref[...], q_mask[...])
    keys = per_head(k_ref[...], k_mask[...])
    own_keys = per_head(k_ref[...], k_own[...])

    def scores_of(i, head):
        start = i * QB
        query = queries[head][start : start + QB]
        scores = [mm_nt(own_keys[head][start : start + QB], query) + table[i]]
        for at in key_blocks(i)[1:]:
            scores.append(mm_nt(keys[head][at : at + QB], query))
        return scores

    def weights_of(i, head, scores):
        largest = scores[0]
        for block in scores[1:]:
            largest = jnp.maximum(largest, block)
        largest = jnp.max(largest, axis=0, keepdims=True)
        raised = [jnp.exp(block - largest) for block in scores]
        total = raised[0]
        for block in raised[1:]:
            total = total + block
        total = jnp.sum(total, axis=0, keepdims=True)
        lse_ref[0, head : head + 1, i * QB : (i + 1) * QB] = largest + jnp.log(total)
        return [block.astype(bf16) for block in raised], total

    def context_of(i, head, raised, total):
        context = 0.0
        for at, block in zip(key_blocks(i), raised, strict=True):
            context = context + mm(
                values_t[head * HDIM : (head + 1) * HDIM, at : at + QB], block
            )
        return context * (1.0 / total)

    units = [(i, head) for i in range(length // QB) for head in range(2)]
    ahead = scores_of(*units[0])
    behind, contexts = None, []
    for index in range(len(units) + 1):
        scores = ahead
        if index + 1 < len(units):
            ahead = scores_of(*units[index + 1])
        made = None
        if index < len(units):
            made = (*units[index], *weights_of(*units[index], scores))
        if behind is not None:
            contexts.append(context_of(*behind))
            if len(contexts) == 2:
                i = behind[0]
                ctx_ref[i * QB : (i + 1) * QB, :] = (
                    jnp.concatenate(contexts, axis=0).T.astype(bf16)
                )
                contexts = []
        behind = made


def attend_call(q, k, v, dcol, vcol):
    length = q.shape[0]
    pairs = HEADS // 2
    column = pl.BlockSpec((length, LANES), lambda p: (0, p))
    return launch(
        attend_kernel,
        [q, k, v, dcol, vcol],
        [column, column, column, whole(dcol.shape), whole(vcol.shape)],
        [column, pl.BlockSpec((1, 2, length), lambda p: (p, 0, 0))],
        [
            jax.ShapeDtypeStruct((length, D), bf16),
            jax.ShapeDtypeStruct((pairs, 2, length), f32),
        ],
        grid=(pairs,),
        scratch_shapes=mask_scratch(length),
        compiler_params=params(VMEM_BYTES),
        cost_estimate=cost(ATT * 20e9, ATT * 8 * length * D),
        name="attend",
    )


def attend_back_kernel(
    q_ref,
    k_ref,
    v_ref,
    g_ref,
    lse_ref,
    dcol_ref,
    vcol_ref,
    cos_ref,
    sin_ref,
    dq_ref,
    dk_ref,
    dv_ref,
    q_mask,
    k_mask,
    k_own,
    table,
    gk_ref,
    gv_ref,
    gq_ref,
):
    length = q_ref.shape[0]

    @pl.when(pl.program_id(0) == 0)
    def _():
        fill_masks(q_mask, k_mask, k_own, table, dcol_ref, vcol_ref)

    keys_t = k_ref[...].astype(f32).T.astype(bf16)
    zero = jnp.zeros(q_ref.shape, bf16)
    queries = per_head(q_ref[...], q_mask[...])
    bare = per_head(q_ref[...], zero)
    grads = per_head(g_ref[...], zero)
    keys = per_head(k_ref[...], k_mask[...])
    own_keys = per_head(k_ref[...], k_own[...])
    begun = set()

    def products_of(i, head):
        start = i * QB
        query = queries[head][start : start + QB]
        grad = grads[head][start : start + QB]
        scores, grad_probs = [], []
        for at in key_blocks(i):
            if at == start:
                scores.append(mm_nt(own_keys[head][at : at + QB], query) + table[i])
            else:
                scores.append(mm_nt(keys[head][at : at + QB], query))
            grad_probs.append(mm_nt(v_ref[at : at + QB, :], grad))
        return scores, grad_probs

    def softmax_back(i, head, scores, grad_probs):
        lse = lse_ref[0, head : head + 1, i * QB : (i + 1) * QB]
        probs = [jnp.exp(block - lse) for block in scores]
        inner = probs[0] * grad_probs[0]
        for p, d in zip(probs[1:], grad_probs[1:], strict=True):
            inner = inner + p * d
        inner = jnp.sum(inner, axis=0, keepdims=True)
        grad_scores = [
            (p * (d - inner)).astype(bf16) for p, d in zip(probs, grad_probs, strict=True)
        ]
        return [p.astype(bf16) for p in probs], grad_scores

    def spread_back(i, head, probs, grad_scores):
        start = i * QB
        grad_q = 0.0
        for at, p, s in zip(key_blocks(i), probs, grad_scores, strict=True):
            grad_v = mm(p, grads[head][start : start + QB])
            grad_k = mm(s, bare[head][start : start + QB])
            if at in begun:
                gv_ref[at : at + QB, :] += grad_v
                gk_ref[at : at + QB, :] += grad_k
            else:
                begun.add(at)
                gv_ref[at : at + QB, :] = grad_v
                gk_ref[at : at + QB, :] = grad_k
            grad_q = grad_q + mm(keys_t[head * HDIM : (head + 1) * HDIM, at : at + QB], s)
        gq_ref[head * HDIM : (head + 1) * HDIM, start : start + QB] = grad_q

    units = [(i, head) for i in range(length // QB) for head in range(2)]
    ahead = products_of(*units[0])
    behind = None
    for index in range(len(units) + 1):
        products = ahead
        if index + 1 < len(units):
            ahead = products_of(*units[index + 1])
        made = None
        if index < len(units):
            made = (*units[index], *softmax_back(*units[index], *products))
        if behind is not None:
            spread_back(*behind)
        behind = made
    cosine, sine = cos_ref[...], sin_ref[...]
    grad_q = gq_ref[...].T * HDIM**-0.5
    grad_k = gk_ref[...]
    dq_ref[...] = (grad_q * cosine - swap_halves(grad_q) * sine).astype(bf16)
    dk_ref[...] = (grad_k * cosine - swap_halves(grad_k) * sine).astype(bf16)
    dv_ref[...] = gv_ref[...].astype(bf16)


def attend_back_call(q, k, v, g, lse, dcol, vcol, cosine, sine):
    length = q.shape[0]
    pairs = HEADS // 2
    column = pl.BlockSpec((length, LANES), lambda p: (0, p))
    return launch(
        attend_back_kernel,
        [q, k, v, g, lse, dcol, vcol, cosine, sine],
        [column] * 4
        + [pl.BlockSpec((1, 2, length), lambda p: (p, 0, 0))]
        + [whole(a.shape) for a in (dcol, vcol, cosine, sine)],
        [column] * 3,
        [jax.ShapeDtypeStruct((length, D), bf16)] * 3,
        grid=(pairs,),
        scratch_shapes=mask_scratch(length)
        + [
            pltpu.VMEM((length, LANES), f32),
            pltpu.VMEM((length, LANES), f32),
            pltpu.VMEM((LANES, length), f32),
        ],
        compiler_params=params(VMEM_BYTES),
        cost_estimate=cost(45e9, 14 * length * D),
        name="attend_back",
    )


def cut_dense_kernel(quarter, widths, who_ref, qkv_ref, proj_ref, *refs):
    smalls, out_ref, mark_ref = refs[:-2], refs[-2], refs[-1]
    mark_ref[...] = qkv_ref[:16, :LANES]
    row = pl.multiple_of(who_ref[0] * quarter, quarter)
    start = 0
    for ref, width in zip((qkv_ref, proj_ref), widths, strict=True):
        column = pl.multiple_of(who_ref[1] * width, LANES)
        out_ref[:quarter, start : start + width] = ref[pl.ds(row, quarter), pl.ds(column, width)]
        start += width
    shard = qkv_ref.shape[0]
    out_ref[quarter:, :] = jnp.zeros((16, start), bf16)
    rows = jnp.concatenate([ref[...].astype(f32) for ref in smalls[:-1]], axis=0)
    out_ref[quarter:, :shard] = rows.astype(bf16)
    prev = smalls[-1]
    out_ref[quarter : quarter + prev.shape[0], 2 * LANES : 2 * LANES + NCH] = prev[...]


def cut_dense(who, qkv, proj, smalls, copies):
    shard = qkv.shape[0]
    quarter = shard // EXPERTS
    widths = (qkv.shape[1] // copies, proj.shape[1] // copies)
    total = sum(widths)
    if quarter % 16 == 0 and all(w % LANES == 0 for w in widths):
        return launch(
            partial(cut_dense_kernel, quarter, widths),
            [who, qkv, proj, *smalls],
            [SMEM] + [VM] * (2 + len(smalls)),
            [VM, VM],
            [
                jax.ShapeDtypeStruct((quarter + 16, total), bf16),
                jax.ShapeDtypeStruct((16, LANES), bf16),
            ],
            compiler_params=pltpu.CompilerParams(vmem_limit_bytes=VMEM_BYTES),
        name="cut_dense",
        )
    row = who[0] * quarter
    cuts = [
        lax.dynamic_slice(w, (row, who[1] * width), (quarter, width))
        for w, width in zip((qkv, proj), widths, strict=True)
    ]
    prev = smalls[-1]
    below = jnp.concatenate(
        [
            jnp.pad(jnp.concatenate(smalls[:-1]), ((0, 0), (0, 2 * LANES - shard))),
            jnp.pad(prev, ((0, 16 - prev.shape[0]), (0, total - 2 * LANES - NCH))),
        ],
        axis=1,
    )
    piece = jnp.concatenate([jnp.concatenate(cuts, axis=1), below])
    return piece, piece[:16, :LANES]


def lay_shards_kernel(count, shard, quarter, width, zi_ref, *refs):
    pieces = refs[:count]
    qkv_ref, proj_ref, small_ref, prev_ref = refs[count:]
    for k in range(count):
        at = lax.rem(zi_ref[0] + count - k, count)
        qkv_ref[at] = pieces[k][:quarter, :width]
        proj_ref[at] = pieces[k][:quarter, width:]
        prev_ref[at] = pieces[k][quarter:, 2 * LANES : 3 * LANES]
    small_ref[16:, :] = jnp.zeros((LANES - 16, D), bf16)
    for z in range(count):
        chosen = pieces[0][quarter:, : 2 * LANES].astype(f32)
        for k in range(1, count):
            here = lax.rem(zi_ref[0] + count - k, count) == z
            chosen = jnp.where(here, pieces[k][quarter:, : 2 * LANES].astype(f32), chosen)
        small_ref[:16, z * shard : (z + 1) * shard] = chosen[:, :shard].astype(bf16)


def lay_shards(zi, pieces, shard, quarter, width, after):
    count = len(pieces)
    return launch(
        partial(lay_shards_kernel, count, shard, quarter, width),
        [zi, *pieces],
        [SMEM] + [VM] * count,
        [VM] * 4,
        [
            jax.ShapeDtypeStruct((count, quarter, width), bf16),
            jax.ShapeDtypeStruct((count, quarter, pieces[0].shape[1] - width), bf16),
            jax.ShapeDtypeStruct((LANES, D), bf16),
            jax.ShapeDtypeStruct((count, 16, LANES), bf16),
        ],
        after,
        compiler_params=pltpu.CompilerParams(vmem_limit_bytes=VMEM_BYTES),
        name="lay_shards",
    )


def lay_xor_kernel(count, own_ref, *refs):
    pieces, out = refs[:count], refs[count]
    for k in range(count):
        out[:, own_ref[0] ^ k] = pieces[k][...]


def lay_xor(own, pieces, after=()):
    count = len(pieces)
    first, rows, columns = pieces[0].shape
    return launch(
        partial(lay_xor_kernel, count),
        [own, *pieces],
        [SMEM] + [VM] * count,
        VM,
        jax.ShapeDtypeStruct((first, count, rows, columns), bf16),
        after,
        name="lay_xor",
    )


def lanes_of(shape):
    return lax.broadcasted_iota(jnp.int32, shape, 1)


def partner(v, lane):
    return jnp.where(lane % 2 == 0, pltpu.roll(v, LANES - 1, 1), pltpu.roll(v, 1, 1))


def selected(choice_ref, lane):
    return (lane == choice_ref[:, 0:1]) | (lane == choice_ref[:, 1:2])


def after_kernel(
    count, part_ref, ctx_ref, x_ref, wsmall_ref, prev_ref, pmix_ref, choice_ref, *refs
):
    pieces = refs[:count]
    res_ref, h_ref, one_ref, gate_ref, w_ref = refs[count:]

    @pl.when(pl.program_id(0) == 0)
    def _():
        lay_columns(w_ref, pieces, part_ref[0])

    gain = row_of(wsmall_ref, GAIN_F)
    lane = lanes_of((SUB, LANES))
    choice = lane < NCH
    is_mix = (lane >= NCH) & (lane < NCH + 4)

    def project(span):
        return (x_ref[span, :].astype(f32) + mm(ctx_ref[span, :], w_ref[...]),)

    def norm(span, res):
        res_ref[span, :] = res
        inverse = lax.rsqrt(jnp.mean(res * res, axis=-1, keepdims=True) + EPS)
        low = (res * inverse * gain).astype(bf16)
        h_ref[span, :] = low
        small = mm_nt(low, wsmall_ref[...])
        return small, small + mm_tn(prev_ref[:, span], pmix_ref[...])

    def route(span, small, logits):
        top = jnp.max(jnp.where(choice, logits, -1e30), axis=-1, keepdims=True)
        raised = jnp.where(choice, jnp.exp(jnp.where(choice, logits - top, 0.0)), 0.0)
        gates = raised / jnp.sum(raised, axis=-1, keepdims=True)
        mixing = 1.0 / (1.0 + jnp.exp(partner(small, lane) - small))
        one_ref[span, :] = jnp.where(choice, gates, jnp.where(is_mix, mixing, 0.0))
        named = (lane == choice_ref[span, 0:1]) | (lane == choice_ref[span, 1:2])
        taken = jnp.where(named, gates, 0.0).T[:NCH]
        high = taken.astype(bf16).astype(f32)
        gate_ref[:, span] = jnp.concatenate([high, taken - high], axis=0).astype(bf16)
        return ()

    staged(res_ref.shape[0], SUB, project, norm, route)


def after_call(part, ctx, x, small, prev, pmix, choices, pieces):
    rows = x.shape[0]
    block = 512
    return launch(
        partial(after_kernel, len(pieces)),
        [part, ctx, x, small, prev, pmix, choices, *pieces],
        [SMEM]
        + [rows_of(block, D)] * 2
        + [
            whole(small.shape),
            pl.BlockSpec((NCH, block), lambda i: (0, i)),
            whole(pmix.shape),
            rows_of(block, 2),
        ]
        + [whole(p.shape) for p in pieces],
        [rows_of(block, D)] * 2
        + [rows_of(block, LANES), pl.BlockSpec((2 * NCH, block), lambda i: (0, i))],
        [
            jax.ShapeDtypeStruct((rows, D), f32),
            jax.ShapeDtypeStruct((rows, D), bf16),
            jax.ShapeDtypeStruct((rows, LANES), f32),
            jax.ShapeDtypeStruct((2 * NCH, rows), bf16),
        ],
        grid=(rows // block,),
        scratch_shapes=[pltpu.VMEM((D, D), bf16)],
        compiler_params=params(),
        cost_estimate=cost(2 * rows * D * D, 10 * rows * D),
        name="after_attention",
    )


EXTRA = 16
SUB = 256
COEF, INVERSE = 16, 17


def dispatch_kernel(gated, mine_ref, spot_ref, v_ref, *refs):
    if gated:
        gate_ref, refs = refs[0], refs[1:]
    rows = v_ref.shape[0]
    slot = lax.broadcasted_iota(jnp.int32, (CAP, rows), 0)
    all_hits = [
        jnp.where(slot == spot_ref[k : k + 1, :], 1.0, 0.0).astype(bf16) for k in range(EXPERTS)
    ]
    for k in range(EXPERTS):
        hits = all_hits[k]
        refs[k][:CAP, :] = mm(hits, v_ref[...]).astype(bf16)
        if gated:
            moved = mm_nt(gate_ref[...], hits)
            row = lax.broadcasted_iota(jnp.int32, moved.shape, 0) % NCH
            moved = jnp.where(row == (mine_ref[0] ^ k), moved, 0.0)
            high = jnp.sum(moved[:NCH], axis=0, keepdims=True)
            rest = jnp.sum(moved[NCH:], axis=0, keepdims=True)
            tail = jnp.concatenate(
                [high, rest, jnp.zeros((EXTRA - 2, CAP), f32)], axis=0
            ).astype(bf16)
            refs[k][CAP:, :CAP] = tail
            refs[k][CAP:, CAP:] = jnp.zeros((EXTRA, D - CAP), bf16)


def dispatch_call(mine, spot, values, gates=None, after=()):
    size = CAP + (0 if gates is None else EXTRA)
    operands = [mine, spot, values] + ([] if gates is None else [gates])
    rows = values.shape[0]
    return launch(
        partial(dispatch_kernel, gates is not None),
        operands,
        [SMEM] + [VM] * (len(operands) - 1),
        [VM] * EXPERTS,
        [jax.ShapeDtypeStruct((size, D), bf16)] * EXPERTS,
        after,
        cost_estimate=cost(2 * rows * D * CAP * EXPERTS, 2 * rows * D + 2 * EXPERTS * CAP * D),
        name="dispatch",
    )


class Plan:
    def __init__(self, replicas, shards, shard, hidden, chunks):
        self.copies = replicas // EXPERTS
        self.shards = shards
        self.shard = shard
        self.hidden = hidden
        self.chunks = chunks
        self.seg = hidden // (shards * self.copies * chunks)
        self.width = self.seg * shards
        self.wide = min(256, self.width)
        self.tiles = self.width // self.wide
        self.spans = self.wide // self.seg
        self.downs = D // self.wide
        self.rows = 2 * self.tiles * shard + self.downs * self.seg

    def column(self, half, tile, span, part, chunk):
        z = tile * self.spans + span
        base = half * self.hidden + z * (self.hidden // self.shards)
        return base + (chunk * self.copies + part) * self.seg

    def down_row(self, part, chunk):
        return (chunk * self.copies + part) * self.seg


def pack_kernel(plan, who_ref, in_ref, out_ref, *packs):
    mine, part = who_ref[0], who_ref[1]
    seg, shard = plan.seg, plan.shard
    step = pl.program_id(0)
    half, z = step // plan.shards, step % plan.shards
    row = pl.multiple_of((half * plan.tiles + z // plan.spans) * shard, shard)
    column = pl.multiple_of(z % plan.spans * seg, seg)
    for e in range(EXPERTS):

        @pl.when(mine == e)
        def _(e=e):
            value = in_ref[:, e, :]
            for chunk in range(plan.chunks):
                at = chunk * plan.copies * seg
                piece = value[:, at : at + seg]
                for p in range(1, plan.copies):
                    at = (chunk * plan.copies + p) * seg
                    piece = jnp.where(part == p, value[:, at : at + seg], piece)
                packs[chunk][pl.ds(row, shard), pl.ds(column, seg)] = piece

        @pl.when((mine == e) & (step == 0))
        def _(e=e):
            for chunk in range(plan.chunks):
                start = 2 * plan.tiles * shard
                at = pl.multiple_of(plan.down_row(part, chunk), seg)
                value = out_ref[pl.ds(at, seg), e, :]
                for down in range(plan.downs):
                    packs[chunk][start + down * seg : start + (down + 1) * seg, :] = value[
                        :, down * plan.wide : (down + 1) * plan.wide
                    ]


def pack_pieces(plan, who, expert_in, expert_out, after):
    if plan.seg % LANES == 0:
        per = plan.hidden // plan.shards
        return launch(
            partial(pack_kernel, plan),
            [who, expert_in, expert_out],
            [
                SMEM,
                pl.BlockSpec((plan.shard, EXPERTS, per), lambda i: (0, 0, i)),
                whole(expert_out.shape),
            ],
            [whole((plan.rows, plan.wide))] * plan.chunks,
            [jax.ShapeDtypeStruct((plan.rows, plan.wide), bf16)] * plan.chunks,
            after,
            grid=(2 * plan.shards,),
            compiler_params=params(VMEM_BYTES),
            cost_estimate=cost(0, 0),
            name="pack",
        )
    mine, part = who[0], who[1:]
    own_in = lax.dynamic_index_in_dim(expert_in, mine, 1, keepdims=False)
    own_out = lax.dynamic_index_in_dim(expert_out, mine, 1, keepdims=False)
    packs = []
    for chunk in range(plan.chunks):
        blocks = []
        for half in range(2):
            for tile in range(plan.tiles):
                spans = [
                    lax.dynamic_slice_in_dim(
                        own_in, plan.column(half, tile, span, part[0], chunk), plan.seg, 1
                    )
                    for span in range(plan.spans)
                ]
                blocks.append(jnp.concatenate(spans, axis=1))
        rows = lax.dynamic_slice_in_dim(own_out, plan.down_row(part[0], chunk), plan.seg, 0)
        blocks += [rows[:, d * plan.wide : (d + 1) * plan.wide] for d in range(plan.downs)]
        packs.append(jnp.concatenate(blocks, axis=0))
    return packs


def unpack_kernel(plan, begun, who_ref, *refs):
    copies, seg = plan.copies, plan.seg
    ins, downs = refs[:copies], refs[copies : 2 * copies]
    in_out, down_out = refs[2 * copies + 2 * begun :]
    mine, part = who_ref[0], who_ref[1]
    step = pl.program_id(0)
    z = step % plan.shards

    def of_replica(arrays, p, index):
        chosen = arrays[0][index].astype(f32)
        for m in range(1, copies):
            chosen = jnp.where(part == (p ^ m), arrays[m][index].astype(f32), chosen)
        return chosen

    for j in range(EXPERTS):
        for p in range(copies):
            chosen = of_replica(ins, p, j ^ mine)
            piece = chosen[:, :seg]
            for span in range(1, plan.spans):
                here = z % plan.spans == span
                piece = jnp.where(here, chosen[:, span * seg : (span + 1) * seg], piece)
            in_out[:, j, p * seg : (p + 1) * seg] = piece

    rows = down_out.shape[0]
    p, at = step // (seg // rows), step % (seg // rows) * rows
    for j in range(EXPERTS):
        for down in range(plan.downs):
            span = pl.ds(pl.multiple_of(down * seg + at, rows), rows)
            chosen = downs[0][j ^ mine, span, :].astype(f32)
            for m in range(1, copies):
                chosen = jnp.where(
                    part == (p ^ m), downs[m][j ^ mine, span, :].astype(f32), chosen
                )
            down_out[:, j, down * plan.wide : (down + 1) * plan.wide] = chosen


def unpack_chunk(plan, who, chunk, sums, begun):
    copies, shards = plan.copies, plan.shards
    per = plan.hidden // shards
    start = 2 * plan.tiles * plan.shard
    down_rows = plan.downs * plan.seg
    both = copies * plan.seg

    def in_block(i):
        return (0, i // shards * plan.tiles + i % shards // plan.spans, 0)

    down_in = pl.BlockSpec(
        (EXPERTS, down_rows, plan.wide),
        lambda i: (0, start // down_rows, 0),
        pipeline_mode=pl.Buffered(1),
    )
    hbm = pl.BlockSpec(memory_space=pl.ANY)
    operands = [who, *sums, *sums, *begun]
    return launch(
        partial(unpack_kernel, plan, len(begun) // 2),
        operands,
        [SMEM]
        + [pl.BlockSpec((EXPERTS, plan.shard, plan.wide), in_block)] * copies
        + [down_in] * copies
        + [hbm] * len(begun),
        [
            pl.BlockSpec((plan.shard, EXPERTS, both), lambda i: (0, 0, i * plan.chunks + chunk)),
            pl.BlockSpec(
                (both // (2 * shards), EXPERTS, D), lambda i: (chunk * 2 * shards + i, 0, 0)
            ),
        ],
        [
            jax.ShapeDtypeStruct((plan.shard, EXPERTS, 2 * plan.hidden), f32),
            jax.ShapeDtypeStruct((per, EXPERTS, D), f32),
        ],
        grid=(2 * shards,),
        input_output_aliases={len(operands) - 2 + i: i for i in range(len(begun))},
        compiler_params=params(VMEM_BYTES),
        cost_estimate=cost(0, 12 * plan.shard * plan.hidden * EXPERTS),
        name="unpack",
    )


def unpack_grads(plan, who, sums, begun):
    if begun:
        for chunk in range(1, plan.chunks):
            begun = unpack_chunk(plan, who, chunk, sums[chunk], begun)
        return begun
    mine, part = who[0], who[1]
    ins, outs = [], []
    for j in range(EXPERTS):
        columns = {}
        rows = []
        for chunk in range(plan.chunks):
            for p in range(plan.copies):
                stacked = jnp.stack(sums[chunk])
                piece = lax.dynamic_index_in_dim(stacked, part ^ p, 0, keepdims=False)
                piece = lax.dynamic_index_in_dim(piece, mine ^ j, 0, keepdims=False)
                for half in range(2):
                    for tile in range(plan.tiles):
                        row = (half * plan.tiles + tile) * plan.shard
                        for span in range(plan.spans):
                            columns[plan.column(half, tile, span, p, chunk)] = piece[
                                row : row + plan.shard, span * plan.seg : (span + 1) * plan.seg
                            ]
                row = 2 * plan.tiles * plan.shard
                rows.append(
                    jnp.concatenate(
                        [
                            piece[row + d * plan.seg : row + (d + 1) * plan.seg]
                            for d in range(plan.downs)
                        ],
                        axis=1,
                    )
                )
        ins.append(jnp.concatenate([columns[c] for c in sorted(columns)], axis=1))
        outs.append(jnp.concatenate(rows, axis=0))
    return jnp.stack(ins, axis=1).astype(f32), jnp.stack(outs, axis=1).astype(f32)


def weight_grads(plan, part, xt, ds, act, grad_gate, grad_up, grads):
    shard, seg, wide, tiles = plan.shard, plan.seg, plan.wide, plan.tiles
    for half, source in ((0, grad_gate), (1, grad_up)):
        for tile in range(tiles):
            made = mm(xt[...], source[part, :, tile * wide : (tile + 1) * wide]).astype(bf16)
            row = (half * tiles + tile) * shard
            for z in range(plan.shards):
                grads[part, z, row : row + shard, :] = made[z * shard : (z + 1) * shard, :]
    for tile in range(tiles):
        made = mm_tn(act[part, :, tile * wide : (tile + 1) * wide], ds[...]).astype(bf16)
        for span in range(plan.spans):
            z = tile * plan.spans + span
            for down in range(plan.downs):
                row = 2 * tiles * shard + down * seg
                grads[part, z, row : row + seg, :] = made[
                    span * seg : (span + 1) * seg, down * wide : (down + 1) * wide
                ]


def expert_kernel(plan, first, last, *refs):
    refs = list(refs)

    def take(n):
        out = refs[:n]
        del refs[:n]
        return out

    copies = plan.copies
    x_refs, y_refs = take(EXPERTS), take(EXPERTS)
    w_refs = take(copies)
    if first:
        carry_in = []
    else:
        carry_in = take(2)
        (ds,) = take(1)
    if last:
        dx_outs, ret_outs, saved = take(EXPERTS), take(EXPERTS), take(3)
    else:
        grad_outs, carry_out, saved = take(copies), take(2), take(2)
    xs, gcol, ret_acc, dx_acc, act_s, dg_s, du_s = take(7)
    waiting = [take(3), take(3)]
    if last:
        y_held, sems = refs
    else:
        ds, xt, grads, sems = refs
    shard, seg, wide, tiles = plan.shard, plan.seg, plan.wide, plan.tiles
    started = []

    def copy(src, dst):
        made = pltpu.make_async_copy(src, dst, sems.at[len(started)])
        started.append(made)
        made.start()
        return made

    carries = [copy(src, dst) for src, dst in zip(carry_in, (ret_acc, dx_acc))]
    if last:
        held = [
            copy(y_refs[k].at[pl.ds(0, CAP)], y_held.at[pl.ds(k * CAP, CAP)])
            for k in range(EXPERTS)
        ]
    for k in range(EXPERTS):
        span = slice(k * CAP, (k + 1) * CAP)
        x = x_refs[k][:CAP, :]
        xs[span, :] = x
        extra = x_refs[k][CAP:, :CAP].astype(f32)
        gate = (extra[0:1] + extra[1:2]).T
        gcol[span, :] = jnp.broadcast_to(gate, (CAP, LANES))
        if not last:
            xt[:, span] = x.astype(f32).T.astype(bf16)
            ds[span, :] = (y_refs[k][:CAP, :].astype(f32) * gate).astype(bf16)
    sends = []
    if not last:
        sends = [copy(src, dst) for src, dst in zip((xt, ds), saved, strict=True)]
    if first:
        ret_acc[...] = jnp.zeros_like(ret_acc)
        dx_acc[...] = jnp.zeros_like(dx_acc)

    def columns(part, half, tile):
        row = (half * tiles + tile) * shard
        return w_refs[part][:, row : row + shard, :].reshape(D, wide)

    def down_columns(part, down):
        row = 2 * tiles * shard + down * seg
        return w_refs[part][:, row : row + seg, :].reshape(plan.width, wide)

    def products(part, b, held):
        span = slice(b * CAP, (b + 1) * CAP)
        x, d = xs[span, :], ds[span, :]
        for tile in range(tiles):
            at = slice(tile * wide, (tile + 1) * wide)
            held[0][:, at] = mm(x, columns(part, 0, tile))
            held[1][:, at] = mm(x, columns(part, 1, tile))
        grad = 0.0
        for down in range(plan.downs):
            grad = grad + mm_nt(
                d[:, down * wide : (down + 1) * wide], down_columns(part, down)
            )
        held[2][...] = grad

    def gating(part, b, held):
        span = slice(b * CAP, (b + 1) * CAP)
        gate, up, grad_act = held[0][...], held[1][...], held[2][...]
        sig = 1.0 / (1.0 + jnp.exp(-gate))
        silu = gate * sig
        act_s[part, span, :] = (silu * up).astype(bf16)
        du_s[part, span, :] = (grad_act * silu).astype(bf16)
        dg_s[part, span, :] = (grad_act * up * (sig + silu * (1.0 - sig))).astype(bf16)

    def back(part, b):
        span = slice(b * CAP, (b + 1) * CAP)
        act = act_s[part, span, :]
        for down in range(plan.downs):
            ret_acc[span, down * wide : (down + 1) * wide] += mm(act, down_columns(part, down))
        total = 0.0
        for tile in range(tiles):
            at = slice(tile * wide, (tile + 1) * wide)
            total = total + mm_nt(dg_s[part, span, at], columns(part, 0, tile))
            total = total + mm_nt(du_s[part, span, at], columns(part, 1, tile))
        dx_acc[span, :] += total

    for part in range(copies):
        products(part, 0, waiting[0])
        for b in range(EXPERTS):
            if b + 1 < EXPERTS:
                products(part, b + 1, waiting[(b + 1) % 2])
            gating(part, b, waiting[b % 2])
            if b > 0:
                if part == 0 and b == 1:
                    for made in carries:
                        made.wait()
                back(part, b - 1)
        back(part, EXPERTS - 1)
        if last:
            sends += [
                copy(src.at[part], dst.at[part])
                for src, dst in zip((act_s, dg_s, du_s), saved, strict=True)
            ]
        else:
            if part == copies - 1:
                sends += [
                    copy(src, dst) for src, dst in zip((ret_acc, dx_acc), carry_out, strict=True)
                ]
            weight_grads(plan, part, xt, ds, act_s, dg_s, du_s, grads)
            sends.append(copy(grads.at[part], grad_outs[part]))
    if last:
        for made in held:
            made.wait()
        for k in range(EXPERTS):
            span = slice(k * CAP, (k + 1) * CAP)
            ret = ret_acc[span, :]
            dgate = jnp.sum(ret * y_held[span, :].astype(f32), axis=-1, keepdims=True)
            dgate = jnp.broadcast_to(dgate, (CAP, LANES)).T[:1]
            ret_outs[k][...] = (ret * gcol[span, :1]).astype(bf16)
            dx_outs[k][:CAP, :] = dx_acc[span, :].astype(bf16)
            high = dgate.astype(bf16).astype(f32)
            tail = jnp.concatenate(
                [high, dgate - high, jnp.zeros((EXTRA - 2, CAP), f32)], axis=0
            ).astype(bf16)
            dx_outs[k][CAP:, :CAP] = tail
            dx_outs[k][CAP:, CAP:] = jnp.zeros((EXTRA, D - CAP), bf16)
    for made in sends:
        made.wait()


def expert_call(plan, xs, ys, weights, chunk, carried):
    first, last = chunk == 0, chunk == plan.chunks - 1
    rows = EXPERTS * CAP
    hbm = pl.BlockSpec(memory_space=pl.ANY)
    copies = plan.copies
    block = pl.BlockSpec(
        (plan.shards, plan.rows, plan.wide),
        lambda i: (0, 0, 0),
        pipeline_mode=pl.Buffered(1),
    )
    in_specs = [whole(a.shape) for a in xs]
    in_specs += [hbm if last else whole(a.shape) for a in ys] + [block] * copies
    operands = list(xs) + list(ys) + list(weights)
    if not first:
        in_specs += [hbm] * 2 + [whole((rows, D))]
        operands += list(carried)
    held = jax.ShapeDtypeStruct((copies, rows, plan.width), bf16)
    if last:
        out_specs = [whole((CAP + EXTRA, D))] * EXPERTS + [whole((CAP, D))] * EXPERTS
        out_shape = [jax.ShapeDtypeStruct((CAP + EXTRA, D), bf16)] * EXPERTS
        out_shape += [jax.ShapeDtypeStruct((CAP, D), bf16)] * EXPERTS
        out_specs += [hbm] * 3
        out_shape += [held] * 3
    else:
        out_specs = [hbm] * (copies + 4)
        out_shape = [jax.ShapeDtypeStruct((plan.shards, plan.rows, plan.wide), bf16)] * copies
        out_shape += [jax.ShapeDtypeStruct((rows, D), f32)] * 2
        out_shape += [
            jax.ShapeDtypeStruct((D, rows), bf16),
            jax.ShapeDtypeStruct((rows, D), bf16),
        ]
    scratch = [
        pltpu.VMEM((rows, D), bf16),
        pltpu.VMEM((rows, LANES), f32),
        pltpu.VMEM((rows, D), f32),
        pltpu.VMEM((rows, D), f32),
    ]
    scratch += [pltpu.VMEM((copies, rows, plan.width), bf16)] * 3
    scratch += [pltpu.VMEM((CAP, plan.width), f32)] * 6
    if last:
        scratch.append(pltpu.VMEM((rows, D), bf16))
    else:
        scratch += [
            pltpu.VMEM((rows, D), bf16),
            pltpu.VMEM((D, rows), bf16),
            pltpu.VMEM((copies, plan.shards, plan.rows, plan.wide), bf16),
        ]
    scratch.append(pltpu.SemaphoreType.DMA((6 + 3 * copies,)))
    return pl.pallas_call(
        partial(expert_kernel, plan, first, last),
        grid=(1,),
        in_specs=in_specs,
        out_specs=out_specs,
        out_shape=out_shape,
        scratch_shapes=scratch,
        compiler_params=params(VMEM_BYTES),
        cost_estimate=cost(
            18 * rows * D * plan.width * copies, 12 * D * plan.width * copies + 12 * rows * D
        ),
        name="experts",
    )(*operands)


def expert_grads_kernel(plan, act, grad_gate, grad_up, xt, ds, *refs):
    outs, (grads, sems) = refs[: plan.copies], refs[plan.copies :]
    sends = []
    for part in range(plan.copies):
        weight_grads(plan, part, xt, ds, act, grad_gate, grad_up, grads)
        sends.append(pltpu.make_async_copy(grads.at[part], outs[part], sems.at[part]))
        sends[-1].start()
    for made in sends:
        made.wait()


def expert_grads(plan, held):
    copies = plan.copies
    packed = (plan.shards, plan.rows, plan.wide)
    return launch(
        partial(expert_grads_kernel, plan),
        list(held),
        [whole(a.shape) for a in held],
        [pl.BlockSpec(memory_space=pl.ANY)] * copies,
        [jax.ShapeDtypeStruct(packed, bf16)] * copies,
        grid=(1,),
        scratch_shapes=[
            pltpu.VMEM((copies, *packed), bf16),
            pltpu.SemaphoreType.DMA((copies,)),
        ],
        compiler_params=params(VMEM_BYTES),
        cost_estimate=cost(0, 0),
        name="expert_grads",
    )


def spots_of(place_ref, rows):
    slot = lax.broadcasted_iota(jnp.int32, (rows, EXPERTS * CAP), 1)
    hit = (slot == place_ref[:, 0:1]) | (slot == place_ref[:, 1:2])
    return jnp.where(hit, 1.0, 0.0).astype(bf16)


def constant_gates(one, chosen, m):
    a0 = one[:, NCH + 2 * m : NCH + 2 * m + 1]
    a1 = one[:, NCH + 2 * m + 1 : NCH + 2 * m + 2]
    gate = chosen[:, EXPERTS + 2 + m : EXPERTS + 3 + m]
    return gate, a0, a1


def side_kernel(
    res_ref, dy_ref, one_ref, place_ref, choice_ref, small_ref, two_ref, spots_ref, cvec_out
):
    @pl.when(pl.program_id(0) == 0)
    def _():
        cvec_out[...] = jnp.zeros_like(cvec_out)

    res = res_ref[...]
    one = one_ref[...]
    lane = lanes_of(one.shape)
    named = selected(choice_ref, lane)
    chosen = jnp.where(named, one, 0.0)
    is_mix = (lane >= NCH) & (lane < NCH + 4)
    spots_ref[...] = spots_of(place_ref, res.shape[0])
    inverse = lax.rsqrt(jnp.mean(res * res, axis=-1, keepdims=True) + EPS)
    dy = dy_ref[...]
    spread = res * inverse * row_of(small_ref, GAIN_F)
    hd = jnp.sum(spread * dy.astype(f32), axis=-1, keepdims=True)
    cd = mm_nt(dy, small_ref[...])
    coef = chosen[:, EXPERTS + 1 : EXPERTS + 2]
    grads = jnp.where(lane == EXPERTS + 1, hd, 0.0)
    made = jnp.zeros_like(one)
    for m in range(2):
        gate, a0, a1 = constant_gates(one, chosen, m)
        dot = cd[:, CVEC + m : CVEC + m + 1]
        coef = coef + gate * a0
        grads = jnp.where(lane == EXPERTS + 2 + m, a0 * hd + a1 * dot, grads)
        grads = jnp.where(lane == NCH + 2 * m, gate * hd, grads)
        grads = jnp.where(lane == NCH + 2 * m + 1, gate * dot, grads)
        made = jnp.where(lane == m, gate * a1, made)
    two = jnp.where(is_mix | named, grads, 0.0)
    two = jnp.where(lane == COEF, coef, two)
    two_ref[...] = jnp.where(lane == INVERSE, inverse, two)
    high = made.astype(bf16)
    rest = (made - high.astype(f32)).astype(bf16)
    cvec_out[...] += mm_tn(high, dy) + mm_tn(rest, dy)


def side_call(res, dy, one, places, choices, small):
    rows = res.shape[0]
    block = 256
    return launch(
        side_kernel,
        [res, dy, one, places, choices, small],
        [rows_of(block, D)] * 2
        + [rows_of(block, LANES)]
        + [rows_of(block, 2)] * 2
        + [whole(small.shape)],
        [rows_of(block, LANES), rows_of(block, EXPERTS * CAP), whole((LANES, D))],
        [
            jax.ShapeDtypeStruct((rows, LANES), f32),
            jax.ShapeDtypeStruct((rows, EXPERTS * CAP), bf16),
            jax.ShapeDtypeStruct((LANES, D), f32),
        ],
        grid=(rows // block,),
        compiler_params=params(VMEM_BYTES),
        cost_estimate=cost(0, 0),
        name="side",
    )


def back_kernel(
    count,
    who_ref,
    res_ref,
    h_ref,
    dy_ref,
    one_ref,
    two_ref,
    spots_ref,
    prev_ref,
    wsmall_ref,
    *refs,
):
    dx_refs, refs = refs[:EXPERTS], refs[EXPERTS:]
    pieces, refs = refs[:count], refs[count:]
    (
        dres_ref,
        branch_ref,
        dctx_ref,
        dsmall_ref,
        gain_out,
        prev_out,
        w_ref,
        dg_ref,
    ) = refs

    @pl.when(pl.program_id(0) == 0)
    def _():
        gain_out[...] = jnp.zeros_like(gain_out)
        prev_out[...] = jnp.zeros_like(prev_out)
        dsmall_ref[...] = jnp.zeros_like(dsmall_ref)
        lay_columns(w_ref, pieces, who_ref[1])
        lane = lanes_of((CAP, LANES))
        for k in range(EXPERTS):
            columns = dx_refs[k][CAP:, :CAP].astype(f32).T
            at = who_ref[0] ^ k
            made = jnp.where(lane == at, columns[:, 0:1], 0.0)
            made = jnp.where(lane == at + 16, columns[:, 1:2], made)
            dg_ref[k * CAP : (k + 1) * CAP, :] = made.astype(bf16)

    gain = row_of(wsmall_ref, GAIN_F)
    lane = lanes_of((SUB, LANES))
    choice = lane < NCH
    is_mix = (lane >= NCH) & (lane < NCH + 4)

    def gather(span):
        spots = spots_ref[span, :]
        from_experts = mm(spots, dg_ref[...])
        moved = mm(spots[:, :CAP], dx_refs[0][:CAP, :])
        for k in range(1, EXPERTS):
            moved = moved + mm(spots[:, k * CAP : (k + 1) * CAP], dx_refs[k][:CAP, :])
        return from_experts, moved

    def route(span, from_experts, moved):
        one, two = one_ref[span, :], two_ref[span, :]
        from_experts = from_experts + pltpu.roll(from_experts, LANES - 16, 1)
        grads = jnp.where(lane < EXPERTS, from_experts, jnp.where(lane < NCH + 4, two, 0.0))
        weighted = one * grads
        mean_choice = jnp.sum(jnp.where(choice, weighted, 0.0), axis=-1, keepdims=True)
        d_logits = jnp.where(choice, one * (grads - mean_choice), 0.0)
        d_mix = one * (grads - (weighted + partner(weighted, lane)))
        low = jnp.where(choice, d_logits, jnp.where(is_mix, d_mix, 0.0)).astype(bf16)
        high = d_logits.astype(bf16)
        rest = (d_logits - high.astype(f32)).astype(bf16)
        return low, high, rest, moved + mm(low, wsmall_ref[...])

    def norm(span, low, high, rest, moved):
        two = two_ref[span, :]
        coef, inverse = two[:, COEF : COEF + 1], two[:, INVERSE : INVERSE + 1]
        res = res_ref[span, :]
        dyf = dy_ref[span, :].astype(f32)
        spread_grad = moved + coef * dyf
        scaled = spread_grad * gain
        mean_dot = jnp.mean(res * scaled, axis=-1, keepdims=True)
        d_res = dyf + inverse * scaled - res * (inverse * inverse * inverse * mean_dot)
        dres_ref[span, :] = d_res
        branch = d_res.astype(bf16)
        branch_ref[span, :] = branch
        by_gain = jnp.sum(spread_grad * (res * inverse), axis=0, keepdims=True)
        return low, high, rest, branch, by_gain

    def project(span, low, high, rest, branch, by_gain):
        dctx_ref[span, :] = mm_nt(branch, w_ref[...]).astype(bf16)
        prev = prev_ref[:, span]
        by_prev = mm(prev, high) + mm(prev, rest)
        return mm_tn(low, h_ref[span, :]), by_gain, by_prev

    for by_small, by_gain, by_prev in staged(res_ref.shape[0], SUB, gather, route, norm, project):
        dsmall_ref[...] += by_small
        gain_out[...] += by_gain
        prev_out[...] += by_prev


def back_call(who, res, h, dy, one, two, spots, prev, small, dx, pieces, after):
    rows = res.shape[0]
    block = 512
    return launch(
        partial(back_kernel, len(pieces)),
        [who, res, h, dy, one, two, spots, prev, small, *dx, *pieces],
        [SMEM]
        + [rows_of(block, D)] * 3
        + [rows_of(block, LANES)] * 2
        + [rows_of(block, EXPERTS * CAP)]
        + [pl.BlockSpec((NCH, block), lambda i: (0, i))]
        + [whole(a.shape) for a in (small, *dx, *pieces)],
        [rows_of(block, D)] * 3
        + [whole((LANES, D)), whole((1, D)), whole((NCH, LANES))],
        [
            jax.ShapeDtypeStruct((rows, D), f32),
            jax.ShapeDtypeStruct((rows, D), bf16),
            jax.ShapeDtypeStruct((rows, D), bf16),
            jax.ShapeDtypeStruct((LANES, D), f32),
            jax.ShapeDtypeStruct((1, D), f32),
            jax.ShapeDtypeStruct((NCH, LANES), f32),
        ],
        after,
        grid=(rows // block,),
        scratch_shapes=[pltpu.VMEM((D, D), bf16), pltpu.VMEM((EXPERTS * CAP, LANES), bf16)],
        compiler_params=params(VMEM_BYTES),
        cost_estimate=cost(BACK * 2 * rows * D * (D + 2048), BACK * 20 * rows * D),
        name="combine_back",
    )


def finish_kernel(res_ref, one_ref, spots_ref, choice_ref, small_ref, *refs):
    ret_refs, out_ref = refs[:EXPERTS], refs[EXPERTS]
    res = res_ref[...]
    one = one_ref[...]
    lane = lanes_of(one.shape)
    chosen = jnp.where(selected(choice_ref, lane), one, 0.0)
    inverse = lax.rsqrt(jnp.mean(res * res, axis=-1, keepdims=True) + EPS)
    total = res
    coef = chosen[:, EXPERTS + 1 : EXPERTS + 2]
    for m in range(2):
        gate, a0, a1 = constant_gates(one, chosen, m)
        coef = coef + gate * a0
        total = total + (gate * a1) * row_of(small_ref, CVEC + m)
    total = total + (coef * inverse) * res * row_of(small_ref, GAIN_F)
    spots = spots_ref[...]
    for k in range(EXPERTS):
        total = total + mm(spots[:, k * CAP : (k + 1) * CAP], ret_refs[k][...])
    out_ref[...] = total.astype(bf16)


def finish_call(res, one, spots, choices, small, ret, after):
    rows = res.shape[0]
    block = 256
    return launch(
        finish_kernel,
        [res, one, spots, choices, small, *ret],
        [rows_of(block, D), rows_of(block, LANES)]
        + [rows_of(block, EXPERTS * CAP), rows_of(block, 2)]
        + [whole(a.shape) for a in (small, *ret)],
        rows_of(block, D),
        jax.ShapeDtypeStruct((rows, D), bf16),
        after,
        grid=(rows // block,),
        compiler_params=params(VMEM_BYTES),
        cost_estimate=cost(2 * rows * D * 1536, 10 * rows * D),
        name="layer_out",
    )


def turn_kernel(count, *refs):
    for source, out in zip(refs[:count], refs[count:], strict=True):
        out[...] = source[...].astype(f32).T.astype(bf16)


def turn_call(arrays):
    rows, columns = arrays[0].shape
    return launch(
        partial(turn_kernel, len(arrays)),
        arrays,
        [pl.BlockSpec((rows, 256), lambda i: (0, i))] * len(arrays),
        [pl.BlockSpec((256, rows), lambda i: (i, 0))] * len(arrays),
        [jax.ShapeDtypeStruct((columns, rows), bf16)] * len(arrays),
        grid=(columns // 256,),
        compiler_params=params(VMEM_BYTES),
        cost_estimate=cost(0, 0),
        name="turn",
    )


def dense_kernel(copies, each, own, part_ref, mine_ref, ht_ref, ct_ref, *refs):
    rights, refs = refs[:4], refs[4:]
    step = pl.program_id(0)
    if own:
        got, outs, total_ref = refs[: copies - 1], refs[copies - 1 : -1], refs[-1]
    else:
        outs = refs
    per = pl.num_programs(0) if own else pl.num_programs(0) // (copies - 1)
    source = (part_ref[0] if own else (step // per + 1) ^ part_ref[0]) * per + step % per
    for index, right in enumerate(rights):
        left = ct_ref if index == 3 else ht_ref

        @pl.when(source // each == index)
        def _(left=left, right=right):
            made = mm(left[...], right[...])
            if own:
                for ref in got:
                    made = made + ref[...].astype(f32)
                total_ref[...] = made.astype(bf16).reshape(total_ref.shape)
            else:
                for m, out in enumerate(outs):
                    if len(outs) == 1:
                        out[...] = made.astype(bf16)
                    else:

                        @pl.when(step // per == m)
                        def _(out=out):
                            out[...] = made.astype(bf16)

    if own:
        for k, out in enumerate(outs):
            out[...] = total_ref[:, mine_ref[0] ^ k]


def dense_call(copies, shards, part, mine, ht, ct, rights, got=None):
    rows = ht.shape[1]
    cut = 4 * D // copies
    step = D // 2 if cut % D == 0 else cut
    per = cut // step
    each = D // step
    quarter = D // (shards * EXPERTS)
    own = got is not None

    def right_block(index):
        def block(i, part_ref, mine_ref):
            replica = part_ref[0] if own else (i // per + 1) ^ part_ref[0]
            return (0, jnp.clip(replica * per + i % per - each * index, 0, each - 1))

        return block

    def other_block(m):
        return lambda i, *_: (0, jnp.clip(i - m * per, 0, per - 1))

    def fixed(shape):
        return pl.BlockSpec(shape, lambda i, *_: (0, 0), pipeline_mode=pl.Buffered(1))

    in_specs = [fixed(ht.shape), fixed(ct.shape)]
    in_specs += [pl.BlockSpec((rows, step), right_block(index)) for index in range(4)]
    if own:
        in_specs += [pl.BlockSpec((D, step), lambda i, *_: (0, i))] * (copies - 1)
        out_specs = [pl.BlockSpec((shards, quarter, step), lambda i, *_: (0, 0, i))] * EXPERTS
        out_shape = [jax.ShapeDtypeStruct((shards, quarter, cut), bf16)] * EXPERTS
        scratch = [pltpu.VMEM((shards, EXPERTS, quarter, step), bf16)]
    else:
        out_specs = [pl.BlockSpec((D, step), other_block(m)) for m in range(copies - 1)]
        out_shape = [jax.ShapeDtypeStruct((D, cut), bf16)] * (copies - 1)
        scratch = []
    return pl.pallas_call(
        partial(dense_kernel, copies, each, own),
        grid_spec=pltpu.PrefetchScalarGridSpec(
            num_scalar_prefetch=2,
            grid=(per if own else per * (copies - 1),),
            in_specs=in_specs,
            out_specs=out_specs,
            scratch_shapes=scratch,
        ),
        out_shape=out_shape,
        compiler_params=params(VMEM_BYTES),
        cost_estimate=cost(8 * rows * D * D, 12 * rows * D + 8 * D * D),
        name="dense_own" if own else "dense_others",
    )(part, mine, ht, ct, *rights, *(got or ()))


def fold_quarters_kernel(count, zi_ref, small_ref, *refs):
    pieces, outs = refs[:count], refs[count:]
    rows, cut = pieces[0].shape[1:]
    spare = outs[0].shape[0] - rows
    for k, out in enumerate(outs):
        at = lax.rem(zi_ref[0] + k, len(outs))
        total = pieces[0][at].astype(f32)
        for piece in pieces[1:]:
            total = total + piece[at].astype(f32)
        out[:rows, :] = total.astype(bf16)
        for c in range(cut // LANES):
            out[rows:, c * LANES : (c + 1) * LANES] = small_ref[at, c * spare : (c + 1) * spare, :]


def fold_quarters(zi, small, pieces, after=()):
    shards, rows, cut = pieces[0].shape
    spare = D // shards * LANES // cut
    return launch(
        partial(fold_quarters_kernel, len(pieces)),
        [zi, small.reshape(shards, D // shards, LANES), *pieces],
        [SMEM] + [VM] * (len(pieces) + 1),
        [VM] * shards,
        [jax.ShapeDtypeStruct((rows + spare, cut), bf16)] * shards,
        after,
        compiler_params=pltpu.CompilerParams(vmem_limit_bytes=VMEM_BYTES),
        name="fold_quarters",
    )


def lay_tail_kernel(count, rows, own_ref, *refs):
    pieces, out = refs[:count], refs[count]
    total = pieces[0][rows:, :].astype(f32)
    for k in range(count):
        at = pl.multiple_of((own_ref[0] ^ k) * rows, rows)
        out[pl.ds(at, rows), :] = pieces[k][:rows, :]
        if k:
            total = total + pieces[k][rows:, :].astype(f32)
    out[count * rows :, :] = total.astype(bf16)


def lay_tail(own, pieces, rows, after):
    count = len(pieces)
    size, cut = pieces[0].shape
    return launch(
        partial(lay_tail_kernel, count, rows),
        [own, *pieces],
        [SMEM] + [VM] * count,
        VM,
        jax.ShapeDtypeStruct((count * rows + size - rows, cut), bf16),
        after,
        compiler_params=pltpu.CompilerParams(vmem_limit_bytes=VMEM_BYTES),
        name="lay_tail",
    )


def fold_copies(pieces):
    total = pieces[0].astype(f32)
    for piece in pieces[1:]:
        total = total + piece.astype(f32)
    return total.astype(bf16)


def fold_shards_kernel(*refs):
    total = refs[0][...].astype(f32)
    for ref in refs[1:-1]:
        total = total + ref[...].astype(f32)
    refs[-1][...] = total.astype(bf16)


def fold_shards(pieces):
    return launch(
        fold_shards_kernel,
        pieces,
        [VM] * len(pieces),
        VM,
        jax.ShapeDtypeStruct(pieces[0].shape, bf16),
        compiler_params=pltpu.CompilerParams(vmem_limit_bytes=VMEM_BYTES),
        name="fold_shards",
    )


def unpack_dense_kernel(count, rows, part_ref, *refs):
    pieces = refs[:count]
    qkv_ref, proj_ref, router_ref, mix_ref, cvec_ref, gain_a_ref, gain_f_ref, prev_ref = refs[count:-1]
    small_ref = refs[-1]
    cut = pieces[0].shape[1]
    small = pieces[0][rows:, :].astype(f32)
    for piece in pieces[1:]:
        small = small + piece[rows:, :].astype(f32)
    spare = small.shape[0]
    for c in range(cut // LANES):
        small_ref[c * spare : (c + 1) * spare, :] = small[:, c * LANES : (c + 1) * LANES]
    turned = small_ref[...].T
    router_ref[...] = turned[:NCH]
    mix_ref[...] = turned[NCH:CVEC]
    cvec_ref[...] = turned[CVEC:GAIN_A]
    gain_a_ref[...] = turned[GAIN_A:GAIN_F]
    gain_f_ref[...] = turned[GAIN_F : GAIN_F + 1]
    prev_ref[...] = small_ref[: prev_ref.shape[0], 16 : 16 + NCH]
    for p in range(count):
        chosen = pieces[0][:rows, :].astype(f32)
        for m in range(1, count):
            chosen = jnp.where(part_ref[0] == (p ^ m), pieces[m][:rows, :].astype(f32), chosen)
        start = p * cut
        in_qkv = max(0, min(cut, 3 * D - start))
        if in_qkv:
            qkv_ref[:, start : start + in_qkv] = chosen[:, :in_qkv]
        if in_qkv < cut:
            at = start + in_qkv - 3 * D
            proj_ref[:, at : at + cut - in_qkv] = chosen[:, in_qkv:]


def unpack_dense(part, pieces, rows, owned):
    heights = (NCH, 4, 2, 1, 1)
    return launch(
        partial(unpack_dense_kernel, len(pieces), rows),
        [part, *pieces],
        [SMEM] + [VM] * len(pieces),
        [VM] * 8,
        [jax.ShapeDtypeStruct((rows, 3 * D), f32), jax.ShapeDtypeStruct((rows, D), f32)]
        + [jax.ShapeDtypeStruct((height, rows), f32) for height in heights]
        + [jax.ShapeDtypeStruct((owned, NCH), f32)],
        scratch_shapes=[pltpu.VMEM((rows, LANES), f32)],
        compiler_params=pltpu.CompilerParams(vmem_limit_bytes=VMEM_BYTES),
        name="unpack_dense",
    )


def last_kernel(
    count,
    shards,
    part_ref,
    dq_ref,
    dk_ref,
    dv_ref,
    x_ref,
    dres_ref,
    small_ref,
    dsmall_ref,
    gain_f_ref,
    prev_ref,
    cvec_ref,
    *refs,
):
    pieces = refs[:count]
    out_ref, small_out, w_ref, gain_ref = refs[count:]

    @pl.when(pl.program_id(0) == 0)
    def _():
        gain_ref[...] = jnp.zeros_like(gain_ref)
        lay_columns(w_ref, pieces, part_ref[0])

    grad = mm_nt(dq_ref[...], w_ref[:, :D])
    grad = grad + mm_nt(dk_ref[...], w_ref[:, D : 2 * D])
    grad = grad + mm_nt(dv_ref[...], w_ref[:, 2 * D :])
    x = x_ref[...].astype(f32)
    inverse = lax.rsqrt(jnp.mean(x * x, axis=-1, keepdims=True) + EPS)
    scaled = grad * row_of(small_ref, GAIN_A)
    mean_dot = jnp.mean(x * scaled, axis=-1, keepdims=True)
    d_x = inverse * scaled - x * (inverse * inverse * inverse * mean_dot)
    out_ref[...] = (dres_ref[...] + d_x).astype(bf16)
    gain_ref[...] += jnp.sum(grad * x * inverse, axis=0, keepdims=True)

    @pl.when(pl.program_id(0) == pl.num_programs(0) - 1)
    def _():
        row = lax.broadcasted_iota(jnp.int32, (LANES, D), 0)
        total = jnp.where(row < CVEC, dsmall_ref[...], 0.0)
        for m in range(2):
            total = jnp.where(row == CVEC + m, cvec_ref[m : m + 1, :], total)
        total = jnp.where(row == GAIN_A, gain_ref[...], total)
        total = jnp.where(row == GAIN_F, gain_f_ref[...], total)
        total = total.T
        owned = NCH // shards
        shard = D // shards
        row = lax.broadcasted_iota(jnp.int32, total.shape, 0)
        lane = lanes_of((NCH, LANES))
        prev = pltpu.roll(jnp.where(lane < NCH, prev_ref[...], 0.0), 16, 1)
        for index in range(NCH):
            at = (index // owned) * shard + index % owned
            total = jnp.where(row == at, total + prev[index : index + 1, :], total)
        small_out[...] = total.astype(bf16)


def last_call(part, shards, dq, dk, dv, x, dres, small, smalls, pieces, after):
    rows = x.shape[0]
    block = 256
    return launch(
        partial(last_kernel, len(pieces), shards),
        [part, dq, dk, dv, x, dres, small, *smalls, *pieces],
        [SMEM]
        + [rows_of(block, D)] * 5
        + [whole(a.shape) for a in (small, *smalls, *pieces)],
        [rows_of(block, D), whole((D, LANES))],
        [jax.ShapeDtypeStruct((rows, D), bf16), jax.ShapeDtypeStruct((D, LANES), bf16)],
        after,
        grid=(rows // block,),
        scratch_shapes=[pltpu.VMEM((D, 3 * D), bf16), pltpu.VMEM((1, D), f32)],
        compiler_params=params(VMEM_BYTES),
        cost_estimate=cost(6 * rows * D * D, 14 * rows * D),
        name="input_grad",
    )


def body(
    replicas,
    shards,
    tokens,
    prev_logits,
    out_grad,
    routes,
    doc_ids,
    valid_mask,
    qkv_weight,
    proj_weight,
    gain_attn,
    gain_ffn,
    router,
    const_mix,
    prev_mix,
    const_vec,
    expert_in,
    expert_out,
):
    me = lax.axis_index("rep")
    zi = lax.axis_index("fsdp")
    copies = replicas // EXPERTS
    mine = me // copies
    part = me % copies
    rows = tokens.shape[0]
    shard = qkv_weight.shape[0]
    hidden = expert_in.shape[2] // 2
    quarter = shard // EXPERTS
    plan = Plan(replicas, shards, shard, hidden, 2)
    zi_s = zi.reshape(1).astype(jnp.int32)
    mine_s = mine.reshape(1).astype(jnp.int32)
    part_s = part.reshape(1).astype(jnp.int32)
    who = jnp.concatenate([mine_s, part_s])

    def to_expert(a, k):
        return lax.ppermute(a, "rep", [(i, i ^ (k * copies)) for i in range(replicas)])

    def to_part(a, m):
        return lax.ppermute(a, "rep", [(i, i ^ m) for i in range(replicas)])

    def spin(a, k):
        return lax.ppermute(a, "fsdp", [(i, (i + k) % shards) for i in range(shards)])

    def by_xor(pieces, own, axis):
        size = pieces[0].shape[axis]
        shape = list(pieces[0].shape)
        shape[axis] = size * len(pieces)
        full = jnp.zeros(shape, pieces[0].dtype)
        for k, piece in enumerate(pieces):
            full = lax.dynamic_update_slice_in_dim(full, piece, (own ^ k) * size, axis)
        return full

    width = 3 * D // copies
    owned = prev_mix.shape[0]
    smalls = [router.T, const_mix.T, const_vec.T, jnp.stack([gain_attn, gain_ffn]), prev_mix]
    piece, mark = cut_dense(who, qkv_weight, proj_weight, smalls, copies)
    spun = [piece] + [spin(piece, k) for k in range(1, shards)]

    docs = doc_ids.reshape(-1)
    drow = docs[None, :]
    dcol = docs[:, None]
    vcol = valid_mask.reshape(-1)[:, None]
    first_place = jnp.sum((drow < dcol).astype(jnp.int32), axis=1)
    offset = (jnp.arange(rows, dtype=jnp.int32) - first_place).astype(f32)
    frequency = jnp.exp(
        jnp.arange(HDIM // 2, dtype=f32) * (-2.0 * math.log(10000.0) / HDIM)
    )
    angles = offset[:, None] * frequency[None, :]
    cosine, sine = jnp.cos(angles), jnp.sin(angles)
    cosine = jnp.concatenate([cosine] * 4, axis=1)
    sine = jnp.concatenate([-sine, sine, -sine, sine], axis=1)

    routes_t = routes.T
    chosen = jnp.where(routes_t < EXPERTS, routes_t ^ mine, routes_t)
    kinds = jnp.arange(EXPERTS, dtype=jnp.int32)
    named = jnp.any(chosen[:, None, :] == kinds[None, :, None], axis=0)
    later = jnp.triu(jnp.ones((rows, rows), bf16), 1)
    rank = mm(named.astype(bf16), later).astype(jnp.int32)
    spot = jnp.where(named, rank, CAP)
    hit = chosen[:, None, :] == kinds[None, :, None]
    places = jnp.sum(jnp.where(hit, (kinds[:, None] * CAP + rank)[None], 0), axis=1)
    places = jnp.where(chosen < EXPERTS, places, -1).T

    tables = (cosine, sine, spot, dcol, vcol, places)
    packed = pack_pieces(plan, who, expert_in, expert_out, (to_part(mark, 1),))
    gathered = [lax.all_gather(p, "fsdp", axis=0, tiled=False) for p in packed]
    qkv_part, proj_part, small, prevs = lay_shards(
        zi_s, spun, shard, quarter, width, tuple(packed)
    )
    pmix = prevs[:, :owned].reshape(NCH, LANES)

    def exchanged(blocks):
        return [blocks[0]] + [to_expert(blocks[k], k) for k in range(1, EXPERTS)]

    def over_parts(half):
        half = half.reshape(D, half.shape[3])
        pieces = [half] + [to_part(half, m) for m in range(1, copies)]
        if half.shape[1] % LANES == 0:
            return pieces
        return [by_xor(pieces, part, 1)]

    ys = dispatch_call(mine_s, spot, out_grad)
    qkv_half = lay_xor(mine_s, exchanged([qkv_part] * EXPERTS), (*tables, ys[0]))
    qkv_pieces = over_parts(qkv_half)
    part_q = part_s if len(qkv_pieces) == copies else jnp.zeros_like(part_s)
    proj_from = exchanged([tie(proj_part, qkv_half)] * EXPERTS)

    prev = prev_logits.T
    h1, q, k, v = qkv_call(part_q, tokens, small, cosine, sine, qkv_pieces, ())
    proj_half = lay_xor(mine_s, tie(proj_from, h1))
    q = tie(q, proj_half)
    proj_pieces = over_parts(proj_half)
    part_p = part_s if len(proj_pieces) == copies else jnp.zeros_like(part_s)
    ys = exchanged(tie(ys, h1))
    ctx, lse = attend_call(q, k, v, dcol, vcol)
    res, h2, one, gates = after_call(
        part_p, ctx, tokens, small, prev, pmix, routes, proj_pieces
    )

    xs = dispatch_call(mine_s, spot, h2, gates)
    h1_t, ctx_t = turn_call([tie(h1, xs[0]), ctx])
    two, spots, cvec_grad = side_call(tie(res, xs[0]), out_grad, one, places, routes, small)
    sent, xs = xs[0], exchanged(tie(xs, ys))
    weights = []
    for chunk, full in enumerate(gathered):
        full = tie(full, xs if chunk else h1)
        weights.append([full] + [to_part(full, m) for m in range(1, copies)])
    weights[0] = tie(weights[0], (h1_t, two))
    xs = tie(xs, weights[1][0])
    carried, turned = None, None
    chunk_grads = []
    for chunk in range(plan.chunks):
        made = expert_call(plan, xs, ys, weights[chunk], chunk, carried)
        if chunk < plan.chunks - 1:
            chunk_grads.append(made[:copies])
            carried = [*made[copies : copies + 2], made[copies + 3]]
            turned = made[copies + 2]
    dx, returned = exchanged(made[:EXPERTS]), made[EXPERTS : 2 * EXPERTS]
    chunk_grads.append(expert_grads(plan, [*made[2 * EXPERTS :], turned, carried[2]]))

    chunk_grads = [
        [grads[0]] + [to_part(grads[m], m) for m in range(1, copies)] for grads in chunk_grads
    ]
    total = fold_copies(tie(chunk_grads[0], returned[0]))

    def over_shards(t):
        return lax.psum_scatter(t, "fsdp", scatter_dimension=0, tiled=False)

    who_p = jnp.concatenate([mine_s, part_p])
    dres, branch, dctx, dsmall, gain_f_grad, prev_grad = back_call(
        who_p,
        res,
        h2,
        out_grad,
        one,
        two,
        spots,
        prev,
        small,
        dx,
        proj_pieces,
        (total,),
    )
    summed = [over_shards(total)]
    summed += [over_shards(fold_copies(tie(grads, branch))) for grads in chunk_grads[1:]]
    ret = exchanged(tie(returned, dx))
    first = tie(summed[0], branch)
    spread = [[first] + [to_expert(first, k) for k in range(1, EXPERTS - 1)]]
    dq, dk, dv = attend_back_call(q, k, v, dctx, lse, dcol, vcol, cosine, sine)
    rights = [tie(dq, ret, spread[0]), dk, dv, branch]
    others = dense_call(copies, shards, part_s, mine_s, h1_t, ctx_t, rights)
    spread[0].append(to_expert(tie(first, others[0]), EXPERTS - 1))
    out = finish_call(res, one, spots, routes, small, tie(ret, others), ())
    got = [to_part(others[m - 1], m) for m in range(1, copies)]
    got = tie(got, (out, summed[1:]))
    quarters = dense_call(copies, shards, part_s, mine_s, h1_t, ctx_t, rights, got)
    def over_copies(pieces):
        stacked = jnp.stack(pieces)
        return [stacked] + [to_part(stacked, m) for m in range(1, copies)]

    spread[0] = over_copies(tie(spread[0], quarters))
    input_grad, smalls = last_call(
        part_q,
        shards,
        dq,
        dk,
        dv,
        tokens,
        tie(dres, quarters),
        small,
        (dsmall, gain_f_grad, prev_grad, cvec_grad),
        qkv_pieces,
        (),
    )
    for piece in summed[1:]:
        piece = tie(piece, smalls)
        spread.append([piece] + [to_expert(piece, k) for k in range(1, EXPERTS - 1)])
    begun = ()
    if plan.seg % LANES == 0:
        begun = unpack_chunk(plan, who, 0, spread[0], begun)
    bands = fold_quarters(zi_s, smalls, exchanged(quarters), tuple(begun))
    for pieces in spread[1:]:
        pieces.append(to_expert(tie(pieces[0], bands), EXPERTS - 1))
    spun = [bands[0]] + [spin(bands[k], k) for k in range(1, shards)]
    spread[1:] = [over_copies(tie(pieces, spun)) for pieces in spread[1:]]
    tail = fold_shards(spun)
    full_in, full_out = unpack_grads(plan, who, spread, begun)
    tail = lay_tail(mine_s, exchanged([tail] * EXPERTS), quarter, (full_out,))
    tails = [tail] + [to_part(tail, m) for m in range(1, copies)]
    qkv_grad, proj_grad, router_t, mix_t, cvec_t, gain_a, gain_f, prev_out = unpack_dense(
        part_s, tails, shard, owned
    )

    return (
        out,
        input_grad,
        qkv_grad,
        proj_grad,
        gain_a[0],
        gain_f[0],
        router_t.T,
        mix_t.T,
        prev_out,
        cvec_t.T,
        full_in,
        full_out,
    )


def solution(mesh):
    replicas, shards = mesh.shape["rep"], mesh.shape["fsdp"]
    split = P(("rep", "fsdp"), None)
    matrix = P("fsdp", None)
    cube = P("fsdp", None, None)
    in_specs = (split,) * 6 + (matrix, matrix, P("fsdp"), P("fsdp")) + (matrix,) * 4 + (cube, cube)
    out_specs = (split, split, matrix, matrix, P("fsdp"), P("fsdp")) + (matrix,) * 4 + (cube, cube)
    return jax.shard_map(
        partial(body, replicas, shards),
        mesh=mesh,
        in_specs=in_specs,
        out_specs=out_specs,
        check_vma=False,
    )
```
